128 devices in a mesh: ctx: 32 (over y, x, core), tp: 4 (over z).
Axes of the slice: x: 4, y: 4, z: 4, core: 2. Of those that a mesh axis runs over, the one named last changes fastest.
Arguments:
- block_input: float32 [8192, 1536], P('ctx'), may hold values from -6 to 6
- gain_in: bfloat16 [1536], replicated, may hold values from 0.5 to 1.5
- w_query: bfloat16 [1536, 1536], P(None, 'tp'), may hold values from -0.15625 to 0.15625
- w_key: bfloat16 [1536, 1536], P(None, 'tp'), may hold values from -0.15625 to 0.15625
- w_value: bfloat16 [1536, 1536], P(None, 'tp'), may hold values from -0.15625 to 0.15625
- w_path: bfloat16 [1536, 1536], P(None, 'tp'), may hold values from -0.15625 to 0.15625
- w_beta: bfloat16 [1536, 12], P(None, 'tp'), may hold values from -0.15625 to 0.15625
- w_out: bfloat16 [1536, 1536], P('tp'), may hold values from -0.15625 to 0.15625
- gain_mid: bfloat16 [1536], replicated, may hold values from 0.5 to 1.5
- w_gate: bfloat16 [1536, 4096], P(None, 'tp'), may hold values from -0.15625 to 0.15625
- w_up: bfloat16 [1536, 4096], P(None, 'tp'), may hold values from -0.15625 to 0.15625
- w_down: bfloat16 [4096, 1536], P('tp'), may hold values from -0.09375 to 0.09375
- out_grad: float32 [8192, 1536], P('ctx'), may hold values from -6 to 6
- lengths: int32 [3], replicated, may hold values from 1 to 8064, 8192 in all
Outputs:
- block_output: float32 [8192, 1536], P('ctx')
- input_grad: float32 [8192, 1536], P('ctx')
- gain_in_grad: float32 [1536], P('ctx')
- query_grad: float32 [1536, 1536], P('ctx', 'tp')
- key_grad: float32 [1536, 1536], P('ctx', 'tp')
- value_grad: float32 [1536, 1536], P('ctx', 'tp')
- path_grad: float32 [1536, 1536], P('ctx', 'tp')
- beta_grad: float32 [1536, 12], P('ctx', 'tp')
- out_proj_grad: float32 [1536, 1536], P('tp', 'ctx')
- gain_mid_grad: float32 [1536], P('ctx')
- gate_grad: float32 [1536, 4096], P('ctx', 'tp')
- up_grad: float32 [1536, 4096], P('ctx', 'tp')
- down_grad: float32 [4096, 1536], P('tp', 'ctx')
The draws below stay inside these ranges and needn't reach their ends.
Inputs may be any that keep to these rules, and one draw needn't show every extreme that they name: `lengths`: the 3 sequences lie end to end and fill all 8192 tokens; the longest holds exactly 8064 tokens.
All inputs are finite; a program needn't handle non-finite values.
Results may differ from the reference program's by a relative error of at most 0.0085.
The reference program's roundings to bfloat16 on the way count: a program that leaves them out, or rounds other values in their place, can miss the bound.
Values sent between devices are 32-bit elements; how exact they have to be, the bound alone decides.
No kernel may reach another device: no remote copies, remote signals or barrier semaphores. Data moves between devices by JAX's collectives and lax.ppermute only.
A program may use at most 192 MiB of HBM per device.

```python
import math
import jax
import jax.numpy as jnp
import numpy as np
from jax import lax

D = 1536
HEADS = 12
HS = 128
FF = 4096
TOK_DEV = 256
SEQS = 3
TOKENS = 8192


def shard_levels(stream_key, extent, split, smallest, high):
    def one(axis_at, shards_of):
        steps = jax.random.uniform(jax.random.fold_in(jax.random.fold_in(stream_key, 6), axis_at), (shards_of,), jnp.float32, smallest / len(split), high / len(split))
        return jnp.repeat(jnp.exp(steps), extent[axis_at] // shards_of).reshape((-1,) + (1,) * (len(extent) - axis_at - 1))

    loudness = one(*split[0])
    for cut in split[1:]:
        loudness = loudness * one(*cut)
    return loudness


def split_up(number_of, total, bound, skew):
    weights = [(1 << 20) // math.isqrt(rank ** skew) + 1 for rank in range(2, number_of + 1)]
    surplus, counts = total - bound - (number_of - 1), [1] * (number_of - 1)
    while surplus > 0:
        candidates = [i for i in range(number_of - 1) if counts[i] < bound]
        whole, budget = sum([weights[i] for i in candidates]), surplus
        for i in candidates:
            more = min(bound - counts[i], max(1, budget * weights[i] // whole), surplus)
            counts[i] = counts[i] + more
            surplus = surplus - more
    return np.array([bound] + counts)


def uneven_parts(rng, amount, total, most, skew):
    if amount == 2:
        one = jax.random.randint(rng, (), max(1, total - most), min(most, total - 1) + 1)
        return jnp.stack([one, total - one])
    tallies = jnp.asarray(split_up(amount, total, most, skew), jnp.int32)
    pairs = (amount - 1) // 2
    source_of, sink = tallies[1:1 + 2 * pairs:2], tallies[2:2 + 2 * pairs:2]
    margin = jnp.minimum(source_of - 1, most - sink)
    moved = jax.random.randint(jax.random.fold_in(rng, 1), (pairs,), 0, 1 << 20) % (margin + 1)
    tallies = tallies.at[1:1 + 2 * pairs:2].set(source_of - moved).at[2:2 + 2 * pairs:2].set(sink + moved)
    return tallies[jax.random.permutation(jax.random.fold_in(rng, 2), amount)]


def noise(stream_key, shape, scale, bound, cuts=(), held_as=jnp.bfloat16):
    level = shard_levels(stream_key, shape, cuts, -0.22, 0.18) if cuts else 1.0
    drawn = jax.random.normal(stream_key, shape, jnp.float32) * scale * level
    return jnp.minimum(jnp.maximum(drawn, -bound), bound).astype(held_as)


def setup_inputs(seed: int = 0) -> dict:
    key_of = jax.random.split(jax.random.key(seed), 15)
    return {
        "block_input": noise(key_of[0], (TOKENS, D), 1.0, 6.0, ((0, 32),), jnp.float32),
        "gain_in": jnp.clip(1.0 + 0.1 * jax.random.normal(key_of[1], (D,), jnp.float32), 0.5, 1.5).astype(jnp.bfloat16),
        "w_query": noise(key_of[2], (D, HEADS * HS), D ** -0.5, 0.15625, ((1, 4),)),
        "w_key": noise(key_of[3], (D, HEADS * HS), D ** -0.5, 0.15625, ((1, 4),)),
        "w_value": noise(key_of[4], (D, HEADS * HS), D ** -0.5, 0.15625, ((1, 4),)),
        "w_path": noise(key_of[5], (D, HEADS * HS), D ** -0.5, 0.15625, ((1, 4),)),
        "w_beta": noise(key_of[6], (D, HEADS), D ** -0.5, 0.15625, ((1, 4),)),
        "w_out": noise(key_of[7], (HEADS * HS, D), (HEADS * HS) ** -0.5, 0.15625, ((0, 4),)),
        "gain_mid": jnp.clip(1.0 + 0.1 * jax.random.normal(key_of[8], (D,), jnp.float32), 0.5, 1.5).astype(jnp.bfloat16),
        "w_gate": noise(key_of[9], (D, FF), D ** -0.5, 0.15625, ((1, 4),)),
        "w_up": noise(key_of[10], (D, FF), D ** -0.5, 0.15625, ((1, 4),)),
        "w_down": noise(key_of[11], (FF, D), FF ** -0.5, 0.09375, ((0, 4),)),
        "out_grad": noise(key_of[12], (TOKENS, D), 1.0, 6.0, ((0, 32),), jnp.float32),
        "lengths": uneven_parts(key_of[13], SEQS, TOKENS, TOKENS - TOK_DEV // 2, 0).astype(jnp.int32),
    }


EPSILON = 1e-06
HEAD_EPSILON = 0.01
HIGHEST = lax.Precision.HIGHEST

@jax.custom_vjp
def low(v):
    return lax.optimization_barrier(v.astype(jnp.bfloat16)).astype(jnp.float32)

@jax.custom_vjp
def low_back(v):
    return v

def low_keep(v):
    return (low(v), None)

def low_pass(kept, grad):
    return (grad,)

def back_keep(v):
    return (v, None)

def back_low(kept, grad):
    return (low(grad),)
low.defvjp(low_keep, low_pass)
low_back.defvjp(back_keep, back_low)

def rms_scale(values, gain_vec):
    return values * lax.rsqrt(lax.optimization_barrier(jnp.mean(values * values, axis=-1, keepdims=True)) + EPSILON) * gain_vec

def unit_rows(values):
    return values * lax.rsqrt(lax.optimization_barrier(jnp.sum(values * values, axis=-1, keepdims=True)) + EPSILON)

def segment_of(positions, lengths):
    starts = jnp.cumsum(lengths) - lengths
    return lax.optimization_barrier(jnp.sum((starts[None, :] <= positions[:, None]).astype(jnp.int32), axis=1)) - 1

def masks_of(segment, previous, dtype):
    carry_in = (segment == previous).astype(dtype)
    same_seq = segment[:, None] == segment[None, :]
    last_seq = (segment == segment[-1]).astype(dtype)
    return (carry_in, same_seq, last_seq)

def block_parts(query, keys, values, paths, strength, same_seq, last_seq, carry_all):
    length = query.shape[0]
    head_width = query.shape[1]
    indices = jnp.arange(length)
    up_to = indices[:, None] <= indices[None, :]
    later_mask = indices[:, None] < indices[None, :]
    gram_matrix = jnp.dot(paths, paths.T, precision=HIGHEST)
    left_side = jnp.where(later_mask, gram_matrix, 0.0) + jnp.diag(1.0 / strength)
    identity_rows = jnp.eye(length, dtype=query.dtype)
    inverse = jax.scipy.linalg.solve_triangular(left_side, identity_rows, lower=False)
    paths_query = jnp.where(up_to, jnp.dot(paths, query.T, precision=HIGHEST), 0.0)
    coefficient = jnp.dot(inverse, paths_query, precision=HIGHEST)
    turned_query = query - jnp.dot(coefficient.T, paths, precision=HIGHEST)
    keys_paths = jnp.where(later_mask, jnp.dot(keys, paths.T, precision=HIGHEST), 0.0)
    folded = jnp.dot(keys_paths, inverse, precision=HIGHEST)
    turned_keys = keys - jnp.dot(folded, paths, precision=HIGHEST)
    scores = jnp.dot(keys, query.T, precision=HIGHEST) - jnp.dot(folded, paths_query, precision=HIGHEST)
    scores = jnp.where(up_to & same_seq, scores, 0.0)
    inside = jnp.dot(scores.T, values, precision=HIGHEST)
    product = jnp.dot(paths.T, jnp.dot(inverse, paths, precision=HIGHEST), precision=HIGHEST)
    transition = carry_all * (jnp.eye(head_width, dtype=query.dtype) - product)
    update = jnp.dot(values.T, turned_keys * last_seq[:, None], precision=HIGHEST)
    return (inside, turned_query, transition, update)

def heads_pieces(query_raw, keys_raw, values, paths_raw, beta_raw, same_seq, last_seq, carry_all):
    query = unit_rows(query_raw)
    keys = unit_rows(keys_raw)
    paths = unit_rows(paths_raw)
    strength = 1.0 + jax.nn.sigmoid(beta_raw)
    mapped = jax.vmap(block_parts, in_axes=(1, 1, 1, 1, 1, None, None, None), out_axes=(1, 1, 0, 0))
    return mapped(query, keys, values, paths, strength, same_seq, last_seq, carry_all)

def heads_finish(inside, turned_query, carry_in, carried):
    mixed = inside + carry_in[:, None, None] * jnp.einsum('lhs,hvs->lhv', turned_query, carried, precision=HIGHEST)
    return mixed * lax.rsqrt(lax.optimization_barrier(jnp.mean(mixed * mixed, axis=-1, keepdims=True)) + HEAD_EPSILON)

def attention(query_raw, keys_raw, values, paths_raw, beta_raw, lengths):
    blocks = TOKENS // TOK_DEV
    positions = jnp.arange(TOKENS, dtype=jnp.int32)
    segment = segment_of(positions, lengths).reshape(blocks, TOK_DEV)
    previous = segment_of(jnp.arange(blocks, dtype=jnp.int32) * TOK_DEV - 1, lengths)

    def shaped(array):
        return array.reshape((blocks, TOK_DEV) + array.shape[1:])

    def block_step(carried, pieces):
        query_block, keys_block, values_block, paths_block, beta_block, segment_block, previous_block = pieces
        carry_in, same_seq, last_seq = masks_of(segment_block, previous_block, query_block.dtype)
        inside, turned_query, transition, update = heads_pieces(query_block, keys_block, values_block, paths_block, beta_block, same_seq, last_seq, carry_in[-1])
        normed = heads_finish(inside, turned_query, carry_in, carried)
        carried = jnp.einsum('hvs,hst->hvt', carried, transition, precision=HIGHEST) + update
        return (carried, normed)
    initial = jnp.zeros((HEADS, HS, HS), query_raw.dtype)
    inputs = (shaped(query_raw), shaped(keys_raw), shaped(values), shaped(paths_raw), shaped(beta_raw), segment, previous)
    _, normed = lax.scan(jax.checkpoint(block_step), initial, inputs)
    return normed.reshape(TOKENS, HEADS * HS)

def forward(block_input, gain_in, w_query, w_key, w_value, w_path, w_beta, w_out, gain_mid, w_gate, w_up, w_down, lengths):
    first_norm = low(rms_scale(block_input, gain_in))
    query_raw = low_back(jnp.dot(first_norm, w_query, precision=HIGHEST)).reshape(TOKENS, HEADS, HS)
    keys_raw = low_back(jnp.dot(first_norm, w_key, precision=HIGHEST)).reshape(TOKENS, HEADS, HS)
    values = low_back(jnp.dot(first_norm, w_value, precision=HIGHEST)).reshape(TOKENS, HEADS, HS)
    paths_raw = low_back(jnp.dot(first_norm, w_path, precision=HIGHEST)).reshape(TOKENS, HEADS, HS)
    beta_raw = low_back(jnp.dot(first_norm, w_beta, precision=HIGHEST))
    normed = attention(query_raw, keys_raw, values, paths_raw, beta_raw, lengths)
    residual = block_input + low_back(jnp.dot(low(normed), w_out, precision=HIGHEST))
    second_norm = low(rms_scale(residual, gain_mid))
    gate_val = low_back(jnp.dot(second_norm, w_gate, precision=HIGHEST))
    up_val = low_back(jnp.dot(second_norm, w_up, precision=HIGHEST))
    hidden = low(jax.nn.silu(gate_val) * up_val)
    return residual + low_back(jnp.dot(hidden, w_down, precision=HIGHEST))

def reference(block_input, gain_in, w_query, w_key, w_value, w_path, w_beta, w_out, gain_mid, w_gate, w_up, w_down, out_grad, lengths):
    floats = [array.astype(jnp.float32) for array in (block_input, gain_in, w_query, w_key, w_value, w_path, w_beta, w_out, gain_mid, w_gate, w_up, w_down)]
    block_output, pullback = jax.vjp(lambda *params: forward(*params, lengths), *floats)
    gradients = pullback(out_grad.astype(jnp.float32))
    return (block_output, gradients[0], gradients[1], gradients[2], gradients[3], gradients[4], gradients[5], gradients[6], gradients[7], gradients[8], gradients[9], gradients[10], gradients[11])
```

```python
import jax
import jax.numpy as jnp
from jax import lax
from jax.sharding import Mesh
from jax.sharding import PartitionSpec as P

EPSILON = 1e-06
HEAD_EPSILON = 0.01
HIGHEST = lax.Precision.HIGHEST
F32 = jnp.float32
BF16 = jnp.bfloat16
CTX = ("y", "x", "c")


def swap(value):
    return lax.ppermute(value, "c", [(0, 1), (1, 0)])


def shift(value, axis, step):
    count = lax.axis_size(axis)
    return lax.ppermute(value, axis, [(i, (i + step) % count) for i in range(count)])


def gather_all(value, axis):
    count = lax.axis_size(axis)
    spread = jnp.broadcast_to(value[None], (count,) + value.shape)
    return lax.all_to_all(spread, axis, 0, 0)


def pick(array, index, dim=0):
    return lax.dynamic_index_in_dim(array, index, dim, False)


def rms_scale(values, gain_vec):
    return (
        values * lax.rsqrt(jnp.mean(values * values, axis=-1, keepdims=True) + EPSILON) * gain_vec
    )


def unit_rows(values):
    return values * lax.rsqrt(jnp.sum(values * values, axis=-1, keepdims=True) + EPSILON)


def segment_of(positions, lengths):
    starts = jnp.cumsum(lengths) - lengths
    return jnp.sum((starts[None, :] <= positions[:, None]).astype(jnp.int32), axis=1) - 1


def masks_of(segment, previous, dtype):
    carry_in = (segment == previous).astype(dtype)
    same_seq = segment[:, None] == segment[None, :]
    last_seq = (segment == segment[-1]).astype(dtype)
    return (carry_in, same_seq, last_seq)


def upper_inverse(left_side, diagonal_part):
    length = left_side.shape[0]
    indices = jnp.arange(length)
    inverse = jnp.diag(1.0 / diagonal_part)
    width = 1
    while width < length:
        same_pair = indices[:, None] // (2 * width) == indices[None, :] // (2 * width)
        lower_half = indices[:, None] // width < indices[None, :] // width
        linking = jnp.where(same_pair & lower_half, left_side, 0.0)
        inverse = inverse - jnp.dot(
            inverse, jnp.dot(linking, inverse, precision=HIGHEST), precision=HIGHEST
        )
        width = width * 2
    return inverse


def block_parts(query, keys, values, paths, strength, same_seq, last_seq, carry_all):
    length = query.shape[0]
    head_width = query.shape[1]
    indices = jnp.arange(length)
    up_to = indices[:, None] <= indices[None, :]
    later_mask = indices[:, None] < indices[None, :]
    gram_matrix = jnp.dot(paths, paths.T, precision=HIGHEST)
    left_side = jnp.where(later_mask, gram_matrix, 0.0)
    inverse = upper_inverse(left_side, 1.0 / strength)
    paths_query = jnp.where(up_to, jnp.dot(paths, query.T, precision=HIGHEST), 0.0)
    coefficient = jnp.dot(inverse, paths_query, precision=HIGHEST)
    turned_query = query - jnp.dot(coefficient.T, paths, precision=HIGHEST)
    keys_paths = jnp.where(later_mask, jnp.dot(keys, paths.T, precision=HIGHEST), 0.0)
    folded = jnp.dot(keys_paths, inverse, precision=HIGHEST)
    turned_keys = keys - jnp.dot(folded, paths, precision=HIGHEST)
    scores = jnp.dot(keys, query.T, precision=HIGHEST) - jnp.dot(
        folded, paths_query, precision=HIGHEST
    )
    scores = jnp.where(up_to & same_seq, scores, 0.0)
    inside = jnp.dot(scores.T, values, precision=HIGHEST)
    product = jnp.dot(paths.T, jnp.dot(inverse, paths, precision=HIGHEST), precision=HIGHEST)
    transition = carry_all * (jnp.eye(head_width, dtype=query.dtype) - product)
    update = jnp.dot(values.T, turned_keys * last_seq[:, None], precision=HIGHEST)
    return (inside, turned_query, transition, update)


def heads_pieces(query_raw, keys_raw, values, paths_raw, beta_raw, same_seq, last_seq, carry_all):
    query = unit_rows(query_raw)
    keys = unit_rows(keys_raw)
    paths = unit_rows(paths_raw)
    strength = 1.0 + jax.nn.sigmoid(beta_raw)
    mapped = jax.vmap(block_parts, in_axes=(1, 1, 1, 1, 1, None, None, None), out_axes=(1, 1, 0, 0))
    return mapped(query, keys, values, paths, strength, same_seq, last_seq, carry_all)


def heads_finish(inside, turned_query, carry_in, carried):
    mixed = inside + carry_in[:, None, None] * jnp.einsum(
        "lhs,hvs->lhv", turned_query, carried, precision=HIGHEST
    )
    return mixed * lax.rsqrt(jnp.mean(mixed * mixed, axis=-1, keepdims=True) + HEAD_EPSILON)


def mul(left, right):
    return jnp.einsum("hab,hbc->hac", left, right, precision=HIGHEST)


def mul_t(left, right):
    return jnp.einsum("hab,hcb->hac", left, right, precision=HIGHEST)


def join_rows(mine, other, core):
    return jnp.where(
        core == 0,
        jnp.concatenate([mine, other], axis=-2),
        jnp.concatenate([other, mine], axis=-2),
    )


def rows_of(array, core):
    half = array.shape[-2] // 2
    return lax.dynamic_slice_in_dim(array, core * half, half, array.ndim - 2)


def forward_state(transition, update, place):
    row, col, core = place
    mate = swap(jnp.stack([transition, update]))
    first = core == 0
    t_0 = jnp.where(first, transition, mate[0])
    t_1 = jnp.where(first, mate[0], transition)
    u_0 = rows_of(jnp.where(first, update, mate[1]), core)
    u_1 = rows_of(jnp.where(first, mate[1], update), core)
    chip_t = rows_of(mul(t_0, t_1), core)
    chip_u = mul(u_0, t_1) + u_1
    along_x = gather_all(jnp.stack([chip_t, chip_u]), "x")
    t_x = join_rows(along_x[:, 0], swap(along_x[:, 0]), core)
    u_x = along_x[:, 1]
    t_23 = mul(t_x[2], t_x[3])
    row_t = rows_of(mul(mul(t_x[0], t_x[1]), t_23), core)
    row_u = mul(mul(u_x[0], t_x[1]) + u_x[1], t_23) + mul(u_x[2], t_x[3]) + u_x[3]
    along_y = gather_all(jnp.stack([row_t, row_u]), "y")
    t_y = join_rows(along_y[:, 0], swap(along_y[:, 0]), core)
    u_y = along_y[:, 1]
    state = jnp.zeros_like(u_0)
    for at in range(3):
        state = jnp.where(at < row, mul(state, t_y[at]) + u_y[at], state)
    for at in range(3):
        state = jnp.where(at < col, mul(state, t_x[at]) + u_x[at], state)
    state_1 = mul(state, t_0) + u_0
    other = swap(jnp.where(first, state_1, state))
    carried = join_rows(jnp.where(first, state, state_1), other, core)
    return carried, (t_0, t_1, t_x, t_y)


def backward_state(state_grad, kept, place):
    row, col, core = place
    t_0, t_1, t_x, t_y = kept
    first = core == 0
    mate = swap(rows_of(state_grad, 1 - core))
    mine = rows_of(state_grad, core)
    g_0 = jnp.where(first, mine, mate)
    g_1 = jnp.where(first, mate, mine)
    chip_g = mul_t(g_1, t_0) + g_0
    g_x = gather_all(chip_g, "x")
    row_g = g_x[3]
    for at in (2, 1, 0):
        row_g = mul_t(row_g, t_x[at]) + g_x[at]
    g_y = gather_all(row_g, "y")
    later = jnp.zeros_like(g_0)
    for at in (3, 2, 1):
        later = jnp.where(at > row, mul_t(later, t_y[at]) + g_y[at], later)
    for at in (3, 2, 1):
        later = jnp.where(at > col, mul_t(later, t_x[at]) + g_x[at], later)
    later_0 = mul_t(later, t_1) + g_1
    other = swap(jnp.where(first, later, later_0))
    return join_rows(jnp.where(first, later_0, later), other, core)


def contract_cols(left, right):
    return lax.dot_general(
        left, right, (((1,), (1,)), ((), ())), preferred_element_type=jnp.float32
    )


def dot32(left, right):
    return jnp.dot(left, right, preferred_element_type=jnp.float32)


def direct_sum(blocks, axis, dim):
    count = lax.axis_size(axis)
    me = lax.axis_index(axis)
    total = pick(blocks, me, dim)
    arrived = [
        shift(pick(blocks, (me + step) % count, dim), axis, step) for step in (1, count - 1, 2)
    ]
    for one in arrived:
        total = total + one
    return total


def scatter_ctx(groups, place):
    core = place[2]
    sums = []
    for rows, columns in groups:
        parts = rows.reshape(4, 4, 2, rows.shape[0] // 32, rows.shape[1])
        shape = (4, 4, rows.shape[0] // 32, columns.shape[1])
        theirs = dot32(pick(parts, 1 - core, 2).reshape(-1, rows.shape[1]), columns)
        mine = dot32(pick(parts, core, 2).reshape(-1, rows.shape[1]), columns)
        sums.append((mine + swap(theirs)).reshape(shape))
    return sums


def spread_xy(first, second):
    a = direct_sum(first, "x", 1)
    b = direct_sum(second, "y", 0)
    a = direct_sum(a, "y", 0)
    b = direct_sum(b, "x", 0)
    return a, b


def local(
    block_input,
    gain_in,
    w_query,
    w_key,
    w_value,
    w_path,
    w_beta,
    w_out,
    gain_mid,
    w_gate,
    w_up,
    w_down,
    out_grad,
    lengths,
):
    tokens_here, width = block_input.shape
    heads_here = w_beta.shape[1]
    head_width = w_query.shape[1] // heads_here
    head_cols = w_query.shape[1]
    place = tuple(lax.axis_index(name) for name in CTX)
    core = place[2]
    rank = lax.axis_index("z")
    ranks = lax.axis_size("z")
    part = tokens_here // ranks
    positions = lax.axis_index(CTX) * tokens_here + jnp.arange(tokens_here, dtype=jnp.int32)
    segment = segment_of(positions, lengths)
    previous = segment_of(positions[:1] - 1, lengths)[0]
    carry_in, same_seq, last_seq = masks_of(segment, previous, jnp.float32)
    gain_first = gain_in.astype(jnp.float32)
    gain_second = gain_mid.astype(jnp.float32)

    unity = (lengths[0] > 0).astype(F32)

    def part_of(array):
        return lax.dynamic_slice_in_dim(array, rank * part, part, 0)

    out_half = lax.dynamic_slice_in_dim(w_out, core * (head_cols // 2), head_cols // 2, 0)
    out_mine = lax.all_gather(out_half.astype(F32), "z", axis=0)
    out_other = swap(out_mine)
    out_pair = jnp.where(
        core == 0,
        jnp.stack([out_mine, out_other], axis=1),
        jnp.stack([out_other, out_mine], axis=1),
    )
    w_out_all = (out_pair * unity).reshape(width, width).astype(BF16)

    def local_pieces(query_raw, keys_raw, values, paths_raw, beta_local):
        return heads_pieces(
            query_raw, keys_raw, values, paths_raw, beta_local, same_seq, last_seq, carry_in[-1]
        )

    def local_finish(inside_part, turned_part, state):
        return heads_finish(inside_part, turned_part, carry_in, state)

    first_low = rms_scale(block_input, gain_first).astype(jnp.bfloat16)
    raw_list = [
        dot32(first_low, weight).reshape(tokens_here, heads_here, head_width)
        for weight in (w_query, w_key, w_value, w_path)
    ]
    beta_raw = dot32(first_low, w_beta)
    pieces, pieces_pull = jax.vjp(local_pieces, *raw_list, beta_raw)
    inside, turned_query, transition, update = pieces
    carried, kept = forward_state(transition, update, place)
    normed, finish_pull = jax.vjp(local_finish, inside, turned_query, carried)
    normed_low = normed.reshape(tokens_here, head_cols).astype(jnp.bfloat16)
    normed_all = gather_all(normed_low.astype(F32), "z") * unity
    normed_all = jnp.swapaxes(normed_all.astype(BF16), 0, 1).reshape(tokens_here, width)
    residual = block_input + dot32(normed_all, w_out_all)
    second_low = rms_scale(residual, gain_second).astype(jnp.bfloat16)
    gate_val = dot32(second_low, w_gate)
    up_val = dot32(second_low, w_up)
    hidden_low = (jax.nn.silu(gate_val) * up_val).astype(jnp.bfloat16)
    ffn_low = out_grad.astype(jnp.bfloat16)
    hidden_grad = contract_cols(ffn_low, w_down)
    sigmoid_gate = jax.nn.sigmoid(gate_val)
    silu_gate = gate_val * sigmoid_gate
    gate_low = (
        hidden_grad * up_val * sigmoid_gate * (1.0 + gate_val * (1.0 - sigmoid_gate))
    ).astype(jnp.bfloat16)
    up_low = (hidden_grad * silu_gate).astype(jnp.bfloat16)
    second_partial = contract_cols(gate_low, w_gate) + contract_cols(up_low, w_up)
    second_grad = jnp.sum(
        lax.all_to_all(second_partial.reshape(ranks, part, width), "z", 0, 0), axis=0
    )
    middle_part = part_of(residual)
    _, second_pull = jax.vjp(rms_scale, middle_part, gain_second)
    middle_norm_grad, gain_second_term = second_pull(second_grad)
    middle_grad = part_of(out_grad) + middle_norm_grad
    attn_low = middle_grad.astype(jnp.bfloat16)
    normed_grad = contract_cols(attn_low, w_out_all).reshape(part, ranks, head_cols)
    normed_grad = lax.all_to_all(jnp.swapaxes(normed_grad, 0, 1), "z", 0, 0)
    normed_grad = normed_grad.reshape(tokens_here, heads_here, head_width)
    inside_grad, turned_grad, state_grad = finish_pull(normed_grad)
    later_grad = backward_state(state_grad, kept, place)
    transition_grad = jnp.einsum("hvs,hvt->hst", carried, later_grad, precision=HIGHEST)
    raw_grads = pieces_pull((inside_grad, turned_grad, transition_grad, later_grad))
    grad_lows = [
        raw_grads[index].reshape(tokens_here, -1).astype(jnp.bfloat16) for index in range(5)
    ]
    first_partial = contract_cols(grad_lows[0], w_query) + contract_cols(grad_lows[1], w_key)
    first_partial = (
        first_partial + contract_cols(grad_lows[2], w_value) + contract_cols(grad_lows[3], w_path)
    )
    first_partial = first_partial + contract_cols(grad_lows[4], w_beta)
    first_grad = jnp.sum(
        lax.all_to_all(first_partial.reshape(ranks, part, width), "z", 0, 0), axis=0
    )
    _, first_norm_pull = jax.vjp(rms_scale, part_of(block_input), gain_first)
    input_norm_grad, gain_first_term = first_norm_pull(first_grad)
    input_grad = gather_all(middle_grad + input_norm_grad, "z").reshape(tokens_here, width)

    down_partial = dot32(hidden_low, w_down)
    down_partial, _ = lax.optimization_barrier((down_partial, second_grad))
    block_output = residual + lax.psum(down_partial, "z")

    second_t = second_low.T
    ffn_t = ffn_low.T
    first_t = first_low.T
    both_low = jnp.concatenate([gate_low, up_low], axis=1)
    cut = (both_low.shape[1] + hidden_low.shape[1]) // 2
    sums = scatter_ctx(
        [(second_t, both_low[:, :cut]), (second_t, both_low[:, cut:]), (ffn_t, hidden_low)], place
    )
    ffn_a, ffn_b = spread_xy(sums[0], jnp.concatenate(sums[1:], axis=-1))
    ffn_sum = jnp.concatenate([ffn_a, ffn_b], axis=-1)
    hidden_cols = w_gate.shape[1]
    gate_out = ffn_sum[:, :hidden_cols]
    up_out = ffn_sum[:, hidden_cols : 2 * hidden_cols]
    down_out = ffn_sum[:, 2 * hidden_cols :].T

    attn_all = lax.all_gather(attn_low.astype(F32), "z", axis=0, tiled=True)
    attn_t = (attn_all * unity).astype(BF16).T
    sums = scatter_ctx([(first_t, grad_lows[0]), (attn_t, normed_low)], place)
    query_out, out_out = spread_xy(sums[0], sums[1])
    tail = jnp.concatenate(
        grad_lows[1:] + [jnp.zeros((tokens_here, 128 - heads_here), BF16)], axis=1
    )
    cut = tail.shape[1] // 2
    sums = scatter_ctx([(first_t, tail[:, :cut]), (first_t, tail[:, cut:])], place)
    tail_sum = jnp.concatenate(spread_xy(sums[0], sums[1]), axis=-1)
    key_out = tail_sum[:, :head_cols]
    value_out = tail_sum[:, head_cols : 2 * head_cols]
    path_out = tail_sum[:, 2 * head_cols : 3 * head_cols]
    beta_out = tail_sum[:, 3 * head_cols : 3 * head_cols + heads_here]

    gains = jnp.stack([gain_first_term, gain_second_term]).reshape(2, 32, width // 32)
    gains = jnp.sum(lax.all_to_all(jnp.swapaxes(gains, 0, 1), CTX, 0, 0), axis=0)
    gains = jnp.sum(gather_all(gains, "z"), axis=0)
    return (
        block_output,
        input_grad,
        gains[0],
        query_out,
        key_out,
        value_out,
        path_out,
        beta_out,
        out_out.T,
        gains[1],
        gate_out,
        up_out,
        down_out,
    )


def solution(mesh):
    fine = Mesh(mesh.devices.reshape(4, 4, 2, 4), ("y", "x", "c", "z"))
    in_specs = (
        P(CTX, None),
        P(),
        P(None, "z"),
        P(None, "z"),
        P(None, "z"),
        P(None, "z"),
        P(None, "z"),
        P("z", None),
        P(),
        P(None, "z"),
        P(None, "z"),
        P("z", None),
        P(CTX, None),
        P(),
    )
    out_specs = (
        P(CTX, None),
        P(CTX, None),
        P(CTX),
        P(CTX, "z"),
        P(CTX, "z"),
        P(CTX, "z"),
        P(CTX, "z"),
        P(CTX, "z"),
        P("z", CTX),
        P(CTX),
        P(CTX, "z"),
        P(CTX, "z"),
        P("z", CTX),
    )
    return jax.shard_map(local, mesh=fine, in_specs=in_specs, out_specs=out_specs, check_vma=False)
```

```python
import jax
import jax.numpy as jnp
from jax import lax
from jax.experimental import pallas as pl
from jax.experimental.pallas import tpu as pltpu
from jax.sharding import Mesh
from jax.sharding import PartitionSpec as P

EPSILON = 1e-06
HEAD_EPSILON = 0.01
F32 = jnp.float32
BF16 = jnp.bfloat16
HEADS = 3
HW = 128
LEN = 256
RANKS = 4
PART = LEN // RANKS
SIDE = 4
CTX = ("y", "x", "c")
VMEM_LIMIT = 56 * 1024 * 1024


def split(value):
    high = value.astype(BF16)
    return high, (value - high.astype(F32)).astype(BF16)


def dg(left, right, ta, tb):
    dims = (((0 if ta else 1,), (1 if tb else 0,)), ((), ()))
    return lax.dot_general(left, right, dims, preferred_element_type=F32)


def mm(left, right, ta=False, tb=False):
    left = left if isinstance(left, tuple) else split(left)
    right = right if isinstance(right, tuple) else split(right)
    return dg(left[0], right[0], ta, tb) + (
        dg(left[0], right[1], ta, tb) + dg(left[1], right[0], ta, tb)
    )


def iota(shape, dim):
    return lax.broadcasted_iota(jnp.int32, shape, dim)


def cols(head):
    return slice(head * HW, (head + 1) * HW)


def segments(spot, scal):
    second = scal[1]
    third = second + scal[2]
    return (spot >= second).astype(jnp.int32) + (spot >= third).astype(jnp.int32)


def small_inverses(scaled):
    row = iota((HW, HW), 0)
    lane = iota((HW, HW), 1)
    same = (row // 8) == (lane // 8)
    packed = []
    for one in scaled:
        for half in range(2):
            block = jnp.where(same, one[half * HW : (half + 1) * HW, half * HW : (half + 1) * HW], 0.0)
            packed.append(jnp.sum(block.reshape(HW // 8, 8, HW), axis=0))
    count = len(packed)
    high, low = split(jnp.concatenate(packed, axis=0))
    lane_8 = iota((8, HW), 1) % 8
    spread = {}
    for k in range(1, 8):
        unit = ((row // 8 == lane // 8) & (row % 8 == k)).astype(BF16)
        both = dg(high, unit, False, False) + dg(low, unit, False, False)
        spread[k] = both.reshape(count, 8, HW)
    rows = {}
    for i in range(7, -1, -1):
        value = jnp.broadcast_to((lane_8[:1] == i).astype(F32)[None], (count, 1, HW))
        for k in range(i + 1, 8):
            value = value - spread[k][:, i : i + 1, :] * rows[k]
        rows[i] = value
    done = jnp.concatenate([rows[i] for i in range(8)], axis=1)
    out = []
    zero = jnp.zeros((HW, HW), F32)
    for head in range(count // 2):
        halves = [
            jnp.where(same, jnp.concatenate([done[2 * head + half]] * (HW // 8), axis=0), 0.0)
            for half in range(2)
        ]
        out.append(
            jnp.concatenate(
                [
                    jnp.concatenate([halves[0], zero], axis=1),
                    jnp.concatenate([zero, halves[1]], axis=1),
                ],
                axis=0,
            )
        )
    return out


def upper_rows(value, width):
    return jnp.concatenate(
        [value[at : at + width] for at in range(0, value.shape[0], 2 * width)], axis=0
    )


def put_upper(value, upper, width):
    pieces = []
    for n, at in enumerate(range(0, value.shape[0], 2 * width)):
        pieces.append(upper[n * width : (n + 1) * width])
        pieces.append(value[at + width : at + 2 * width])
    return jnp.concatenate(pieces, axis=0)


def inverses(scaled):
    out = small_inverses(scaled)
    row = iota((LEN, LEN), 0)
    lane = iota((LEN, LEN), 1)
    width = 8
    while width < LEN:
        pair = (row // (2 * width) == lane // (2 * width)) & (row // width < lane // width)
        link = [upper_rows(jnp.where(pair, one, 0.0), width) for one in scaled]
        parts = [split(one) for one in out]
        first = [mm(a, b) for a, b in zip(link, parts)]
        empty = jnp.zeros((LEN, LEN), F32)
        wide = [put_upper(empty, one, width) for one in first]
        tops = [
            (upper_rows(a, width), upper_rows(b, width)) for a, b in parts
        ]
        second = [mm(a, b) for a, b in zip(tops, wide)]
        out = [
            put_upper(one, upper_rows(one, width) - new, width) for one, new in zip(out, second)
        ]
        width *= 2
    return out


def unit_rows(value):
    scale = lax.rsqrt(jnp.sum(value * value, axis=-1, keepdims=True) + EPSILON)
    return value * scale, scale


def a1_body(
    scal_ref, x_ref, gain_ref, wq_ref, wk_ref, wv_ref, ww_ref, wb_ref,
    h1_ref, q_ref, k_ref, v_ref, w_ref, aux_ref, inv_ref, kp_ref, b_ref, kt_ref, tu_ref,
):
    x = x_ref[...]
    scale = lax.rsqrt(jnp.mean(x * x, axis=-1, keepdims=True) + EPSILON)
    h1 = (x * scale * gain_ref[...].astype(F32)).astype(BF16)
    h1_ref[...] = h1.astype(F32)
    start = scal_ref[0]
    token = iota((LEN, 1), 0) + start
    segment = segments(token, scal_ref)
    end_segment = segments(jnp.full((1, 1), LEN - 1, jnp.int32) + start, scal_ref)
    before = start - 1
    before_segment = jnp.where(start == 0, -1, segments(jnp.full((1, 1), 0, jnp.int32) + before, scal_ref))
    last = (segment == end_segment).astype(F32)
    carry_all = (end_segment == before_segment).astype(F32)
    row = iota((LEN, LEN), 0)
    lane = iota((LEN, LEN), 1)
    later = row < lane
    bl = dg(h1, wb_ref[...], False, False)
    sig = jax.nn.sigmoid(bl)
    beta = 1.0 + sig
    beta_rows = beta.T
    pr = dg(h1, ww_ref[...], False, False)
    kr = dg(h1, wk_ref[...], False, False)
    w_all, k_all, aux = [], [], []
    for head in range(HEADS):
        w, w_scale = unit_rows(pr[:, cols(head)])
        k, k_scale = unit_rows(kr[:, cols(head)])
        w_ref[:, cols(head)] = w
        k_ref[:, cols(head)] = k
        w_all.append(w)
        k_all.append(k)
        aux.append((w_scale, k_scale))
    w_split = [split(w) for w in w_all]
    k_split = [split(k) for k in k_all]
    scaled = [
        jnp.where(later, mm(w_split[h], w_split[h], tb=True), 0.0) * beta[:, h : h + 1]
        for h in range(HEADS)
    ]
    inverse = [
        one * beta_rows[h : h + 1, :] for h, one in enumerate(inverses(scaled))
    ]
    vr = dg(h1, wv_ref[...], False, False)
    qr = dg(h1, wq_ref[...], False, False)
    v_ref[...] = vr
    lane_aux = iota((LEN, HW), 1)
    packed = jnp.where(lane_aux < HEADS, beta, 0.0)
    eye = (iota((HW, HW), 0) == iota((HW, HW), 1)).astype(F32)
    for head in range(HEADS):
        q, q_scale = unit_rows(qr[:, cols(head)])
        q_ref[:, cols(head)] = q
        for at, value in ((8 + head, q_scale), (16 + head, aux[head][1]), (24 + head, aux[head][0])):
            packed = jnp.where(lane_aux == at, value, packed)
        inv_ref[head] = inverse[head]
        inv_split = split(inverse[head])
        folded = mm(inv_split, w_split[head])
        b_ref[:, cols(head)] = folded
        folded_split = split(folded)
        kp = jnp.where(later, mm(k_split[head], w_split[head], tb=True), 0.0)
        kp_ref[head] = kp
        kt = k_all[head] - mm(kp, folded_split)
        kt_ref[:, cols(head)] = kt
        tu_ref[0, head] = carry_all * (eye - mm(w_split[head], folded_split, ta=True))
        tu_ref[1, head] = mm(vr[:, cols(head)], kt * last, ta=True)
    aux_ref[...] = packed


def shape(*dims, dtype=F32):
    return jax.ShapeDtypeStruct(dims, dtype)


def call(body, outs, name, flops, moved, scratch=()):
    smem = pl.BlockSpec(memory_space=pltpu.SMEM)
    vmem = pl.BlockSpec(memory_space=pltpu.VMEM)

    def run(*operands):
        return pl.pallas_call(
            body,
            out_shape=outs,
            in_specs=[smem] + [vmem] * (len(operands) - 1),
            out_specs=[vmem] * len(outs),
            scratch_shapes=list(scratch),
            name=name,
            cost_estimate=pl.CostEstimate(flops=flops, bytes_accessed=moved, transcendentals=0),
            compiler_params=pltpu.CompilerParams(vmem_limit_bytes=VMEM_LIMIT),
        )(*operands)

    return run


WIDE = HEADS * HW


def run_a1(*operands):
    outs = [
        shape(LEN, operands[1].shape[1]),
        shape(LEN, WIDE), shape(LEN, WIDE), shape(LEN, WIDE), shape(LEN, WIDE),
        shape(LEN, HW),
        shape(HEADS, LEN, LEN), shape(HEADS, LEN, LEN),
        shape(LEN, WIDE), shape(LEN, WIDE),
        shape(2, HEADS, HW, HW),
    ]
    return call(a1_body, outs, "local_parts", 8 * 10**9, 12 * 10**6)(*operands)


def a2_body(
    scal_ref, q_ref, k_ref, v_ref, w_ref, inv_ref, kp_ref,
    c_ref, sc_ref, qt_ref, in_ref,
):
    start = scal_ref[0]
    segment = segments(iota((LEN, LEN), 0) + start, scal_ref)
    segment_t = segments(iota((LEN, LEN), 1) + start, scal_ref)
    row = iota((LEN, LEN), 0)
    lane = iota((LEN, LEN), 1)
    up_to = row <= lane
    seen = up_to & (segment == segment_t)
    for head in range(HEADS):
        q = q_ref[:, cols(head)]
        q_split = split(q)
        w_split = split(w_ref[:, cols(head)])
        pq = jnp.where(up_to, mm(w_split, q_split, tb=True), 0.0)
        c = mm(inv_ref[head], pq)
        c_ref[head] = c
        c_split = split(c)
        qt_ref[:, cols(head)] = q - mm(c_split, w_split, ta=True)
        scores = mm(k_ref[:, cols(head)], q_split, tb=True) - mm(kp_ref[head], c_split)
        scores = jnp.where(seen, scores, 0.0)
        sc_ref[head] = scores
        in_ref[:, cols(head)] = mm(scores, v_ref[:, cols(head)], ta=True)


def run_a2(*operands):
    outs = [shape(HEADS, LEN, LEN), shape(HEADS, LEN, LEN), shape(LEN, WIDE), shape(LEN, WIDE)]
    return call(a2_body, outs, "inside_parts", 4 * 10**9, 6 * 10**6)(*operands)


def carry_of(start, scal_ref):
    token = iota((LEN, 1), 0) + start
    before = jnp.full((1, 1), 0, jnp.int32) + (start - 1)
    before_segment = jnp.where(start == 0, -1, segments(before, scal_ref))
    return (segments(token, scal_ref) == before_segment).astype(F32)


def pair_of(ref, core, head):
    return jnp.concatenate([ref[0, core, head], ref[1, core, head]], axis=0)


def a3_body(scal_ref, in_ref, qt_ref, states_ref, mixed_ref, normed_ref, spread_ref, carried_ref):
    carry = carry_of(scal_ref[0], scal_ref)
    core = scal_ref[5]
    for head in range(HEADS):
        carried = pair_of(states_ref, core, head)
        carried_ref[head] = carried
        mixed = in_ref[:, cols(head)] + carry * mm(qt_ref[:, cols(head)], carried, tb=True)
        mixed_ref[:, cols(head)] = mixed
        scale = lax.rsqrt(jnp.mean(mixed * mixed, axis=-1, keepdims=True) + HEAD_EPSILON)
        low = (mixed * scale).astype(BF16).astype(F32)
        normed_ref[:, cols(head)] = low
        for at in range(RANKS):
            spread_ref[at, :, cols(head)] = low


def run_a3(*operands):
    outs = [shape(LEN, WIDE), shape(LEN, WIDE), shape(RANKS, LEN, WIDE), shape(HEADS, HW, HW)]
    return call(a3_body, outs, "normed_heads", 10**8, 2 * 10**6)(*operands)


def b1_body(scal_ref, dn_ref, mixed_ref, qt_ref, dm_ref, sg_ref):
    carry = carry_of(scal_ref[0], scal_ref)
    for head in range(HEADS):
        mixed = mixed_ref[:, cols(head)]
        dn = dn_ref[:, cols(head)]
        scale = lax.rsqrt(jnp.mean(mixed * mixed, axis=-1, keepdims=True) + HEAD_EPSILON)
        drift = jnp.mean(dn * mixed, axis=-1, keepdims=True) * (scale * scale)
        dm = scale * (dn - mixed * drift)
        dm_ref[:, cols(head)] = dm
        sg_ref[head] = mm(dm * carry, qt_ref[:, cols(head)], ta=True)


def run_b1(*operands):
    outs = [shape(LEN, WIDE), shape(HEADS, HW, HW)]
    return call(b1_body, outs, "state_gradient", 10**8, 2 * 10**6)(*operands)


def unit_pull(unit, scale, grad):
    return scale * (grad - unit * jnp.sum(unit * grad, axis=-1, keepdims=True))


def b2_body(
    scal_ref, dm_ref, carried_ref, q_ref, k_ref, v_ref, w_ref, aux_ref, inv_ref, kp_ref,
    c_ref, sc_ref,
    dq_ref, dk_ref, dv_ref, dw_ref, dkp_ref, xc_ref,
):
    start = scal_ref[0]
    carry = carry_of(start, scal_ref)
    row = iota((LEN, LEN), 0)
    lane = iota((LEN, LEN), 1)
    up_to = row <= lane
    seen = up_to & (
        segments(row + start, scal_ref) == segments(lane + start, scal_ref)
    )
    for head in range(HEADS):
        q = q_ref[:, cols(head)]
        q_split = split(q)
        w_split = split(w_ref[:, cols(head)])
        k_split = split(k_ref[:, cols(head)])
        c_split = split(c_ref[head])
        kp_split = split(kp_ref[head])
        dm = dm_ref[:, cols(head)]
        dm_split = split(dm)
        dqt = mm(dm * carry, carried_ref[head])
        dqt_split = split(dqt)
        ds = jnp.where(seen, mm(v_ref[:, cols(head)], dm_split, tb=True), 0.0)
        ds_split = split(ds)
        dv_ref[:, cols(head)] = mm(sc_ref[head], dm_split)
        dk = mm(ds_split, q_split)
        dq = dqt + mm(ds_split, k_split, ta=True)
        dkp_ref[head] = mm(ds_split, c_split, tb=True)
        dc = mm(kp_split, ds_split, ta=True) + mm(w_split, dqt_split, tb=True)
        dw = mm(c_split, dqt_split)
        x = mm(inv_ref[head], dc, ta=True)
        xc_ref[head] = mm(x, c_split, tb=True)
        dpq_split = split(jnp.where(up_to, x, 0.0))
        dw_ref[:, cols(head)] = dw + mm(dpq_split, q_split)
        dq = dq - mm(dpq_split, w_split, ta=True)
        dk_ref[:, cols(head)] = dk
        scale = aux_ref[:, 8 + head : 9 + head]
        dq_ref[:, cols(head)] = unit_pull(q, scale, dq).astype(BF16).astype(F32)


def run_b2(*operands):
    outs = [
        shape(LEN, WIDE), shape(LEN, WIDE), shape(LEN, WIDE), shape(LEN, WIDE),
        shape(HEADS, LEN, LEN), shape(HEADS, LEN, LEN),
    ]
    return call(b2_body, outs, "inside_gradients", 8 * 10**9, 8 * 10**6)(*operands)


def b3_body(
    scal_ref, x_ref, gain_mid_ref, states_ref, carried_ref, k_ref, v_ref, w_ref, aux_ref,
    inv_ref, kp_ref, b_ref, kt_ref, dq_ref, dk_ref, dv_ref, dw_ref, dkp_ref, xc_ref,
    wq_ref, wk_ref, wv_ref, ww_ref, wb_ref,
    low_ref, dh_ref,
):
    start = scal_ref[0]
    core = scal_ref[5]
    segment = segments(iota((LEN, 1), 0) + start, scal_ref)
    end_segment = segments(jnp.full((1, 1), LEN - 1, jnp.int32) + start, scal_ref)
    before = jnp.full((1, 1), 0, jnp.int32) + (start - 1)
    before_segment = jnp.where(start == 0, -1, segments(before, scal_ref))
    last = (segment == end_segment).astype(F32)
    carry_all = (end_segment == before_segment).astype(F32)
    row = iota((LEN, LEN), 0)
    lane = iota((LEN, LEN), 1)
    later_mask = row < lane
    lane_aux = iota((LEN, HW), 1)
    d_beta = jnp.zeros((LEN, HW), F32)
    for head in range(HEADS):
        later = pair_of(states_ref, core, head)
        later_split = split(later)
        dt_split = split(carry_all * mm(carried_ref[head], later_split, ta=True))
        w = w_ref[:, cols(head)]
        w_split = split(w)
        k = k_ref[:, cols(head)]
        v = v_ref[:, cols(head)]
        b_split = split(b_ref[:, cols(head)])
        kp_split = split(kp_ref[head])
        dv = dv_ref[:, cols(head)] + last * mm(kt_ref[:, cols(head)], later_split, tb=True)
        dkt = last * mm(v, later_split)
        dkt_split = split(dkt)
        db = mm(w_split, dt_split) + mm(kp_split, dkt_split, ta=True)
        y = mm(inv_ref[head], db, ta=True)
        y_split = split(y)
        dw = dw_ref[:, cols(head)] + mm(b_split, dt_split, tb=True) + y
        dkp = jnp.where(later_mask, dkp_ref[head] + mm(dkt_split, b_split, tb=True), 0.0)
        dkp_split = split(dkp)
        dk = dk_ref[:, cols(head)] + dkt - mm(dkp_split, w_split)
        dw = dw + mm(dkp_split, split(k), ta=True)
        dm = xc_ref[head] + mm(y_split, b_split, tb=True)
        dn_split = split(jnp.where(later_mask, dm, 0.0))
        dw = mm(dn_split, w_split) + mm(dn_split, w_split, ta=True) - dw
        diagonal = jnp.sum(jnp.where(row == lane, dm, 0.0), axis=-1, keepdims=True)
        beta = aux_ref[:, head : head + 1]
        sig = beta - 1.0
        dbl = -diagonal / (beta * beta) * sig * (1.0 - sig)
        d_beta = jnp.where(lane_aux == head, dbl, d_beta)
        low_ref[:, cols(head)] = unit_pull(k, aux_ref[:, 16 + head : 17 + head], dk).astype(BF16).astype(F32)
        low_ref[:, WIDE + head * HW : WIDE + (head + 1) * HW] = dv.astype(BF16).astype(F32)
        low_ref[:, 2 * WIDE + head * HW : 2 * WIDE + (head + 1) * HW] = unit_pull(
            w, aux_ref[:, 24 + head : 25 + head], dw
        ).astype(BF16).astype(F32)
    low_ref[:, 3 * WIDE :] = d_beta.astype(BF16).astype(F32)
    total = dg(dq_ref[...].astype(BF16), wq_ref[...], False, True)
    for at, ref in enumerate((wk_ref, wv_ref, ww_ref, wb_ref)):
        low = low_ref[:, at * WIDE : at * WIDE + ref.shape[1]].astype(BF16)
        total = total + dg(low, ref[...], False, True)
    for at in range(RANKS):
        dh_ref[at, :PART, :] = total[at * PART : (at + 1) * PART]
    x = x_ref[...]
    scale = lax.rsqrt(jnp.mean(x * x, axis=-1, keepdims=True) + EPSILON)
    gain_in = jnp.sum(total * x * scale, axis=0, keepdims=True)
    rows = iota((8, x.shape[1]), 0)
    both = jnp.where(rows == 0, gain_in, jnp.where(rows == 1, gain_mid_ref[...], 0.0))
    for at in range(RANKS):
        dh_ref[at, PART:, :] = both


def run_b3(*operands):
    outs = [shape(LEN, 3 * WIDE + HW), shape(RANKS, PART + 8, operands[1].shape[1])]
    return call(b3_body, outs, "late_gradients", 9 * 10**9, 16 * 10**6)(*operands)


def half_of(core):
    return pl.ds(pl.multiple_of(core * (HW // 2), HW // 2), HW // 2)


def s1_body(scal_ref, both_ref, u_ref, out_ref):
    rows = half_of(scal_ref[5])
    for head in range(HEADS):
        t_1 = split(both_ref[1, 0, head])
        u_0 = both_ref[0, 1, head, rows, :]
        u_1 = both_ref[1, 1, head, rows, :]
        u_ref[0, head] = u_0
        u_ref[1, head] = u_1
        chip_t = mm(both_ref[0, 0, head, rows, :], t_1)
        chip_u = mm(u_0, t_1) + u_1
        for at in range(SIDE):
            out_ref[at, 0, head] = chip_t
            out_ref[at, 1, head] = chip_u


def run_s1(*operands):
    outs = [shape(2, HEADS, HW // 2, HW), shape(SIDE, 2, HEADS, HW // 2, HW)]
    return call(s1_body, outs, "chip_state", 10**8, 2 * 10**6)(*operands)


def s2_body(scal_ref, pair_ref, t_ref, u_ref, out_ref):
    core = scal_ref[5]
    rows = half_of(core)
    for head in range(HEADS):
        for at in range(SIDE):
            t_ref[at, head] = jnp.concatenate(
                [pair_ref[0, at, 0, head], pair_ref[1, at, 0, head]], axis=0
            )
            u_ref[at, head] = pair_ref[core, at, 1, head]
    for head in range(HEADS):
        t_1 = split(t_ref[1, head])
        t_3 = split(t_ref[3, head])
        t_23 = split(mm(t_ref[2, head], t_3))
        row_t = mm(mm(t_ref[0, head, rows, :], t_1), t_23)
        row_u = mm(mm(u_ref[0, head], t_1) + u_ref[1, head], t_23)
        row_u = row_u + mm(u_ref[2, head], t_3) + u_ref[3, head]
        for at in range(SIDE):
            out_ref[at, 0, head] = row_t
            out_ref[at, 1, head] = row_u


def run_s2(*operands):
    outs = [
        shape(SIDE, HEADS, HW, HW),
        shape(SIDE, HEADS, HW // 2, HW),
        shape(SIDE, 2, HEADS, HW // 2, HW),
    ]
    return call(s2_body, outs, "row_state", 10**8, 2 * 10**6)(*operands)


def s3_body(scal_ref, pair_ref, tx_ref, ux_ref, both_ref, uc_ref, ty_ref, out_ref):
    row, col, core = scal_ref[3], scal_ref[4], scal_ref[5]
    for head in range(HEADS):
        for at in range(SIDE):
            ty_ref[at, head] = jnp.concatenate(
                [pair_ref[0, at, 0, head], pair_ref[1, at, 0, head]], axis=0
            )
    for head in range(HEADS):
        state = jnp.where(row > 0, pair_ref[core, 0, 1, head], 0.0)
        for at in range(1, SIDE - 1):
            new = mm(state, ty_ref[at, head]) + pair_ref[core, at, 1, head]
            state = jnp.where(at < row, new, state)
        for at in range(SIDE - 1):
            new = mm(state, tx_ref[at, head]) + ux_ref[at, head]
            state = jnp.where(at < col, new, state)
        out_ref[0, head] = state
        out_ref[1, head] = mm(state, both_ref[0, 0, head]) + uc_ref[0, head]


def run_s3(*operands):
    outs = [shape(SIDE, HEADS, HW, HW), shape(2, HEADS, HW // 2, HW)]
    return call(s3_body, outs, "block_state", 10**8, 2 * 10**6)(*operands)


def t1_body(scal_ref, pair_ref, both_ref, g_ref, out_ref):
    rows = half_of(scal_ref[5])
    for head in range(HEADS):
        g_1 = pair_ref[1, head, rows, :]
        g_ref[head] = g_1
        chip = mm(g_1, both_ref[0, 0, head], tb=True) + pair_ref[0, head, rows, :]
        for at in range(SIDE):
            out_ref[at, head] = chip


def run_t1(*operands):
    outs = [shape(HEADS, HW // 2, HW), shape(SIDE, HEADS, HW // 2, HW)]
    return call(t1_body, outs, "chip_gradient", 10**8, 10**6)(*operands)


def t2_body(scal_ref, g_ref, t_ref, out_ref):
    for head in range(HEADS):
        total = g_ref[3, head]
        for at in (2, 1, 0):
            total = mm(total, t_ref[at, head], tb=True) + g_ref[at, head]
        for at in range(SIDE):
            out_ref[at, head] = total


def run_t2(*operands):
    outs = [shape(SIDE, HEADS, HW // 2, HW)]
    return call(t2_body, outs, "row_gradient", 10**8, 10**6)(*operands)[0]


def t3_body(scal_ref, gy_ref, gx_ref, ty_ref, tx_ref, both_ref, g_ref, out_ref):
    row, col = scal_ref[3], scal_ref[4]
    for head in range(HEADS):
        later = jnp.where(row < SIDE - 1, gy_ref[3, head], 0.0)
        for at in (2, 1):
            new = mm(later, ty_ref[at, head], tb=True) + gy_ref[at, head]
            later = jnp.where(at > row, new, later)
        for at in (3, 2, 1):
            new = mm(later, tx_ref[at, head], tb=True) + gx_ref[at, head]
            later = jnp.where(at > col, new, later)
        out_ref[1, head] = later
        out_ref[0, head] = mm(later, both_ref[1, 0, head], tb=True) + g_ref[head]


def run_t3(*operands):
    outs = [shape(2, HEADS, HW // 2, HW)]
    return call(t3_body, outs, "block_gradient", 10**8, 2 * 10**6)(*operands)[0]


def ffn_body(
    scal_ref, normed_ref, out_mine_ref, out_other_ref, x_ref, gain_ref, grad_ref,
    gate_ref, up_ref, down_ref,
    middle_ref, sent_ref, dh_ref, down_part_ref, h_ref, d_ref,
):
    step = pl.program_id(0)
    units = gate_ref.shape[1]
    hidden_all = units * pl.num_programs(0)

    @pl.when(step == 0)
    def _():
        core = scal_ref[5]
        half = x_ref.shape[1] // 2
        for ref, at in ((out_mine_ref, core), (out_other_ref, 1 - core)):
            spot = pl.ds(pl.multiple_of(at * half, half), half)
            total = x_ref[:, spot]
            for rank in range(RANKS):
                total = total + dg(normed_ref[rank].astype(BF16), ref[rank], False, False)
            middle_ref[:, spot] = total
        middle = middle_ref[...]
        scale = lax.rsqrt(jnp.mean(middle * middle, axis=-1, keepdims=True) + EPSILON)
        h2 = (middle * scale * gain_ref[...].astype(F32)).astype(BF16)
        h_ref[...] = h2
        sent_ref[:, 3 * hidden_all :] = h2.astype(F32)
        d_ref[...] = grad_ref[...].astype(BF16)

    h2 = h_ref[...]
    gate = dg(h2, gate_ref[...], False, False)
    up = dg(h2, up_ref[...], False, False)
    sig = jax.nn.sigmoid(gate)
    silu = gate * sig
    hidden = (silu * up).astype(BF16)
    d_hidden = dg(d_ref[...], down_ref[...], False, True)
    d_gate = (d_hidden * up * sig * (1.0 + gate * (1.0 - sig))).astype(BF16)
    d_up = (d_hidden * silu).astype(BF16)
    for n, value in enumerate((d_gate, d_up, hidden)):
        spot = pl.ds(pl.multiple_of(n * hidden_all + step * units, units), units)
        sent_ref[:, spot] = value.astype(F32)
    d_h = dg(d_gate, gate_ref[...], False, True) + dg(d_up, up_ref[...], False, True)
    down = dg(hidden, down_ref[...], False, False)

    @pl.when(step == 0)
    def _():
        dh_ref[...] = d_h
        down_part_ref[...] = down

    @pl.when(step > 0)
    def _():
        dh_ref[...] += d_h
        down_part_ref[...] += down


def run_ffn(scal, normed, out_mine, out_other, x, gain, grad, w_gate, w_up, w_down):
    tokens, width = x.shape
    hidden = w_gate.shape[1]
    steps = 4
    units = hidden // steps

    def whole(array):
        dims = array.shape
        return pl.BlockSpec(dims, lambda i: (0,) * len(dims))

    outs = [
        shape(tokens, width),
        shape(tokens, 3 * hidden + width),
        shape(tokens, width),
        shape(tokens, width),
    ]
    across = pl.BlockSpec((width, units), lambda i: (0, i))
    return pl.pallas_call(
        ffn_body,
        grid=(steps,),
        out_shape=outs,
        in_specs=[pl.BlockSpec(memory_space=pltpu.SMEM)]
        + [whole(a) for a in (normed, out_mine, out_other, x, gain, grad)]
        + [across, across, pl.BlockSpec((units, width), lambda i: (i, 0))],
        out_specs=[whole(a) for a in outs],
        scratch_shapes=[pltpu.VMEM((tokens, width), BF16)] * 2,
        name="feed_forward",
        cost_estimate=pl.CostEstimate(
            flops=6 * 10**9, bytes_accessed=36 * 10**6, transcendentals=tokens * hidden
        ),
        compiler_params=pltpu.CompilerParams(
            vmem_limit_bytes=VMEM_LIMIT, dimension_semantics=("arbitrary",)
        ),
    )(scal, normed, out_mine, out_other, x, gain, grad, w_gate, w_up, w_down)


def norm_pull(grad, values, gain):
    scale = lax.rsqrt(jnp.mean(values * values, axis=-1, keepdims=True) + EPSILON)
    turned = gain * grad
    drift = jnp.mean(turned * values, axis=-1, keepdims=True) * (scale * scale * scale)
    return scale * turned - values * drift, grad * values * scale


def k5_body(
    scal_ref, second_ref, middle_ref, grad_ref, gain_ref, out_mine_ref, out_other_ref,
    d_middle_ref, attn_ref, gain_out_ref, normed_ref,
):
    core = scal_ref[5]
    rows = pl.ds(pl.multiple_of(scal_ref[6] * PART, PART), PART)
    second = second_ref[0] + second_ref[1] + second_ref[2] + second_ref[3]
    pulled, summed = norm_pull(second, middle_ref[rows, :], gain_ref[...].astype(F32))
    d_middle = grad_ref[rows, :] + pulled
    d_middle_ref[...] = d_middle
    gain_out_ref[...] = jnp.sum(summed, axis=0, keepdims=True)
    attn_ref[...] = d_middle.astype(BF16).astype(F32)
    half = d_middle.shape[1] // 2
    mine = attn_ref[:, pl.ds(pl.multiple_of(core * half, half), half)].astype(BF16)
    other = attn_ref[:, pl.ds(pl.multiple_of((1 - core) * half, half), half)].astype(BF16)
    for rank in range(RANKS):
        normed_ref[rank] = dg(mine, out_mine_ref[rank], False, True) + dg(
            other, out_other_ref[rank], False, True
        )


def run_k5(*operands):
    width = operands[2].shape[1]
    outs = [shape(PART, width), shape(PART, width), shape(1, width), shape(RANKS, PART, WIDE)]
    return call(k5_body, outs, "middle_gradient", 10**9, 8 * 10**6)(*operands)


def n_body(scal_ref, first_ref, x_ref, gain_ref, d_middle_ref, out_ref, gains_ref):
    rows = pl.ds(pl.multiple_of(scal_ref[6] * PART, PART), PART)
    total = first_ref[0] + first_ref[1] + first_ref[2] + first_ref[3]
    pulled, _ = norm_pull(total[:PART], x_ref[rows, :], gain_ref[...].astype(F32))
    done = d_middle_ref[...] + pulled
    for at in range(RANKS):
        out_ref[at] = done
    gains_ref[...] = total[PART:]


def run_n(*operands):
    width = operands[2].shape[1]
    outs = [shape(RANKS, PART, width), shape(8, width)]
    return call(n_body, outs, "input_gradient", 10**7, 5 * 10**6)(*operands)


def turn(ref, turned_ref, spot):
    width = ref.shape[1]
    for at in range(0, width, 256):
        turned_ref[at : at + 256, spot] = ref[:, at : at + 256].T.astype(BF16)


def parts_of(turned_ref, scal_ref, along_x, step):
    row, col, core = scal_ref[3], scal_ref[4], scal_ref[5]
    rows = turned_ref.shape[0] // (2 * SIDE * SIDE)
    pieces = []
    for at in range(SIDE):
        if along_x:
            place = (at * SIDE + lax.rem(col + step, SIDE)) * 2 + core
        else:
            place = (lax.rem(row + step, SIDE) * SIDE + at) * 2 + core
        pieces.append(turned_ref[pl.ds(pl.multiple_of(place * rows, rows), rows), :])
    return jnp.concatenate(pieces, axis=0)


def put(ref, value, start):
    rows = value.shape[0] // SIDE
    for at in range(SIDE):
        ref[at, :, start : start + value.shape[1]] = value[at * rows : (at + 1) * rows]


def w1_body(scal_ref, mine_ref, other_ref, grad_ref, grad_other_ref, *rest):
    outs, (cols_ref, h_ref, d_ref) = rest[:8], rest[8:]
    tokens = mine_ref.shape[0]
    wide = cols_ref.shape[1]
    cut = wide // 2
    up_end = 2 * (wide // 3)
    for n, (ref, grad) in enumerate(((mine_ref, grad_ref), (other_ref, grad_other_ref))):
        spot = slice(n * tokens, (n + 1) * tokens)
        cols_ref[spot, :] = ref[:, :wide].astype(BF16)
        turn(ref.at[:, wide:], h_ref, spot)
        turn(grad, d_ref, spot)
    for step in range(SIDE):
        put(outs[step], dg(parts_of(h_ref, scal_ref, True, step), cols_ref[:, :cut], False, False), 0)
    for step in range(SIDE):
        out = outs[SIDE + step]
        rows = parts_of(h_ref, scal_ref, False, step)
        put(out, dg(rows, cols_ref[:, cut:up_end], False, False), 0)
        rows = parts_of(d_ref, scal_ref, False, step)
        put(out, dg(rows, cols_ref[:, up_end:], False, False), up_end - cut)


def run_w1(scal, mine, other, grad, grad_other):
    tokens, width = grad.shape
    wide = mine.shape[1] - width
    outs = [shape(SIDE, width // 32, wide // 2)] * 8
    scratch = [
        pltpu.VMEM((2 * tokens, wide), BF16),
        pltpu.VMEM((width, 2 * tokens), BF16),
        pltpu.VMEM((width, 2 * tokens), BF16),
    ]
    return call(w1_body, outs, "ffn_weight_sums", 3 * 10**9, 24 * 10**6, scratch)(
        scal, mine, other, grad, grad_other
    )


def w2_body(
    scal_ref, low_ref, low_other_ref, dq_ref, dq_other_ref, n_ref, n_other_ref,
    h1_ref, h1_other_ref, attn_ref, attn_other_ref, *rest,
):
    outs, (cols_ref, h_ref, d_ref) = rest[:8], rest[8:]
    tokens = low_ref.shape[0]
    late = low_ref.shape[1]
    cut = cols_ref.shape[1] // 2
    query_end = late + WIDE
    sides = (
        (low_ref, dq_ref, n_ref, h1_ref, attn_ref),
        (low_other_ref, dq_other_ref, n_other_ref, h1_other_ref, attn_other_ref),
    )
    for n, (low, dq, normed, h1, attn) in enumerate(sides):
        spot = slice(n * tokens, (n + 1) * tokens)
        cols_ref[spot, :late] = low[...].astype(BF16)
        cols_ref[spot, late:query_end] = dq[...].astype(BF16)
        cols_ref[spot, query_end:] = normed[...].astype(BF16)
        turn(h1, h_ref, spot)
        turn(attn, d_ref, spot)
    for step in range(SIDE):
        put(outs[step], dg(parts_of(h_ref, scal_ref, True, step), cols_ref[:, :cut], False, False), 0)
    for step in range(SIDE):
        out = outs[SIDE + step]
        rows = parts_of(h_ref, scal_ref, False, step)
        put(out, dg(rows, cols_ref[:, cut:query_end], False, False), 0)
        rows = parts_of(d_ref, scal_ref, False, step)
        put(out, dg(rows, cols_ref[:, query_end:], False, False), query_end - cut)


def run_w2(*operands):
    tokens, late = operands[1].shape
    width = operands[7].shape[1]
    wide = late + 2 * WIDE
    outs = [shape(SIDE, width // 32, wide // 2)] * 8
    scratch = [
        pltpu.VMEM((2 * tokens, wide), BF16),
        pltpu.VMEM((width, 2 * tokens), BF16),
        pltpu.VMEM((width, 2 * tokens), BF16),
    ]
    return call(w2_body, outs, "head_weight_sums", 3 * 10**9, 16 * 10**6, scratch)(*operands)


def fold_body(scal_ref, *refs):
    first, second, outs = refs[:4], refs[4:8], refs[8:]
    for group, place, target in ((first, scal_ref[3], outs[:4]), (second, scal_ref[4], outs[4:])):
        for step in range(SIDE):
            at = lax.rem(place + step, SIDE)
            target[step][...] = (group[0][at] + group[1][at]) + (group[2][at] + group[3][at])


def run_fold(scal, pieces):
    dims = pieces[0].shape[1:]
    return call(fold_body, [shape(*dims)] * 8, "fold_sums", 10**7, 10**7)(scal, *pieces)


def end_1_body(scal_ref, *refs):
    first, second, (gate_ref, up_ref, down_ref) = refs[:4], refs[4:8], refs[8:]
    one = (first[0][...] + first[1][...]) + (first[2][...] + first[3][...])
    two = (second[0][...] + second[1][...]) + (second[2][...] + second[3][...])
    units = gate_ref.shape[1]
    rest = one.shape[1] - units
    gate_ref[...] = one[:, :units]
    up_ref[:, :rest] = one[:, units:]
    up_ref[:, rest:] = two[:, : units - rest]
    down_ref[...] = two[:, units - rest :]


def run_end_1(scal, pieces):
    rows, wide = pieces[0].shape
    outs = [shape(rows, 2 * wide // 3)] * 3
    return call(end_1_body, outs, "ffn_gradients", 10**6, 3 * 10**6)(scal, *pieces)


def end_2_body(scal_ref, *refs):
    first, second, outs = refs[:4], refs[4:8], refs[8:]
    key_ref, value_ref, path_ref, beta_ref, query_ref, out_ref = outs
    one = (first[0][...] + first[1][...]) + (first[2][...] + first[3][...])
    two = (second[0][...] + second[1][...]) + (second[2][...] + second[3][...])
    rest = one.shape[1] - 2 * WIDE
    left = WIDE - rest
    key_ref[...] = one[:, :WIDE]
    value_ref[...] = one[:, WIDE : 2 * WIDE]
    path_ref[:, :rest] = one[:, 2 * WIDE :]
    path_ref[:, rest:] = two[:, :left]
    beta_ref[...] = two[:, left : left + HW]
    query_ref[...] = two[:, left + HW : left + HW + WIDE]
    out_ref[...] = two[:, left + HW + WIDE :]


def run_end_2(scal, pieces):
    rows = pieces[0].shape[0]
    outs = [shape(rows, WIDE)] * 3 + [shape(rows, HW)] + [shape(rows, WIDE)] * 2
    return call(end_2_body, outs, "head_gradients", 10**6, 3 * 10**6)(scal, *pieces)


def swap(value):
    return lax.ppermute(value, "c", [(0, 1), (1, 0)])


def shift(value, axis, step):
    return lax.ppermute(value, axis, [(i, (i + step) % SIDE) for i in range(SIDE)])


def exchange(pieces, first_axis, second_axis):
    moved = {}
    for step in (2, 1, 3):
        moved[step] = shift(pieces[step], first_axis, step)
        moved[4 + step] = shift(pieces[4 + step], second_axis, step)
    return [pieces[0], moved[1], moved[2], moved[3], pieces[4], moved[5], moved[6], moved[7]]


def trade(value, axis):
    return lax.all_to_all(value, axis, 0, 0)


def after(value, *others):
    return lax.optimization_barrier((value,) + others)[0]


def local(
    block_input, gain_in, w_query, w_key, w_value, w_path, w_beta, w_out,
    gain_mid, w_gate, w_up, w_down, out_grad, lengths,
):
    tokens, width = block_input.shape
    row, col, core = (lax.axis_index(name) for name in CTX)
    rank = lax.axis_index("z")
    start = lax.axis_index(CTX) * tokens
    scal = jnp.stack([start, lengths[0], lengths[1], row, col, core, rank]).astype(jnp.int32)
    unity = (lengths[0] > 0).astype(F32)
    gain_1 = gain_in.reshape(1, width)
    gain_2 = gain_mid.reshape(1, width)
    w_beta_wide = jnp.pad(w_beta, ((0, 0), (0, HW - w_beta.shape[1])))
    heads_w = (w_query, w_key, w_value, w_path, w_beta_wide)

    out_half = lax.dynamic_slice_in_dim(w_out, core * (width // 2), width // 2, 1)
    out_mine = lax.all_gather(out_half.astype(F32), "z", axis=0)
    out_other = swap(out_mine)
    grad_other = swap(out_grad)

    h1, q, k, v, w, aux, inv, kp, b, kt, tu = run_a1(scal, block_input, gain_1, *heads_w)
    both = lax.all_gather(tu, "c", axis=0)
    u_c, spread = run_s1(scal, both)
    along_x = lax.all_gather(trade(spread, "x"), "c", axis=0)
    t_x, u_x, spread = run_s2(scal, along_x)
    c, sc, qt, inside = run_a2(scal, q, k, v, w, inv, kp)
    along_y = lax.all_gather(trade(spread, "y"), "c", axis=0)
    t_y, states = run_s3(scal, along_y, t_x, u_x, both, u_c)
    states = lax.all_gather(states, "c", axis=0)
    out_mine_low = (out_mine * unity).astype(BF16)
    out_other_low = (out_other * unity).astype(BF16)
    states = after(states, out_mine_low, out_other_low, inside)
    mixed, normed, spread, carried = run_a3(scal, inside, qt, states)
    normed_all = trade(spread, "z")
    middle, sent, second_part, down_part = run_ffn(
        scal, normed_all, out_mine_low, out_other_low, block_input, gain_2, out_grad,
        w_gate, w_up, w_down,
    )

    second = trade(second_part.reshape(RANKS, PART, width), "z")
    sent_other = swap(sent)
    ffn_pieces = run_w1(scal, sent, sent_other, out_grad, grad_other)
    second = after(second, *ffn_pieces)
    d_middle, attn, gain_mid_part, d_normed = run_k5(
        scal, second, middle, out_grad, gain_2, out_mine_low, out_other_low
    )
    ffn_pieces = exchange(ffn_pieces, "x", "y")
    d_normed = trade(d_normed, "z").reshape(tokens, WIDE)
    block_output = middle + lax.psum(after(down_part, d_normed), "z")
    attn_all = lax.all_gather(attn, "z", axis=0, tiled=True)
    dm, state_grad = run_b1(scal, d_normed, mixed, qt)
    pair = lax.all_gather(state_grad, "c", axis=0)
    g_1, spread = run_t1(scal, pair, both)
    g_x = trade(spread, "x")
    spread = run_t2(scal, g_x, t_x)
    dq, dk, dv, dw, dkp, xc = run_b2(
        scal, dm, carried, q, k, v, w, aux, inv, kp, c, sc
    )
    g_y = trade(spread, "y")
    later = run_t3(scal, g_y, g_x, t_y, t_x, both, g_1)
    later = lax.all_gather(later, "c", axis=0)
    ffn_pieces = run_fold(scal, ffn_pieces)
    later = after(later, *ffn_pieces)
    ffn_pieces = exchange(ffn_pieces, "y", "x")

    low, first_part = run_b3(
        scal, block_input, gain_mid_part, later, carried, k, v, w, aux, inv, kp, b, kt,
        dq, dk, dv, dw, dkp, xc, *heads_w,
    )
    first = trade(first_part, "z")
    gate_out, up_out, down_out = run_end_1(scal, ffn_pieces)
    low_other = swap(low)
    head_pieces = run_w2(
        scal, low, low_other, dq, swap(dq), normed, swap(normed), h1, swap(h1),
        attn_all, swap(attn_all),
    )
    head_pieces = run_fold(scal, exchange(head_pieces, "x", "y"))
    spread, gains = run_n(scal, first, block_input, gain_1, d_middle)
    input_grad = trade(spread, "z").reshape(tokens, width)
    gains = jnp.swapaxes(gains[:2].reshape(2, 32, width // 32), 0, 1)
    gains = jnp.sum(trade(gains, CTX), axis=0)
    key_out, value_out, path_out, beta_out, query_out, out_out = run_end_2(
        scal, exchange(head_pieces, "y", "x")
    )
    return (
        block_output, input_grad, gains[0], query_out, key_out, value_out, path_out,
        beta_out[:, : w_beta.shape[1]], out_out.T, gains[1], gate_out, up_out, down_out.T,
    )


def solution(mesh):
    fine = Mesh(mesh.devices.reshape(SIDE, SIDE, 2, RANKS), ("y", "x", "c", "z"))
    tokens, heads, whole = P(CTX, None), P(None, "z"), P()
    in_specs = (
        tokens, whole, heads, heads, heads, heads, heads, P("z", None),
        whole, heads, heads, P("z", None), tokens, whole,
    )
    weight = P(CTX, "z")
    out_specs = (
        tokens, tokens, P(CTX), weight, weight, weight, weight, weight,
        P("z", CTX), P(CTX), weight, weight, P("z", CTX),
    )
    return jax.shard_map(local, mesh=fine, in_specs=in_specs, out_specs=out_specs, check_vma=False)
```

```python
import jax
import jax.numpy as jnp
from jax import lax
from jax.experimental import pallas as pl
from jax.experimental.pallas import tpu as pltpu
from jax.sharding import Mesh
from jax.sharding import PartitionSpec as P

EPSILON = 1e-06
HEAD_EPSILON = 0.01
F32 = jnp.float32
BF16 = jnp.bfloat16
HEADS = 3
HW = 128
LEN = 256
RANKS = 4
PART = LEN // RANKS
SIDE = 4
CTX = ("y", "x", "c")
VMEM_LIMIT = 56 * 1024 * 1024


def split(value):
    high = value.astype(BF16)
    return high, (value - high.astype(F32)).astype(BF16)


def dg(left, right, ta, tb):
    dims = (((0 if ta else 1,), (1 if tb else 0,)), ((), ()))
    return lax.dot_general(left, right, dims, preferred_element_type=F32)


def mm(left, right, ta=False, tb=False):
    left = left if isinstance(left, tuple) else split(left)
    right = right if isinstance(right, tuple) else split(right)
    return dg(left[0], right[0], ta, tb) + (
        dg(left[0], right[1], ta, tb) + dg(left[1], right[0], ta, tb)
    )


def iota(shape, dim):
    return lax.broadcasted_iota(jnp.int32, shape, dim)


def cols(head):
    return slice(head * HW, (head + 1) * HW)


def segments(spot, scal):
    second = scal[1]
    third = second + scal[2]
    return (spot >= second).astype(jnp.int32) + (spot >= third).astype(jnp.int32)


def small_inverses(scaled):
    row = iota((HW, HW), 0)
    lane = iota((HW, HW), 1)
    same = (row // 8) == (lane // 8)
    packed = []
    for one in scaled:
        for half in range(2):
            block = jnp.where(same, one[half * HW : (half + 1) * HW, half * HW : (half + 1) * HW], 0.0)
            packed.append(jnp.sum(block.reshape(HW // 8, 8, HW), axis=0))
    count = len(packed)
    high, low = split(jnp.concatenate(packed, axis=0))
    lane_8 = iota((8, HW), 1) % 8
    spread = {}
    for k in range(1, 8):
        unit = ((row // 8 == lane // 8) & (row % 8 == k)).astype(BF16)
        both = dg(high, unit, False, False) + dg(low, unit, False, False)
        spread[k] = both.reshape(count, 8, HW)
    rows = {}
    for i in range(7, -1, -1):
        value = jnp.broadcast_to((lane_8[:1] == i).astype(F32)[None], (count, 1, HW))
        for k in range(i + 1, 8):
            value = value - spread[k][:, i : i + 1, :] * rows[k]
        rows[i] = value
    done = jnp.concatenate([rows[i] for i in range(8)], axis=1)
    out = []
    zero = jnp.zeros((HW, HW), F32)
    for head in range(count // 2):
        halves = [
            jnp.where(same, jnp.concatenate([done[2 * head + half]] * (HW // 8), axis=0), 0.0)
            for half in range(2)
        ]
        out.append(
            jnp.concatenate(
                [
                    jnp.concatenate([halves[0], zero], axis=1),
                    jnp.concatenate([zero, halves[1]], axis=1),
                ],
                axis=0,
            )
        )
    return out


def upper_rows(value, width):
    return jnp.concatenate(
        [value[at : at + width] for at in range(0, value.shape[0], 2 * width)], axis=0
    )


def put_upper(value, upper, width):
    pieces = []
    for n, at in enumerate(range(0, value.shape[0], 2 * width)):
        pieces.append(upper[n * width : (n + 1) * width])
        pieces.append(value[at + width : at + 2 * width])
    return jnp.concatenate(pieces, axis=0)


def inverses(scaled):
    out = small_inverses(scaled)
    row = iota((LEN, LEN), 0)
    lane = iota((LEN, LEN), 1)
    width = 8
    while width < LEN:
        pair = (row // (2 * width) == lane // (2 * width)) & (row // width < lane // width)
        link = [upper_rows(jnp.where(pair, one, 0.0), width) for one in scaled]
        parts = [split(one) for one in out]
        first = [mm(a, b) for a, b in zip(link, parts)]
        empty = jnp.zeros((LEN, LEN), F32)
        wide = [put_upper(empty, one, width) for one in first]
        tops = [
            (upper_rows(a, width), upper_rows(b, width)) for a, b in parts
        ]
        second = [mm(a, b) for a, b in zip(tops, wide)]
        out = [
            put_upper(one, upper_rows(one, width) - new, width) for one, new in zip(out, second)
        ]
        width *= 2
    return out


def unit_rows(value):
    scale = lax.rsqrt(jnp.sum(value * value, axis=-1, keepdims=True) + EPSILON)
    return value * scale, scale


def a1_body(
    scal_ref, x_ref, gain_ref, wq_ref, wk_ref, wv_ref, ww_ref, wb_ref,
    h1_ref, q_ref, k_ref, v_ref, w_ref, aux_ref, inv_ref, kp_ref, b_ref, kt_ref, tu_ref,
):
    x = x_ref[...]
    scale = lax.rsqrt(jnp.mean(x * x, axis=-1, keepdims=True) + EPSILON)
    h1 = (x * scale * gain_ref[...].astype(F32)).astype(BF16)
    h1_ref[...] = h1.astype(F32)
    start = scal_ref[0]
    token = iota((LEN, 1), 0) + start
    segment = segments(token, scal_ref)
    end_segment = segments(jnp.full((1, 1), LEN - 1, jnp.int32) + start, scal_ref)
    before = start - 1
    before_segment = jnp.where(start == 0, -1, segments(jnp.full((1, 1), 0, jnp.int32) + before, scal_ref))
    last = (segment == end_segment).astype(F32)
    carry_all = (end_segment == before_segment).astype(F32)
    row = iota((LEN, LEN), 0)
    lane = iota((LEN, LEN), 1)
    later = row < lane
    beta = 1.0 + jax.nn.sigmoid(dg(h1, wb_ref[...], False, True))
    beta_rows = 1.0 + jax.nn.sigmoid(dg(wb_ref[...], h1, False, True))
    pr = dg(h1, ww_ref[...], False, False)
    kr = dg(h1, wk_ref[...], False, False)
    w_all, k_all, aux = [], [], []
    for head in range(HEADS):
        w, w_scale = unit_rows(pr[:, cols(head)])
        k, k_scale = unit_rows(kr[:, cols(head)])
        w_ref[:, cols(head)] = w
        k_ref[:, cols(head)] = k
        w_all.append(w)
        k_all.append(k)
        aux.append((w_scale, k_scale))
    w_split = [split(w) for w in w_all]
    k_split = [split(k) for k in k_all]
    scaled = [
        jnp.where(later, mm(w_split[h], w_split[h], tb=True), 0.0) * beta[:, h : h + 1]
        for h in range(HEADS)
    ]
    inverse = [
        one * beta_rows[h : h + 1, :] for h, one in enumerate(inverses(scaled))
    ]
    vr = dg(h1, wv_ref[...], False, False)
    qr = dg(h1, wq_ref[...], False, False)
    v_ref[...] = vr
    lane_aux = iota((LEN, HW), 1)
    packed = jnp.zeros((LEN, HW), F32)
    eye = (iota((HW, HW), 0) == iota((HW, HW), 1)).astype(F32)
    for head in range(HEADS):
        q, q_scale = unit_rows(qr[:, cols(head)])
        q_ref[:, cols(head)] = q
        spots = (
            (head, beta[:, head : head + 1]),
            (8 + head, q_scale),
            (16 + head, aux[head][1]),
            (24 + head, aux[head][0]),
        )
        for at, value in spots:
            packed = jnp.where(lane_aux == at, value, packed)
        inv_ref[head] = inverse[head]
        inv_split = split(inverse[head])
        folded = mm(inv_split, w_split[head])
        b_ref[:, cols(head)] = folded
        folded_split = split(folded)
        kp = jnp.where(later, mm(k_split[head], w_split[head], tb=True), 0.0)
        kp_ref[head] = kp
        kt = k_all[head] - mm(kp, folded_split)
        kt_ref[:, cols(head)] = kt
        tu_ref[0, head] = carry_all * (eye - mm(w_split[head], folded_split, ta=True))
        tu_ref[1, head] = mm(vr[:, cols(head)], kt * last, ta=True)
    aux_ref[...] = packed


def shape(*dims, dtype=F32):
    return jax.ShapeDtypeStruct(dims, dtype)


MIB = 1024 * 1024
SLACK = 10 * MIB
COST = pl.CostEstimate(flops=10**4, bytes_accessed=10**4, transcendentals=0)


def size_of(*arrays):
    total = 0
    for one in arrays:
        count = one.dtype.itemsize
        for extent in one.shape:
            count *= extent
        total += count
    return total


def call(body, outs, name, scratch=(), limit=None):
    smem = pl.BlockSpec(memory_space=pltpu.SMEM)
    vmem = pl.BlockSpec(memory_space=pltpu.VMEM)

    def run(*operands):
        need = size_of(*operands, *outs, *scratch) + SLACK
        return pl.pallas_call(
            body,
            out_shape=outs,
            in_specs=[smem] + [vmem] * (len(operands) - 1),
            out_specs=[vmem] * len(outs),
            scratch_shapes=list(scratch),
            name=name,
            cost_estimate=COST,
            compiler_params=pltpu.CompilerParams(vmem_limit_bytes=limit or need),
        )(*operands)

    return run


WIDE = HEADS * HW


def run_a1(*operands):
    outs = [
        shape(LEN, operands[1].shape[1]),
        shape(LEN, WIDE), shape(LEN, WIDE), shape(LEN, WIDE), shape(LEN, WIDE),
        shape(LEN, HW),
        shape(HEADS, LEN, LEN), shape(HEADS, LEN, LEN),
        shape(LEN, WIDE), shape(LEN, WIDE),
        shape(2, HEADS, HW, HW),
    ]
    return call(a1_body, outs, "local_parts", limit=VMEM_LIMIT)(*operands)


def a2_body(
    scal_ref, q_ref, k_ref, v_ref, w_ref, inv_ref, kp_ref,
    c_ref, sc_ref, qt_ref, in_ref,
):
    start = scal_ref[0]
    segment = segments(iota((LEN, LEN), 0) + start, scal_ref)
    segment_t = segments(iota((LEN, LEN), 1) + start, scal_ref)
    row = iota((LEN, LEN), 0)
    lane = iota((LEN, LEN), 1)
    up_to = row <= lane
    seen = up_to & (segment == segment_t)
    for head in range(HEADS):
        q = q_ref[:, cols(head)]
        q_split = split(q)
        w_split = split(w_ref[:, cols(head)])
        pq = jnp.where(up_to, mm(w_split, q_split, tb=True), 0.0)
        c = mm(inv_ref[head], pq)
        c_ref[head] = c
        c_split = split(c)
        qt_ref[:, cols(head)] = q - mm(c_split, w_split, ta=True)
        scores = mm(k_ref[:, cols(head)], q_split, tb=True) - mm(kp_ref[head], c_split)
        scores = jnp.where(seen, scores, 0.0)
        sc_ref[head] = scores
        in_ref[:, cols(head)] = mm(scores, v_ref[:, cols(head)], ta=True)


def run_a2(*operands):
    outs = [shape(HEADS, LEN, LEN), shape(HEADS, LEN, LEN), shape(LEN, WIDE), shape(LEN, WIDE)]
    return call(a2_body, outs, "inside_parts", limit=VMEM_LIMIT)(*operands)


def carry_of(start, scal_ref):
    token = iota((LEN, 1), 0) + start
    before = jnp.full((1, 1), 0, jnp.int32) + (start - 1)
    before_segment = jnp.where(start == 0, -1, segments(before, scal_ref))
    return (segments(token, scal_ref) == before_segment).astype(F32)


def pair_of(ref, core, head):
    return jnp.concatenate([ref[0, core, head], ref[1, core, head]], axis=0)


def a3_body(scal_ref, in_ref, qt_ref, states_ref, mixed_ref, normed_ref, spread_ref, carried_ref):
    carry = carry_of(scal_ref[0], scal_ref)
    core = scal_ref[5]
    for head in range(HEADS):
        carried = pair_of(states_ref, core, head)
        carried_ref[head] = carried
        mixed = in_ref[:, cols(head)] + carry * mm(qt_ref[:, cols(head)], carried, tb=True)
        mixed_ref[:, cols(head)] = mixed
        scale = lax.rsqrt(jnp.mean(mixed * mixed, axis=-1, keepdims=True) + HEAD_EPSILON)
        low = (mixed * scale).astype(BF16).astype(F32)
        normed_ref[:, cols(head)] = low
        for at in range(RANKS):
            spread_ref[at, :, cols(head)] = low


def run_a3(*operands):
    outs = [shape(LEN, WIDE), shape(LEN, WIDE), shape(RANKS, LEN, WIDE), shape(HEADS, HW, HW)]
    return call(a3_body, outs, "normed_heads")(*operands)


def b1_body(scal_ref, dn_ref, mixed_ref, qt_ref, dm_ref, sg_ref):
    carry = carry_of(scal_ref[0], scal_ref)
    for head in range(HEADS):
        mixed = mixed_ref[:, cols(head)]
        dn = dn_ref[:, cols(head)]
        scale = lax.rsqrt(jnp.mean(mixed * mixed, axis=-1, keepdims=True) + HEAD_EPSILON)
        drift = jnp.mean(dn * mixed, axis=-1, keepdims=True) * (scale * scale)
        dm = scale * (dn - mixed * drift)
        dm_ref[:, cols(head)] = dm
        sg_ref[head] = mm(dm * carry, qt_ref[:, cols(head)], ta=True)


def run_b1(*operands):
    outs = [shape(LEN, WIDE), shape(HEADS, HW, HW)]
    return call(b1_body, outs, "state_gradient")(*operands)


def unit_pull(unit, scale, grad):
    return scale * (grad - unit * jnp.sum(unit * grad, axis=-1, keepdims=True))


def b2_body(
    scal_ref, dm_ref, carried_ref, q_ref, k_ref, v_ref, w_ref, aux_ref, inv_ref, kp_ref,
    c_ref, sc_ref,
    dq_ref, dk_ref, dv_ref, dw_ref, dkp_ref, xc_ref,
):
    start = scal_ref[0]
    carry = carry_of(start, scal_ref)
    row = iota((LEN, LEN), 0)
    lane = iota((LEN, LEN), 1)
    up_to = row <= lane
    seen = up_to & (
        segments(row + start, scal_ref) == segments(lane + start, scal_ref)
    )
    for head in range(HEADS):
        q = q_ref[:, cols(head)]
        q_split = split(q)
        w_split = split(w_ref[:, cols(head)])
        k_split = split(k_ref[:, cols(head)])
        c_split = split(c_ref[head])
        kp_split = split(kp_ref[head])
        dm = dm_ref[:, cols(head)]
        dm_split = split(dm)
        dqt = mm(dm * carry, carried_ref[head])
        dqt_split = split(dqt)
        ds = jnp.where(seen, mm(v_ref[:, cols(head)], dm_split, tb=True), 0.0)
        ds_split = split(ds)
        dv_ref[:, cols(head)] = mm(sc_ref[head], dm_split)
        dk = mm(ds_split, q_split)
        dq = dqt + mm(ds_split, k_split, ta=True)
        dkp_ref[head] = mm(ds_split, c_split, tb=True)
        dc = mm(kp_split, ds_split, ta=True) + mm(w_split, dqt_split, tb=True)
        dw = mm(c_split, dqt_split)
        x = mm(inv_ref[head], dc, ta=True)
        xc_ref[head] = mm(x, c_split, tb=True)
        dpq_split = split(jnp.where(up_to, x, 0.0))
        dw_ref[:, cols(head)] = dw + mm(dpq_split, q_split)
        dq = dq - mm(dpq_split, w_split, ta=True)
        dk_ref[:, cols(head)] = dk
        scale = aux_ref[:, 8 + head : 9 + head]
        dq_ref[:, cols(head)] = unit_pull(q, scale, dq).astype(BF16).astype(F32)


def run_b2(*operands):
    outs = [
        shape(LEN, WIDE), shape(LEN, WIDE), shape(LEN, WIDE), shape(LEN, WIDE),
        shape(HEADS, LEN, LEN), shape(HEADS, LEN, LEN),
    ]
    return call(b2_body, outs, "inside_gradients", limit=VMEM_LIMIT)(*operands)


def b3_body(
    scal_ref, states_ref, carried_ref, k_ref, v_ref, w_ref, aux_ref,
    inv_ref, kp_ref, b_ref, kt_ref, dk_ref, dv_ref, dw_ref, dkp_ref, xc_ref,
    low_ref,
):
    start = scal_ref[0]
    core = scal_ref[5]
    segment = segments(iota((LEN, 1), 0) + start, scal_ref)
    end_segment = segments(jnp.full((1, 1), LEN - 1, jnp.int32) + start, scal_ref)
    before = jnp.full((1, 1), 0, jnp.int32) + (start - 1)
    before_segment = jnp.where(start == 0, -1, segments(before, scal_ref))
    last = (segment == end_segment).astype(F32)
    carry_all = (end_segment == before_segment).astype(F32)
    row = iota((LEN, LEN), 0)
    lane = iota((LEN, LEN), 1)
    later_mask = row < lane
    lane_aux = iota((LEN, HW), 1)
    d_beta = jnp.zeros((LEN, HW), F32)
    for head in range(HEADS):
        later = pair_of(states_ref, core, head)
        later_split = split(later)
        dt_split = split(carry_all * mm(carried_ref[head], later_split, ta=True))
        w = w_ref[:, cols(head)]
        w_split = split(w)
        k = k_ref[:, cols(head)]
        v = v_ref[:, cols(head)]
        b_split = split(b_ref[:, cols(head)])
        kp_split = split(kp_ref[head])
        dv = dv_ref[:, cols(head)] + last * mm(kt_ref[:, cols(head)], later_split, tb=True)
        dkt = last * mm(v, later_split)
        dkt_split = split(dkt)
        db = mm(w_split, dt_split) + mm(kp_split, dkt_split, ta=True)
        y = mm(inv_ref[head], db, ta=True)
        y_split = split(y)
        dw = dw_ref[:, cols(head)] + mm(b_split, dt_split, tb=True) + y
        dkp = jnp.where(later_mask, dkp_ref[head] + mm(dkt_split, b_split, tb=True), 0.0)
        dkp_split = split(dkp)
        dk = dk_ref[:, cols(head)] + dkt - mm(dkp_split, w_split)
        dw = dw + mm(dkp_split, split(k), ta=True)
        dm = xc_ref[head] + mm(y_split, b_split, tb=True)
        dn_split = split(jnp.where(later_mask, dm, 0.0))
        dw = mm(dn_split, w_split) + mm(dn_split, w_split, ta=True) - dw
        diagonal = jnp.sum(jnp.where(row == lane, dm, 0.0), axis=-1, keepdims=True)
        beta = aux_ref[:, head : head + 1]
        sig = beta - 1.0
        dbl = -diagonal / (beta * beta) * sig * (1.0 - sig)
        d_beta = jnp.where(lane_aux == head, dbl, d_beta)
        low_ref[:, cols(head)] = unit_pull(k, aux_ref[:, 16 + head : 17 + head], dk).astype(BF16).astype(F32)
        low_ref[:, WIDE + head * HW : WIDE + (head + 1) * HW] = dv.astype(BF16).astype(F32)
        low_ref[:, 2 * WIDE + head * HW : 2 * WIDE + (head + 1) * HW] = unit_pull(
            w, aux_ref[:, 24 + head : 25 + head], dw
        ).astype(BF16).astype(F32)
    low_ref[:, 3 * WIDE :] = d_beta.astype(BF16).astype(F32)


def run_b3(*operands):
    outs = [shape(LEN, 3 * WIDE + HW)]
    return call(b3_body, outs, "late_gradients", limit=VMEM_LIMIT)(*operands)[0]


def b4_body(
    scal_ref, x_ref, gain_mid_ref, dq_ref, low_ref, wq_ref, wk_ref, wv_ref, ww_ref, wb_ref, dh_ref
):
    total = dg(dq_ref[...].astype(BF16), wq_ref[...], False, True)
    for at, ref in enumerate((wk_ref, wv_ref, ww_ref)):
        low = low_ref[:, at * WIDE : at * WIDE + ref.shape[1]].astype(BF16)
        total = total + dg(low, ref[...], False, True)
    beta_cols = wb_ref[...].astype(F32)
    for head in range(HEADS):
        at = 3 * WIDE + head
        total = total + low_ref[:, at : at + 1] * beta_cols[head : head + 1, :]
    for at in range(RANKS):
        dh_ref[at, :PART, :] = total[at * PART : (at + 1) * PART]
    x = x_ref[...]
    scale = lax.rsqrt(jnp.mean(x * x, axis=-1, keepdims=True) + EPSILON)
    gain_in = jnp.sum(total * x * scale, axis=0, keepdims=True)
    rows = iota((8, x.shape[1]), 0)
    both = jnp.where(rows == 0, gain_in, jnp.where(rows == 1, gain_mid_ref[...], 0.0))
    for at in range(RANKS):
        dh_ref[at, PART:, :] = both


def run_b4(*operands):
    outs = [shape(RANKS, PART + 8, operands[1].shape[1])]
    return call(b4_body, outs, "first_norm_part", limit=VMEM_LIMIT)(*operands)[0]


def half_of(core):
    return pl.ds(pl.multiple_of(core * (HW // 2), HW // 2), HW // 2)


def s1_body(scal_ref, both_ref, u_ref, out_ref):
    rows = half_of(scal_ref[5])
    for head in range(HEADS):
        t_1 = split(both_ref[1, 0, head])
        u_0 = both_ref[0, 1, head, rows, :]
        u_1 = both_ref[1, 1, head, rows, :]
        u_ref[0, head] = u_0
        u_ref[1, head] = u_1
        chip_t = mm(both_ref[0, 0, head, rows, :], t_1)
        chip_u = mm(u_0, t_1) + u_1
        for at in range(SIDE):
            out_ref[at, 0, head] = chip_t
            out_ref[at, 1, head] = chip_u


def run_s1(*operands):
    outs = [shape(2, HEADS, HW // 2, HW), shape(SIDE, 2, HEADS, HW // 2, HW)]
    return call(s1_body, outs, "chip_state")(*operands)


def join_halves(t_ref, mine_ref, other_ref, core, at, head):
    t_ref[at, head, half_of(core), :] = mine_ref[at, 0, head]
    t_ref[at, head, half_of(1 - core), :] = other_ref[at, 0, head]


def s2_body(scal_ref, mine_ref, other_ref, t_ref, u_ref, out_ref):
    core = scal_ref[5]
    rows = half_of(core)
    for head in range(HEADS):
        for at in range(SIDE):
            join_halves(t_ref, mine_ref, other_ref, core, at, head)
            u_ref[at, head] = mine_ref[at, 1, head]
    for head in range(HEADS):
        t_1 = split(t_ref[1, head])
        t_3 = split(t_ref[3, head])
        t_23 = split(mm(t_ref[2, head], t_3))
        row_t = mm(mm(t_ref[0, head, rows, :], t_1), t_23)
        row_u = mm(mm(u_ref[0, head], t_1) + u_ref[1, head], t_23)
        row_u = row_u + mm(u_ref[2, head], t_3) + u_ref[3, head]
        for at in range(SIDE):
            out_ref[at, 0, head] = row_t
            out_ref[at, 1, head] = row_u


def run_s2(*operands):
    outs = [
        shape(SIDE, HEADS, HW, HW),
        shape(SIDE, HEADS, HW // 2, HW),
        shape(SIDE, 2, HEADS, HW // 2, HW),
    ]
    return call(s2_body, outs, "row_state")(*operands)


def s3_body(scal_ref, mine_ref, other_ref, tx_ref, ux_ref, both_ref, uc_ref, ty_ref, out_ref):
    row, col, core = scal_ref[3], scal_ref[4], scal_ref[5]
    for head in range(HEADS):
        for at in range(SIDE):
            join_halves(ty_ref, mine_ref, other_ref, core, at, head)
    for head in range(HEADS):
        state = jnp.where(row > 0, mine_ref[0, 1, head], 0.0)
        for at in range(1, SIDE - 1):
            new = mm(state, ty_ref[at, head]) + mine_ref[at, 1, head]
            state = jnp.where(at < row, new, state)
        for at in range(SIDE - 1):
            new = mm(state, tx_ref[at, head]) + ux_ref[at, head]
            state = jnp.where(at < col, new, state)
        out_ref[0, head] = state
        out_ref[1, head] = mm(state, both_ref[0, 0, head]) + uc_ref[0, head]


def run_s3(*operands):
    outs = [shape(SIDE, HEADS, HW, HW), shape(2, HEADS, HW // 2, HW)]
    return call(s3_body, outs, "block_state")(*operands)


def t1_body(scal_ref, pair_ref, both_ref, g_ref, out_ref):
    rows = half_of(scal_ref[5])
    for head in range(HEADS):
        g_1 = pair_ref[1, head, rows, :]
        g_ref[head] = g_1
        chip = mm(g_1, both_ref[0, 0, head], tb=True) + pair_ref[0, head, rows, :]
        for at in range(SIDE):
            out_ref[at, head] = chip


def run_t1(*operands):
    outs = [shape(HEADS, HW // 2, HW), shape(SIDE, HEADS, HW // 2, HW)]
    return call(t1_body, outs, "chip_gradient")(*operands)


def t2_body(scal_ref, g_ref, t_ref, out_ref):
    for head in range(HEADS):
        total = g_ref[3, head]
        for at in (2, 1, 0):
            total = mm(total, t_ref[at, head], tb=True) + g_ref[at, head]
        for at in range(SIDE):
            out_ref[at, head] = total


def run_t2(*operands):
    outs = [shape(SIDE, HEADS, HW // 2, HW)]
    return call(t2_body, outs, "row_gradient")(*operands)[0]


def t3_body(scal_ref, gy_ref, gx_ref, ty_ref, tx_ref, both_ref, g_ref, out_ref):
    row, col = scal_ref[3], scal_ref[4]
    for head in range(HEADS):
        later = jnp.where(row < SIDE - 1, gy_ref[3, head], 0.0)
        for at in (2, 1):
            new = mm(later, ty_ref[at, head], tb=True) + gy_ref[at, head]
            later = jnp.where(at > row, new, later)
        for at in (3, 2, 1):
            new = mm(later, tx_ref[at, head], tb=True) + gx_ref[at, head]
            later = jnp.where(at > col, new, later)
        out_ref[1, head] = later
        out_ref[0, head] = mm(later, both_ref[1, 0, head], tb=True) + g_ref[head]


def run_t3(*operands):
    outs = [shape(2, HEADS, HW // 2, HW)]
    return call(t3_body, outs, "block_gradient")(*operands)[0]


def middle_body(
    scal_ref, normed_ref, out_mine_ref, out_other_ref, x_ref, gain_ref, middle_ref, h_ref
):
    core = scal_ref[5]
    half = x_ref.shape[1] // 2
    low = [normed_ref[rank].astype(BF16) for rank in range(RANKS)]
    for ref, at in ((out_mine_ref, core), (out_other_ref, 1 - core)):
        spot = pl.ds(pl.multiple_of(at * half, half), half)
        total = x_ref[:, spot]
        for rank in range(RANKS):
            total = total + dg(low[rank], ref[rank], False, False)
        middle_ref[:, spot] = total
    middle = middle_ref[...]
    scale = lax.rsqrt(jnp.mean(middle * middle, axis=-1, keepdims=True) + EPSILON)
    h_ref[...] = (middle * scale * gain_ref[...].astype(F32)).astype(BF16).astype(F32)


def run_middle(*operands):
    outs = [shape(*operands[4].shape)] * 2
    return call(middle_body, outs, "middle", limit=VMEM_LIMIT)(*operands)


def ffn_body(
    h_ref, grad_ref, gate_ref, up_ref, down_ref, sent_ref, dh_ref, down_part_ref, low_ref, d_ref
):
    step = pl.program_id(0)
    units = gate_ref.shape[1]
    hidden_all = units * pl.num_programs(0)

    @pl.when(step == 0)
    def _():
        low_ref[...] = h_ref[...].astype(BF16)
        d_ref[...] = grad_ref[...].astype(BF16)

    h2 = low_ref[...]
    gate = dg(h2, gate_ref[...], False, False)
    up = dg(h2, up_ref[...], False, False)
    sig = jax.nn.sigmoid(gate)
    silu = gate * sig
    hidden = (silu * up).astype(BF16)
    d_hidden = dg(d_ref[...], down_ref[...], False, True)
    d_gate = (d_hidden * up * sig * (1.0 + gate * (1.0 - sig))).astype(BF16)
    d_up = (d_hidden * silu).astype(BF16)
    for n, value in enumerate((d_gate, d_up, hidden)):
        spot = pl.ds(pl.multiple_of(n * hidden_all + step * units, units), units)
        sent_ref[:, spot] = value.astype(F32)
    d_h = dg(d_gate, gate_ref[...], False, True) + dg(d_up, up_ref[...], False, True)
    down = dg(hidden, down_ref[...], False, False)

    @pl.when(step == 0)
    def _():
        dh_ref[...] = d_h
        down_part_ref[...] = down

    @pl.when(step > 0)
    def _():
        dh_ref[...] += d_h
        down_part_ref[...] += down


def run_ffn(h2, grad, w_gate, w_up, w_down):
    tokens, width = grad.shape
    hidden = w_gate.shape[1]
    steps = 4
    units = hidden // steps

    def whole(array):
        dims = array.shape
        return pl.BlockSpec(dims, lambda i: (0,) * len(dims))

    outs = [shape(tokens, 3 * hidden), shape(tokens, width), shape(tokens, width)]
    across = pl.BlockSpec((width, units), lambda i: (0, i))
    return pl.pallas_call(
        ffn_body,
        grid=(steps,),
        out_shape=outs,
        in_specs=[whole(h2), whole(grad), across, across]
        + [pl.BlockSpec((units, width), lambda i: (i, 0))],
        out_specs=[whole(a) for a in outs],
        scratch_shapes=[pltpu.VMEM((tokens, width), BF16)] * 2,
        name="feed_forward",
        cost_estimate=COST,
        compiler_params=pltpu.CompilerParams(
            vmem_limit_bytes=VMEM_LIMIT, dimension_semantics=("arbitrary",)
        ),
    )(h2, grad, w_gate, w_up, w_down)


def norm_pull(grad, values, gain):
    scale = lax.rsqrt(jnp.mean(values * values, axis=-1, keepdims=True) + EPSILON)
    turned = gain * grad
    drift = jnp.mean(turned * values, axis=-1, keepdims=True) * (scale * scale * scale)
    return scale * turned - values * drift, grad * values * scale


def k5_body(
    scal_ref, second_ref, middle_ref, grad_ref, gain_ref, out_mine_ref, out_other_ref,
    d_middle_ref, attn_ref, gain_out_ref, normed_ref,
):
    core = scal_ref[5]
    second = second_ref[0] + second_ref[1] + second_ref[2] + second_ref[3]
    pulled, summed = norm_pull(second, middle_ref[...], gain_ref[...].astype(F32))
    d_middle = grad_ref[...] + pulled
    d_middle_ref[...] = d_middle
    gain_out_ref[...] = jnp.sum(summed, axis=0, keepdims=True)
    attn_ref[...] = d_middle.astype(BF16).astype(F32)
    half = d_middle.shape[1] // 2
    mine = attn_ref[:, pl.ds(pl.multiple_of(core * half, half), half)].astype(BF16)
    other = attn_ref[:, pl.ds(pl.multiple_of((1 - core) * half, half), half)].astype(BF16)
    for rank in range(RANKS):
        normed_ref[rank] = dg(mine, out_mine_ref[rank], False, True) + dg(
            other, out_other_ref[rank], False, True
        )


def call_part(body, outs, name, operands, parts):
    def whole(array):
        dims = array.shape
        return pl.BlockSpec(dims, lambda i, scal: (0,) * len(dims))

    specs = [whole(a) for a in operands[1:]]
    for at in parts:
        specs[at - 1] = pl.BlockSpec((PART, operands[at].shape[1]), lambda i, scal: (scal[6], 0))
    return pl.pallas_call(
        body,
        grid_spec=pltpu.PrefetchScalarGridSpec(
            num_scalar_prefetch=1, grid=(1,), in_specs=specs, out_specs=[whole(a) for a in outs]
        ),
        out_shape=outs,
        name=name,
        cost_estimate=COST,
        compiler_params=pltpu.CompilerParams(
            vmem_limit_bytes=2 * size_of(*operands, *outs) + SLACK, dimension_semantics=("arbitrary",)
        ),
    )(*operands)


def run_k5(*operands):
    width = operands[2].shape[1]
    outs = [shape(PART, width), shape(PART, width), shape(1, width), shape(RANKS, PART, WIDE)]
    return call_part(k5_body, outs, "middle_gradient", operands, (2, 3))


def n_body(scal_ref, first_ref, x_ref, gain_ref, d_middle_ref, out_ref, gains_ref):
    total = first_ref[0] + first_ref[1] + first_ref[2] + first_ref[3]
    pulled, _ = norm_pull(total[:PART], x_ref[...], gain_ref[...].astype(F32))
    done = d_middle_ref[...] + pulled
    for at in range(RANKS):
        out_ref[at] = done
    gains_ref[...] = total[PART:]


def run_n(*operands):
    width = operands[2].shape[1]
    outs = [shape(RANKS, PART, width), shape(8, width)]
    return call_part(n_body, outs, "input_gradient", operands, (2,))


def turn_body(scal_ref, mine_ref, other_ref, out_ref):
    tokens, width = mine_ref.shape
    for n, ref in enumerate((mine_ref, other_ref)):
        for at in range(0, width, 256):
            block = ref[:, at : at + 256].T.astype(BF16)
            out_ref[at : at + 256, n * tokens : (n + 1) * tokens] = block


def run_turn(scal, mine, other):
    tokens, width = mine.shape
    outs = [shape(width, 2 * tokens, dtype=BF16)]
    return call(turn_body, outs, "turned", limit=VMEM_LIMIT)(scal, mine, other)[0]


def parts_of(turned_ref, scal_ref, along_x, step):
    row, col, core = scal_ref[3], scal_ref[4], scal_ref[5]
    rows = turned_ref.shape[0] // (2 * SIDE * SIDE)
    pieces = []
    for at in range(SIDE):
        if along_x:
            place = (at * SIDE + lax.rem(col + step, SIDE)) * 2 + core
        else:
            place = (lax.rem(row + step, SIDE) * SIDE + at) * 2 + core
        pieces.append(turned_ref[pl.ds(pl.multiple_of(place * rows, rows), rows), :])
    return jnp.concatenate(pieces, axis=0)


def put(ref, value, start):
    rows = value.shape[0] // SIDE
    for at in range(SIDE):
        ref[at, :, start : start + value.shape[1]] = value[at * rows : (at + 1) * rows]


def send_parts(outs, along_x, scal_ref, products):
    keep_ref, on_ref, back_ref, held_ref = outs
    half = keep_ref.shape[2] // 2
    low_to = {1: held_ref.at[0], 2: on_ref.at[1], 3: back_ref.at[0]}
    high_to = {1: on_ref.at[0], 2: back_ref.at[1], 3: held_ref.at[1]}
    for step in range(SIDE):
        for turned_ref, columns, first in products:
            value = dg(parts_of(turned_ref, scal_ref, along_x, step), columns, False, False)
            last = first + columns.shape[1]
            if step == 0:
                put(keep_ref, value, first)
                continue
            if first < half:
                stop = min(last, half)
                put(low_to[step], value[:, : stop - first], first)
            if last > half:
                begin = max(first, half)
                put(high_to[step], value[:, begin - first :], begin - half)


def part_shapes(rows, wide):
    side = [shape(SIDE, rows, wide)] + [shape(2, SIDE, rows, wide // 2)] * 3
    return side * 2


def w1_body(scal_ref, mine_ref, other_ref, h_ref, d_ref, *rest):
    outs, cols_ref = rest[:8], rest[8]
    tokens, wide = mine_ref.shape
    cut = wide // 2
    up_end = 2 * (wide // 3)
    cols_ref[:tokens, :] = mine_ref[...].astype(BF16)
    cols_ref[tokens:, :] = other_ref[...].astype(BF16)
    send_parts(outs[:4], True, scal_ref, [(h_ref, cols_ref[:, :cut], 0)])
    send_parts(
        outs[4:],
        False,
        scal_ref,
        [(h_ref, cols_ref[:, cut:up_end], 0), (d_ref, cols_ref[:, up_end:], up_end - cut)],
    )


def run_w1(*operands):
    tokens, wide = operands[1].shape
    width = operands[3].shape[0]
    scratch = [pltpu.VMEM((2 * tokens, wide), BF16)]
    return call(w1_body, part_shapes(width // 32, wide // 2), "ffn_weight_sums", scratch, VMEM_LIMIT)(*operands)


def w2_body(
    scal_ref, low_ref, low_other_ref, dq_ref, dq_other_ref, n_ref, n_other_ref, h_ref, d_ref, *rest
):
    outs, cols_ref = rest[:8], rest[8]
    tokens, late = low_ref.shape
    cut = cols_ref.shape[1] // 2
    query_end = late + WIDE
    sides = ((low_ref, dq_ref, n_ref), (low_other_ref, dq_other_ref, n_other_ref))
    for n, (low, dq, normed) in enumerate(sides):
        spot = slice(n * tokens, (n + 1) * tokens)
        cols_ref[spot, :late] = low[...].astype(BF16)
        cols_ref[spot, late:query_end] = dq[...].astype(BF16)
        cols_ref[spot, query_end:] = normed[...].astype(BF16)
    send_parts(outs[:4], True, scal_ref, [(h_ref, cols_ref[:, :cut], 0)])
    send_parts(
        outs[4:],
        False,
        scal_ref,
        [(h_ref, cols_ref[:, cut:query_end], 0), (d_ref, cols_ref[:, query_end:], query_end - cut)],
    )


def run_w2(*operands):
    tokens, late = operands[1].shape
    width = operands[7].shape[0]
    wide = late + 2 * WIDE
    scratch = [pltpu.VMEM((2 * tokens, wide), BF16)]
    return call(
        w2_body, part_shapes(width // 32, wide // 2), "head_weight_sums", scratch, VMEM_LIMIT
    )(*operands)


def relay_body(scal_ref, *refs):
    ins, outs = refs[:6], refs[6:]
    for n in range(2):
        held_ref, on_ref, back_ref = ins[3 * n : 3 * n + 3]
        outs[2 * n][...] = held_ref[0] + on_ref[1]
        outs[2 * n + 1][...] = held_ref[1] + back_ref[1]


def run_relay(scal, *pieces):
    dims = pieces[0].shape[1:]
    return call(relay_body, [shape(*dims)] * 4, "relay_sums")(scal, *pieces)


def folded(refs, at):
    keep_ref, on_ref, back_ref, on_2_ref, back_2_ref = refs
    half = keep_ref.shape[2] // 2
    low = keep_ref[at, :, :half] + on_2_ref[at] + back_ref[0, at]
    high = keep_ref[at, :, half:] + on_ref[0, at] + back_2_ref[at]
    return low, high


def fold_1_body(scal_ref, *refs):
    for n, target in enumerate(refs[10:]):
        half = target.shape[2] // 2
        for at in range(SIDE):
            low, high = folded(refs[5 * n : 5 * n + 5], at)
            target[at, :, :half] = low
            target[at, :, half:] = high


def run_fold_1(scal, pieces):
    outs = [shape(*pieces[0].shape)] * 2
    return call(fold_1_body, outs, "fold_sums")(scal, *pieces)


def fold_2_body(scal_ref, *refs):
    outs = refs[10:]
    for n in range(2):
        for step in range(SIDE):
            target = outs[SIDE * n + step]
            half = target.shape[1] // 2
            low, high = folded(refs[5 * n : 5 * n + 5], lax.rem(scal_ref[3 + n] + step, SIDE))
            target[:, :half] = low
            target[:, half:] = high


def run_fold_2(scal, pieces):
    outs = [shape(*pieces[0].shape[1:])] * 8
    return call(fold_2_body, outs, "fold_parts")(scal, *pieces)


def end_1_body(scal_ref, one_ref, two_ref, gate_ref, up_ref, down_ref):
    units = gate_ref.shape[1]
    rest = one_ref.shape[1] - units
    gate_ref[...] = one_ref[:, :units]
    up_ref[:, :rest] = one_ref[:, units:]
    up_ref[:, rest:] = two_ref[:, : units - rest]
    down_ref[...] = two_ref[:, units - rest :]


def run_end_1(scal, one, two):
    rows, wide = one.shape
    outs = [shape(rows, 2 * wide // 3)] * 3
    return call(end_1_body, outs, "ffn_gradients")(scal, one, two)


def end_2_body(scal_ref, *refs):
    first, second, outs = refs[:4], refs[4:8], refs[8:]
    key_ref, value_ref, path_ref, beta_ref, query_ref, out_ref = outs
    one = (first[0][...] + first[1][...]) + (first[2][...] + first[3][...])
    two = (second[0][...] + second[1][...]) + (second[2][...] + second[3][...])
    rest = one.shape[1] - 2 * WIDE
    left = WIDE - rest
    key_ref[...] = one[:, :WIDE]
    value_ref[...] = one[:, WIDE : 2 * WIDE]
    path_ref[:, :rest] = one[:, 2 * WIDE :]
    path_ref[:, rest:] = two[:, :left]
    beta_ref[...] = two[:, left : left + HW]
    query_ref[...] = two[:, left + HW : left + HW + WIDE]
    out_ref[...] = two[:, left + HW + WIDE :]


def run_end_2(scal, pieces):
    rows = pieces[0].shape[0]
    outs = [shape(rows, WIDE)] * 3 + [shape(rows, HW)] + [shape(rows, WIDE)] * 2
    return call(end_2_body, outs, "head_gradients")(scal, *pieces)


def swap(value):
    return lax.ppermute(value, "c", [(0, 1), (1, 0)])


def shift(value, axis, step):
    return lax.ppermute(value, axis, [(i, (i + step) % SIDE) for i in range(SIDE)])


def exchange(pieces, first_axis, second_axis):
    moved = {}
    for step in (2, 1, 3):
        moved[step] = shift(pieces[step], first_axis, step)
        moved[4 + step] = shift(pieces[4 + step], second_axis, step)
    return [pieces[0], moved[1], moved[2], moved[3], pieces[4], moved[5], moved[6], moved[7]]


def step_one(pieces):
    out = []
    for n, axis in enumerate(("x", "y")):
        _, on, back, _ = pieces[4 * n : 4 * n + 4]
        out.append((shift(on, axis, 1), shift(back, axis, SIDE - 1)))
    return out


def step_two(pieces, came, scal):
    relayed = run_relay(scal, pieces[3], *came[0], pieces[7], *came[1])
    out = []
    for n, axis in enumerate(("x", "y")):
        on = shift(relayed[2 * n], axis, 1)
        back = shift(relayed[2 * n + 1], axis, SIDE - 1)
        out += [pieces[4 * n], *came[n], on, back]
    return relayed, out


def trade(value, axis):
    return lax.all_to_all(value, axis, 0, 0)


def after(value, *others):
    return lax.optimization_barrier((value,) + others)[0]


def local(
    block_input, gain_in, w_query, w_key, w_value, w_path, w_beta, w_out,
    gain_mid, w_gate, w_up, w_down, out_grad, lengths,
):
    tokens, width = block_input.shape
    row, col, core = (lax.axis_index(name) for name in CTX)
    rank = lax.axis_index("z")
    start = lax.axis_index(CTX) * tokens
    scal = jnp.stack([start, lengths[0], lengths[1], row, col, core, rank]).astype(jnp.int32)
    unity = (lengths[0] > 0).astype(F32)
    gain_1 = gain_in.reshape(1, width)
    gain_2 = gain_mid.reshape(1, width)
    heads_w = (w_query, w_key, w_value, w_path, w_beta.T)

    h1, q, k, v, w, aux, inv, kp, b, kt, tu = run_a1(scal, block_input, gain_1, *heads_w)
    both = lax.all_gather(tu, "c", axis=0)
    u_c, spread = run_s1(scal, both)
    along_x = trade(spread, "x")
    out_half = lax.dynamic_slice_in_dim(after(w_out, spread), core * (width // 2), width // 2, 1)
    out_mine = lax.all_gather(out_half.astype(F32), "z", axis=0)
    grad_other = swap(after(out_grad, spread))
    h1_other = swap(after(h1, spread))
    along_x = after(along_x, grad_other, h1_other)
    t_x, u_x, spread = run_s2(scal, along_x, swap(along_x))
    along_y = trade(spread, "y")
    c, sc, qt, inside = run_a2(scal, after(q, spread), k, v, w, inv, kp)
    h1_turned = run_turn(scal, after(h1, spread), h1_other)
    grad_turned = run_turn(scal, after(out_grad, spread), grad_other)
    along_y = after(along_y, inside, h1_turned, grad_turned)
    t_y, states = run_s3(scal, along_y, swap(along_y), t_x, u_x, both, u_c)
    states = lax.all_gather(states, "c", axis=0)
    mixed, normed, spread, carried = run_a3(scal, inside, qt, states)
    normed_all = trade(spread, "z")
    out_mine = after(out_mine, spread)
    out_mine_low = (out_mine * unity).astype(BF16)
    out_other_low = (swap(out_mine) * unity).astype(BF16)
    normed_all = after(normed_all, out_mine_low, out_other_low)
    middle, h2 = run_middle(scal, normed_all, out_mine_low, out_other_low, block_input, gain_2)
    sent, second_part, down_part = run_ffn(h2, out_grad, w_gate, w_up, w_down)

    second = trade(second_part.reshape(RANKS, PART, width), "z")
    h2_other = swap(h2)
    h2_turned = run_turn(scal, after(h2, sent), h2_other)
    ffn_pieces = run_w1(scal, sent, swap(sent), h2_turned, grad_turned)
    second = after(second, *ffn_pieces)
    came = step_one(ffn_pieces)
    d_middle, attn, gain_mid_part, d_normed = run_k5(
        scal, second, middle, out_grad, gain_2, out_mine_low, out_other_low
    )
    attn_all = lax.all_gather(attn, "z", axis=0, tiled=True)
    d_normed = trade(d_normed, "z").reshape(tokens, WIDE)
    down_sum = lax.psum(after(down_part, d_normed), "z")
    dm, state_grad = run_b1(scal, d_normed, mixed, qt)
    pair = lax.all_gather(state_grad, "c", axis=0)
    g_1, spread = run_t1(scal, pair, both)
    g_x = trade(spread, "x")
    came[0] = (after(came[0][0], spread), came[0][1])
    relayed, ffn_pieces = step_two(ffn_pieces, came, scal)
    g_x = after(g_x, *relayed)
    spread = run_t2(scal, g_x, t_x)
    g_y = trade(spread, "y")
    dq, dk, dv, dw, dkp, xc = run_b2(
        scal, after(dm, spread), carried, q, k, v, w, aux, inv, kp, c, sc
    )
    attn_turned = run_turn(scal, after(attn_all, spread), swap(attn_all))
    ffn_pieces[0] = after(ffn_pieces[0], dq)
    ffn_one, ffn_two = run_fold_1(scal, ffn_pieces)
    g_y = after(g_y, dq, attn_turned, ffn_one)
    later = run_t3(scal, g_y, g_x, t_y, t_x, both, g_1)
    later = lax.all_gather(later, "c", axis=0)
    later = after(later, down_sum)
    block_output = middle + down_sum
    ffn_one = lax.psum_scatter(ffn_one, "y", scatter_dimension=0)
    ffn_two = lax.psum_scatter(ffn_two, "x", scatter_dimension=0)

    low = run_b3(scal, later, carried, k, v, w, aux, inv, kp, b, kt, dk, dv, dw, dkp, xc)
    low_other = swap(low)
    first_part = run_b4(scal, block_input, gain_mid_part, dq, low, *heads_w)
    head_pieces = run_w2(
        scal, low, low_other, dq, swap(dq), normed, swap(normed), h1_turned, attn_turned
    )
    first = trade(after(first_part, head_pieces[0]), "z")
    relayed, head_pieces = step_two(head_pieces, step_one(head_pieces), scal)
    spread, gains = run_n(scal, after(first, relayed[0]), block_input, gain_1, d_middle)
    input_grad = trade(spread, "z").reshape(tokens, width)
    head_pieces = run_fold_2(scal, head_pieces)
    gains = jnp.swapaxes(after(gains, head_pieces[0])[:2].reshape(2, 32, width // 32), 0, 1)
    gains = jnp.sum(trade(gains, CTX), axis=0)
    key_out, value_out, path_out, beta_out, query_out, out_out = run_end_2(
        scal, exchange(head_pieces, "y", "x")
    )
    gate_out, up_out, down_out = run_end_1(scal, ffn_one, ffn_two)
    return (
        block_output, input_grad, gains[0], query_out, key_out, value_out, path_out,
        beta_out[:, : w_beta.shape[1]], out_out.T, gains[1], gate_out, up_out, down_out.T,
    )


def solution(mesh):
    fine = Mesh(mesh.devices.reshape(SIDE, SIDE, 2, RANKS), ("y", "x", "c", "z"))
    tokens, heads, whole = P(CTX, None), P(None, "z"), P()
    in_specs = (
        tokens, whole, heads, heads, heads, heads, heads, P("z", None),
        whole, heads, heads, P("z", None), tokens, whole,
    )
    weight = P(CTX, "z")
    out_specs = (
        tokens, tokens, P(CTX), weight, weight, weight, weight, weight,
        P("z", CTX), P(CTX), weight, weight, P("z", CTX),
    )
    return jax.shard_map(local, mesh=fine, in_specs=in_specs, out_specs=out_specs, check_vma=False)
```

```python
import jax
import jax.numpy as jnp
from jax import lax
from jax.experimental import pallas as pl
from jax.experimental.pallas import tpu as pltpu
from jax.sharding import Mesh
from jax.sharding import PartitionSpec as P

EPSILON = 1e-06
HEAD_EPSILON = 0.01
F32 = jnp.float32
BF16 = jnp.bfloat16
HEADS = 3
HW = 128
LEN = 256
RANKS = 4
PART = LEN // RANKS
SIDE = 4
CTX = ("y", "x", "c")


def split(value):
    high = value.astype(BF16)
    return high, (value - high.astype(F32)).astype(BF16)


def dg(left, right, ta, tb):
    dims = (((0 if ta else 1,), (1 if tb else 0,)), ((), ()))
    return lax.dot_general(left, right, dims, preferred_element_type=F32)


def mm(left, right, ta=False, tb=False):
    left = left if isinstance(left, tuple) else split(left)
    right = right if isinstance(right, tuple) else split(right)
    return dg(left[0], right[0], ta, tb) + (
        dg(left[0], right[1], ta, tb) + dg(left[1], right[0], ta, tb)
    )


def iota(shape, dim):
    return lax.broadcasted_iota(jnp.int32, shape, dim)


def cols(head):
    return slice(head * HW, (head + 1) * HW)


def segments(spot, scal):
    second = scal[1]
    third = second + scal[2]
    return (spot >= second).astype(jnp.int32) + (spot >= third).astype(jnp.int32)


def small_inverses(scaled):
    row = iota((HW, HW), 0)
    lane = iota((HW, HW), 1)
    same = (row // 8) == (lane // 8)
    packed = []
    for one in scaled:
        for half in range(2):
            block = jnp.where(same, one[half * HW : (half + 1) * HW, half * HW : (half + 1) * HW], 0.0)
            packed.append(jnp.sum(block.reshape(HW // 8, 8, HW), axis=0))
    count = len(packed)
    high, low = split(jnp.concatenate(packed, axis=0))
    lane_8 = iota((8, HW), 1) % 8
    spread = {}
    for k in range(1, 8):
        unit = ((row // 8 == lane // 8) & (row % 8 == k)).astype(BF16)
        both = dg(high, unit, False, False) + dg(low, unit, False, False)
        spread[k] = both.reshape(count, 8, HW)
    rows = {}
    for i in range(7, -1, -1):
        value = jnp.broadcast_to((lane_8[:1] == i).astype(F32)[None], (count, 1, HW))
        for k in range(i + 1, 8):
            value = value - spread[k][:, i : i + 1, :] * rows[k]
        rows[i] = value
    done = jnp.concatenate([rows[i] for i in range(8)], axis=1)
    out = []
    zero = jnp.zeros((HW, HW), F32)
    for head in range(count // 2):
        halves = [
            jnp.where(same, jnp.concatenate([done[2 * head + half]] * (HW // 8), axis=0), 0.0)
            for half in range(2)
        ]
        out.append(
            jnp.concatenate(
                [
                    jnp.concatenate([halves[0], zero], axis=1),
                    jnp.concatenate([zero, halves[1]], axis=1),
                ],
                axis=0,
            )
        )
    return out


def upper_rows(value, width):
    return jnp.concatenate(
        [value[at : at + width] for at in range(0, value.shape[0], 2 * width)], axis=0
    )


def put_upper(value, upper, width):
    pieces = []
    for n, at in enumerate(range(0, value.shape[0], 2 * width)):
        pieces.append(upper[n * width : (n + 1) * width])
        pieces.append(value[at + width : at + 2 * width])
    return jnp.concatenate(pieces, axis=0)


def inverses(scaled):
    out = small_inverses(scaled)
    row = iota((LEN, LEN), 0)
    lane = iota((LEN, LEN), 1)
    width = 8
    while width < LEN:
        pair = (row // (2 * width) == lane // (2 * width)) & (row // width < lane // width)
        link = [upper_rows(jnp.where(pair, one, 0.0), width) for one in scaled]
        parts = [split(one) for one in out]
        first = [mm(a, b) for a, b in zip(link, parts)]
        empty = jnp.zeros((LEN, LEN), F32)
        wide = [put_upper(empty, one, width) for one in first]
        tops = [
            (upper_rows(a, width), upper_rows(b, width)) for a, b in parts
        ]
        second = [mm(a, b) for a, b in zip(tops, wide)]
        out = [
            put_upper(one, upper_rows(one, width) - new, width) for one, new in zip(out, second)
        ]
        width *= 2
    return out


def unit_rows(value):
    scale = lax.rsqrt(jnp.sum(value * value, axis=-1, keepdims=True) + EPSILON)
    return value * scale, scale


def a1_body(
    scal_ref, x_ref, gain_ref, wq_ref, wk_ref, wv_ref, ww_ref, wb_ref,
    h1_ref, q_ref, k_ref, v_ref, w_ref, aux_ref, inv_ref, kp_ref, b_ref, kt_ref, tu_ref,
):
    x = x_ref[...]
    scale = lax.rsqrt(jnp.mean(x * x, axis=-1, keepdims=True) + EPSILON)
    h1 = (x * scale * gain_ref[...].astype(F32)).astype(BF16)
    h1_ref[...] = h1.astype(F32)
    start = scal_ref[0]
    token = iota((LEN, 1), 0) + start
    segment = segments(token, scal_ref)
    end_segment = segments(jnp.full((1, 1), LEN - 1, jnp.int32) + start, scal_ref)
    before = start - 1
    before_segment = jnp.where(start == 0, -1, segments(jnp.full((1, 1), 0, jnp.int32) + before, scal_ref))
    last = (segment == end_segment).astype(F32)
    carry_all = (end_segment == before_segment).astype(F32)
    row = iota((LEN, LEN), 0)
    lane = iota((LEN, LEN), 1)
    later = row < lane
    beta = 1.0 + jax.nn.sigmoid(dg(h1, wb_ref[...], False, True))
    beta_rows = 1.0 + jax.nn.sigmoid(dg(wb_ref[...], h1, False, True))
    pr = dg(h1, ww_ref[...], False, False)
    kr = dg(h1, wk_ref[...], False, False)
    w_all, k_all, aux = [], [], []
    for head in range(HEADS):
        w, w_scale = unit_rows(pr[:, cols(head)])
        k, k_scale = unit_rows(kr[:, cols(head)])
        w_ref[:, cols(head)] = w
        k_ref[:, cols(head)] = k
        w_all.append(w)
        k_all.append(k)
        aux.append((w_scale, k_scale))
    w_split = [split(w) for w in w_all]
    k_split = [split(k) for k in k_all]
    scaled = [
        jnp.where(later, mm(w_split[h], w_split[h], tb=True), 0.0) * beta[:, h : h + 1]
        for h in range(HEADS)
    ]
    inverse = [
        one * beta_rows[h : h + 1, :] for h, one in enumerate(inverses(scaled))
    ]
    vr = dg(h1, wv_ref[...], False, False)
    qr = dg(h1, wq_ref[...], False, False)
    v_ref[...] = vr
    lane_aux = iota((LEN, HW), 1)
    packed = jnp.zeros((LEN, HW), F32)
    eye = (iota((HW, HW), 0) == iota((HW, HW), 1)).astype(F32)
    for head in range(HEADS):
        q, q_scale = unit_rows(qr[:, cols(head)])
        q_ref[:, cols(head)] = q
        spots = (
            (head, beta[:, head : head + 1]),
            (8 + head, q_scale),
            (16 + head, aux[head][1]),
            (24 + head, aux[head][0]),
        )
        for at, value in spots:
            packed = jnp.where(lane_aux == at, value, packed)
        inv_ref[head] = inverse[head]
        inv_split = split(inverse[head])
        folded = mm(inv_split, w_split[head])
        b_ref[:, cols(head)] = folded
        folded_split = split(folded)
        kp = jnp.where(later, mm(k_split[head], w_split[head], tb=True), 0.0)
        kp_ref[head] = kp
        kt = k_all[head] - mm(kp, folded_split)
        kt_ref[:, cols(head)] = kt
        tu_ref[0, head] = carry_all * (eye - mm(w_split[head], folded_split, ta=True))
        tu_ref[1, head] = mm(vr[:, cols(head)], kt * last, ta=True)
    aux_ref[...] = packed


def shape(*dims, dtype=F32):
    return jax.ShapeDtypeStruct(dims, dtype)


MIB = 1024 * 1024
SLACK = 10 * MIB
LIGHT = pl.CostEstimate(flops=10**4, bytes_accessed=10**4, transcendentals=0)
WORK = pl.CostEstimate(flops=8 * 10**9, bytes_accessed=10**7, transcendentals=0)


def size_of(*arrays):
    total = 0
    for one in arrays:
        count = one.dtype.itemsize
        for extent in one.shape:
            count *= extent
        total += count
    return total


class Late:
    def __init__(self, copy, buffer):
        self.copy, self.buffer, self.shape = copy, buffer, buffer.shape
        copy.start()

    def here(self):
        if self.copy is not None:
            self.copy.wait()
            self.copy = None
        return self.buffer

    def __getitem__(self, spot):
        return self.here()[spot]


class Early:
    def __init__(self, copy, buffer):
        self.copy, self.buffer, self.shape, self.sent = copy, buffer, buffer.shape, False

    def __getitem__(self, spot):
        return self.buffer[spot]

    def __setitem__(self, spot, value):
        self.buffer[spot] = value

    @property
    def at(self):
        return self.buffer.at


def whole_now(*refs):
    for ref in refs:
        if isinstance(ref, Early):
            ref.copy.start()
            ref.sent = True


def call(body, outs, name, scratch=(), late=(), early=(), cost=LIGHT, alone=False):
    def run(*operands):
        count = len(operands)
        moved = sorted(late)
        leaving = sorted(early)
        vmem = pl.BlockSpec(memory_space=pltpu.VMEM)
        anywhere = pl.BlockSpec(memory_space=pl.ANY)
        held = [operands[at] for at in moved] + [outs[at] for at in leaving]
        buffers = [pltpu.VMEM(one.shape, one.dtype) for one in held]
        marks = [pltpu.SemaphoreType.DMA((len(buffers),))] if buffers else []

        def wrapped(*refs):
            refs = list(refs)
            own = len(refs) - len(buffers) - len(marks)
            for n, at in enumerate(moved):
                copy = pltpu.make_async_copy(refs[at], refs[own + n], refs[-1].at[n])
                refs[at] = Late(copy, refs[own + n])
            for n, at in enumerate(leaving, len(moved)):
                copy = pltpu.make_async_copy(refs[own + n], refs[count + at], refs[-1].at[n])
                refs[count + at] = Early(copy, refs[own + n])
            body(*refs[:own])
            for at in moved:
                refs[at].here()
            for at in leaving:
                if not refs[count + at].sent:
                    refs[count + at].copy.start()
            for at in leaving:
                refs[count + at].copy.wait()

        need = size_of(*operands, *outs, *scratch) + SLACK
        return pl.pallas_call(
            wrapped,
            out_shape=outs,
            in_specs=[pl.BlockSpec(memory_space=pltpu.SMEM)]
            + [anywhere if at in moved else vmem for at in range(1, count)],
            out_specs=[anywhere if at in leaving else vmem for at in range(len(outs))],
            scratch_shapes=list(scratch) + buffers + marks,
            name=name,
            cost_estimate=cost,
            compiler_params=pltpu.CompilerParams(vmem_limit_bytes=56 * MIB if alone else need),
        )(*operands)

    return run


WIDE = HEADS * HW


def run_a1(*operands):
    outs = [
        shape(LEN, operands[1].shape[1]),
        shape(LEN, WIDE), shape(LEN, WIDE), shape(LEN, WIDE), shape(LEN, WIDE),
        shape(LEN, HW),
        shape(HEADS, LEN, LEN), shape(HEADS, LEN, LEN),
        shape(LEN, WIDE), shape(LEN, WIDE),
        shape(2, HEADS, HW, HW),
    ]
    return call(a1_body, outs, "local_parts", alone=True)(*operands)


def a2_body(
    scal_ref, q_ref, k_ref, v_ref, w_ref, inv_ref, kp_ref,
    c_ref, sc_ref, qt_ref, in_ref,
):
    start = scal_ref[0]
    segment = segments(iota((LEN, LEN), 0) + start, scal_ref)
    segment_t = segments(iota((LEN, LEN), 1) + start, scal_ref)
    row = iota((LEN, LEN), 0)
    lane = iota((LEN, LEN), 1)
    up_to = row <= lane
    seen = up_to & (segment == segment_t)
    for head in range(HEADS):
        q = q_ref[:, cols(head)]
        q_split = split(q)
        w_split = split(w_ref[:, cols(head)])
        pq = jnp.where(up_to, mm(w_split, q_split, tb=True), 0.0)
        c = mm(inv_ref[head], pq)
        c_ref[head] = c
        c_split = split(c)
        qt_ref[:, cols(head)] = q - mm(c_split, w_split, ta=True)
        scores = mm(k_ref[:, cols(head)], q_split, tb=True) - mm(kp_ref[head], c_split)
        scores = jnp.where(seen, scores, 0.0)
        sc_ref[head] = scores
        in_ref[:, cols(head)] = mm(scores, v_ref[:, cols(head)], ta=True)


def run_a2(*operands):
    outs = [shape(HEADS, LEN, LEN), shape(HEADS, LEN, LEN), shape(LEN, WIDE), shape(LEN, WIDE)]
    return call(a2_body, outs, "inside_parts", alone=True, cost=WORK)(*operands)


def carry_of(start, scal_ref):
    token = iota((LEN, 1), 0) + start
    before = jnp.full((1, 1), 0, jnp.int32) + (start - 1)
    before_segment = jnp.where(start == 0, -1, segments(before, scal_ref))
    return (segments(token, scal_ref) == before_segment).astype(F32)


def pair_of(ref, core, head):
    return jnp.concatenate([ref[0, core, head], ref[1, core, head]], axis=0)


def a3_body(scal_ref, in_ref, qt_ref, states_ref, mixed_ref, normed_ref, spread_ref, carried_ref):
    carry = carry_of(scal_ref[0], scal_ref)
    core = scal_ref[5]
    for head in range(HEADS):
        carried = pair_of(states_ref, core, head)
        carried_ref[head] = carried
        mixed = in_ref[:, cols(head)] + carry * mm(qt_ref[:, cols(head)], carried, tb=True)
        mixed_ref[:, cols(head)] = mixed
        scale = lax.rsqrt(jnp.mean(mixed * mixed, axis=-1, keepdims=True) + HEAD_EPSILON)
        low = (mixed * scale).astype(BF16).astype(F32)
        normed_ref[:, cols(head)] = low
        for at in range(RANKS):
            spread_ref[at, :, cols(head)] = low


def run_a3(*operands):
    outs = [shape(LEN, WIDE), shape(LEN, WIDE), shape(RANKS, LEN, WIDE), shape(HEADS, HW, HW)]
    return call(a3_body, outs, "normed_heads")(*operands)


def b1_body(scal_ref, dn_ref, mixed_ref, qt_ref, dm_ref, sg_ref):
    carry = carry_of(scal_ref[0], scal_ref)
    for head in range(HEADS):
        mixed = mixed_ref[:, cols(head)]
        dn = dn_ref[:, cols(head)]
        scale = lax.rsqrt(jnp.mean(mixed * mixed, axis=-1, keepdims=True) + HEAD_EPSILON)
        drift = jnp.mean(dn * mixed, axis=-1, keepdims=True) * (scale * scale)
        dm = scale * (dn - mixed * drift)
        dm_ref[:, cols(head)] = dm
        sg_ref[head] = mm(dm * carry, qt_ref[:, cols(head)], ta=True)


def run_b1(*operands):
    outs = [shape(LEN, WIDE), shape(HEADS, HW, HW)]
    return call(b1_body, outs, "state_gradient")(*operands)


def unit_pull(unit, scale, grad):
    return scale * (grad - unit * jnp.sum(unit * grad, axis=-1, keepdims=True))


def b2_body(
    scal_ref, dm_ref, carried_ref, q_ref, k_ref, v_ref, w_ref, aux_ref, inv_ref, kp_ref,
    c_ref, sc_ref,
    dq_ref, dk_ref, dv_ref, dw_ref, dkp_ref, xc_ref,
):
    start = scal_ref[0]
    carry = carry_of(start, scal_ref)
    row = iota((LEN, LEN), 0)
    lane = iota((LEN, LEN), 1)
    up_to = row <= lane
    seen = up_to & (
        segments(row + start, scal_ref) == segments(lane + start, scal_ref)
    )
    for head in range(HEADS):
        q = q_ref[:, cols(head)]
        q_split = split(q)
        w_split = split(w_ref[:, cols(head)])
        k_split = split(k_ref[:, cols(head)])
        c_split = split(c_ref[head])
        kp_split = split(kp_ref[head])
        dm = dm_ref[:, cols(head)]
        dm_split = split(dm)
        dqt = mm(dm * carry, carried_ref[head])
        dqt_split = split(dqt)
        ds = jnp.where(seen, mm(v_ref[:, cols(head)], dm_split, tb=True), 0.0)
        ds_split = split(ds)
        dv_ref[:, cols(head)] = mm(sc_ref[head], dm_split)
        dk = mm(ds_split, q_split)
        dq = dqt + mm(ds_split, k_split, ta=True)
        dkp_ref[head] = mm(ds_split, c_split, tb=True)
        dc = mm(kp_split, ds_split, ta=True) + mm(w_split, dqt_split, tb=True)
        dw = mm(c_split, dqt_split)
        x = mm(inv_ref[head], dc, ta=True)
        xc_ref[head] = mm(x, c_split, tb=True)
        dpq_split = split(jnp.where(up_to, x, 0.0))
        dw_ref[:, cols(head)] = dw + mm(dpq_split, q_split)
        dq = dq - mm(dpq_split, w_split, ta=True)
        dk_ref[:, cols(head)] = dk
        scale = aux_ref[:, 8 + head : 9 + head]
        dq_ref[:, cols(head)] = unit_pull(q, scale, dq).astype(BF16).astype(F32)


def run_b2(*operands):
    outs = [
        shape(LEN, WIDE), shape(LEN, WIDE), shape(LEN, WIDE), shape(LEN, WIDE),
        shape(HEADS, LEN, LEN), shape(HEADS, LEN, LEN),
    ]
    return call(b2_body, outs, "inside_gradients", alone=True, cost=WORK)(*operands)


def b3_body(
    scal_ref, states_ref, carried_ref, k_ref, v_ref, w_ref, aux_ref,
    inv_ref, kp_ref, b_ref, kt_ref, dk_ref, dv_ref, dw_ref, dkp_ref, xc_ref,
    low_ref,
):
    start = scal_ref[0]
    core = scal_ref[5]
    segment = segments(iota((LEN, 1), 0) + start, scal_ref)
    end_segment = segments(jnp.full((1, 1), LEN - 1, jnp.int32) + start, scal_ref)
    before = jnp.full((1, 1), 0, jnp.int32) + (start - 1)
    before_segment = jnp.where(start == 0, -1, segments(before, scal_ref))
    last = (segment == end_segment).astype(F32)
    carry_all = (end_segment == before_segment).astype(F32)
    row = iota((LEN, LEN), 0)
    lane = iota((LEN, LEN), 1)
    later_mask = row < lane
    lane_aux = iota((LEN, HW), 1)
    d_beta = jnp.zeros((LEN, HW), F32)
    for head in range(HEADS):
        later = pair_of(states_ref, core, head)
        later_split = split(later)
        dt_split = split(carry_all * mm(carried_ref[head], later_split, ta=True))
        w = w_ref[:, cols(head)]
        w_split = split(w)
        k = k_ref[:, cols(head)]
        v = v_ref[:, cols(head)]
        b_split = split(b_ref[:, cols(head)])
        kp_split = split(kp_ref[head])
        dv = dv_ref[:, cols(head)] + last * mm(kt_ref[:, cols(head)], later_split, tb=True)
        dkt = last * mm(v, later_split)
        dkt_split = split(dkt)
        db = mm(w_split, dt_split) + mm(kp_split, dkt_split, ta=True)
        y = mm(inv_ref[head], db, ta=True)
        y_split = split(y)
        dw = dw_ref[:, cols(head)] + mm(b_split, dt_split, tb=True) + y
        dkp = jnp.where(later_mask, dkp_ref[head] + mm(dkt_split, b_split, tb=True), 0.0)
        dkp_split = split(dkp)
        dk = dk_ref[:, cols(head)] + dkt - mm(dkp_split, w_split)
        dw = dw + mm(dkp_split, split(k), ta=True)
        dm = xc_ref[head] + mm(y_split, b_split, tb=True)
        dn_split = split(jnp.where(later_mask, dm, 0.0))
        dw = mm(dn_split, w_split) + mm(dn_split, w_split, ta=True) - dw
        diagonal = jnp.sum(jnp.where(row == lane, dm, 0.0), axis=-1, keepdims=True)
        beta = aux_ref[:, head : head + 1]
        sig = beta - 1.0
        dbl = -diagonal / (beta * beta) * sig * (1.0 - sig)
        d_beta = jnp.where(lane_aux == head, dbl, d_beta)
        low_ref[:, cols(head)] = unit_pull(k, aux_ref[:, 16 + head : 17 + head], dk).astype(BF16).astype(F32)
        low_ref[:, WIDE + head * HW : WIDE + (head + 1) * HW] = dv.astype(BF16).astype(F32)
        low_ref[:, 2 * WIDE + head * HW : 2 * WIDE + (head + 1) * HW] = unit_pull(
            w, aux_ref[:, 24 + head : 25 + head], dw
        ).astype(BF16).astype(F32)
    low_ref[:, 3 * WIDE :] = d_beta.astype(BF16).astype(F32)


def run_b3(*operands):
    outs = [shape(LEN, 3 * WIDE + HW)]
    return call(b3_body, outs, "late_gradients", alone=True)(*operands)[0]


def b4_body(
    scal_ref, x_ref, gain_mid_ref, dq_ref, low_ref, wq_ref, wk_ref, wv_ref, ww_ref, wb_ref, dh_ref
):
    total = dg(dq_ref[...].astype(BF16), wq_ref[...], False, True)
    for at, ref in enumerate((wk_ref, wv_ref, ww_ref)):
        low = low_ref[:, at * WIDE : at * WIDE + ref.shape[1]].astype(BF16)
        total = total + dg(low, ref[...], False, True)
    beta_cols = wb_ref[...].astype(F32)
    for head in range(HEADS):
        at = 3 * WIDE + head
        total = total + low_ref[:, at : at + 1] * beta_cols[head : head + 1, :]
    for at in range(RANKS):
        dh_ref[at, :PART, :] = total[at * PART : (at + 1) * PART]
    x = x_ref[...]
    scale = lax.rsqrt(jnp.mean(x * x, axis=-1, keepdims=True) + EPSILON)
    gain_in = jnp.sum(total * x * scale, axis=0, keepdims=True)
    rows = iota((8, x.shape[1]), 0)
    both = jnp.where(rows == 0, gain_in, jnp.where(rows == 1, gain_mid_ref[...], 0.0))
    for at in range(RANKS):
        dh_ref[at, PART:, :] = both


def run_b4(*operands):
    outs = [shape(RANKS, PART + 8, operands[1].shape[1])]
    return call(b4_body, outs, "first_norm_part", alone=True)(*operands)[0]


def half_of(core):
    return pl.ds(pl.multiple_of(core * (HW // 2), HW // 2), HW // 2)


def s1_body(scal_ref, both_ref, u_ref, out_ref):
    rows = half_of(scal_ref[5])
    for head in range(HEADS):
        t_1 = split(both_ref[1, 0, head])
        u_0 = both_ref[0, 1, head, rows, :]
        u_1 = both_ref[1, 1, head, rows, :]
        u_ref[0, head] = u_0
        u_ref[1, head] = u_1
        chip_t = mm(both_ref[0, 0, head, rows, :], t_1)
        chip_u = mm(u_0, t_1) + u_1
        for at in range(SIDE):
            out_ref[at, 0, head] = chip_t
            out_ref[at, 1, head] = chip_u


def run_s1(*operands):
    outs = [shape(2, HEADS, HW // 2, HW), shape(SIDE, 2, HEADS, HW // 2, HW)]
    return call(s1_body, outs, "chip_state")(*operands)


def join_halves(t_ref, mine_ref, other_ref, core, at, head):
    t_ref[at, head, half_of(core), :] = mine_ref[at, 0, head]
    t_ref[at, head, half_of(1 - core), :] = other_ref[at, 0, head]


def s2_body(scal_ref, mine_ref, other_ref, t_ref, u_ref, out_ref):
    core = scal_ref[5]
    rows = half_of(core)
    for head in range(HEADS):
        for at in range(SIDE):
            join_halves(t_ref, mine_ref, other_ref, core, at, head)
            u_ref[at, head] = mine_ref[at, 1, head]
    for head in range(HEADS):
        t_1 = split(t_ref[1, head])
        t_3 = split(t_ref[3, head])
        t_23 = split(mm(t_ref[2, head], t_3))
        row_t = mm(mm(t_ref[0, head, rows, :], t_1), t_23)
        row_u = mm(mm(u_ref[0, head], t_1) + u_ref[1, head], t_23)
        row_u = row_u + mm(u_ref[2, head], t_3) + u_ref[3, head]
        for at in range(SIDE):
            out_ref[at, 0, head] = row_t
            out_ref[at, 1, head] = row_u


def run_s2(*operands):
    outs = [
        shape(SIDE, HEADS, HW, HW),
        shape(SIDE, HEADS, HW // 2, HW),
        shape(SIDE, 2, HEADS, HW // 2, HW),
    ]
    return call(s2_body, outs, "row_state")(*operands)


def s3_body(scal_ref, mine_ref, other_ref, tx_ref, ux_ref, both_ref, uc_ref, ty_ref, out_ref):
    row, col, core = scal_ref[3], scal_ref[4], scal_ref[5]
    for head in range(HEADS):
        for at in range(SIDE):
            join_halves(ty_ref, mine_ref, other_ref, core, at, head)
    for head in range(HEADS):
        state = jnp.where(row > 0, mine_ref[0, 1, head], 0.0)
        for at in range(1, SIDE - 1):
            new = mm(state, ty_ref[at, head]) + mine_ref[at, 1, head]
            state = jnp.where(at < row, new, state)
        for at in range(SIDE - 1):
            new = mm(state, tx_ref[at, head]) + ux_ref[at, head]
            state = jnp.where(at < col, new, state)
        out_ref[0, head] = state
        out_ref[1, head] = mm(state, both_ref[0, 0, head]) + uc_ref[0, head]


def run_s3(*operands):
    outs = [shape(SIDE, HEADS, HW, HW), shape(2, HEADS, HW // 2, HW)]
    return call(s3_body, outs, "block_state")(*operands)


def t1_body(scal_ref, pair_ref, both_ref, g_ref, out_ref):
    rows = half_of(scal_ref[5])
    for head in range(HEADS):
        g_1 = pair_ref[1, head, rows, :]
        g_ref[head] = g_1
        chip = mm(g_1, both_ref[0, 0, head], tb=True) + pair_ref[0, head, rows, :]
        for at in range(SIDE):
            out_ref[at, head] = chip


def run_t1(*operands):
    outs = [shape(HEADS, HW // 2, HW), shape(SIDE, HEADS, HW // 2, HW)]
    return call(t1_body, outs, "chip_gradient")(*operands)


def t2_body(scal_ref, g_ref, t_ref, out_ref):
    for head in range(HEADS):
        total = g_ref[3, head]
        for at in (2, 1, 0):
            total = mm(total, t_ref[at, head], tb=True) + g_ref[at, head]
        for at in range(SIDE):
            out_ref[at, head] = total


def run_t2(*operands):
    outs = [shape(SIDE, HEADS, HW // 2, HW)]
    return call(t2_body, outs, "row_gradient")(*operands)[0]


def t3_body(scal_ref, gy_ref, gx_ref, ty_ref, tx_ref, both_ref, g_ref, out_ref):
    row, col = scal_ref[3], scal_ref[4]
    for head in range(HEADS):
        later = jnp.where(row < SIDE - 1, gy_ref[3, head], 0.0)
        for at in (2, 1):
            new = mm(later, ty_ref[at, head], tb=True) + gy_ref[at, head]
            later = jnp.where(at > row, new, later)
        for at in (3, 2, 1):
            new = mm(later, tx_ref[at, head], tb=True) + gx_ref[at, head]
            later = jnp.where(at > col, new, later)
        out_ref[1, head] = later
        out_ref[0, head] = mm(later, both_ref[1, 0, head], tb=True) + g_ref[head]


def run_t3(*operands):
    outs = [shape(2, HEADS, HW // 2, HW)]
    return call(t3_body, outs, "block_gradient")(*operands)[0]


def ffn_body(
    scal_ref, normed_ref, out_mine_ref, out_other_ref, x_ref, gain_ref, grad_ref,
    gate_ref, up_ref, down_ref,
    middle_ref, sent_ref, dh_ref, down_part_ref,
):
    core = scal_ref[5]
    half = x_ref.shape[1] // 2
    units = gate_ref.shape[1]
    low = [normed_ref[rank].astype(BF16) for rank in range(RANKS)]
    for ref, at in ((out_mine_ref, core), (out_other_ref, 1 - core)):
        spot = pl.ds(pl.multiple_of(at * half, half), half)
        total = x_ref[:, spot]
        for rank in range(RANKS):
            total = total + dg(low[rank], ref[rank], False, False)
        middle_ref[:, spot] = total
    middle = middle_ref[...]
    scale = lax.rsqrt(jnp.mean(middle * middle, axis=-1, keepdims=True) + EPSILON)
    h2 = (middle * scale * gain_ref[...].astype(F32)).astype(BF16)
    sent_ref[:, 3 * units :] = h2.astype(F32)
    gate = dg(h2, gate_ref[...], False, False)
    up = dg(h2, up_ref[...], False, False)
    sig = jax.nn.sigmoid(gate)
    silu = gate * sig
    hidden = (silu * up).astype(BF16)
    sent_ref[:, 2 * units : 3 * units] = hidden.astype(F32)
    d_hidden = dg(grad_ref[...].astype(BF16), down_ref[...], False, True)
    d_gate = (d_hidden * up * sig * (1.0 + gate * (1.0 - sig))).astype(BF16)
    sent_ref[:, :units] = d_gate.astype(F32)
    d_up = (d_hidden * silu).astype(BF16)
    sent_ref[:, units : 2 * units] = d_up.astype(F32)
    whole_now(middle_ref, sent_ref)
    dh_ref[...] = dg(d_gate, gate_ref[...], False, True) + dg(d_up, up_ref[...], False, True)
    whole_now(dh_ref)
    down_part_ref[...] = dg(hidden, down_ref[...], False, False)


def run_ffn(*operands):
    tokens, width = operands[4].shape
    units = operands[7].shape[1]
    outs = [
        shape(tokens, width), shape(tokens, 3 * units + width), shape(tokens, width), shape(tokens, width)
    ]
    return call(ffn_body, outs, "feed_forward", alone=True, late=(6, 7, 8, 9))(*operands)


def norm_pull(grad, values, gain):
    scale = lax.rsqrt(jnp.mean(values * values, axis=-1, keepdims=True) + EPSILON)
    turned = gain * grad
    drift = jnp.mean(turned * values, axis=-1, keepdims=True) * (scale * scale * scale)
    return scale * turned - values * drift, grad * values * scale


def k5_body(
    scal_ref, second_ref, middle_ref, grad_ref, gain_ref, out_mine_ref, out_other_ref,
    d_middle_ref, attn_ref, gain_out_ref, normed_ref,
):
    core = scal_ref[5]
    rows = pl.ds(pl.multiple_of(scal_ref[6] * PART, PART), PART)
    second = second_ref[0] + second_ref[1] + second_ref[2] + second_ref[3]
    pulled, summed = norm_pull(second, middle_ref[rows, :], gain_ref[...].astype(F32))
    d_middle = grad_ref[rows, :] + pulled
    d_middle_ref[...] = d_middle
    gain_out_ref[...] = jnp.sum(summed, axis=0, keepdims=True)
    attn_ref[...] = d_middle.astype(BF16).astype(F32)
    half = d_middle.shape[1] // 2
    mine = attn_ref[:, pl.ds(pl.multiple_of(core * half, half), half)].astype(BF16)
    other = attn_ref[:, pl.ds(pl.multiple_of((1 - core) * half, half), half)].astype(BF16)
    for rank in range(RANKS):
        normed_ref[rank] = dg(mine, out_mine_ref[rank], False, True) + dg(
            other, out_other_ref[rank], False, True
        )


def run_k5(*operands):
    width = operands[2].shape[1]
    outs = [shape(PART, width), shape(PART, width), shape(1, width), shape(RANKS, PART, WIDE)]
    return call(k5_body, outs, "middle_gradient", alone=True)(*operands)


def n_body(scal_ref, first_ref, x_ref, gain_ref, d_middle_ref, out_ref, gains_ref):
    rows = pl.ds(pl.multiple_of(scal_ref[6] * PART, PART), PART)
    total = first_ref[0] + first_ref[1] + first_ref[2] + first_ref[3]
    pulled, _ = norm_pull(total[:PART], x_ref[rows, :], gain_ref[...].astype(F32))
    out_ref[...] = d_middle_ref[...] + pulled
    gains_ref[...] = total[PART:]


def run_n(*operands):
    width = operands[2].shape[1]
    outs = [shape(PART, width), shape(8, width)]
    return call(n_body, outs, "input_gradient", alone=True)(*operands)


def turn_body(scal_ref, mine_ref, other_ref, out_ref):
    tokens, width = mine_ref.shape
    for n, ref in enumerate((mine_ref, other_ref)):
        for at in range(0, width, 256):
            block = ref[:, at : at + 256].T.astype(BF16)
            out_ref[at : at + 256, n * tokens : (n + 1) * tokens] = block


def run_turn(scal, mine, other):
    tokens, width = mine.shape
    outs = [shape(width, 2 * tokens, dtype=BF16)]
    return call(turn_body, outs, "turned", alone=True, cost=WORK)(scal, mine, other)[0]


def parts_of(turned_ref, scal_ref, along_x, step):
    row, col, core = scal_ref[3], scal_ref[4], scal_ref[5]
    rows = turned_ref.shape[0] // (2 * SIDE * SIDE)
    pieces = []
    for at in range(SIDE):
        if along_x:
            place = (at * SIDE + lax.rem(col + step, SIDE)) * 2 + core
        else:
            place = (lax.rem(row + step, SIDE) * SIDE + at) * 2 + core
        pieces.append(turned_ref[pl.ds(pl.multiple_of(place * rows, rows), rows), :])
    return jnp.concatenate(pieces, axis=0)


def put(ref, value, start):
    rows = value.shape[0] // SIDE
    for at in range(SIDE):
        ref[at, :, start : start + value.shape[1]] = value[at * rows : (at + 1) * rows]


def send_parts(outs, along_x, scal_ref, products):
    keep_ref, on_ref, back_ref, held_ref = outs
    half = keep_ref.shape[2] // 2
    low_to = {1: held_ref.at[0], 2: on_ref.at[1], 3: back_ref.at[0]}
    high_to = {1: on_ref.at[0], 2: back_ref.at[1], 3: held_ref.at[1]}
    for step in range(SIDE):
        for turned_ref, columns, first in products:
            value = dg(parts_of(turned_ref, scal_ref, along_x, step), columns, False, False)
            last = first + columns.shape[1]
            if step == 0:
                put(keep_ref, value, first)
                continue
            if first < half:
                stop = min(last, half)
                put(low_to[step], value[:, : stop - first], first)
            if last > half:
                begin = max(first, half)
                put(high_to[step], value[:, begin - first :], begin - half)


def part_shapes(rows, wide):
    side = [shape(SIDE, rows, wide)] + [shape(2, SIDE, rows, wide // 2)] * 3
    return side * 2


def w1_body(scal_ref, mine_ref, other_ref, d_ref, *rest):
    outs, (cols_ref, h_ref) = rest[:8], rest[8:]
    tokens = mine_ref.shape[0]
    wide = cols_ref.shape[1]
    cut = wide // 2
    up_end = 2 * (wide // 3)
    for n, ref in enumerate((mine_ref, other_ref)):
        spot = slice(n * tokens, (n + 1) * tokens)
        cols_ref[spot, :] = ref[:, :wide].astype(BF16)
        for at in range(0, h_ref.shape[0], 256):
            h_ref[at : at + 256, spot] = ref[:, wide + at : wide + at + 256].T.astype(BF16)
    send_parts(outs[:4], True, scal_ref, [(h_ref, cols_ref[:, :cut], 0)])
    whole_now(*outs[:4])
    send_parts(
        outs[4:],
        False,
        scal_ref,
        [(h_ref, cols_ref[:, cut:up_end], 0), (d_ref, cols_ref[:, up_end:], up_end - cut)],
    )
    whole_now(*outs[4:])


def run_w1(*operands):
    width = operands[3].shape[0]
    tokens, wide = operands[1].shape
    wide = wide - width
    scratch = [pltpu.VMEM((2 * tokens, wide), BF16), pltpu.VMEM((width, 2 * tokens), BF16)]
    return call(
        w1_body, part_shapes(width // 32, wide // 2), "ffn_weight_sums", scratch,
        late=(2, 3), early=range(8), cost=WORK, alone=True
    )(*operands)


def w2_body(
    scal_ref, low_ref, low_other_ref, dq_ref, dq_other_ref, n_ref, n_other_ref, h_ref, d_ref, *rest
):
    outs, cols_ref = rest[:8], rest[8]
    tokens, late = low_ref.shape
    cut = cols_ref.shape[1] // 2
    query_end = late + WIDE
    sides = ((low_ref, dq_ref, n_ref), (low_other_ref, dq_other_ref, n_other_ref))
    for n, (low, dq, normed) in enumerate(sides):
        spot = slice(n * tokens, (n + 1) * tokens)
        cols_ref[spot, :late] = low[...].astype(BF16)
        cols_ref[spot, late:query_end] = dq[...].astype(BF16)
        cols_ref[spot, query_end:] = normed[...].astype(BF16)
    send_parts(outs[:4], True, scal_ref, [(h_ref, cols_ref[:, :cut], 0)])
    whole_now(*outs[:4])
    send_parts(
        outs[4:],
        False,
        scal_ref,
        [(h_ref, cols_ref[:, cut:query_end], 0), (d_ref, cols_ref[:, query_end:], query_end - cut)],
    )


def run_w2(*operands):
    tokens, late = operands[1].shape
    width = operands[7].shape[0]
    wide = late + 2 * WIDE
    scratch = [pltpu.VMEM((2 * tokens, wide), BF16)]
    return call(
        w2_body, part_shapes(width // 32, wide // 2), "head_weight_sums", scratch, late=(7, 8), early=range(8), alone=True
    )(*operands)


def relay_body(scal_ref, *refs):
    ins, outs = refs[:6], refs[6:]
    for n in range(2):
        held_ref, on_ref, back_ref = ins[3 * n : 3 * n + 3]
        outs[2 * n][...] = held_ref[0] + on_ref[1]
        outs[2 * n + 1][...] = held_ref[1] + back_ref[1]


def run_relay(scal, *pieces):
    dims = pieces[0].shape[1:]
    return call(relay_body, [shape(*dims)] * 4, "relay_sums", cost=WORK, alone=True)(scal, *pieces)


def folded(refs, at):
    keep_ref, on_ref, back_ref, on_2_ref, back_2_ref = refs
    half = keep_ref.shape[2] // 2
    low = keep_ref[at, :, :half] + on_2_ref[at] + back_ref[0, at]
    high = keep_ref[at, :, half:] + on_ref[0, at] + back_2_ref[at]
    return low, high


def fold_1_body(scal_ref, *refs):
    for n, target in enumerate(refs[10:]):
        half = target.shape[2] // 2
        for at in range(SIDE):
            low, high = folded(refs[5 * n : 5 * n + 5], at)
            target[at, :, :half] = low
            target[at, :, half:] = high


def run_fold_1(scal, pieces):
    outs = [shape(*pieces[0].shape)] * 2
    return call(fold_1_body, outs, "fold_sums", cost=WORK, alone=True)(scal, *pieces)


def fold_2_body(scal_ref, *refs):
    outs = refs[10:]
    for n in range(2):
        for step in range(SIDE):
            target = outs[SIDE * n + step]
            half = target.shape[1] // 2
            low, high = folded(refs[5 * n : 5 * n + 5], lax.rem(scal_ref[3 + n] + step, SIDE))
            target[:, :half] = low
            target[:, half:] = high


def run_fold_2(scal, pieces):
    outs = [shape(*pieces[0].shape[1:])] * 8
    return call(fold_2_body, outs, "fold_parts", cost=WORK, alone=True)(scal, *pieces)


def end_1_body(scal_ref, one_ref, two_ref, gate_ref, up_ref, down_ref):
    units = gate_ref.shape[1]
    rest = one_ref.shape[1] - units
    gate_ref[...] = one_ref[:, :units]
    up_ref[:, :rest] = one_ref[:, units:]
    up_ref[:, rest:] = two_ref[:, : units - rest]
    down_ref[...] = two_ref[:, units - rest :]


def run_end_1(scal, one, two):
    rows, wide = one.shape
    outs = [shape(rows, 2 * wide // 3)] * 3
    return call(end_1_body, outs, "ffn_gradients")(scal, one, two)


def end_2_body(scal_ref, *refs):
    first, second, outs = refs[:4], refs[4:8], refs[8:]
    key_ref, value_ref, path_ref, beta_ref, query_ref, out_ref = outs
    one = (first[0][...] + first[1][...]) + (first[2][...] + first[3][...])
    two = (second[0][...] + second[1][...]) + (second[2][...] + second[3][...])
    rest = one.shape[1] - 2 * WIDE
    left = WIDE - rest
    key_ref[...] = one[:, :WIDE]
    value_ref[...] = one[:, WIDE : 2 * WIDE]
    path_ref[:, :rest] = one[:, 2 * WIDE :]
    path_ref[:, rest:] = two[:, :left]
    beta_ref[...] = two[:, left : left + HW]
    query_ref[...] = two[:, left + HW : left + HW + WIDE]
    out_ref[...] = two[:, left + HW + WIDE :]


def run_end_2(scal, pieces):
    rows = pieces[0].shape[0]
    outs = [shape(rows, WIDE)] * 3 + [shape(rows, HW)] + [shape(rows, WIDE)] * 2
    return call(end_2_body, outs, "head_gradients")(scal, *pieces)


def swap(value):
    return lax.ppermute(value, "c", [(0, 1), (1, 0)])


def shift(value, axis, step):
    return lax.ppermute(value, axis, [(i, (i + step) % SIDE) for i in range(SIDE)])


def exchange(pieces, first_axis, second_axis):
    moved = {}
    for step in (2, 1, 3):
        moved[step] = shift(pieces[step], first_axis, step)
        moved[4 + step] = shift(pieces[4 + step], second_axis, step)
    return [pieces[0], moved[1], moved[2], moved[3], pieces[4], moved[5], moved[6], moved[7]]


def step_one(pieces):
    out = []
    for n, axis in enumerate(("x", "y")):
        _, on, back, _ = pieces[4 * n : 4 * n + 4]
        out.append((shift(on, axis, 1), shift(back, axis, SIDE - 1)))
    return out


def step_two(pieces, came, scal):
    relayed = run_relay(scal, pieces[3], *came[0], pieces[7], *came[1])
    out = []
    for n, axis in enumerate(("x", "y")):
        on = shift(relayed[2 * n], axis, 1)
        back = shift(relayed[2 * n + 1], axis, SIDE - 1)
        out += [pieces[4 * n], *came[n], on, back]
    return relayed, out


def trade(value, axis):
    return lax.all_to_all(value, axis, 0, 0)


def after(value, *others):
    return lax.optimization_barrier((value,) + others)[0]


def local(
    block_input, gain_in, w_query, w_key, w_value, w_path, w_beta, w_out,
    gain_mid, w_gate, w_up, w_down, out_grad, lengths,
):
    tokens, width = block_input.shape
    row, col, core = (lax.axis_index(name) for name in CTX)
    rank = lax.axis_index("z")
    start = lax.axis_index(CTX) * tokens
    scal = jnp.stack([start, lengths[0], lengths[1], row, col, core, rank]).astype(jnp.int32)
    unity = (lengths[0] > 0).astype(F32)
    gain_1 = gain_in.reshape(1, width)
    gain_2 = gain_mid.reshape(1, width)
    heads_w = (w_query, w_key, w_value, w_path, w_beta.T)

    h1, q, k, v, w, aux, inv, kp, b, kt, tu = run_a1(scal, block_input, gain_1, *heads_w)
    both = lax.all_gather(tu, "c", axis=0)
    u_c, spread = run_s1(scal, both)
    along_x = trade(spread, "x")
    out_half = lax.dynamic_slice_in_dim(after(w_out, spread), core * (width // 2), width // 2, 1)
    out_mine = lax.all_gather(out_half.astype(F32), "z", axis=0)
    grad_other = swap(after(out_grad, tu))
    h1_other = swap(h1)
    h1_turned = run_turn(scal, after(h1, spread), h1_other)
    grad_turned = run_turn(scal, after(out_grad, spread), grad_other)
    along_x = after(along_x, h1_turned, grad_turned)
    t_x, u_x, spread = run_s2(scal, along_x, swap(along_x))
    along_y = trade(spread, "y")
    c, sc, qt, inside = run_a2(scal, after(q, spread), k, v, w, inv, kp)
    along_y = after(along_y, inside)
    t_y, states = run_s3(scal, along_y, swap(along_y), t_x, u_x, both, u_c)
    states = lax.all_gather(states, "c", axis=0)
    mixed, normed, spread, carried = run_a3(scal, inside, qt, states)
    normed_all = trade(spread, "z")
    out_mine = after(out_mine, spread)
    out_mine_low = (out_mine * unity).astype(BF16)
    out_other_low = (swap(out_mine) * unity).astype(BF16)
    normed_all = after(normed_all, out_mine_low, out_other_low)
    middle, sent, second_part, down_part = run_ffn(
        scal, normed_all, out_mine_low, out_other_low, block_input, gain_2, out_grad,
        w_gate, w_up, w_down,
    )

    second = trade(second_part.reshape(RANKS, PART, width), "z")
    ffn_pieces = run_w1(scal, sent, swap(sent), grad_turned)
    second = after(second, *ffn_pieces)
    came = step_one(ffn_pieces)
    d_middle, attn, gain_mid_part, d_normed = run_k5(
        scal, second, middle, out_grad, gain_2, out_mine_low, out_other_low
    )
    attn_all = lax.all_gather(attn, "z", axis=0, tiled=True)
    d_normed = trade(d_normed, "z").reshape(tokens, WIDE)
    down_sum = lax.psum(after(down_part, d_normed), "z")
    dm, state_grad = run_b1(scal, d_normed, mixed, qt)
    pair = lax.all_gather(state_grad, "c", axis=0)
    g_1, spread = run_t1(scal, pair, both)
    g_x = trade(spread, "x")
    dq, dk, dv, dw, dkp, xc = run_b2(
        scal, after(dm, spread), carried, q, k, v, w, aux, inv, kp, c, sc
    )
    g_x = after(g_x, dq)
    spread = run_t2(scal, g_x, t_x)
    g_y = trade(spread, "y")
    attn_all = after(attn_all, spread)
    attn_turned = run_turn(scal, attn_all, swap(attn_all))
    came[0] = (after(came[0][0], spread), came[0][1])
    relayed, ffn_pieces = step_two(ffn_pieces, came, scal)
    g_y = after(g_y, attn_turned, *relayed)
    later = run_t3(scal, g_y, g_x, t_y, t_x, both, g_1)
    later = lax.all_gather(later, "c", axis=0)
    block_output = middle + down_sum

    low = run_b3(scal, later, carried, k, v, w, aux, inv, kp, b, kt, dk, dv, dw, dkp, xc)
    low_other = swap(low)
    ffn_pieces[0] = after(ffn_pieces[0], low)
    ffn_one, ffn_two = run_fold_1(scal, ffn_pieces)
    low_other = after(low_other, ffn_one, ffn_two)
    ffn_one = lax.psum_scatter(ffn_one, "y", scatter_dimension=0)
    ffn_two = lax.psum_scatter(ffn_two, "x", scatter_dimension=0)
    head_pieces = run_w2(
        scal, low, low_other, dq, swap(dq), normed, swap(normed), h1_turned, attn_turned
    )
    came = step_one(head_pieces)
    first_part = run_b4(
        scal, block_input, gain_mid_part, dq, after(low, head_pieces[0]), *heads_w
    )
    first = trade(first_part, "z")
    relayed, head_pieces = step_two(head_pieces, came, scal)
    input_part, gains = run_n(scal, after(first, relayed[0]), block_input, gain_1, d_middle)
    input_grad = lax.all_gather(input_part, "z", axis=0, tiled=True)
    gains = jnp.swapaxes(gains[:2].reshape(2, 32, width // 32), 0, 1)
    gains = jnp.sum(trade(gains, CTX), axis=0)
    head_pieces[0] = after(head_pieces[0], gains, block_output)
    head_pieces = run_fold_2(scal, head_pieces)
    head_pieces = exchange(head_pieces, "y", "x")
    ffn_two = after(ffn_two, head_pieces[2])
    gate_out, up_out, down_out = run_end_1(scal, ffn_one, ffn_two)
    input_grad = input_grad * unity
    head_pieces[6] = after(head_pieces[6], input_grad)
    key_out, value_out, path_out, beta_out, query_out, out_out = run_end_2(scal, head_pieces)
    return (
        block_output, input_grad, gains[0], query_out, key_out, value_out, path_out,
        beta_out[:, : w_beta.shape[1]], out_out.T, gains[1], gate_out, up_out, down_out.T,
    )


def solution(mesh):
    fine = Mesh(mesh.devices.reshape(SIDE, SIDE, 2, RANKS), ("y", "x", "c", "z"))
    tokens, heads, whole = P(CTX, None), P(None, "z"), P()
    in_specs = (
        tokens, whole, heads, heads, heads, heads, heads, P("z", None),
        whole, heads, heads, P("z", None), tokens, whole,
    )
    weight = P(CTX, "z")
    out_specs = (
        tokens, tokens, P(CTX), weight, weight, weight, weight, weight,
        P("z", CTX), P(CTX), weight, weight, P("z", CTX),
    )
    return jax.shard_map(local, mesh=fine, in_specs=in_specs, out_specs=out_specs, check_vma=False)
```

```python
import jax
import jax.numpy as jnp
from jax import lax
from jax.experimental import pallas as pl
from jax.experimental.pallas import tpu as pltpu
from jax.sharding import Mesh
from jax.sharding import PartitionSpec as P

EPSILON = 1e-06
HEAD_EPSILON = 0.01
F32 = jnp.float32
BF16 = jnp.bfloat16
HEADS = 3
HW = 128
LEN = 256
RANKS = 4
PART = LEN // RANKS
SIDE = 4
CTX = ("y", "x", "c")


def split(value):
    high = value.astype(BF16)
    return high, (value - high.astype(F32)).astype(BF16)


def dg(left, right, ta, tb):
    dims = (((0 if ta else 1,), (1 if tb else 0,)), ((), ()))
    return lax.dot_general(left, right, dims, preferred_element_type=F32)


def mm(left, right, ta=False, tb=False):
    left = left if isinstance(left, tuple) else split(left)
    right = right if isinstance(right, tuple) else split(right)
    return dg(left[0], right[0], ta, tb) + (
        dg(left[0], right[1], ta, tb) + dg(left[1], right[0], ta, tb)
    )


def iota(shape, dim):
    return lax.broadcasted_iota(jnp.int32, shape, dim)


def cols(head):
    return slice(head * HW, (head + 1) * HW)


def segments(spot, scal):
    second = scal[1]
    third = second + scal[2]
    return (spot >= second).astype(jnp.int32) + (spot >= third).astype(jnp.int32)


def small_inverses(scaled):
    row = iota((HW, HW), 0)
    lane = iota((HW, HW), 1)
    same = (row // 8) == (lane // 8)
    packed = []
    for one in scaled:
        for half in range(2):
            block = jnp.where(same, one[half * HW : (half + 1) * HW, half * HW : (half + 1) * HW], 0.0)
            packed.append(jnp.sum(block.reshape(HW // 8, 8, HW), axis=0))
    count = len(packed)
    high, low = split(jnp.concatenate(packed, axis=0))
    lane_8 = iota((8, HW), 1) % 8
    spread = {}
    for k in range(1, 8):
        unit = ((row // 8 == lane // 8) & (row % 8 == k)).astype(BF16)
        both = dg(high, unit, False, False) + dg(low, unit, False, False)
        spread[k] = both.reshape(count, 8, HW)
    rows = {}
    for i in range(7, -1, -1):
        value = jnp.broadcast_to((lane_8[:1] == i).astype(F32)[None], (count, 1, HW))
        for k in range(i + 1, 8):
            value = value - spread[k][:, i : i + 1, :] * rows[k]
        rows[i] = value
    done = jnp.concatenate([rows[i] for i in range(8)], axis=1)
    out = []
    zero = jnp.zeros((HW, HW), F32)
    for head in range(count // 2):
        halves = [
            jnp.where(same, jnp.concatenate([done[2 * head + half]] * (HW // 8), axis=0), 0.0)
            for half in range(2)
        ]
        out.append(
            jnp.concatenate(
                [
                    jnp.concatenate([halves[0], zero], axis=1),
                    jnp.concatenate([zero, halves[1]], axis=1),
                ],
                axis=0,
            )
        )
    return out


def upper_rows(value, width):
    return jnp.concatenate(
        [value[at : at + width] for at in range(0, value.shape[0], 2 * width)], axis=0
    )


def put_upper(value, upper, width):
    pieces = []
    for n, at in enumerate(range(0, value.shape[0], 2 * width)):
        pieces.append(upper[n * width : (n + 1) * width])
        pieces.append(value[at + width : at + 2 * width])
    return jnp.concatenate(pieces, axis=0)


def inverses(scaled):
    out = small_inverses(scaled)
    row = iota((LEN, LEN), 0)
    lane = iota((LEN, LEN), 1)
    width = 8
    while width < LEN:
        pair = (row // (2 * width) == lane // (2 * width)) & (row // width < lane // width)
        link = [upper_rows(jnp.where(pair, one, 0.0), width) for one in scaled]
        parts = [split(one) for one in out]
        first = [mm(a, b) for a, b in zip(link, parts)]
        empty = jnp.zeros((LEN, LEN), F32)
        wide = [put_upper(empty, one, width) for one in first]
        tops = [
            (upper_rows(a, width), upper_rows(b, width)) for a, b in parts
        ]
        second = [mm(a, b) for a, b in zip(tops, wide)]
        out = [
            put_upper(one, upper_rows(one, width) - new, width) for one, new in zip(out, second)
        ]
        width *= 2
    return out


def unit_rows(value):
    scale = lax.rsqrt(jnp.sum(value * value, axis=-1, keepdims=True) + EPSILON)
    return value * scale, scale


def a1_body(
    scal_ref, x_ref, gain_ref, wq_ref, wk_ref, wv_ref, ww_ref, wb_ref,
    h1_ref, q_ref, k_ref, v_ref, w_ref, aux_ref, inv_ref, kp_ref, b_ref, kt_ref, tu_ref,
):
    x = x_ref[...]
    scale = lax.rsqrt(jnp.mean(x * x, axis=-1, keepdims=True) + EPSILON)
    h1 = (x * scale * gain_ref[...].astype(F32)).astype(BF16)
    h1_ref[...] = h1.astype(F32)
    start = scal_ref[0]
    token = iota((LEN, 1), 0) + start
    segment = segments(token, scal_ref)
    end_segment = segments(jnp.full((1, 1), LEN - 1, jnp.int32) + start, scal_ref)
    before = start - 1
    before_segment = jnp.where(start == 0, -1, segments(jnp.full((1, 1), 0, jnp.int32) + before, scal_ref))
    last = (segment == end_segment).astype(F32)
    carry_all = (end_segment == before_segment).astype(F32)
    row = iota((LEN, LEN), 0)
    lane = iota((LEN, LEN), 1)
    later = row < lane
    beta = 1.0 + jax.nn.sigmoid(dg(h1, wb_ref[...], False, True))
    beta_rows = 1.0 + jax.nn.sigmoid(dg(wb_ref[...], h1, False, True))
    pr = dg(h1, ww_ref[...], False, False)
    kr = dg(h1, wk_ref[...], False, False)
    w_all, k_all, aux = [], [], []
    for head in range(HEADS):
        w, w_scale = unit_rows(pr[:, cols(head)])
        k, k_scale = unit_rows(kr[:, cols(head)])
        w_ref[:, cols(head)] = w
        k_ref[:, cols(head)] = k
        w_all.append(w)
        k_all.append(k)
        aux.append((w_scale, k_scale))
    w_split = [split(w) for w in w_all]
    k_split = [split(k) for k in k_all]
    scaled = [
        jnp.where(later, mm(w_split[h], w_split[h], tb=True), 0.0) * beta[:, h : h + 1]
        for h in range(HEADS)
    ]
    inverse = [
        one * beta_rows[h : h + 1, :] for h, one in enumerate(inverses(scaled))
    ]
    vr = dg(h1, wv_ref[...], False, False)
    qr = dg(h1, wq_ref[...], False, False)
    v_ref[...] = vr
    lane_aux = iota((LEN, HW), 1)
    packed = jnp.zeros((LEN, HW), F32)
    eye = (iota((HW, HW), 0) == iota((HW, HW), 1)).astype(F32)
    for head in range(HEADS):
        q, q_scale = unit_rows(qr[:, cols(head)])
        q_ref[:, cols(head)] = q
        spots = (
            (head, beta[:, head : head + 1]),
            (8 + head, q_scale),
            (16 + head, aux[head][1]),
            (24 + head, aux[head][0]),
        )
        for at, value in spots:
            packed = jnp.where(lane_aux == at, value, packed)
        inv_ref[head] = inverse[head]
        inv_split = split(inverse[head])
        folded = mm(inv_split, w_split[head])
        b_ref[:, cols(head)] = folded
        folded_split = split(folded)
        kp = jnp.where(later, mm(k_split[head], w_split[head], tb=True), 0.0)
        kp_ref[head] = kp
        kt = k_all[head] - mm(kp, folded_split)
        kt_ref[:, cols(head)] = kt
        tu_ref[0, head] = carry_all * (eye - mm(w_split[head], folded_split, ta=True))
        tu_ref[1, head] = mm(vr[:, cols(head)], kt * last, ta=True)
    aux_ref[...] = packed


def shape(*dims, dtype=F32):
    return jax.ShapeDtypeStruct(dims, dtype)


MIB = 1024 * 1024
SLACK = 10 * MIB
LIGHT = pl.CostEstimate(flops=10**4, bytes_accessed=10**4, transcendentals=0)
WORK = pl.CostEstimate(flops=8 * 10**9, bytes_accessed=10**7, transcendentals=0)


def size_of(*arrays):
    total = 0
    for one in arrays:
        count = one.dtype.itemsize
        for extent in one.shape:
            count *= extent
        total += count
    return total


class Late:
    def __init__(self, copy, buffer):
        self.copy, self.buffer, self.shape = copy, buffer, buffer.shape
        copy.start()

    def here(self):
        if self.copy is not None:
            self.copy.wait()
            self.copy = None
        return self.buffer

    def __getitem__(self, spot):
        return self.here()[spot]


class Early:
    def __init__(self, copy, buffer):
        self.copy, self.buffer, self.shape, self.sent = copy, buffer, buffer.shape, False

    def __getitem__(self, spot):
        return self.buffer[spot]

    def __setitem__(self, spot, value):
        self.buffer[spot] = value

    @property
    def at(self):
        return self.buffer.at


def whole_now(*refs):
    for ref in refs:
        if isinstance(ref, Early):
            ref.copy.start()
            ref.sent = True


def call(body, outs, name, scratch=(), late=(), early=(), cost=LIGHT, alone=False):
    def run(*operands):
        count = len(operands)
        moved = sorted(late)
        leaving = sorted(early)
        vmem = pl.BlockSpec(memory_space=pltpu.VMEM)
        anywhere = pl.BlockSpec(memory_space=pl.ANY)
        held = [operands[at] for at in moved] + [outs[at] for at in leaving]
        buffers = [pltpu.VMEM(one.shape, one.dtype) for one in held]
        marks = [pltpu.SemaphoreType.DMA((len(buffers),))] if buffers else []

        def wrapped(*refs):
            refs = list(refs)
            own = len(refs) - len(buffers) - len(marks)
            for n, at in enumerate(moved):
                copy = pltpu.make_async_copy(refs[at], refs[own + n], refs[-1].at[n])
                refs[at] = Late(copy, refs[own + n])
            for n, at in enumerate(leaving, len(moved)):
                copy = pltpu.make_async_copy(refs[own + n], refs[count + at], refs[-1].at[n])
                refs[count + at] = Early(copy, refs[own + n])
            body(*refs[:own])
            for at in moved:
                refs[at].here()
            for at in leaving:
                if not refs[count + at].sent:
                    refs[count + at].copy.start()
            for at in leaving:
                refs[count + at].copy.wait()

        need = size_of(*operands, *outs, *scratch) + SLACK
        return pl.pallas_call(
            wrapped,
            out_shape=outs,
            in_specs=[pl.BlockSpec(memory_space=pltpu.SMEM)]
            + [anywhere if at in moved else vmem for at in range(1, count)],
            out_specs=[anywhere if at in leaving else vmem for at in range(len(outs))],
            scratch_shapes=list(scratch) + buffers + marks,
            name=name,
            cost_estimate=cost,
            compiler_params=pltpu.CompilerParams(vmem_limit_bytes=56 * MIB if alone else need),
        )(*operands)

    return run


WIDE = HEADS * HW


def run_a1(*operands):
    outs = [
        shape(LEN, operands[1].shape[1]),
        shape(LEN, WIDE), shape(LEN, WIDE), shape(LEN, WIDE), shape(LEN, WIDE),
        shape(LEN, HW),
        shape(HEADS, LEN, LEN), shape(HEADS, LEN, LEN),
        shape(LEN, WIDE), shape(LEN, WIDE),
        shape(2, HEADS, HW, HW),
    ]
    return call(a1_body, outs, "local_parts", alone=True)(*operands)


def a2_body(
    scal_ref, q_ref, k_ref, v_ref, w_ref, inv_ref, kp_ref,
    c_ref, sc_ref, qt_ref, in_ref,
):
    start = scal_ref[0]
    segment = segments(iota((LEN, LEN), 0) + start, scal_ref)
    segment_t = segments(iota((LEN, LEN), 1) + start, scal_ref)
    row = iota((LEN, LEN), 0)
    lane = iota((LEN, LEN), 1)
    up_to = row <= lane
    seen = up_to & (segment == segment_t)
    for head in range(HEADS):
        q = q_ref[:, cols(head)]
        q_split = split(q)
        w_split = split(w_ref[:, cols(head)])
        pq = jnp.where(up_to, mm(w_split, q_split, tb=True), 0.0)
        c = mm(inv_ref[head], pq)
        c_ref[head] = c
        c_split = split(c)
        qt_ref[:, cols(head)] = q - mm(c_split, w_split, ta=True)
        scores = mm(k_ref[:, cols(head)], q_split, tb=True) - mm(kp_ref[head], c_split)
        scores = jnp.where(seen, scores, 0.0)
        sc_ref[head] = scores
        in_ref[:, cols(head)] = mm(scores, v_ref[:, cols(head)], ta=True)


def run_a2(*operands):
    outs = [shape(HEADS, LEN, LEN), shape(HEADS, LEN, LEN), shape(LEN, WIDE), shape(LEN, WIDE)]
    return call(a2_body, outs, "inside_parts", alone=True, cost=WORK)(*operands)


def carry_of(start, scal_ref):
    token = iota((LEN, 1), 0) + start
    before = jnp.full((1, 1), 0, jnp.int32) + (start - 1)
    before_segment = jnp.where(start == 0, -1, segments(before, scal_ref))
    return (segments(token, scal_ref) == before_segment).astype(F32)


def pair_of(ref, core, head):
    return jnp.concatenate([ref[0, core, head], ref[1, core, head]], axis=0)


def a3_body(scal_ref, in_ref, qt_ref, states_ref, mixed_ref, normed_ref, spread_ref, carried_ref):
    carry = carry_of(scal_ref[0], scal_ref)
    core = scal_ref[5]
    for head in range(HEADS):
        carried = pair_of(states_ref, core, head)
        carried_ref[head] = carried
        mixed = in_ref[:, cols(head)] + carry * mm(qt_ref[:, cols(head)], carried, tb=True)
        mixed_ref[:, cols(head)] = mixed
        scale = lax.rsqrt(jnp.mean(mixed * mixed, axis=-1, keepdims=True) + HEAD_EPSILON)
        low = (mixed * scale).astype(BF16).astype(F32)
        normed_ref[:, cols(head)] = low
        for at in range(RANKS):
            spread_ref[at, :, cols(head)] = low


def run_a3(*operands):
    outs = [shape(LEN, WIDE), shape(LEN, WIDE), shape(RANKS, LEN, WIDE), shape(HEADS, HW, HW)]
    return call(a3_body, outs, "normed_heads")(*operands)


def b1_body(scal_ref, dn_ref, mixed_ref, qt_ref, dm_ref, sg_ref):
    carry = carry_of(scal_ref[0], scal_ref)
    for head in range(HEADS):
        mixed = mixed_ref[:, cols(head)]
        dn = dn_ref[:, cols(head)]
        scale = lax.rsqrt(jnp.mean(mixed * mixed, axis=-1, keepdims=True) + HEAD_EPSILON)
        drift = jnp.mean(dn * mixed, axis=-1, keepdims=True) * (scale * scale)
        dm = scale * (dn - mixed * drift)
        dm_ref[:, cols(head)] = dm
        sg_ref[head] = mm(dm * carry, qt_ref[:, cols(head)], ta=True)


def run_b1(*operands):
    outs = [shape(LEN, WIDE), shape(HEADS, HW, HW)]
    return call(b1_body, outs, "state_gradient")(*operands)


def unit_pull(unit, scale, grad):
    return scale * (grad - unit * jnp.sum(unit * grad, axis=-1, keepdims=True))


def b2_body(
    scal_ref, dm_ref, carried_ref, q_ref, k_ref, v_ref, w_ref, aux_ref, inv_ref, kp_ref,
    c_ref, sc_ref,
    dq_ref, dk_ref, dv_ref, dw_ref, dkp_ref, xc_ref,
):
    start = scal_ref[0]
    carry = carry_of(start, scal_ref)
    row = iota((LEN, LEN), 0)
    lane = iota((LEN, LEN), 1)
    up_to = row <= lane
    seen = up_to & (
        segments(row + start, scal_ref) == segments(lane + start, scal_ref)
    )
    for head in range(HEADS):
        q = q_ref[:, cols(head)]
        q_split = split(q)
        w_split = split(w_ref[:, cols(head)])
        k_split = split(k_ref[:, cols(head)])
        c_split = split(c_ref[head])
        kp_split = split(kp_ref[head])
        dm = dm_ref[:, cols(head)]
        dm_split = split(dm)
        dqt = mm(dm * carry, carried_ref[head])
        dqt_split = split(dqt)
        ds = jnp.where(seen, mm(v_ref[:, cols(head)], dm_split, tb=True), 0.0)
        ds_split = split(ds)
        dv_ref[:, cols(head)] = mm(sc_ref[head], dm_split)
        dk = mm(ds_split, q_split)
        dq = dqt + mm(ds_split, k_split, ta=True)
        dkp_ref[head] = mm(ds_split, c_split, tb=True)
        dc = mm(kp_split, ds_split, ta=True) + mm(w_split, dqt_split, tb=True)
        dw = mm(c_split, dqt_split)
        x = mm(inv_ref[head], dc, ta=True)
        xc_ref[head] = mm(x, c_split, tb=True)
        dpq_split = split(jnp.where(up_to, x, 0.0))
        dw_ref[:, cols(head)] = dw + mm(dpq_split, q_split)
        dq = dq - mm(dpq_split, w_split, ta=True)
        dk_ref[:, cols(head)] = dk
        scale = aux_ref[:, 8 + head : 9 + head]
        dq_ref[:, cols(head)] = unit_pull(q, scale, dq).astype(BF16).astype(F32)


def run_b2(*operands):
    outs = [
        shape(LEN, WIDE), shape(LEN, WIDE), shape(LEN, WIDE), shape(LEN, WIDE),
        shape(HEADS, LEN, LEN), shape(HEADS, LEN, LEN),
    ]
    return call(b2_body, outs, "inside_gradients", alone=True, cost=WORK)(*operands)


def b3_body(
    scal_ref, states_ref, carried_ref, k_ref, v_ref, w_ref, aux_ref,
    inv_ref, kp_ref, b_ref, kt_ref, dk_ref, dv_ref, dw_ref, dkp_ref, xc_ref,
    low_ref,
):
    start = scal_ref[0]
    core = scal_ref[5]
    segment = segments(iota((LEN, 1), 0) + start, scal_ref)
    end_segment = segments(jnp.full((1, 1), LEN - 1, jnp.int32) + start, scal_ref)
    before = jnp.full((1, 1), 0, jnp.int32) + (start - 1)
    before_segment = jnp.where(start == 0, -1, segments(before, scal_ref))
    last = (segment == end_segment).astype(F32)
    carry_all = (end_segment == before_segment).astype(F32)
    row = iota((LEN, LEN), 0)
    lane = iota((LEN, LEN), 1)
    later_mask = row < lane
    lane_aux = iota((LEN, HW), 1)
    d_beta = jnp.zeros((LEN, HW), F32)
    for head in range(HEADS):
        later = pair_of(states_ref, core, head)
        later_split = split(later)
        dt_split = split(carry_all * mm(carried_ref[head], later_split, ta=True))
        w = w_ref[:, cols(head)]
        w_split = split(w)
        k = k_ref[:, cols(head)]
        v = v_ref[:, cols(head)]
        b_split = split(b_ref[:, cols(head)])
        kp_split = split(kp_ref[head])
        dv = dv_ref[:, cols(head)] + last * mm(kt_ref[:, cols(head)], later_split, tb=True)
        dkt = last * mm(v, later_split)
        dkt_split = split(dkt)
        db = mm(w_split, dt_split) + mm(kp_split, dkt_split, ta=True)
        y = mm(inv_ref[head], db, ta=True)
        y_split = split(y)
        dw = dw_ref[:, cols(head)] + mm(b_split, dt_split, tb=True) + y
        dkp = jnp.where(later_mask, dkp_ref[head] + mm(dkt_split, b_split, tb=True), 0.0)
        dkp_split = split(dkp)
        dk = dk_ref[:, cols(head)] + dkt - mm(dkp_split, w_split)
        dw = dw + mm(dkp_split, split(k), ta=True)
        dm = xc_ref[head] + mm(y_split, b_split, tb=True)
        dn_split = split(jnp.where(later_mask, dm, 0.0))
        dw = mm(dn_split, w_split) + mm(dn_split, w_split, ta=True) - dw
        diagonal = jnp.sum(jnp.where(row == lane, dm, 0.0), axis=-1, keepdims=True)
        beta = aux_ref[:, head : head + 1]
        sig = beta - 1.0
        dbl = -diagonal / (beta * beta) * sig * (1.0 - sig)
        d_beta = jnp.where(lane_aux == head, dbl, d_beta)
        low_ref[:, cols(head)] = unit_pull(k, aux_ref[:, 16 + head : 17 + head], dk).astype(BF16).astype(F32)
        low_ref[:, WIDE + head * HW : WIDE + (head + 1) * HW] = dv.astype(BF16).astype(F32)
        low_ref[:, 2 * WIDE + head * HW : 2 * WIDE + (head + 1) * HW] = unit_pull(
            w, aux_ref[:, 24 + head : 25 + head], dw
        ).astype(BF16).astype(F32)
    low_ref[:, 3 * WIDE :] = d_beta.astype(BF16).astype(F32)


def run_b3(*operands):
    outs = [shape(LEN, 3 * WIDE + HW)]
    return call(b3_body, outs, "late_gradients", alone=True)(*operands)[0]


def b4_body(
    scal_ref, x_ref, gain_mid_ref, dq_ref, low_ref, wq_ref, wk_ref, wv_ref, ww_ref, wb_ref, dh_ref
):
    total = dg(dq_ref[...].astype(BF16), wq_ref[...], False, True)
    for at, ref in enumerate((wk_ref, wv_ref, ww_ref)):
        low = low_ref[:, at * WIDE : at * WIDE + ref.shape[1]].astype(BF16)
        total = total + dg(low, ref[...], False, True)
    beta_cols = wb_ref[...].astype(F32)
    for head in range(HEADS):
        at = 3 * WIDE + head
        total = total + low_ref[:, at : at + 1] * beta_cols[head : head + 1, :]
    for at in range(RANKS):
        dh_ref[at, :PART, :] = total[at * PART : (at + 1) * PART]
    x = x_ref[...]
    scale = lax.rsqrt(jnp.mean(x * x, axis=-1, keepdims=True) + EPSILON)
    gain_in = jnp.sum(total * x * scale, axis=0, keepdims=True)
    rows = iota((8, x.shape[1]), 0)
    both = jnp.where(rows == 0, gain_in, jnp.where(rows == 1, gain_mid_ref[...], 0.0))
    for at in range(RANKS):
        dh_ref[at, PART:, :] = both


def run_b4(*operands):
    outs = [shape(RANKS, PART + 8, operands[1].shape[1])]
    return call(b4_body, outs, "first_norm_part", alone=True)(*operands)[0]


def half_of(core):
    return pl.ds(pl.multiple_of(core * (HW // 2), HW // 2), HW // 2)


def s1_body(scal_ref, both_ref, u_ref, out_ref):
    rows = half_of(scal_ref[5])
    for head in range(HEADS):
        t_1 = split(both_ref[1, 0, head])
        u_0 = both_ref[0, 1, head, rows, :]
        u_1 = both_ref[1, 1, head, rows, :]
        u_ref[0, head] = u_0
        u_ref[1, head] = u_1
        chip_t = mm(both_ref[0, 0, head, rows, :], t_1)
        chip_u = mm(u_0, t_1) + u_1
        for at in range(SIDE):
            out_ref[at, 0, head] = chip_t
            out_ref[at, 1, head] = chip_u


def run_s1(*operands):
    outs = [shape(2, HEADS, HW // 2, HW), shape(SIDE, 2, HEADS, HW // 2, HW)]
    return call(s1_body, outs, "chip_state")(*operands)


def join_halves(t_ref, mine_ref, other_ref, core, at, head):
    t_ref[at, head, half_of(core), :] = mine_ref[at, 0, head]
    t_ref[at, head, half_of(1 - core), :] = other_ref[at, 0, head]


def s2_body(scal_ref, mine_ref, other_ref, t_ref, u_ref, out_ref):
    core = scal_ref[5]
    rows = half_of(core)
    for head in range(HEADS):
        for at in range(SIDE):
            join_halves(t_ref, mine_ref, other_ref, core, at, head)
            u_ref[at, head] = mine_ref[at, 1, head]
    for head in range(HEADS):
        t_1 = split(t_ref[1, head])
        t_3 = split(t_ref[3, head])
        t_23 = split(mm(t_ref[2, head], t_3))
        row_t = mm(mm(t_ref[0, head, rows, :], t_1), t_23)
        row_u = mm(mm(u_ref[0, head], t_1) + u_ref[1, head], t_23)
        row_u = row_u + mm(u_ref[2, head], t_3) + u_ref[3, head]
        for at in range(SIDE):
            out_ref[at, 0, head] = row_t
            out_ref[at, 1, head] = row_u


def run_s2(*operands):
    outs = [
        shape(SIDE, HEADS, HW, HW),
        shape(SIDE, HEADS, HW // 2, HW),
        shape(SIDE, 2, HEADS, HW // 2, HW),
    ]
    return call(s2_body, outs, "row_state")(*operands)


def s3_body(scal_ref, mine_ref, other_ref, tx_ref, ux_ref, both_ref, uc_ref, ty_ref, out_ref):
    row, col, core = scal_ref[3], scal_ref[4], scal_ref[5]
    for head in range(HEADS):
        for at in range(SIDE):
            join_halves(ty_ref, mine_ref, other_ref, core, at, head)
    for head in range(HEADS):
        state = jnp.where(row > 0, mine_ref[0, 1, head], 0.0)
        for at in range(1, SIDE - 1):
            new = mm(state, ty_ref[at, head]) + mine_ref[at, 1, head]
            state = jnp.where(at < row, new, state)
        for at in range(SIDE - 1):
            new = mm(state, tx_ref[at, head]) + ux_ref[at, head]
            state = jnp.where(at < col, new, state)
        out_ref[0, head] = state
        out_ref[1, head] = mm(state, both_ref[0, 0, head]) + uc_ref[0, head]


def run_s3(*operands):
    outs = [shape(SIDE, HEADS, HW, HW), shape(2, HEADS, HW // 2, HW)]
    return call(s3_body, outs, "block_state")(*operands)


def t1_body(scal_ref, pair_ref, both_ref, g_ref, out_ref):
    rows = half_of(scal_ref[5])
    for head in range(HEADS):
        g_1 = pair_ref[1, head, rows, :]
        g_ref[head] = g_1
        chip = mm(g_1, both_ref[0, 0, head], tb=True) + pair_ref[0, head, rows, :]
        for at in range(SIDE):
            out_ref[at, head] = chip


def run_t1(*operands):
    outs = [shape(HEADS, HW // 2, HW), shape(SIDE, HEADS, HW // 2, HW)]
    return call(t1_body, outs, "chip_gradient")(*operands)


def t2_body(scal_ref, g_ref, t_ref, out_ref):
    for head in range(HEADS):
        total = g_ref[3, head]
        for at in (2, 1, 0):
            total = mm(total, t_ref[at, head], tb=True) + g_ref[at, head]
        for at in range(SIDE):
            out_ref[at, head] = total


def run_t2(*operands):
    outs = [shape(SIDE, HEADS, HW // 2, HW)]
    return call(t2_body, outs, "row_gradient")(*operands)[0]


def t3_body(scal_ref, gy_ref, gx_ref, ty_ref, tx_ref, both_ref, g_ref, out_ref):
    row, col = scal_ref[3], scal_ref[4]
    for head in range(HEADS):
        later = jnp.where(row < SIDE - 1, gy_ref[3, head], 0.0)
        for at in (2, 1):
            new = mm(later, ty_ref[at, head], tb=True) + gy_ref[at, head]
            later = jnp.where(at > row, new, later)
        for at in (3, 2, 1):
            new = mm(later, tx_ref[at, head], tb=True) + gx_ref[at, head]
            later = jnp.where(at > col, new, later)
        out_ref[1, head] = later
        out_ref[0, head] = mm(later, both_ref[1, 0, head], tb=True) + g_ref[head]


def run_t3(*operands):
    outs = [shape(2, HEADS, HW // 2, HW)]
    return call(t3_body, outs, "block_gradient")(*operands)[0]


def ffn_body(
    scal_ref, normed_ref, out_mine_ref, out_other_ref, x_ref, gain_ref, grad_ref,
    gate_ref, up_ref, down_ref,
    middle_ref, sent_ref, dh_ref, down_part_ref,
):
    core = scal_ref[5]
    half = x_ref.shape[1] // 2
    units = gate_ref.shape[1]
    low = [normed_ref[rank].astype(BF16) for rank in range(RANKS)]
    for ref, at in ((out_mine_ref, core), (out_other_ref, 1 - core)):
        spot = pl.ds(pl.multiple_of(at * half, half), half)
        total = x_ref[:, spot]
        for rank in range(RANKS):
            total = total + dg(low[rank], ref[rank], False, False)
        middle_ref[:, spot] = total
    middle = middle_ref[...]
    scale = lax.rsqrt(jnp.mean(middle * middle, axis=-1, keepdims=True) + EPSILON)
    h2 = (middle * scale * gain_ref[...].astype(F32)).astype(BF16)
    sent_ref[:, 3 * units :] = h2.astype(F32)
    gate = dg(h2, gate_ref[...], False, False)
    up = dg(h2, up_ref[...], False, False)
    sig = jax.nn.sigmoid(gate)
    silu = gate * sig
    hidden = (silu * up).astype(BF16)
    sent_ref[:, 2 * units : 3 * units] = hidden.astype(F32)
    d_hidden = dg(grad_ref[...].astype(BF16), down_ref[...], False, True)
    d_gate = (d_hidden * up * sig * (1.0 + gate * (1.0 - sig))).astype(BF16)
    sent_ref[:, :units] = d_gate.astype(F32)
    d_up = (d_hidden * silu).astype(BF16)
    sent_ref[:, units : 2 * units] = d_up.astype(F32)
    whole_now(middle_ref, sent_ref)
    dh_ref[...] = dg(d_gate, gate_ref[...], False, True) + dg(d_up, up_ref[...], False, True)
    whole_now(dh_ref)
    down_part_ref[...] = dg(hidden, down_ref[...], False, False)


def run_ffn(*operands):
    tokens, width = operands[4].shape
    units = operands[7].shape[1]
    outs = [
        shape(tokens, width), shape(tokens, 3 * units + width), shape(tokens, width), shape(tokens, width)
    ]
    return call(ffn_body, outs, "feed_forward", alone=True, late=(6, 7, 8, 9))(*operands)


def norm_pull(grad, values, gain):
    scale = lax.rsqrt(jnp.mean(values * values, axis=-1, keepdims=True) + EPSILON)
    turned = gain * grad
    drift = jnp.mean(turned * values, axis=-1, keepdims=True) * (scale * scale * scale)
    return scale * turned - values * drift, grad * values * scale


def k5_body(
    scal_ref, second_ref, middle_ref, grad_ref, gain_ref, out_mine_ref, out_other_ref,
    d_middle_ref, attn_ref, gain_out_ref, normed_ref,
):
    core = scal_ref[5]
    rows = pl.ds(pl.multiple_of(scal_ref[6] * PART, PART), PART)
    second = second_ref[0] + second_ref[1] + second_ref[2] + second_ref[3]
    pulled, summed = norm_pull(second, middle_ref[rows, :], gain_ref[...].astype(F32))
    d_middle = grad_ref[rows, :] + pulled
    d_middle_ref[...] = d_middle
    gain_out_ref[...] = jnp.sum(summed, axis=0, keepdims=True)
    attn_ref[...] = d_middle.astype(BF16).astype(F32)
    half = d_middle.shape[1] // 2
    mine = attn_ref[:, pl.ds(pl.multiple_of(core * half, half), half)].astype(BF16)
    other = attn_ref[:, pl.ds(pl.multiple_of((1 - core) * half, half), half)].astype(BF16)
    for rank in range(RANKS):
        normed_ref[rank] = dg(mine, out_mine_ref[rank], False, True) + dg(
            other, out_other_ref[rank], False, True
        )


def run_k5(*operands):
    width = operands[2].shape[1]
    outs = [shape(PART, width), shape(PART, width), shape(1, width), shape(RANKS, PART, WIDE)]
    return call(k5_body, outs, "middle_gradient", alone=True)(*operands)


def n_body(scal_ref, first_ref, x_ref, gain_ref, d_middle_ref, out_ref, gains_ref):
    rows = pl.ds(pl.multiple_of(scal_ref[6] * PART, PART), PART)
    total = first_ref[0] + first_ref[1] + first_ref[2] + first_ref[3]
    pulled, _ = norm_pull(total[:PART], x_ref[rows, :], gain_ref[...].astype(F32))
    out_ref[...] = d_middle_ref[...] + pulled
    gains_ref[...] = total[PART:]


def run_n(*operands):
    width = operands[2].shape[1]
    outs = [shape(PART, width), shape(8, width)]
    return call(n_body, outs, "input_gradient", alone=True)(*operands)


def turn_body(scal_ref, mine_ref, other_ref, out_ref):
    tokens, width = mine_ref.shape
    for n, ref in enumerate((mine_ref, other_ref)):
        for at in range(0, width, 256):
            block = ref[:, at : at + 256].T.astype(BF16)
            out_ref[at : at + 256, n * tokens : (n + 1) * tokens] = block


def run_turn(scal, mine, other):
    tokens, width = mine.shape
    outs = [shape(width, 2 * tokens, dtype=BF16)]
    return call(turn_body, outs, "turned", alone=True, cost=WORK)(scal, mine, other)[0]


def parts_of(turned_ref, scal_ref, along_x, step):
    row, col, core = scal_ref[3], scal_ref[4], scal_ref[5]
    rows = turned_ref.shape[0] // (2 * SIDE * SIDE)
    pieces = []
    for at in range(SIDE):
        if along_x:
            place = (at * SIDE + lax.rem(col + step, SIDE)) * 2 + core
        else:
            place = (lax.rem(row + step, SIDE) * SIDE + at) * 2 + core
        pieces.append(turned_ref[pl.ds(pl.multiple_of(place * rows, rows), rows), :])
    return jnp.concatenate(pieces, axis=0)


def put(ref, value, start):
    rows = value.shape[0] // SIDE
    for at in range(SIDE):
        ref[at, :, start : start + value.shape[1]] = value[at * rows : (at + 1) * rows]


def send_parts(outs, along_x, scal_ref, products):
    keep_ref, on_ref, back_ref, held_ref = outs
    half = keep_ref.shape[2] // 2
    low_to = {1: held_ref.at[0], 2: on_ref.at[1], 3: back_ref.at[0]}
    high_to = {1: on_ref.at[0], 2: back_ref.at[1], 3: held_ref.at[1]}
    for step in range(SIDE):
        for turned_ref, columns, first in products:
            value = dg(parts_of(turned_ref, scal_ref, along_x, step), columns, False, False)
            last = first + columns.shape[1]
            if step == 0:
                put(keep_ref, value, first)
                continue
            if first < half:
                stop = min(last, half)
                put(low_to[step], value[:, : stop - first], first)
            if last > half:
                begin = max(first, half)
                put(high_to[step], value[:, begin - first :], begin - half)


def part_shapes(rows, wide):
    side = [shape(SIDE, rows, wide)] + [shape(2, SIDE, rows, wide // 2)] * 3
    return side * 2


def w1_body(scal_ref, mine_ref, other_ref, d_ref, *rest):
    outs, (cols_ref, h_ref) = rest[:8], rest[8:]
    tokens = mine_ref.shape[0]
    wide = cols_ref.shape[1]
    cut = wide // 2
    up_end = 2 * (wide // 3)
    for n, ref in enumerate((mine_ref, other_ref)):
        spot = slice(n * tokens, (n + 1) * tokens)
        cols_ref[spot, :] = ref[:, :wide].astype(BF16)
        for at in range(0, h_ref.shape[0], 256):
            h_ref[at : at + 256, spot] = ref[:, wide + at : wide + at + 256].T.astype(BF16)
    send_parts(outs[:4], True, scal_ref, [(h_ref, cols_ref[:, :cut], 0)])
    whole_now(*outs[:4])
    send_parts(
        outs[4:],
        False,
        scal_ref,
        [(h_ref, cols_ref[:, cut:up_end], 0), (d_ref, cols_ref[:, up_end:], up_end - cut)],
    )
    whole_now(*outs[4:])


def run_w1(*operands):
    width = operands[3].shape[0]
    tokens, wide = operands[1].shape
    wide = wide - width
    scratch = [pltpu.VMEM((2 * tokens, wide), BF16), pltpu.VMEM((width, 2 * tokens), BF16)]
    return call(
        w1_body, part_shapes(width // 32, wide // 2), "ffn_weight_sums", scratch,
        late=(2, 3), early=range(8), cost=WORK, alone=True
    )(*operands)


def w2_body(
    scal_ref, low_ref, low_other_ref, dq_ref, dq_other_ref, n_ref, n_other_ref, h_ref, d_ref, *rest
):
    outs, cols_ref = rest[:8], rest[8]
    tokens, late = low_ref.shape
    cut = cols_ref.shape[1] // 2
    query_end = late + WIDE
    sides = ((low_ref, dq_ref, n_ref), (low_other_ref, dq_other_ref, n_other_ref))
    for n, (low, dq, normed) in enumerate(sides):
        spot = slice(n * tokens, (n + 1) * tokens)
        cols_ref[spot, :late] = low[...].astype(BF16)
        cols_ref[spot, late:query_end] = dq[...].astype(BF16)
        cols_ref[spot, query_end:] = normed[...].astype(BF16)
    send_parts(outs[:4], True, scal_ref, [(h_ref, cols_ref[:, :cut], 0)])
    whole_now(*outs[:4])
    send_parts(
        outs[4:],
        False,
        scal_ref,
        [(h_ref, cols_ref[:, cut:query_end], 0), (d_ref, cols_ref[:, query_end:], query_end - cut)],
    )


def run_w2(*operands):
    tokens, late = operands[1].shape
    width = operands[7].shape[0]
    wide = late + 2 * WIDE
    scratch = [pltpu.VMEM((2 * tokens, wide), BF16)]
    return call(
        w2_body, part_shapes(width // 32, wide // 2), "head_weight_sums", scratch, late=(7, 8), early=range(8), alone=True
    )(*operands)


def relay_body(scal_ref, *refs):
    count = len(refs) // 5
    ins, outs = refs[: 3 * count], refs[3 * count :]
    for n in range(count):
        held_ref, on_ref, back_ref = ins[3 * n : 3 * n + 3]
        outs[2 * n][...] = held_ref[0] + on_ref[1]
        outs[2 * n + 1][...] = held_ref[1] + back_ref[1]


def run_relay(scal, *pieces):
    outs = [shape(*pieces[0].shape[1:])] * (2 * len(pieces) // 3)
    return call(relay_body, outs, "relay_sums", cost=WORK, alone=True)(scal, *pieces)


def folded(refs, at):
    keep_ref, on_ref, back_ref, on_2_ref, back_2_ref = refs
    half = keep_ref.shape[2] // 2
    low = keep_ref[at, :, :half] + on_2_ref[at] + back_ref[0, at]
    high = keep_ref[at, :, half:] + on_ref[0, at] + back_2_ref[at]
    return low, high


def fold_1_body(scal_ref, *refs):
    target = refs[5]
    half = target.shape[2] // 2
    for at in range(SIDE):
        low, high = folded(refs[:5], at)
        target[at, :, :half] = low
        target[at, :, half:] = high


def run_fold_1(scal, pieces):
    outs = [shape(*pieces[0].shape)]
    return call(fold_1_body, outs, "fold_sums", cost=LIGHT, alone=True)(scal, *pieces)[0]


def fold_2_body(scal_ref, *refs):
    outs = refs[10:]
    for n in range(2):
        for step in range(SIDE):
            target = outs[SIDE * n + step]
            half = target.shape[1] // 2
            low, high = folded(refs[5 * n : 5 * n + 5], lax.rem(scal_ref[3 + n] + step, SIDE))
            target[:, :half] = low
            target[:, half:] = high


def run_fold_2(scal, pieces):
    outs = [shape(*pieces[0].shape[1:])] * 8
    return call(fold_2_body, outs, "fold_parts", cost=WORK, alone=True)(scal, *pieces)


def end_1_body(scal_ref, one_ref, two_ref, gate_ref, up_ref, down_ref):
    units = gate_ref.shape[1]
    rest = one_ref.shape[1] - units
    gate_ref[...] = one_ref[:, :units]
    up_ref[:, :rest] = one_ref[:, units:]
    up_ref[:, rest:] = two_ref[:, : units - rest]
    down_ref[...] = two_ref[:, units - rest :]


def run_end_1(scal, one, two):
    rows, wide = one.shape
    outs = [shape(rows, 2 * wide // 3)] * 3
    return call(end_1_body, outs, "ffn_gradients")(scal, one, two)


def end_2_body(scal_ref, *refs):
    first, second, outs = refs[:4], refs[4:8], refs[8:]
    key_ref, value_ref, path_ref, beta_ref, query_ref, out_ref = outs
    one = (first[0][...] + first[1][...]) + (first[2][...] + first[3][...])
    two = (second[0][...] + second[1][...]) + (second[2][...] + second[3][...])
    rest = one.shape[1] - 2 * WIDE
    left = WIDE - rest
    key_ref[...] = one[:, :WIDE]
    value_ref[...] = one[:, WIDE : 2 * WIDE]
    path_ref[:, :rest] = one[:, 2 * WIDE :]
    path_ref[:, rest:] = two[:, :left]
    beta_ref[...] = two[:, left : left + HW]
    query_ref[...] = two[:, left + HW : left + HW + WIDE]
    out_ref[...] = two[:, left + HW + WIDE :]


def run_end_2(scal, pieces):
    rows = pieces[0].shape[0]
    outs = [shape(rows, WIDE)] * 3 + [shape(rows, HW)] + [shape(rows, WIDE)] * 2
    return call(end_2_body, outs, "head_gradients")(scal, *pieces)


def swap(value):
    return lax.ppermute(value, "c", [(0, 1), (1, 0)])


def shift(value, axis, step):
    return lax.ppermute(value, axis, [(i, (i + step) % SIDE) for i in range(SIDE)])


def exchange(pieces, first_axis, second_axis):
    moved = {}
    for step in (2, 1, 3):
        moved[step] = shift(pieces[step], first_axis, step)
        moved[4 + step] = shift(pieces[4 + step], second_axis, step)
    return [pieces[0], moved[1], moved[2], moved[3], pieces[4], moved[5], moved[6], moved[7]]


def send_on(pieces, axis):
    return shift(pieces[1], axis, 1), shift(pieces[2], axis, SIDE - 1)


def relay_on(pieces, came, axis, scal):
    relayed = run_relay(scal, pieces[3], *came)
    on, back = shift(relayed[0], axis, 1), shift(relayed[1], axis, SIDE - 1)
    return relayed, [pieces[0], *came, on, back]


def relay_both(pieces, came, scal):
    relayed = run_relay(scal, pieces[3], *came[0], pieces[7], *came[1])
    out = []
    for n, axis in enumerate(("x", "y")):
        on, back = shift(relayed[2 * n], axis, 1), shift(relayed[2 * n + 1], axis, SIDE - 1)
        out += [pieces[4 * n], *came[n], on, back]
    return relayed, out


def trade(value, axis):
    return lax.all_to_all(value, axis, 0, 0)


def after(value, *others):
    return lax.optimization_barrier((value,) + others)[0]


def local(
    block_input, gain_in, w_query, w_key, w_value, w_path, w_beta, w_out,
    gain_mid, w_gate, w_up, w_down, out_grad, lengths,
):
    tokens, width = block_input.shape
    row, col, core = (lax.axis_index(name) for name in CTX)
    rank = lax.axis_index("z")
    start = lax.axis_index(CTX) * tokens
    scal = jnp.stack([start, lengths[0], lengths[1], row, col, core, rank]).astype(jnp.int32)
    unity = (lengths[0] > 0).astype(F32)
    gain_1 = gain_in.reshape(1, width)
    gain_2 = gain_mid.reshape(1, width)
    heads_w = (w_query, w_key, w_value, w_path, w_beta.T)

    h1, q, k, v, w, aux, inv, kp, b, kt, tu = run_a1(scal, block_input, gain_1, *heads_w)
    both = lax.all_gather(tu, "c", axis=0)
    u_c, spread = run_s1(scal, both)
    along_x = trade(spread, "x")
    out_half = lax.dynamic_slice_in_dim(after(w_out, spread), core * (width // 2), width // 2, 1)
    out_mine = lax.all_gather(out_half.astype(F32), "z", axis=0)
    grad_other = swap(after(out_grad, tu))
    h1_other = swap(h1)
    h1_turned = run_turn(scal, after(h1, spread), h1_other)
    grad_turned = run_turn(scal, after(out_grad, spread), grad_other)
    along_x = after(along_x, h1_turned, grad_turned)
    t_x, u_x, spread = run_s2(scal, along_x, swap(along_x))
    along_y = trade(spread, "y")
    c, sc, qt, inside = run_a2(scal, after(q, spread), k, v, w, inv, kp)
    along_y = after(along_y, inside)
    t_y, states = run_s3(scal, along_y, swap(along_y), t_x, u_x, both, u_c)
    states = lax.all_gather(states, "c", axis=0)
    mixed, normed, spread, carried = run_a3(scal, inside, qt, states)
    normed_all = trade(spread, "z")
    out_mine = after(out_mine, spread)
    out_mine_low = (out_mine * unity).astype(BF16)
    out_other_low = (swap(out_mine) * unity).astype(BF16)
    normed_all = after(normed_all, out_mine_low, out_other_low)
    middle, sent, second_part, down_part = run_ffn(
        scal, normed_all, out_mine_low, out_other_low, block_input, gain_2, out_grad,
        w_gate, w_up, w_down,
    )

    second = trade(second_part.reshape(RANKS, PART, width), "z")
    ffn_pieces = list(run_w1(scal, sent, swap(sent), grad_turned))
    second = after(second, *ffn_pieces)
    along_y = send_on(ffn_pieces[4:], "y")
    d_middle, attn, gain_mid_part, d_normed = run_k5(
        scal, second, middle, out_grad, gain_2, out_mine_low, out_other_low
    )
    attn_all = lax.all_gather(attn, "z", axis=0, tiled=True)
    d_normed = trade(d_normed, "z").reshape(tokens, WIDE)
    down_sum = lax.psum(after(down_part, d_normed), "z")
    dm, state_grad = run_b1(scal, d_normed, mixed, qt)
    pair = lax.all_gather(state_grad, "c", axis=0)
    g_1, spread = run_t1(scal, pair, both)
    g_x = trade(spread, "x")
    dq, dk, dv, dw, dkp, xc = run_b2(
        scal, after(dm, spread), carried, q, k, v, w, aux, inv, kp, c, sc
    )
    g_x = after(g_x, dq)
    spread = run_t2(scal, g_x, t_x)
    g_y = trade(spread, "y")
    attn_all = after(attn_all, spread)
    attn_turned = run_turn(scal, attn_all, swap(attn_all))
    ffn_pieces[1] = after(ffn_pieces[1], spread)
    along_x = send_on(ffn_pieces[:4], "x")
    along_y = (after(along_y[0], spread), along_y[1])
    relayed, ffn_two = relay_on(ffn_pieces[4:], along_y, "y", scal)
    g_y = after(g_y, attn_turned, *relayed)
    later = run_t3(scal, g_y, g_x, t_y, t_x, both, g_1)
    later = lax.all_gather(later, "c", axis=0)
    block_output = middle + down_sum

    low = run_b3(scal, later, carried, k, v, w, aux, inv, kp, b, kt, dk, dv, dw, dkp, xc)
    low_other = swap(low)
    along_x = (after(along_x[0], low), along_x[1])
    relayed, ffn_one = relay_on(ffn_pieces[:4], along_x, "x", scal)
    ffn_two[0] = after(ffn_two[0], low)
    ffn_two = run_fold_1(scal, ffn_two)
    low_other = after(low_other, relayed[0], ffn_two)
    ffn_two = lax.psum_scatter(ffn_two, "x", scatter_dimension=0)
    head_pieces = run_w2(
        scal, low, low_other, dq, swap(dq), normed, swap(normed), h1_turned, attn_turned
    )
    came = [send_on(head_pieces[:4], "x"), send_on(head_pieces[4:], "y")]
    first_part = run_b4(
        scal, block_input, gain_mid_part, dq, after(low, head_pieces[0]), *heads_w
    )
    first = trade(first_part, "z")
    ffn_one[0] = after(ffn_one[0], head_pieces[0])
    ffn_one = run_fold_1(scal, ffn_one)
    came[0] = (after(came[0][0], first_part, ffn_one), came[0][1])
    ffn_one = lax.psum_scatter(ffn_one, "y", scatter_dimension=0)
    relayed, head_pieces = relay_both(head_pieces, came, scal)
    input_part, gains = run_n(scal, after(first, relayed[0]), block_input, gain_1, d_middle)
    input_grad = lax.all_gather(input_part, "z", axis=0, tiled=True)
    gains = jnp.swapaxes(gains[:2].reshape(2, 32, width // 32), 0, 1)
    gains = jnp.sum(trade(gains, CTX), axis=0)
    head_pieces[0] = after(head_pieces[0], gains, block_output)
    head_pieces = run_fold_2(scal, head_pieces)
    head_pieces = exchange(head_pieces, "y", "x")
    ffn_two = after(ffn_two, head_pieces[2])
    gate_out, up_out, down_out = run_end_1(scal, ffn_one, ffn_two)
    input_grad = input_grad * unity
    head_pieces[6] = after(head_pieces[6], input_grad)
    key_out, value_out, path_out, beta_out, query_out, out_out = run_end_2(scal, head_pieces)
    return (
        block_output, input_grad, gains[0], query_out, key_out, value_out, path_out,
        beta_out[:, : w_beta.shape[1]], out_out.T, gains[1], gate_out, up_out, down_out.T,
    )


def solution(mesh):
    fine = Mesh(mesh.devices.reshape(SIDE, SIDE, 2, RANKS), ("y", "x", "c", "z"))
    tokens, heads, whole = P(CTX, None), P(None, "z"), P()
    in_specs = (
        tokens, whole, heads, heads, heads, heads, heads, P("z", None),
        whole, heads, heads, P("z", None), tokens, whole,
    )
    weight = P(CTX, "z")
    out_specs = (
        tokens, tokens, P(CTX), weight, weight, weight, weight, weight,
        P("z", CTX), P(CTX), weight, weight, P("z", CTX),
    )
    return jax.shard_map(local, mesh=fine, in_specs=in_specs, out_specs=out_specs, check_vma=False)
```

```python
import jax
import jax.numpy as jnp
from jax import lax
from jax.experimental import pallas as pl
from jax.experimental.pallas import tpu as pltpu
from jax.sharding import Mesh
from jax.sharding import PartitionSpec as P

EPSILON = 1e-06
HEAD_EPSILON = 0.01
F32 = jnp.float32
BF16 = jnp.bfloat16
HEADS = 3
HW = 128
LEN = 256
RANKS = 4
PART = LEN // RANKS
SIDE = 4
CTX = ("y", "x", "c")


def split(value):
    high = value.astype(BF16)
    return high, (value - high.astype(F32)).astype(BF16)


def dg(left, right, ta, tb):
    dims = (((0 if ta else 1,), (1 if tb else 0,)), ((), ()))
    return lax.dot_general(left, right, dims, preferred_element_type=F32)


def mm(left, right, ta=False, tb=False):
    left = left if isinstance(left, tuple) else split(left)
    right = right if isinstance(right, tuple) else split(right)
    return dg(left[0], right[0], ta, tb) + (
        dg(left[0], right[1], ta, tb) + dg(left[1], right[0], ta, tb)
    )


def iota(shape, dim):
    return lax.broadcasted_iota(jnp.int32, shape, dim)


def cols(head):
    return slice(head * HW, (head + 1) * HW)


def segments(spot, scal):
    second = scal[1]
    third = second + scal[2]
    return (spot >= second).astype(jnp.int32) + (spot >= third).astype(jnp.int32)


def small_inverses(scaled):
    row = iota((HW, HW), 0)
    lane = iota((HW, HW), 1)
    same = (row // 8) == (lane // 8)
    packed = []
    for one in scaled:
        for half in range(2):
            block = jnp.where(same, one[half * HW : (half + 1) * HW, half * HW : (half + 1) * HW], 0.0)
            packed.append(jnp.sum(block.reshape(HW // 8, 8, HW), axis=0))
    count = len(packed)
    high, low = split(jnp.concatenate(packed, axis=0))
    lane_8 = iota((8, HW), 1) % 8
    spread = {}
    for k in range(1, 8):
        unit = ((row // 8 == lane // 8) & (row % 8 == k)).astype(BF16)
        both = dg(high, unit, False, False) + dg(low, unit, False, False)
        spread[k] = both.reshape(count, 8, HW)
    rows = {}
    for i in range(7, -1, -1):
        value = jnp.broadcast_to((lane_8[:1] == i).astype(F32)[None], (count, 1, HW))
        for k in range(i + 1, 8):
            value = value - spread[k][:, i : i + 1, :] * rows[k]
        rows[i] = value
    done = jnp.concatenate([rows[i] for i in range(8)], axis=1)
    out = []
    zero = jnp.zeros((HW, HW), F32)
    for head in range(count // 2):
        halves = [
            jnp.where(same, jnp.concatenate([done[2 * head + half]] * (HW // 8), axis=0), 0.0)
            for half in range(2)
        ]
        out.append(
            jnp.concatenate(
                [
                    jnp.concatenate([halves[0], zero], axis=1),
                    jnp.concatenate([zero, halves[1]], axis=1),
                ],
                axis=0,
            )
        )
    return out


def upper_rows(value, width):
    return jnp.concatenate(
        [value[at : at + width] for at in range(0, value.shape[0], 2 * width)], axis=0
    )


def put_upper(value, upper, width):
    pieces = []
    for n, at in enumerate(range(0, value.shape[0], 2 * width)):
        pieces.append(upper[n * width : (n + 1) * width])
        pieces.append(value[at + width : at + 2 * width])
    return jnp.concatenate(pieces, axis=0)


def inverses(scaled):
    out = small_inverses(scaled)
    row = iota((LEN, LEN), 0)
    lane = iota((LEN, LEN), 1)
    width = 8
    while width < LEN:
        pair = (row // (2 * width) == lane // (2 * width)) & (row // width < lane // width)
        link = [upper_rows(jnp.where(pair, one, 0.0), width) for one in scaled]
        parts = [split(one) for one in out]
        first = [mm(a, b) for a, b in zip(link, parts)]
        empty = jnp.zeros((LEN, LEN), F32)
        wide = [put_upper(empty, one, width) for one in first]
        tops = [
            (upper_rows(a, width), upper_rows(b, width)) for a, b in parts
        ]
        second = [mm(a, b) for a, b in zip(tops, wide)]
        out = [
            put_upper(one, upper_rows(one, width) - new, width) for one, new in zip(out, second)
        ]
        width *= 2
    return out


def unit_rows(value):
    scale = lax.rsqrt(jnp.sum(value * value, axis=-1, keepdims=True) + EPSILON)
    return value * scale, scale


def first_norm(x_ref, gain_ref):
    x = x_ref[...]
    scale = lax.rsqrt(jnp.mean(x * x, axis=-1, keepdims=True) + EPSILON)
    return (x * scale * gain_ref[...].astype(F32)).astype(BF16)


def a1_body(
    scal_ref, x_ref, gain_ref, wk_ref, wv_ref, ww_ref, wb_ref,
    k_ref, v_ref, w_ref, aux_ref, inv_ref, kp_ref, b_ref, kt_ref, tu_ref,
):
    h1 = first_norm(x_ref, gain_ref)
    start = scal_ref[0]
    token = iota((LEN, 1), 0) + start
    segment = segments(token, scal_ref)
    end_segment = segments(jnp.full((1, 1), LEN - 1, jnp.int32) + start, scal_ref)
    before = start - 1
    before_segment = jnp.where(start == 0, -1, segments(jnp.full((1, 1), 0, jnp.int32) + before, scal_ref))
    last = (segment == end_segment).astype(F32)
    carry_all = (end_segment == before_segment).astype(F32)
    row = iota((LEN, LEN), 0)
    lane = iota((LEN, LEN), 1)
    later = row < lane
    beta = 1.0 + jax.nn.sigmoid(dg(h1, wb_ref[...], False, True))
    beta_rows = 1.0 + jax.nn.sigmoid(dg(wb_ref[...], h1, False, True))
    pr = dg(h1, ww_ref[...], False, False)
    kr = dg(h1, wk_ref[...], False, False)
    w_all, k_all, aux = [], [], []
    for head in range(HEADS):
        w, w_scale = unit_rows(pr[:, cols(head)])
        k, k_scale = unit_rows(kr[:, cols(head)])
        w_ref[:, cols(head)] = w
        k_ref[:, cols(head)] = k
        w_all.append(w)
        k_all.append(k)
        aux.append((w_scale, k_scale))
    w_split = [split(w) for w in w_all]
    k_split = [split(k) for k in k_all]
    scaled = [
        jnp.where(later, mm(w_split[h], w_split[h], tb=True), 0.0) * beta[:, h : h + 1]
        for h in range(HEADS)
    ]
    inverse = [
        one * beta_rows[h : h + 1, :] for h, one in enumerate(inverses(scaled))
    ]
    vr = dg(h1, wv_ref[...], False, False)
    v_ref[...] = vr
    lane_aux = iota((LEN, HW), 1)
    packed = jnp.zeros((LEN, HW), F32)
    eye = (iota((HW, HW), 0) == iota((HW, HW), 1)).astype(F32)
    for head in range(HEADS):
        spots = (
            (head, beta[:, head : head + 1]),
            (16 + head, aux[head][1]),
            (24 + head, aux[head][0]),
        )
        for at, value in spots:
            packed = jnp.where(lane_aux == at, value, packed)
        inv_ref[head] = inverse[head]
        inv_split = split(inverse[head])
        folded = mm(inv_split, w_split[head])
        b_ref[:, cols(head)] = folded
        folded_split = split(folded)
        kp = jnp.where(later, mm(k_split[head], w_split[head], tb=True), 0.0)
        kp_ref[head] = kp
        kt = k_all[head] - mm(kp, folded_split)
        kt_ref[:, cols(head)] = kt
        tu_ref[0, head] = carry_all * (eye - mm(w_split[head], folded_split, ta=True))
        tu_ref[1, head] = mm(vr[:, cols(head)], kt * last, ta=True)
    aux_ref[...] = packed


def shape(*dims, dtype=F32):
    return jax.ShapeDtypeStruct(dims, dtype)


MIB = 1024 * 1024
SLACK = 10 * MIB
LIGHT = pl.CostEstimate(flops=10**4, bytes_accessed=10**4, transcendentals=0)
HEAVY = pl.CostEstimate(flops=10**12, bytes_accessed=10**8, transcendentals=0)
WORK = pl.CostEstimate(flops=8 * 10**9, bytes_accessed=10**7, transcendentals=0)


def size_of(*arrays):
    total = 0
    for one in arrays:
        count = one.dtype.itemsize
        for extent in one.shape:
            count *= extent
        total += count
    return total


class Late:
    def __init__(self, copy, buffer):
        self.copy, self.buffer, self.shape = copy, buffer, buffer.shape
        copy.start()

    def here(self):
        if self.copy is not None:
            self.copy.wait()
            self.copy = None
        return self.buffer

    def __getitem__(self, spot):
        return self.here()[spot]


class Early:
    def __init__(self, copy, buffer):
        self.copy, self.buffer, self.shape, self.sent = copy, buffer, buffer.shape, False

    def __getitem__(self, spot):
        return self.buffer[spot]

    def __setitem__(self, spot, value):
        self.buffer[spot] = value

    @property
    def at(self):
        return self.buffer.at


def whole_now(*refs):
    for ref in refs:
        if isinstance(ref, Early):
            ref.copy.start()
            ref.sent = True


def call(body, outs, name, scratch=(), late=(), early=(), cost=LIGHT, alone=False):
    def run(*operands):
        count = len(operands)
        moved = sorted(late)
        leaving = sorted(early)
        vmem = pl.BlockSpec(memory_space=pltpu.VMEM)
        anywhere = pl.BlockSpec(memory_space=pl.ANY)
        held = [operands[at] for at in moved] + [outs[at] for at in leaving]
        buffers = [pltpu.VMEM(one.shape, one.dtype) for one in held]
        marks = [pltpu.SemaphoreType.DMA((len(buffers),))] if buffers else []

        def wrapped(*refs):
            refs = list(refs)
            own = len(refs) - len(buffers) - len(marks)
            for n, at in enumerate(moved):
                copy = pltpu.make_async_copy(refs[at], refs[own + n], refs[-1].at[n])
                refs[at] = Late(copy, refs[own + n])
            for n, at in enumerate(leaving, len(moved)):
                copy = pltpu.make_async_copy(refs[own + n], refs[count + at], refs[-1].at[n])
                refs[count + at] = Early(copy, refs[own + n])
            body(*refs[:own])
            for at in moved:
                refs[at].here()
            for at in leaving:
                if not refs[count + at].sent:
                    refs[count + at].copy.start()
            for at in leaving:
                refs[count + at].copy.wait()

        need = size_of(*operands, *outs, *scratch) + SLACK
        return pl.pallas_call(
            wrapped,
            out_shape=outs,
            in_specs=[pl.BlockSpec(memory_space=pltpu.SMEM)]
            + [anywhere if at in moved else vmem for at in range(1, count)],
            out_specs=[anywhere if at in leaving else vmem for at in range(len(outs))],
            scratch_shapes=list(scratch) + buffers + marks,
            name=name,
            cost_estimate=cost,
            compiler_params=pltpu.CompilerParams(vmem_limit_bytes=56 * MIB if alone else need),
        )(*operands)

    return run


WIDE = HEADS * HW


def run_a1(*operands):
    outs = [
        shape(LEN, WIDE), shape(LEN, WIDE), shape(LEN, WIDE),
        shape(LEN, HW),
        shape(HEADS, LEN, LEN), shape(HEADS, LEN, LEN),
        shape(LEN, WIDE), shape(LEN, WIDE),
        shape(2, HEADS, HW, HW),
    ]
    return call(a1_body, outs, "local_parts", alone=True)(*operands)


def a2_body(
    scal_ref, x_ref, gain_ref, wq_ref, k_ref, v_ref, w_ref, inv_ref, kp_ref,
    q_ref, aux_ref, c_ref, sc_ref, qt_ref, in_ref,
):
    start = scal_ref[0]
    segment = segments(iota((LEN, LEN), 0) + start, scal_ref)
    segment_t = segments(iota((LEN, LEN), 1) + start, scal_ref)
    row = iota((LEN, LEN), 0)
    lane = iota((LEN, LEN), 1)
    up_to = row <= lane
    seen = up_to & (segment == segment_t)
    qr = dg(first_norm(x_ref, gain_ref), wq_ref[...], False, False)
    lane_aux = iota((LEN, HW), 1)
    packed = jnp.zeros((LEN, HW), F32)
    for head in range(HEADS):
        q, q_scale = unit_rows(qr[:, cols(head)])
        q_ref[:, cols(head)] = q
        packed = jnp.where(lane_aux == head, q_scale, packed)
        q_split = split(q)
        w_split = split(w_ref[:, cols(head)])
        pq = jnp.where(up_to, mm(w_split, q_split, tb=True), 0.0)
        c = mm(inv_ref[head], pq)
        c_ref[head] = c
        c_split = split(c)
        qt_ref[:, cols(head)] = q - mm(c_split, w_split, ta=True)
        scores = mm(k_ref[:, cols(head)], q_split, tb=True) - mm(kp_ref[head], c_split)
        scores = jnp.where(seen, scores, 0.0)
        sc_ref[head] = scores
        in_ref[:, cols(head)] = mm(scores, v_ref[:, cols(head)], ta=True)
    aux_ref[...] = packed


def run_a2(*operands):
    outs = [
        shape(LEN, WIDE), shape(LEN, HW),
        shape(HEADS, LEN, LEN), shape(HEADS, LEN, LEN), shape(LEN, WIDE), shape(LEN, WIDE),
    ]
    return call(a2_body, outs, "inside_parts", alone=True, cost=WORK)(*operands)


def carry_of(start, scal_ref):
    token = iota((LEN, 1), 0) + start
    before = jnp.full((1, 1), 0, jnp.int32) + (start - 1)
    before_segment = jnp.where(start == 0, -1, segments(before, scal_ref))
    return (segments(token, scal_ref) == before_segment).astype(F32)


def pair_of(ref, core, head):
    return jnp.concatenate([ref[0, core, head], ref[1, core, head]], axis=0)


def b1_body(scal_ref, dn_ref, mixed_ref, qt_ref, dm_ref, sg_ref):
    carry = carry_of(scal_ref[0], scal_ref)
    for head in range(HEADS):
        mixed = mixed_ref[:, cols(head)]
        dn = dn_ref[:, cols(head)]
        scale = lax.rsqrt(jnp.mean(mixed * mixed, axis=-1, keepdims=True) + HEAD_EPSILON)
        drift = jnp.mean(dn * mixed, axis=-1, keepdims=True) * (scale * scale)
        dm = scale * (dn - mixed * drift)
        dm_ref[:, cols(head)] = dm
        sg_ref[head] = mm(dm * carry, qt_ref[:, cols(head)], ta=True)


def run_b1(*operands):
    outs = [shape(LEN, WIDE), shape(HEADS, HW, HW)]
    return call(b1_body, outs, "state_gradient")(*operands)


def unit_pull(unit, scale, grad):
    return scale * (grad - unit * jnp.sum(unit * grad, axis=-1, keepdims=True))


def b2_body(
    scal_ref, dm_ref, carried_ref, q_ref, k_ref, v_ref, w_ref, aux_ref, inv_ref, kp_ref,
    c_ref, sc_ref,
    dq_ref, dk_ref, dv_ref, dw_ref, dkp_ref, xc_ref,
):
    start = scal_ref[0]
    carry = carry_of(start, scal_ref)
    row = iota((LEN, LEN), 0)
    lane = iota((LEN, LEN), 1)
    up_to = row <= lane
    seen = up_to & (
        segments(row + start, scal_ref) == segments(lane + start, scal_ref)
    )
    for head in range(HEADS):
        q = q_ref[:, cols(head)]
        q_split = split(q)
        w_split = split(w_ref[:, cols(head)])
        k_split = split(k_ref[:, cols(head)])
        c_split = split(c_ref[head])
        kp_split = split(kp_ref[head])
        dm = dm_ref[:, cols(head)]
        dm_split = split(dm)
        dqt = mm(dm * carry, carried_ref[head])
        dqt_split = split(dqt)
        ds = jnp.where(seen, mm(v_ref[:, cols(head)], dm_split, tb=True), 0.0)
        ds_split = split(ds)
        dv_ref[:, cols(head)] = mm(sc_ref[head], dm_split)
        dk = mm(ds_split, q_split)
        dq = dqt + mm(ds_split, k_split, ta=True)
        dkp_ref[head] = mm(ds_split, c_split, tb=True)
        dc = mm(kp_split, ds_split, ta=True) + mm(w_split, dqt_split, tb=True)
        dw = mm(c_split, dqt_split)
        x = mm(inv_ref[head], dc, ta=True)
        xc_ref[head] = mm(x, c_split, tb=True)
        dpq_split = split(jnp.where(up_to, x, 0.0))
        dw_ref[:, cols(head)] = dw + mm(dpq_split, q_split)
        dq = dq - mm(dpq_split, w_split, ta=True)
        dk_ref[:, cols(head)] = dk
        scale = aux_ref[:, head : head + 1]
        dq_ref[:, cols(head)] = unit_pull(q, scale, dq).astype(BF16).astype(F32)


def run_b2(*operands):
    outs = [
        shape(LEN, WIDE), shape(LEN, WIDE), shape(LEN, WIDE), shape(LEN, WIDE),
        shape(HEADS, LEN, LEN), shape(HEADS, LEN, LEN),
    ]
    return call(b2_body, outs, "inside_gradients", alone=True, cost=WORK)(*operands)


def b3_body(
    scal_ref, states_ref, carried_ref, k_ref, v_ref, w_ref, aux_ref,
    inv_ref, kp_ref, b_ref, kt_ref, dk_ref, dv_ref, dw_ref, dkp_ref, xc_ref,
    low_ref,
):
    start = scal_ref[0]
    core = scal_ref[5]
    segment = segments(iota((LEN, 1), 0) + start, scal_ref)
    end_segment = segments(jnp.full((1, 1), LEN - 1, jnp.int32) + start, scal_ref)
    before = jnp.full((1, 1), 0, jnp.int32) + (start - 1)
    before_segment = jnp.where(start == 0, -1, segments(before, scal_ref))
    last = (segment == end_segment).astype(F32)
    carry_all = (end_segment == before_segment).astype(F32)
    row = iota((LEN, LEN), 0)
    lane = iota((LEN, LEN), 1)
    later_mask = row < lane
    lane_aux = iota((LEN, HW), 1)
    d_beta = jnp.zeros((LEN, HW), F32)
    for head in range(HEADS):
        later = pair_of(states_ref, core, head)
        later_split = split(later)
        dt_split = split(carry_all * mm(carried_ref[head], later_split, ta=True))
        w = w_ref[:, cols(head)]
        w_split = split(w)
        k = k_ref[:, cols(head)]
        v = v_ref[:, cols(head)]
        b_split = split(b_ref[:, cols(head)])
        kp_split = split(kp_ref[head])
        dv = dv_ref[:, cols(head)] + last * mm(kt_ref[:, cols(head)], later_split, tb=True)
        dkt = last * mm(v, later_split)
        dkt_split = split(dkt)
        db = mm(w_split, dt_split) + mm(kp_split, dkt_split, ta=True)
        y = mm(inv_ref[head], db, ta=True)
        y_split = split(y)
        dw = dw_ref[:, cols(head)] + mm(b_split, dt_split, tb=True) + y
        dkp = jnp.where(later_mask, dkp_ref[head] + mm(dkt_split, b_split, tb=True), 0.0)
        dkp_split = split(dkp)
        dk = dk_ref[:, cols(head)] + dkt - mm(dkp_split, w_split)
        dw = dw + mm(dkp_split, split(k), ta=True)
        dm = xc_ref[head] + mm(y_split, b_split, tb=True)
        dn_split = split(jnp.where(later_mask, dm, 0.0))
        dw = mm(dn_split, w_split) + mm(dn_split, w_split, ta=True) - dw
        diagonal = jnp.sum(jnp.where(row == lane, dm, 0.0), axis=-1, keepdims=True)
        beta = aux_ref[:, head : head + 1]
        sig = beta - 1.0
        dbl = -diagonal / (beta * beta) * sig * (1.0 - sig)
        d_beta = jnp.where(lane_aux == head, dbl, d_beta)
        low_ref[:, cols(head)] = unit_pull(k, aux_ref[:, 16 + head : 17 + head], dk).astype(BF16).astype(F32)
        low_ref[:, WIDE + head * HW : WIDE + (head + 1) * HW] = dv.astype(BF16).astype(F32)
        low_ref[:, 2 * WIDE + head * HW : 2 * WIDE + (head + 1) * HW] = unit_pull(
            w, aux_ref[:, 24 + head : 25 + head], dw
        ).astype(BF16).astype(F32)
    low_ref[:, 3 * WIDE :] = d_beta.astype(BF16).astype(F32)


def run_b3(*operands):
    outs = [shape(LEN, 3 * WIDE + HW)]
    return call(b3_body, outs, "late_gradients", alone=True)(*operands)[0]


def b4_body(
    scal_ref, x_ref, gain_mid_ref, dq_ref, low_ref, wq_ref, wk_ref, wv_ref, ww_ref, wb_ref, dh_ref
):
    total = dg(dq_ref[...].astype(BF16), wq_ref[...], False, True)
    for at, ref in enumerate((wk_ref, wv_ref, ww_ref)):
        low = low_ref[:, at * WIDE : at * WIDE + ref.shape[1]].astype(BF16)
        total = total + dg(low, ref[...], False, True)
    beta_cols = wb_ref[...].astype(F32)
    for head in range(HEADS):
        at = 3 * WIDE + head
        total = total + low_ref[:, at : at + 1] * beta_cols[head : head + 1, :]
    for at in range(RANKS):
        dh_ref[at, :PART, :] = total[at * PART : (at + 1) * PART]
    x = x_ref[...]
    scale = lax.rsqrt(jnp.mean(x * x, axis=-1, keepdims=True) + EPSILON)
    gain_in = jnp.sum(total * x * scale, axis=0, keepdims=True)
    rows = iota((8, x.shape[1]), 0)
    both = jnp.where(rows == 0, gain_in, jnp.where(rows == 1, gain_mid_ref[...], 0.0))
    for at in range(RANKS):
        dh_ref[at, PART:, :] = both


def run_b4(*operands):
    outs = [shape(RANKS, PART + 8, operands[1].shape[1])]
    return call(b4_body, outs, "first_norm_part", alone=True)(*operands)[0]


def half_of(core):
    return pl.ds(pl.multiple_of(core * (HW // 2), HW // 2), HW // 2)


def s1_body(scal_ref, both_ref, out_ref):
    rows = half_of(scal_ref[5])
    for head in range(HEADS):
        t_1 = split(both_ref[1, 0, head])
        u_0 = both_ref[0, 1, head, rows, :]
        u_1 = both_ref[1, 1, head, rows, :]
        chip_t = mm(both_ref[0, 0, head, rows, :], t_1)
        chip_u = mm(u_0, t_1) + u_1
        for at in range(SIDE):
            out_ref[at, 0, head] = chip_t
            out_ref[at, 1, head] = chip_u


def run_s1(*operands):
    outs = [shape(SIDE, 2, HEADS, HW // 2, HW)]
    return call(s1_body, outs, "chip_state")(*operands)[0]


def join_halves(out_ref, mine_ref, other_ref, core, at, which, head):
    out_ref[at, head, half_of(core), :] = mine_ref[at, which, head]
    out_ref[at, head, half_of(1 - core), :] = other_ref[at, which, head]


def s2_body(scal_ref, mine_ref, other_ref, t_ref, u_ref, out_ref):
    core = scal_ref[5]
    rows = half_of(core)
    for head in range(HEADS):
        for at in range(SIDE):
            join_halves(t_ref, mine_ref, other_ref, core, at, 0, head)
            join_halves(u_ref, mine_ref, other_ref, core, at, 1, head)
    for head in range(HEADS):
        t_1 = split(t_ref[1, head])
        t_3 = split(t_ref[3, head])
        t_23 = split(mm(t_ref[2, head], t_3))
        row_t = mm(mm(t_ref[0, head, rows, :], t_1), t_23)
        u = [mine_ref[at, 1, head] for at in range(SIDE)]
        row_u = mm(mm(u[0], t_1) + u[1], t_23) + mm(u[2], t_3) + u[3]
        for at in range(SIDE):
            out_ref[at, 0, head] = row_t
            out_ref[at, 1, head] = row_u


def run_s2(*operands):
    outs = [
        shape(SIDE, HEADS, HW, HW),
        shape(SIDE, HEADS, HW, HW),
        shape(SIDE, 2, HEADS, HW // 2, HW),
    ]
    return call(s2_body, outs, "row_state")(*operands)


def s3_body(
    scal_ref, mine_ref, other_ref, tx_ref, ux_ref, both_ref, in_ref, qt_ref,
    ty_ref, mixed_ref, normed_ref, spread_ref, carried_ref, uy_ref,
):
    row, col, core = scal_ref[3], scal_ref[4], scal_ref[5]
    carry = carry_of(scal_ref[0], scal_ref)
    for head in range(HEADS):
        for at in range(SIDE):
            join_halves(ty_ref, mine_ref, other_ref, core, at, 0, head)
        for at in range(SIDE - 1):
            join_halves(uy_ref, mine_ref, other_ref, core, at, 1, head)
    for head in range(HEADS):
        state = jnp.where(row > 0, uy_ref[0, head], 0.0)
        for at in range(1, SIDE - 1):
            new = mm(state, ty_ref[at, head]) + uy_ref[at, head]
            state = jnp.where(at < row, new, state)
        for at in range(SIDE - 1):
            new = mm(state, tx_ref[at, head]) + ux_ref[at, head]
            state = jnp.where(at < col, new, state)
        new = mm(state, both_ref[0, 0, head]) + both_ref[0, 1, head]
        state = jnp.where(core > 0, new, state)
        carried_ref[head] = state
        mixed = in_ref[:, cols(head)] + carry * mm(qt_ref[:, cols(head)], state, tb=True)
        mixed_ref[:, cols(head)] = mixed
        scale = lax.rsqrt(jnp.mean(mixed * mixed, axis=-1, keepdims=True) + HEAD_EPSILON)
        low = (mixed * scale).astype(BF16).astype(F32)
        normed_ref[:, cols(head)] = low
        for at in range(RANKS):
            spread_ref[at, :, cols(head)] = low


def run_s3(*operands):
    outs = [
        shape(SIDE, HEADS, HW, HW), shape(LEN, WIDE), shape(LEN, WIDE), shape(RANKS, LEN, WIDE),
        shape(HEADS, HW, HW),
    ]
    scratch = [pltpu.VMEM((SIDE - 1, HEADS, HW, HW), F32)]
    return call(s3_body, outs, "normed_heads", scratch, alone=True)(*operands)


def t1_body(scal_ref, pair_ref, both_ref, g_ref, out_ref):
    rows = half_of(scal_ref[5])
    for head in range(HEADS):
        g_1 = pair_ref[1, head, rows, :]
        g_ref[head] = g_1
        chip = mm(g_1, both_ref[0, 0, head], tb=True) + pair_ref[0, head, rows, :]
        for at in range(SIDE):
            out_ref[at, head] = chip


def run_t1(*operands):
    outs = [shape(HEADS, HW // 2, HW), shape(SIDE, HEADS, HW // 2, HW)]
    return call(t1_body, outs, "chip_gradient")(*operands)


def t2_body(scal_ref, g_ref, t_ref, out_ref):
    for head in range(HEADS):
        total = g_ref[3, head]
        for at in (2, 1, 0):
            total = mm(total, t_ref[at, head], tb=True) + g_ref[at, head]
        for at in range(SIDE):
            out_ref[at, head] = total


def run_t2(*operands):
    outs = [shape(SIDE, HEADS, HW // 2, HW)]
    return call(t2_body, outs, "row_gradient")(*operands)[0]


def t3_body(scal_ref, gy_ref, gx_ref, ty_ref, tx_ref, both_ref, g_ref, out_ref):
    row, col = scal_ref[3], scal_ref[4]
    for head in range(HEADS):
        later = jnp.where(row < SIDE - 1, gy_ref[3, head], 0.0)
        for at in (2, 1):
            new = mm(later, ty_ref[at, head], tb=True) + gy_ref[at, head]
            later = jnp.where(at > row, new, later)
        for at in (3, 2, 1):
            new = mm(later, tx_ref[at, head], tb=True) + gx_ref[at, head]
            later = jnp.where(at > col, new, later)
        out_ref[1, head] = later
        out_ref[0, head] = mm(later, both_ref[1, 0, head], tb=True) + g_ref[head]


def run_t3(*operands):
    outs = [shape(2, HEADS, HW // 2, HW)]
    return call(t3_body, outs, "block_gradient")(*operands)[0]


def ffn_body(
    scal_ref, normed_ref, out_mine_ref, out_other_ref, x_ref, gain_ref, grad_ref,
    gate_ref, up_ref, down_ref,
    middle_ref, sent_ref, dh_ref, down_part_ref,
):
    core = scal_ref[5]
    half = x_ref.shape[1] // 2
    units = gate_ref.shape[1]
    low = [normed_ref[rank].astype(BF16) for rank in range(RANKS)]
    for ref, at in ((out_mine_ref, core), (out_other_ref, 1 - core)):
        spot = pl.ds(pl.multiple_of(at * half, half), half)
        total = x_ref[:, spot]
        for rank in range(RANKS):
            total = total + dg(low[rank], ref[rank], False, False)
        middle_ref[:, spot] = total
    middle = middle_ref[...]
    scale = lax.rsqrt(jnp.mean(middle * middle, axis=-1, keepdims=True) + EPSILON)
    h2 = (middle * scale * gain_ref[...].astype(F32)).astype(BF16)
    sent_ref[:, 3 * units :] = h2.astype(F32)
    gate = dg(h2, gate_ref[...], False, False)
    up = dg(h2, up_ref[...], False, False)
    sig = jax.nn.sigmoid(gate)
    silu = gate * sig
    hidden = (silu * up).astype(BF16)
    sent_ref[:, 2 * units : 3 * units] = hidden.astype(F32)
    d_hidden = dg(grad_ref[...].astype(BF16), down_ref[...], False, True)
    d_gate = (d_hidden * up * sig * (1.0 + gate * (1.0 - sig))).astype(BF16)
    sent_ref[:, :units] = d_gate.astype(F32)
    d_up = (d_hidden * silu).astype(BF16)
    sent_ref[:, units : 2 * units] = d_up.astype(F32)
    whole_now(middle_ref, sent_ref)
    dh_ref[...] = dg(d_gate, gate_ref[...], False, True) + dg(d_up, up_ref[...], False, True)
    whole_now(dh_ref)
    down_part_ref[...] = dg(hidden, down_ref[...], False, False)


def run_ffn(*operands):
    tokens, width = operands[4].shape
    units = operands[7].shape[1]
    outs = [
        shape(tokens, width), shape(tokens, 3 * units + width), shape(tokens, width), shape(tokens, width)
    ]
    return call(ffn_body, outs, "feed_forward", alone=True, late=(6, 7, 8, 9))(*operands)


def norm_pull(grad, values, gain):
    scale = lax.rsqrt(jnp.mean(values * values, axis=-1, keepdims=True) + EPSILON)
    turned = gain * grad
    drift = jnp.mean(turned * values, axis=-1, keepdims=True) * (scale * scale * scale)
    return scale * turned - values * drift, grad * values * scale


def k5_body(
    scal_ref, second_ref, middle_ref, grad_ref, gain_ref, out_mine_ref, out_other_ref,
    d_middle_ref, attn_ref, gain_out_ref, normed_ref,
):
    core = scal_ref[5]
    rows = pl.ds(pl.multiple_of(scal_ref[6] * PART, PART), PART)
    second = second_ref[0] + second_ref[1] + second_ref[2] + second_ref[3]
    pulled, summed = norm_pull(second, middle_ref[rows, :], gain_ref[...].astype(F32))
    d_middle = grad_ref[rows, :] + pulled
    d_middle_ref[...] = d_middle
    gain_out_ref[...] = jnp.sum(summed, axis=0, keepdims=True)
    attn_ref[...] = d_middle.astype(BF16).astype(F32)
    half = d_middle.shape[1] // 2
    mine = attn_ref[:, pl.ds(pl.multiple_of(core * half, half), half)].astype(BF16)
    other = attn_ref[:, pl.ds(pl.multiple_of((1 - core) * half, half), half)].astype(BF16)
    for rank in range(RANKS):
        normed_ref[rank] = dg(mine, out_mine_ref[rank], False, True) + dg(
            other, out_other_ref[rank], False, True
        )


def run_k5(*operands):
    width = operands[2].shape[1]
    outs = [shape(PART, width), shape(PART, width), shape(1, width), shape(RANKS, PART, WIDE)]
    return call(k5_body, outs, "middle_gradient", alone=True)(*operands)


def n_body(scal_ref, first_ref, x_ref, gain_ref, d_middle_ref, out_ref, gains_ref):
    rows = pl.ds(pl.multiple_of(scal_ref[6] * PART, PART), PART)
    total = first_ref[0] + first_ref[1] + first_ref[2] + first_ref[3]
    pulled, _ = norm_pull(total[:PART], x_ref[rows, :], gain_ref[...].astype(F32))
    out_ref[...] = d_middle_ref[...] + pulled
    gains_ref[...] = total[PART:]


def run_n(*operands):
    width = operands[2].shape[1]
    outs = [shape(PART, width), shape(8, width)]
    return call(n_body, outs, "input_gradient", alone=True)(*operands)


def turn_body(scal_ref, mine_ref, other_ref, out_ref):
    tokens, width = mine_ref.shape
    for n, ref in enumerate((mine_ref, other_ref)):
        for at in range(0, width, 256):
            block = ref[:, at : at + 256].T.astype(BF16)
            out_ref[at : at + 256, n * tokens : (n + 1) * tokens] = block


def turn_norm_body(scal_ref, mine_ref, other_ref, gain_ref, out_ref):
    tokens, width = mine_ref.shape
    for n, ref in enumerate((mine_ref, other_ref)):
        h1 = first_norm(ref, gain_ref).astype(F32)
        for at in range(0, width, 256):
            block = h1[:, at : at + 256].T.astype(BF16)
            out_ref[at : at + 256, n * tokens : (n + 1) * tokens] = block


def run_turn_norm(scal, mine, other, gain):
    tokens, width = mine.shape
    outs = [shape(width, 2 * tokens, dtype=BF16)]
    return call(turn_norm_body, outs, "norm_turned", cost=WORK, alone=True)(scal, mine, other, gain)[0]


def run_turn(scal, mine, other):
    tokens, width = mine.shape
    outs = [shape(width, 2 * tokens, dtype=BF16)]
    return call(turn_body, outs, "turned", alone=True, cost=WORK)(scal, mine, other)[0]


def parts_of(turned_ref, scal_ref, along_x, step):
    row, col, core = scal_ref[3], scal_ref[4], scal_ref[5]
    rows = turned_ref.shape[0] // (2 * SIDE * SIDE)
    pieces = []
    for at in range(SIDE):
        if along_x:
            place = (at * SIDE + lax.rem(col + step, SIDE)) * 2 + core
        else:
            place = (lax.rem(row + step, SIDE) * SIDE + at) * 2 + core
        pieces.append(turned_ref[pl.ds(pl.multiple_of(place * rows, rows), rows), :])
    return jnp.concatenate(pieces, axis=0)


def put(ref, value, start):
    rows = value.shape[0] // SIDE
    for at in range(SIDE):
        ref[at, :, start : start + value.shape[1]] = value[at * rows : (at + 1) * rows]


def send_parts(outs, along_x, scal_ref, products):
    keep_ref, on_ref, back_ref, held_ref = outs
    half = keep_ref.shape[2] // 2
    low_to = {1: held_ref.at[0], 2: on_ref.at[1], 3: back_ref.at[0]}
    high_to = {1: on_ref.at[0], 2: back_ref.at[1], 3: held_ref.at[1]}
    for step in range(SIDE):
        for turned_ref, columns, first in products:
            value = dg(parts_of(turned_ref, scal_ref, along_x, step), columns, False, False)
            last = first + columns.shape[1]
            if step == 0:
                put(keep_ref, value, first)
                continue
            if first < half:
                stop = min(last, half)
                put(low_to[step], value[:, : stop - first], first)
            if last > half:
                begin = max(first, half)
                put(high_to[step], value[:, begin - first :], begin - half)


def part_shapes(rows, *widths):
    outs = []
    for wide in widths:
        outs += [shape(SIDE, rows, wide)] + [shape(2, SIDE, rows, wide // 2)] * 3
    return outs


def w1_body(scal_ref, mine_ref, other_ref, d_ref, *rest):
    outs, (cols_ref, h_ref) = rest[:8], rest[8:]
    tokens = mine_ref.shape[0]
    wide = cols_ref.shape[1]
    cut = wide // 2
    up_end = 2 * (wide // 3)
    for n, ref in enumerate((mine_ref, other_ref)):
        spot = slice(n * tokens, (n + 1) * tokens)
        cols_ref[spot, :] = ref[:, :wide].astype(BF16)
        for at in range(0, h_ref.shape[0], 256):
            h_ref[at : at + 256, spot] = ref[:, wide + at : wide + at + 256].T.astype(BF16)
    send_parts(outs[:4], True, scal_ref, [(h_ref, cols_ref[:, :cut], 0)])
    whole_now(*outs[:4])
    send_parts(
        outs[4:],
        False,
        scal_ref,
        [(h_ref, cols_ref[:, cut:up_end], 0), (d_ref, cols_ref[:, up_end:], up_end - cut)],
    )
    whole_now(*outs[4:])


def run_w1(*operands):
    width = operands[3].shape[0]
    tokens, wide = operands[1].shape
    wide = wide - width
    scratch = [pltpu.VMEM((2 * tokens, wide), BF16), pltpu.VMEM((width, 2 * tokens), BF16)]
    return call(
        w1_body, part_shapes(width // 32, wide // 2, wide // 2), "ffn_weight_sums", scratch,
        late=(2, 3), early=range(8), cost=WORK, alone=True
    )(*operands)


def w2_body(
    scal_ref, low_ref, low_other_ref, dq_ref, dq_other_ref, n_ref, n_other_ref, h_ref, d_ref, *rest
):
    outs, cols_ref = rest[:8], rest[8]
    tokens, late = low_ref.shape
    cut = outs[0].shape[2]
    query_end = late + WIDE
    sides = ((low_ref, dq_ref, n_ref), (low_other_ref, dq_other_ref, n_other_ref))
    for n, (low, dq, normed) in enumerate(sides):
        spot = slice(n * tokens, (n + 1) * tokens)
        cols_ref[spot, :late] = low[...].astype(BF16)
        cols_ref[spot, late:query_end] = dq[...].astype(BF16)
        cols_ref[spot, query_end:] = normed[...].astype(BF16)
    send_parts(outs[:4], True, scal_ref, [(h_ref, cols_ref[:, :cut], 0)])
    whole_now(*outs[:4])
    send_parts(
        outs[4:],
        False,
        scal_ref,
        [(h_ref, cols_ref[:, cut:query_end], 0), (d_ref, cols_ref[:, query_end:], query_end - cut)],
    )


def run_w2(*operands):
    tokens, late = operands[1].shape
    width = operands[7].shape[0]
    wide = late + 2 * WIDE
    scratch = [pltpu.VMEM((2 * tokens, wide), BF16)]
    return call(
        w2_body, part_shapes(width // 32, 2 * WIDE, wide - 2 * WIDE), "head_weight_sums", scratch, late=(7, 8), early=range(8), alone=True
    )(*operands)


def relay_body(scal_ref, *refs):
    count = len(refs) // 5
    ins, outs = refs[: 3 * count], refs[3 * count :]
    for n in range(count):
        held_ref, on_ref, back_ref = ins[3 * n : 3 * n + 3]
        outs[2 * n][...] = held_ref[0] + on_ref[1]
        outs[2 * n + 1][...] = held_ref[1] + back_ref[1]


def run_relay(scal, *pieces):
    outs = [shape(*one.shape[1:]) for one in pieces[::3] for _ in range(2)]
    return call(relay_body, outs, "relay_sums", cost=WORK, alone=True)(scal, *pieces)


def folded(refs, at):
    keep_ref, on_ref, back_ref, on_2_ref, back_2_ref = refs
    half = keep_ref.shape[2] // 2
    low = keep_ref[at, :, :half] + on_2_ref[at] + back_ref[0, at]
    high = keep_ref[at, :, half:] + on_ref[0, at] + back_2_ref[at]
    return low, high


def fold_1_body(scal_ref, *refs):
    target = refs[5]
    half = target.shape[2] // 2
    for at in range(SIDE):
        low, high = folded(refs[:5], at)
        target[at, :, :half] = low
        target[at, :, half:] = high


def run_fold_1(scal, pieces):
    outs = [shape(*pieces[0].shape)]
    return call(fold_1_body, outs, "fold_sums", cost=LIGHT, alone=True)(scal, *pieces)[0]


def fold_2_body(scal_ref, *refs):
    outs = refs[10:]
    for n in range(2):
        for step in range(SIDE):
            target = outs[SIDE * n + step]
            half = target.shape[1] // 2
            low, high = folded(refs[5 * n : 5 * n + 5], lax.rem(scal_ref[3 + n] + step, SIDE))
            target[:, :half] = low
            target[:, half:] = high


def run_fold_2(scal, pieces):
    outs = [shape(*pieces[at].shape[1:]) for at in (0, 5) for _ in range(SIDE)]
    return call(fold_2_body, outs, "fold_parts", cost=HEAVY, alone=True)(scal, *pieces)


def end_1_body(scal_ref, one_ref, two_ref, gate_ref, up_ref, down_ref):
    units = gate_ref.shape[1]
    rest = one_ref.shape[1] - units
    gate_ref[...] = one_ref[:, :units]
    up_ref[:, :rest] = one_ref[:, units:]
    up_ref[:, rest:] = two_ref[:, : units - rest]
    down_ref[...] = two_ref[:, units - rest :]


def run_end_1(scal, one, two):
    rows, wide = one.shape
    outs = [shape(rows, 2 * wide // 3)] * 3
    return call(end_1_body, outs, "ffn_gradients")(scal, one, two)


def end_2_body(scal_ref, *refs):
    first, second, outs = refs[:4], refs[4:8], refs[8:]
    key_ref, value_ref, path_ref, beta_ref, query_ref, out_ref = outs
    one = (first[0][...] + first[1][...]) + (first[2][...] + first[3][...])
    two = (second[0][...] + second[1][...]) + (second[2][...] + second[3][...])
    key_ref[...] = one[:, :WIDE]
    value_ref[...] = one[:, WIDE:]
    path_ref[...] = two[:, :WIDE]
    beta_ref[...] = two[:, WIDE : WIDE + HW]
    query_ref[...] = two[:, WIDE + HW : 2 * WIDE + HW]
    out_ref[...] = two[:, 2 * WIDE + HW :]


def run_end_2(scal, pieces):
    rows = pieces[0].shape[0]
    outs = [shape(rows, WIDE)] * 3 + [shape(rows, HW)] + [shape(rows, WIDE)] * 2
    return call(end_2_body, outs, "head_gradients")(scal, *pieces)


def swap(value):
    return lax.ppermute(value, "c", [(0, 1), (1, 0)])


def shift(value, axis, step):
    return lax.ppermute(value, axis, [(i, (i + step) % SIDE) for i in range(SIDE)])


def exchange(pieces, first_axis, second_axis):
    moved = {}
    for step in (2, 1, 3):
        moved[step] = shift(pieces[step], first_axis, step)
        moved[4 + step] = shift(pieces[4 + step], second_axis, step)
    return [pieces[0], moved[1], moved[2], moved[3], pieces[4], moved[5], moved[6], moved[7]]


def send_on(pieces, axis):
    return shift(pieces[1], axis, 1), shift(pieces[2], axis, SIDE - 1)


def relay_on(pieces, came, axis, scal):
    relayed = run_relay(scal, pieces[3], *came)
    on, back = shift(relayed[0], axis, 1), shift(relayed[1], axis, SIDE - 1)
    return relayed, [pieces[0], *came, on, back]


def relay_both(pieces, came, scal):
    relayed = run_relay(scal, pieces[3], *came[0], pieces[7], *came[1])
    out = []
    for n, axis in enumerate(("x", "y")):
        on, back = shift(relayed[2 * n], axis, 1), shift(relayed[2 * n + 1], axis, SIDE - 1)
        out += [pieces[4 * n], *came[n], on, back]
    return relayed, out


def trade(value, axis):
    return lax.all_to_all(value, axis, 0, 0)


def after(value, *others):
    return lax.optimization_barrier((value,) + others)[0]


def local(
    block_input, gain_in, w_query, w_key, w_value, w_path, w_beta, w_out,
    gain_mid, w_gate, w_up, w_down, out_grad, lengths,
):
    tokens, width = block_input.shape
    row, col, core = (lax.axis_index(name) for name in CTX)
    rank = lax.axis_index("z")
    start = lax.axis_index(CTX) * tokens
    scal = jnp.stack([start, lengths[0], lengths[1], row, col, core, rank]).astype(jnp.int32)
    unity = (lengths[0] > 0).astype(F32)
    gain_1 = gain_in.reshape(1, width)
    gain_2 = gain_mid.reshape(1, width)
    heads_w = (w_query, w_key, w_value, w_path, w_beta.T)

    k, v, w, aux, inv, kp, b, kt, tu = run_a1(scal, block_input, gain_1, *heads_w[1:])
    both = lax.all_gather(tu, "c", axis=0)
    spread = run_s1(scal, both)
    along_x = trade(spread, "x")
    out_half = lax.dynamic_slice_in_dim(after(w_out, both), core * (width // 2), width // 2, 1)
    out_mine = lax.all_gather(out_half.astype(F32), "z", axis=0)
    grad_other = swap(after(out_grad, tu))
    input_other = swap(after(block_input, tu))
    h1_turned = run_turn_norm(scal, after(block_input, spread), input_other, gain_1)
    grad_turned = run_turn(scal, after(out_grad, spread), grad_other)
    along_x = after(along_x, h1_turned, grad_turned)
    t_x, u_x, spread = run_s2(scal, along_x, swap(along_x))
    along_y = trade(spread, "y")
    q, aux_q, c, sc, qt, inside = run_a2(
        scal, block_input, gain_1, w_query, after(k, spread), v, w, inv, kp
    )
    along_y = after(along_y, inside)
    t_y, mixed, normed, spread, carried = run_s3(
        scal, along_y, swap(along_y), t_x, u_x, both, inside, qt
    )
    normed_all = trade(spread, "z")
    out_mine = after(out_mine, spread)
    out_mine_low = (out_mine * unity).astype(BF16)
    out_other_low = (swap(out_mine) * unity).astype(BF16)
    normed_all = after(normed_all, out_mine_low, out_other_low)
    middle, sent, second_part, down_part = run_ffn(
        scal, normed_all, out_mine_low, out_other_low, block_input, gain_2, out_grad,
        w_gate, w_up, w_down,
    )

    second = trade(second_part.reshape(RANKS, PART, width), "z")
    ffn_pieces = list(run_w1(scal, sent, swap(sent), grad_turned))
    second = after(second, *ffn_pieces)
    along_y = send_on(ffn_pieces[4:], "y")
    d_middle, attn, gain_mid_part, d_normed = run_k5(
        scal, second, middle, out_grad, gain_2, out_mine_low, out_other_low
    )
    attn_all = lax.all_gather(attn, "z", axis=0, tiled=True)
    d_normed = trade(d_normed, "z").reshape(tokens, WIDE)
    down_sum = lax.psum(after(down_part, d_normed), "z")
    dm, state_grad = run_b1(scal, d_normed, mixed, qt)
    pair = lax.all_gather(state_grad, "c", axis=0)
    g_1, spread = run_t1(scal, pair, both)
    g_x = trade(spread, "x")
    dq, dk, dv, dw, dkp, xc = run_b2(
        scal, after(dm, spread), carried, q, k, v, w, aux_q, inv, kp, c, sc
    )
    g_x = after(g_x, dq)
    spread = run_t2(scal, g_x, t_x)
    g_y = trade(spread, "y")
    attn_all = after(attn_all, spread)
    attn_turned = run_turn(scal, attn_all, swap(attn_all))
    ffn_pieces[1] = after(ffn_pieces[1], spread)
    along_x = send_on(ffn_pieces[:4], "x")
    along_y = (after(along_y[0], spread), along_y[1])
    relayed, ffn_two = relay_on(ffn_pieces[4:], along_y, "y", scal)
    g_y = after(g_y, attn_turned, *relayed)
    later = run_t3(scal, g_y, g_x, t_y, t_x, both, g_1)
    later = lax.all_gather(later, "c", axis=0)
    block_output = middle + down_sum

    low = run_b3(scal, later, carried, k, v, w, aux, inv, kp, b, kt, dk, dv, dw, dkp, xc)
    low_other = swap(low)
    along_x = (after(along_x[0], low), along_x[1])
    relayed, ffn_one = relay_on(ffn_pieces[:4], along_x, "x", scal)
    ffn_two[0] = after(ffn_two[0], low)
    ffn_two = run_fold_1(scal, ffn_two)
    low_other = after(low_other, relayed[0], ffn_two)
    ffn_two = lax.psum_scatter(ffn_two, "x", scatter_dimension=0)
    head_pieces = run_w2(
        scal, low, low_other, dq, swap(dq), normed, swap(normed), h1_turned, attn_turned
    )
    came = [send_on(head_pieces[:4], "x"), send_on(head_pieces[4:], "y")]
    first_part = run_b4(
        scal, block_input, gain_mid_part, dq, after(low, head_pieces[0]), *heads_w
    )
    first = trade(first_part, "z")
    ffn_one[0] = after(ffn_one[0], head_pieces[0])
    ffn_one = run_fold_1(scal, ffn_one)
    came[0] = (after(came[0][0], first_part, ffn_one), came[0][1])
    ffn_one = lax.psum_scatter(ffn_one, "y", scatter_dimension=0)
    relayed, head_pieces = relay_both(head_pieces, came, scal)
    input_part, gains = run_n(scal, after(first, relayed[0]), block_input, gain_1, d_middle)
    input_grad = lax.all_gather(input_part, "z", axis=0, tiled=True)
    head_pieces[0] = after(head_pieces[0], input_part, block_output)
    head_pieces = run_fold_2(scal, head_pieces)
    gains = jnp.swapaxes(after(gains, head_pieces[0])[:2].reshape(2, 32, width // 32), 0, 1)
    gains = trade(gains, CTX)
    head_pieces = exchange(head_pieces, "y", "x")
    ffn_two = after(ffn_two, head_pieces[2])
    gate_out, up_out, down_out = run_end_1(scal, ffn_one, ffn_two)
    gains = jnp.sum(after(gains, gate_out), axis=0)
    input_grad = input_grad * unity
    head_pieces[6] = after(head_pieces[6], input_grad)
    key_out, value_out, path_out, beta_out, query_out, out_out = run_end_2(scal, head_pieces)
    return (
        block_output, input_grad, gains[0], query_out, key_out, value_out, path_out,
        beta_out[:, : w_beta.shape[1]], out_out.T, gains[1], gate_out, up_out, down_out.T,
    )


def solution(mesh):
    fine = Mesh(mesh.devices.reshape(SIDE, SIDE, 2, RANKS), ("y", "x", "c", "z"))
    tokens, heads, whole = P(CTX, None), P(None, "z"), P()
    in_specs = (
        tokens, whole, heads, heads, heads, heads, heads, P("z", None),
        whole, heads, heads, P("z", None), tokens, whole,
    )
    weight = P(CTX, "z")
    out_specs = (
        tokens, tokens, P(CTX), weight, weight, weight, weight, weight,
        P("z", CTX), P(CTX), weight, weight, P("z", CTX),
    )
    return jax.shard_map(local, mesh=fine, in_specs=in_specs, out_specs=out_specs, check_vma=False)
```

```python
import jax
import jax.numpy as jnp
from jax import lax
from jax.experimental import pallas as pl
from jax.experimental.pallas import tpu as pltpu
from jax.sharding import Mesh
from jax.sharding import PartitionSpec as P

EPSILON = 1e-06
HEAD_EPSILON = 0.01
F32 = jnp.float32
BF16 = jnp.bfloat16
HEADS = 3
HW = 128
LEN = 256
RANKS = 4
PART = LEN // RANKS
SIDE = 4
CTX = ("y", "x", "c")


def split(value):
    high = value.astype(BF16)
    return high, (value - high.astype(F32)).astype(BF16)


def dg(left, right, ta, tb):
    dims = (((0 if ta else 1,), (1 if tb else 0,)), ((), ()))
    return lax.dot_general(left, right, dims, preferred_element_type=F32)


def mm(left, right, ta=False, tb=False):
    left = left if isinstance(left, tuple) else split(left)
    right = right if isinstance(right, tuple) else split(right)
    return dg(left[0], right[0], ta, tb) + (
        dg(left[0], right[1], ta, tb) + dg(left[1], right[0], ta, tb)
    )


def iota(shape, dim):
    return lax.broadcasted_iota(jnp.int32, shape, dim)


def cols(head):
    return slice(head * HW, (head + 1) * HW)


def segments(spot, scal):
    second = scal[1]
    third = second + scal[2]
    return (spot >= second).astype(jnp.int32) + (spot >= third).astype(jnp.int32)


def small_inverses(scaled):
    row = iota((HW, HW), 0)
    lane = iota((HW, HW), 1)
    same = (row // 8) == (lane // 8)
    packed = []
    for one in scaled:
        for half in range(2):
            block = jnp.where(same, one[half * HW : (half + 1) * HW, half * HW : (half + 1) * HW], 0.0)
            packed.append(jnp.sum(block.reshape(HW // 8, 8, HW), axis=0))
    count = len(packed)
    high, low = split(jnp.concatenate(packed, axis=0))
    lane_8 = iota((8, HW), 1) % 8
    spread = {}
    for k in range(1, 8):
        unit = ((row // 8 == lane // 8) & (row % 8 == k)).astype(BF16)
        both = dg(high, unit, False, False) + dg(low, unit, False, False)
        spread[k] = both.reshape(count, 8, HW)
    rows = {}
    for i in range(7, -1, -1):
        value = jnp.broadcast_to((lane_8[:1] == i).astype(F32)[None], (count, 1, HW))
        for k in range(i + 1, 8):
            value = value - spread[k][:, i : i + 1, :] * rows[k]
        rows[i] = value
    done = jnp.concatenate([rows[i] for i in range(8)], axis=1)
    out = []
    zero = jnp.zeros((HW, HW), F32)
    for head in range(count // 2):
        halves = [
            jnp.where(same, jnp.concatenate([done[2 * head + half]] * (HW // 8), axis=0), 0.0)
            for half in range(2)
        ]
        out.append(
            jnp.concatenate(
                [
                    jnp.concatenate([halves[0], zero], axis=1),
                    jnp.concatenate([zero, halves[1]], axis=1),
                ],
                axis=0,
            )
        )
    return out


def upper_rows(value, width):
    return jnp.concatenate(
        [value[at : at + width] for at in range(0, value.shape[0], 2 * width)], axis=0
    )


def put_upper(value, upper, width):
    pieces = []
    for n, at in enumerate(range(0, value.shape[0], 2 * width)):
        pieces.append(upper[n * width : (n + 1) * width])
        pieces.append(value[at + width : at + 2 * width])
    return jnp.concatenate(pieces, axis=0)


def inverses(scaled):
    out = small_inverses(scaled)
    row = iota((LEN, LEN), 0)
    lane = iota((LEN, LEN), 1)
    width = 8
    while width < LEN:
        pair = (row // (2 * width) == lane // (2 * width)) & (row // width < lane // width)
        link = [upper_rows(jnp.where(pair, one, 0.0), width) for one in scaled]
        parts = [split(one) for one in out]
        first = [mm(a, b) for a, b in zip(link, parts)]
        empty = jnp.zeros((LEN, LEN), F32)
        wide = [put_upper(empty, one, width) for one in first]
        tops = [
            (upper_rows(a, width), upper_rows(b, width)) for a, b in parts
        ]
        second = [mm(a, b) for a, b in zip(tops, wide)]
        out = [
            put_upper(one, upper_rows(one, width) - new, width) for one, new in zip(out, second)
        ]
        width *= 2
    return out


def unit_rows(value):
    scale = lax.rsqrt(jnp.sum(value * value, axis=-1, keepdims=True) + EPSILON)
    return value * scale, scale


def first_norm(x_ref, gain_ref):
    x = x_ref[...]
    scale = lax.rsqrt(jnp.mean(x * x, axis=-1, keepdims=True) + EPSILON)
    return (x * scale * gain_ref[...].astype(F32).reshape(1, -1)).astype(BF16)


def a1_body(
    scal_ref, x_ref, gain_ref, wk_ref, wv_ref, ww_ref, wb_ref,
    k_ref, v_ref, w_ref, aux_ref, inv_ref, kp_ref, b_ref, kt_ref, tu_ref,
):
    h1 = first_norm(x_ref, gain_ref)
    start = scal_ref[0]
    token = iota((LEN, 1), 0) + start
    segment = segments(token, scal_ref)
    end_segment = segments(jnp.full((1, 1), LEN - 1, jnp.int32) + start, scal_ref)
    before = start - 1
    before_segment = jnp.where(start == 0, -1, segments(jnp.full((1, 1), 0, jnp.int32) + before, scal_ref))
    last = (segment == end_segment).astype(F32)
    carry_all = (end_segment == before_segment).astype(F32)
    row = iota((LEN, LEN), 0)
    lane = iota((LEN, LEN), 1)
    later = row < lane
    beta = 1.0 + jax.nn.sigmoid(dg(h1, wb_ref[...], False, True))
    beta_rows = 1.0 + jax.nn.sigmoid(dg(wb_ref[...], h1, False, True))
    pr = dg(h1, ww_ref[...], False, False)
    kr = dg(h1, wk_ref[...], False, False)
    w_all, k_all, aux = [], [], []
    for head in range(HEADS):
        w, w_scale = unit_rows(pr[:, cols(head)])
        k, k_scale = unit_rows(kr[:, cols(head)])
        w_ref[:, cols(head)] = w
        k_ref[:, cols(head)] = k
        w_all.append(w)
        k_all.append(k)
        aux.append((w_scale, k_scale))
    w_split = [split(w) for w in w_all]
    k_split = [split(k) for k in k_all]
    scaled = [
        jnp.where(later, mm(w_split[h], w_split[h], tb=True), 0.0) * beta[:, h : h + 1]
        for h in range(HEADS)
    ]
    inverse = [
        one * beta_rows[h : h + 1, :] for h, one in enumerate(inverses(scaled))
    ]
    vr = dg(h1, wv_ref[...], False, False)
    v_ref[...] = vr
    lane_aux = iota((LEN, HW), 1)
    packed = jnp.zeros((LEN, HW), F32)
    eye = (iota((HW, HW), 0) == iota((HW, HW), 1)).astype(F32)
    for head in range(HEADS):
        spots = (
            (head, beta[:, head : head + 1]),
            (16 + head, aux[head][1]),
            (24 + head, aux[head][0]),
        )
        for at, value in spots:
            packed = jnp.where(lane_aux == at, value, packed)
        inv_ref[head] = inverse[head]
        inv_split = split(inverse[head])
        folded = mm(inv_split, w_split[head])
        b_ref[:, cols(head)] = folded
        folded_split = split(folded)
        kp = jnp.where(later, mm(k_split[head], w_split[head], tb=True), 0.0)
        kp_ref[head] = kp
        kt = k_all[head] - mm(kp, folded_split)
        kt_ref[:, cols(head)] = kt
        tu_ref[0, head] = carry_all * (eye - mm(w_split[head], folded_split, ta=True))
        tu_ref[1, head] = mm(vr[:, cols(head)], kt * last, ta=True)
    aux_ref[...] = packed


def shape(*dims, dtype=F32):
    return jax.ShapeDtypeStruct(dims, dtype)


MIB = 1024 * 1024
SLACK = 10 * MIB
LIGHT = pl.CostEstimate(flops=10**4, bytes_accessed=10**4, transcendentals=0)
HEAVY = pl.CostEstimate(flops=10**12, bytes_accessed=10**8, transcendentals=0)
WORK = pl.CostEstimate(flops=8 * 10**9, bytes_accessed=10**7, transcendentals=0)


def size_of(*arrays):
    total = 0
    for one in arrays:
        count = one.dtype.itemsize
        for extent in one.shape:
            count *= extent
        total += count
    return total


class Late:
    def __init__(self, copy, buffer):
        self.copy, self.buffer, self.shape = copy, buffer, buffer.shape
        copy.start()

    def here(self):
        if self.copy is not None:
            self.copy.wait()
            self.copy = None
        return self.buffer

    def __getitem__(self, spot):
        return self.here()[spot]


class Early:
    def __init__(self, copy, buffer):
        self.copy, self.buffer, self.shape, self.sent = copy, buffer, buffer.shape, False

    def __getitem__(self, spot):
        return self.buffer[spot]

    def __setitem__(self, spot, value):
        self.buffer[spot] = value

    @property
    def at(self):
        return self.buffer.at


def whole_now(*refs):
    for ref in refs:
        if isinstance(ref, Early):
            ref.copy.start()
            ref.sent = True


def call(body, outs, name, scratch=(), late=(), early=(), cost=LIGHT, alone=False):
    def run(*operands):
        count = len(operands)
        moved = sorted(late)
        leaving = sorted(early)
        vmem = pl.BlockSpec(memory_space=pltpu.VMEM)
        anywhere = pl.BlockSpec(memory_space=pl.ANY)
        held = [operands[at] for at in moved] + [outs[at] for at in leaving]
        buffers = [pltpu.VMEM(one.shape, one.dtype) for one in held]
        marks = [pltpu.SemaphoreType.DMA((len(buffers),))] if buffers else []

        def wrapped(*refs):
            refs = list(refs)
            own = len(refs) - len(buffers) - len(marks)
            for n, at in enumerate(moved):
                copy = pltpu.make_async_copy(refs[at], refs[own + n], refs[-1].at[n])
                refs[at] = Late(copy, refs[own + n])
            for n, at in enumerate(leaving, len(moved)):
                copy = pltpu.make_async_copy(refs[own + n], refs[count + at], refs[-1].at[n])
                refs[count + at] = Early(copy, refs[own + n])
            body(*refs[:own])
            for at in moved:
                refs[at].here()
            for at in leaving:
                if not refs[count + at].sent:
                    refs[count + at].copy.start()
            for at in leaving:
                refs[count + at].copy.wait()

        need = size_of(*operands, *outs, *scratch) + SLACK
        return pl.pallas_call(
            wrapped,
            out_shape=outs,
            in_specs=[pl.BlockSpec(memory_space=pltpu.SMEM)]
            + [anywhere if at in moved else vmem for at in range(1, count)],
            out_specs=[anywhere if at in leaving else vmem for at in range(len(outs))],
            scratch_shapes=list(scratch) + buffers + marks,
            name=name,
            cost_estimate=cost,
            compiler_params=pltpu.CompilerParams(vmem_limit_bytes=56 * MIB if alone else need),
        )(*operands)

    return run


WIDE = HEADS * HW


def run_a1(*operands):
    outs = [
        shape(LEN, WIDE), shape(LEN, WIDE), shape(LEN, WIDE),
        shape(LEN, HW),
        shape(HEADS, LEN, LEN), shape(HEADS, LEN, LEN),
        shape(LEN, WIDE), shape(LEN, WIDE),
        shape(2, HEADS, HW, HW),
    ]
    return call(a1_body, outs, "local_parts", alone=True)(*operands)


def a2_body(
    scal_ref, x_ref, gain_ref, wq_ref, k_ref, v_ref, w_ref, inv_ref, kp_ref,
    q_ref, aux_ref, c_ref, sc_ref, qt_ref, in_ref,
):
    start = scal_ref[0]
    segment = segments(iota((LEN, LEN), 0) + start, scal_ref)
    segment_t = segments(iota((LEN, LEN), 1) + start, scal_ref)
    row = iota((LEN, LEN), 0)
    lane = iota((LEN, LEN), 1)
    up_to = row <= lane
    seen = up_to & (segment == segment_t)
    qr = dg(first_norm(x_ref, gain_ref), wq_ref[...], False, False)
    lane_aux = iota((LEN, HW), 1)
    packed = jnp.zeros((LEN, HW), F32)
    for head in range(HEADS):
        q, q_scale = unit_rows(qr[:, cols(head)])
        q_ref[:, cols(head)] = q
        packed = jnp.where(lane_aux == head, q_scale, packed)
        q_split = split(q)
        w_split = split(w_ref[:, cols(head)])
        pq = jnp.where(up_to, mm(w_split, q_split, tb=True), 0.0)
        c = mm(inv_ref[head], pq)
        c_ref[head] = c
        c_split = split(c)
        qt_ref[:, cols(head)] = q - mm(c_split, w_split, ta=True)
        scores = mm(k_ref[:, cols(head)], q_split, tb=True) - mm(kp_ref[head], c_split)
        scores = jnp.where(seen, scores, 0.0)
        sc_ref[head] = scores
        in_ref[:, cols(head)] = mm(scores, v_ref[:, cols(head)], ta=True)
    aux_ref[...] = packed


def run_a2(*operands):
    outs = [
        shape(LEN, WIDE), shape(LEN, HW),
        shape(HEADS, LEN, LEN), shape(HEADS, LEN, LEN), shape(LEN, WIDE), shape(LEN, WIDE),
    ]
    return call(a2_body, outs, "inside_parts", alone=True, cost=WORK)(*operands)


def carry_of(start, scal_ref):
    token = iota((LEN, 1), 0) + start
    before = jnp.full((1, 1), 0, jnp.int32) + (start - 1)
    before_segment = jnp.where(start == 0, -1, segments(before, scal_ref))
    return (segments(token, scal_ref) == before_segment).astype(F32)


def pair_of(ref, core, head):
    return jnp.concatenate([ref[0, core, head], ref[1, core, head]], axis=0)


def b1_body(scal_ref, dn_ref, mixed_ref, qt_ref, dm_ref, sg_ref):
    carry = carry_of(scal_ref[0], scal_ref)
    for head in range(HEADS):
        mixed = mixed_ref[:, cols(head)]
        dn = dn_ref[:, cols(head)]
        scale = lax.rsqrt(jnp.mean(mixed * mixed, axis=-1, keepdims=True) + HEAD_EPSILON)
        drift = jnp.mean(dn * mixed, axis=-1, keepdims=True) * (scale * scale)
        dm = scale * (dn - mixed * drift)
        dm_ref[:, cols(head)] = dm
        sg_ref[head] = mm(dm * carry, qt_ref[:, cols(head)], ta=True)


def run_b1(*operands):
    outs = [shape(LEN, WIDE), shape(HEADS, HW, HW)]
    return call(b1_body, outs, "state_gradient")(*operands)


def unit_pull(unit, scale, grad):
    return scale * (grad - unit * jnp.sum(unit * grad, axis=-1, keepdims=True))


def b2_body(
    scal_ref, dm_ref, carried_ref, q_ref, k_ref, v_ref, w_ref, aux_ref, inv_ref, kp_ref,
    c_ref, sc_ref,
    dq_ref, dk_ref, dv_ref, dw_ref, dkp_ref, xc_ref,
):
    start = scal_ref[0]
    carry = carry_of(start, scal_ref)
    row = iota((LEN, LEN), 0)
    lane = iota((LEN, LEN), 1)
    up_to = row <= lane
    seen = up_to & (
        segments(row + start, scal_ref) == segments(lane + start, scal_ref)
    )
    for head in range(HEADS):
        q = q_ref[:, cols(head)]
        q_split = split(q)
        w_split = split(w_ref[:, cols(head)])
        k_split = split(k_ref[:, cols(head)])
        c_split = split(c_ref[head])
        kp_split = split(kp_ref[head])
        dm = dm_ref[:, cols(head)]
        dm_split = split(dm)
        dqt = mm(dm * carry, carried_ref[head])
        dqt_split = split(dqt)
        ds = jnp.where(seen, mm(v_ref[:, cols(head)], dm_split, tb=True), 0.0)
        ds_split = split(ds)
        dv_ref[:, cols(head)] = mm(sc_ref[head], dm_split)
        dk = mm(ds_split, q_split)
        dq = dqt + mm(ds_split, k_split, ta=True)
        dkp_ref[head] = mm(ds_split, c_split, tb=True)
        dc = mm(kp_split, ds_split, ta=True) + mm(w_split, dqt_split, tb=True)
        dw = mm(c_split, dqt_split)
        x = mm(inv_ref[head], dc, ta=True)
        xc_ref[head] = mm(x, c_split, tb=True)
        dpq_split = split(jnp.where(up_to, x, 0.0))
        dw_ref[:, cols(head)] = dw + mm(dpq_split, q_split)
        dq = dq - mm(dpq_split, w_split, ta=True)
        dk_ref[:, cols(head)] = dk
        scale = aux_ref[:, head : head + 1]
        dq_ref[:, cols(head)] = unit_pull(q, scale, dq).astype(BF16).astype(F32)


def run_b2(*operands):
    outs = [
        shape(LEN, WIDE), shape(LEN, WIDE), shape(LEN, WIDE), shape(LEN, WIDE),
        shape(HEADS, LEN, LEN), shape(HEADS, LEN, LEN),
    ]
    return call(b2_body, outs, "inside_gradients", alone=True, cost=WORK)(*operands)


def b3_body(
    scal_ref, states_ref, carried_ref, k_ref, v_ref, w_ref, aux_ref,
    inv_ref, kp_ref, b_ref, kt_ref, dk_ref, dv_ref, dw_ref, dkp_ref, xc_ref,
    low_ref,
):
    start = scal_ref[0]
    core = scal_ref[5]
    segment = segments(iota((LEN, 1), 0) + start, scal_ref)
    end_segment = segments(jnp.full((1, 1), LEN - 1, jnp.int32) + start, scal_ref)
    before = jnp.full((1, 1), 0, jnp.int32) + (start - 1)
    before_segment = jnp.where(start == 0, -1, segments(before, scal_ref))
    last = (segment == end_segment).astype(F32)
    carry_all = (end_segment == before_segment).astype(F32)
    row = iota((LEN, LEN), 0)
    lane = iota((LEN, LEN), 1)
    later_mask = row < lane
    lane_aux = iota((LEN, HW), 1)
    d_beta = jnp.zeros((LEN, HW), F32)
    for head in range(HEADS):
        later = pair_of(states_ref, core, head)
        later_split = split(later)
        dt_split = split(carry_all * mm(carried_ref[head], later_split, ta=True))
        w = w_ref[:, cols(head)]
        w_split = split(w)
        k = k_ref[:, cols(head)]
        v = v_ref[:, cols(head)]
        b_split = split(b_ref[:, cols(head)])
        kp_split = split(kp_ref[head])
        dv = dv_ref[:, cols(head)] + last * mm(kt_ref[:, cols(head)], later_split, tb=True)
        dkt = last * mm(v, later_split)
        dkt_split = split(dkt)
        db = mm(w_split, dt_split) + mm(kp_split, dkt_split, ta=True)
        y = mm(inv_ref[head], db, ta=True)
        y_split = split(y)
        dw = dw_ref[:, cols(head)] + mm(b_split, dt_split, tb=True) + y
        dkp = jnp.where(later_mask, dkp_ref[head] + mm(dkt_split, b_split, tb=True), 0.0)
        dkp_split = split(dkp)
        dk = dk_ref[:, cols(head)] + dkt - mm(dkp_split, w_split)
        dw = dw + mm(dkp_split, split(k), ta=True)
        dm = xc_ref[head] + mm(y_split, b_split, tb=True)
        dn_split = split(jnp.where(later_mask, dm, 0.0))
        dw = mm(dn_split, w_split) + mm(dn_split, w_split, ta=True) - dw
        diagonal = jnp.sum(jnp.where(row == lane, dm, 0.0), axis=-1, keepdims=True)
        beta = aux_ref[:, head : head + 1]
        sig = beta - 1.0
        dbl = -diagonal / (beta * beta) * sig * (1.0 - sig)
        d_beta = jnp.where(lane_aux == head, dbl, d_beta)
        low_ref[:, cols(head)] = unit_pull(k, aux_ref[:, 16 + head : 17 + head], dk).astype(BF16).astype(F32)
        low_ref[:, WIDE + head * HW : WIDE + (head + 1) * HW] = dv.astype(BF16).astype(F32)
        low_ref[:, 2 * WIDE + head * HW : 2 * WIDE + (head + 1) * HW] = unit_pull(
            w, aux_ref[:, 24 + head : 25 + head], dw
        ).astype(BF16).astype(F32)
    low_ref[:, 3 * WIDE :] = d_beta.astype(BF16).astype(F32)


def run_b3(*operands):
    outs = [shape(LEN, 3 * WIDE + HW)]
    return call(b3_body, outs, "late_gradients", alone=True)(*operands)[0]


def b4_body(
    scal_ref, x_ref, gain_mid_ref, dq_ref, low_ref, wq_ref, wk_ref, wv_ref, ww_ref, wb_ref, dh_ref
):
    total = dg(dq_ref[...].astype(BF16), wq_ref[...], False, True)
    for at, ref in enumerate((wk_ref, wv_ref, ww_ref)):
        low = low_ref[:, at * WIDE : at * WIDE + ref.shape[1]].astype(BF16)
        total = total + dg(low, ref[...], False, True)
    beta_cols = wb_ref[...].astype(F32)
    for head in range(HEADS):
        at = 3 * WIDE + head
        total = total + low_ref[:, at : at + 1] * beta_cols[head : head + 1, :]
    for at in range(RANKS):
        dh_ref[at, :PART, :] = total[at * PART : (at + 1) * PART]
    x = x_ref[...]
    scale = lax.rsqrt(jnp.mean(x * x, axis=-1, keepdims=True) + EPSILON)
    gain_in = jnp.sum(total * x * scale, axis=0, keepdims=True)
    rows = iota((8, x.shape[1]), 0)
    both = jnp.where(rows == 0, gain_in, jnp.where(rows == 1, gain_mid_ref[...], 0.0))
    for at in range(RANKS):
        dh_ref[at, PART:, :] = both


def run_b4(*operands):
    outs = [shape(RANKS, PART + 8, operands[1].shape[1])]
    return call(b4_body, outs, "first_norm_part", alone=True)(*operands)[0]


def half_of(core):
    return pl.ds(pl.multiple_of(core * (HW // 2), HW // 2), HW // 2)


def s1_body(scal_ref, both_ref, out_ref):
    rows = half_of(scal_ref[5])
    for head in range(HEADS):
        t_1 = split(both_ref[1, 0, head])
        u_0 = both_ref[0, 1, head, rows, :]
        u_1 = both_ref[1, 1, head, rows, :]
        chip_t = mm(both_ref[0, 0, head, rows, :], t_1)
        chip_u = mm(u_0, t_1) + u_1
        for at in range(SIDE):
            out_ref[at, 0, head] = chip_t
            out_ref[at, 1, head] = chip_u


def run_s1(*operands):
    outs = [shape(SIDE, 2, HEADS, HW // 2, HW)]
    return call(s1_body, outs, "chip_state")(*operands)[0]


def join_halves(out_ref, mine_ref, other_ref, core, at, which, head):
    out_ref[at, head, half_of(core), :] = mine_ref[at, which, head]
    out_ref[at, head, half_of(1 - core), :] = other_ref[at, which, head]


def s2_body(scal_ref, mine_ref, other_ref, t_ref, u_ref, out_ref):
    core = scal_ref[5]
    rows = half_of(core)
    for head in range(HEADS):
        for at in range(SIDE):
            join_halves(t_ref, mine_ref, other_ref, core, at, 0, head)
            join_halves(u_ref, mine_ref, other_ref, core, at, 1, head)
    for head in range(HEADS):
        t_1 = split(t_ref[1, head])
        t_3 = split(t_ref[3, head])
        t_23 = split(mm(t_ref[2, head], t_3))
        row_t = mm(mm(t_ref[0, head, rows, :], t_1), t_23)
        u = [mine_ref[at, 1, head] for at in range(SIDE)]
        row_u = mm(mm(u[0], t_1) + u[1], t_23) + mm(u[2], t_3) + u[3]
        for at in range(SIDE):
            out_ref[at, 0, head] = row_t
            out_ref[at, 1, head] = row_u


def run_s2(*operands):
    outs = [
        shape(SIDE, HEADS, HW, HW),
        shape(SIDE, HEADS, HW, HW),
        shape(SIDE, 2, HEADS, HW // 2, HW),
    ]
    return call(s2_body, outs, "row_state")(*operands)


def s3_body(
    scal_ref, mine_ref, other_ref, tx_ref, ux_ref, both_ref, in_ref, qt_ref,
    ty_ref, mixed_ref, normed_ref, spread_ref, carried_ref, uy_ref,
):
    row, col, core = scal_ref[3], scal_ref[4], scal_ref[5]
    carry = carry_of(scal_ref[0], scal_ref)
    for head in range(HEADS):
        for at in range(SIDE):
            join_halves(ty_ref, mine_ref, other_ref, core, at, 0, head)
        for at in range(SIDE - 1):
            join_halves(uy_ref, mine_ref, other_ref, core, at, 1, head)
    for head in range(HEADS):
        state = jnp.where(row > 0, uy_ref[0, head], 0.0)
        for at in range(1, SIDE - 1):
            new = mm(state, ty_ref[at, head]) + uy_ref[at, head]
            state = jnp.where(at < row, new, state)
        for at in range(SIDE - 1):
            new = mm(state, tx_ref[at, head]) + ux_ref[at, head]
            state = jnp.where(at < col, new, state)
        new = mm(state, both_ref[0, 0, head]) + both_ref[0, 1, head]
        state = jnp.where(core > 0, new, state)
        carried_ref[head] = state
        mixed = in_ref[:, cols(head)] + carry * mm(qt_ref[:, cols(head)], state, tb=True)
        mixed_ref[:, cols(head)] = mixed
        scale = lax.rsqrt(jnp.mean(mixed * mixed, axis=-1, keepdims=True) + HEAD_EPSILON)
        low = (mixed * scale).astype(BF16).astype(F32)
        normed_ref[:, cols(head)] = low
        for at in range(RANKS):
            spread_ref[at, :, cols(head)] = low


def run_s3(*operands):
    outs = [
        shape(SIDE, HEADS, HW, HW), shape(LEN, WIDE), shape(LEN, WIDE), shape(RANKS, LEN, WIDE),
        shape(HEADS, HW, HW),
    ]
    scratch = [pltpu.VMEM((SIDE - 1, HEADS, HW, HW), F32)]
    return call(s3_body, outs, "normed_heads", scratch, alone=True)(*operands)


def t1_body(scal_ref, pair_ref, both_ref, g_ref, out_ref):
    rows = half_of(scal_ref[5])
    for head in range(HEADS):
        g_1 = pair_ref[1, head, rows, :]
        g_ref[head] = g_1
        chip = mm(g_1, both_ref[0, 0, head], tb=True) + pair_ref[0, head, rows, :]
        for at in range(SIDE):
            out_ref[at, head] = chip


def run_t1(*operands):
    outs = [shape(HEADS, HW // 2, HW), shape(SIDE, HEADS, HW // 2, HW)]
    return call(t1_body, outs, "chip_gradient")(*operands)


def t2_body(scal_ref, g_ref, t_ref, out_ref):
    for head in range(HEADS):
        total = g_ref[3, head]
        for at in (2, 1, 0):
            total = mm(total, t_ref[at, head], tb=True) + g_ref[at, head]
        for at in range(SIDE):
            out_ref[at, head] = total


def run_t2(*operands):
    outs = [shape(SIDE, HEADS, HW // 2, HW)]
    return call(t2_body, outs, "row_gradient")(*operands)[0]


def t3_body(scal_ref, gy_ref, gx_ref, ty_ref, tx_ref, both_ref, g_ref, out_ref):
    row, col = scal_ref[3], scal_ref[4]
    for head in range(HEADS):
        later = jnp.where(row < SIDE - 1, gy_ref[3, head], 0.0)
        for at in (2, 1):
            new = mm(later, ty_ref[at, head], tb=True) + gy_ref[at, head]
            later = jnp.where(at > row, new, later)
        for at in (3, 2, 1):
            new = mm(later, tx_ref[at, head], tb=True) + gx_ref[at, head]
            later = jnp.where(at > col, new, later)
        out_ref[1, head] = later
        out_ref[0, head] = mm(later, both_ref[1, 0, head], tb=True) + g_ref[head]


def run_t3(*operands):
    outs = [shape(2, HEADS, HW // 2, HW)]
    return call(t3_body, outs, "block_gradient")(*operands)[0]


def ffn_body(
    scal_ref, normed_ref, out_mine_ref, out_other_ref, x_ref, gain_ref, grad_ref,
    gate_ref, up_ref, down_ref,
    middle_ref, sent_ref, dh_ref, down_part_ref,
):
    core = scal_ref[5]
    half = x_ref.shape[1] // 2
    units = gate_ref.shape[1]
    low = [normed_ref[rank].astype(BF16) for rank in range(RANKS)]
    for ref, at in ((out_mine_ref, core), (out_other_ref, 1 - core)):
        spot = pl.ds(pl.multiple_of(at * half, half), half)
        total = x_ref[:, spot]
        for rank in range(RANKS):
            total = total + dg(low[rank], ref[rank], False, False)
        middle_ref[:, spot] = total
    middle = middle_ref[...]
    scale = lax.rsqrt(jnp.mean(middle * middle, axis=-1, keepdims=True) + EPSILON)
    h2 = (middle * scale * gain_ref[...].astype(F32).reshape(1, -1)).astype(BF16)
    sent_ref[:, 3 * units :] = h2.astype(F32)
    gate = dg(h2, gate_ref[...], False, False)
    up = dg(h2, up_ref[...], False, False)
    sig = jax.nn.sigmoid(gate)
    silu = gate * sig
    hidden = (silu * up).astype(BF16)
    sent_ref[:, 2 * units : 3 * units] = hidden.astype(F32)
    d_hidden = dg(grad_ref[...].astype(BF16), down_ref[...], False, True)
    d_gate = (d_hidden * up * sig * (1.0 + gate * (1.0 - sig))).astype(BF16)
    sent_ref[:, :units] = d_gate.astype(F32)
    d_up = (d_hidden * silu).astype(BF16)
    sent_ref[:, units : 2 * units] = d_up.astype(F32)
    whole_now(middle_ref, sent_ref)
    dh_ref[...] = dg(d_gate, gate_ref[...], False, True) + dg(d_up, up_ref[...], False, True)
    whole_now(dh_ref)
    down_part_ref[...] = dg(hidden, down_ref[...], False, False)


def run_ffn(*operands):
    tokens, width = operands[4].shape
    units = operands[7].shape[1]
    outs = [
        shape(tokens, width), shape(tokens, 3 * units + width), shape(tokens, width), shape(tokens, width)
    ]
    return call(ffn_body, outs, "feed_forward", alone=True, late=(6, 7, 8, 9))(*operands)


def norm_pull(grad, values, gain):
    scale = lax.rsqrt(jnp.mean(values * values, axis=-1, keepdims=True) + EPSILON)
    turned = gain * grad
    drift = jnp.mean(turned * values, axis=-1, keepdims=True) * (scale * scale * scale)
    return scale * turned - values * drift, grad * values * scale


def k5_body(
    scal_ref, second_ref, middle_ref, grad_ref, gain_ref, out_mine_ref, out_other_ref,
    d_middle_ref, attn_ref, gain_out_ref, normed_ref,
):
    core = scal_ref[5]
    second = second_ref[0] + second_ref[1] + second_ref[2] + second_ref[3]
    pulled, summed = norm_pull(second, middle_ref[...], gain_ref[...].astype(F32).reshape(1, -1))
    d_middle = grad_ref[...] + pulled
    d_middle_ref[...] = d_middle
    gain_out_ref[...] = jnp.sum(summed, axis=0, keepdims=True)
    attn_ref[...] = d_middle.astype(BF16).astype(F32)
    half = d_middle.shape[1] // 2
    mine = attn_ref[:, pl.ds(pl.multiple_of(core * half, half), half)].astype(BF16)
    other = attn_ref[:, pl.ds(pl.multiple_of((1 - core) * half, half), half)].astype(BF16)
    for rank in range(RANKS):
        normed_ref[rank] = dg(mine, out_mine_ref[rank], False, True) + dg(
            other, out_other_ref[rank], False, True
        )


def run_k5(*operands):
    width = operands[2].shape[1]
    outs = [shape(PART, width), shape(PART, width), shape(1, width), shape(RANKS, PART, WIDE)]
    return call(k5_body, outs, "middle_gradient", alone=True)(*operands)


def n_body(scal_ref, first_ref, x_ref, gain_ref, d_middle_ref, out_ref, gains_ref):
    rows = pl.ds(pl.multiple_of(scal_ref[6] * PART, PART), PART)
    total = first_ref[0] + first_ref[1] + first_ref[2] + first_ref[3]
    pulled, _ = norm_pull(total[:PART], x_ref[rows, :], gain_ref[...].astype(F32).reshape(1, -1))
    out_ref[...] = d_middle_ref[...] + pulled
    gains_ref[...] = total[PART:]


def run_n(*operands):
    width = operands[2].shape[1]
    outs = [shape(PART, width), shape(8, width)]
    return call(n_body, outs, "input_gradient", alone=True)(*operands)


def turn_body(scal_ref, mine_ref, other_ref, out_ref):
    tokens, width = mine_ref.shape
    for n, ref in enumerate((mine_ref, other_ref)):
        for at in range(0, width, 256):
            block = ref[:, at : at + 256].T.astype(BF16)
            out_ref[at : at + 256, n * tokens : (n + 1) * tokens] = block


def turn_norm_body(scal_ref, mine_ref, other_ref, gain_ref, out_ref):
    tokens, width = mine_ref.shape
    for n, ref in enumerate((mine_ref, other_ref)):
        h1 = first_norm(ref, gain_ref).astype(F32)
        for at in range(0, width, 256):
            block = h1[:, at : at + 256].T.astype(BF16)
            out_ref[at : at + 256, n * tokens : (n + 1) * tokens] = block


def run_turn_norm(scal, mine, other, gain):
    tokens, width = mine.shape
    outs = [shape(width, 2 * tokens, dtype=BF16)]
    return call(turn_norm_body, outs, "norm_turned", cost=WORK, alone=True)(scal, mine, other, gain)[0]


def run_turn(scal, mine, other):
    tokens, width = mine.shape
    outs = [shape(width, 2 * tokens, dtype=BF16)]
    return call(turn_body, outs, "turned", alone=True, cost=WORK)(scal, mine, other)[0]


def parts_of(turned_ref, scal_ref, along_x, step):
    row, col, core = scal_ref[3], scal_ref[4], scal_ref[5]
    rows = turned_ref.shape[0] // (2 * SIDE * SIDE)
    pieces = []
    for at in range(SIDE):
        if along_x:
            place = (at * SIDE + lax.rem(col + step, SIDE)) * 2 + core
        else:
            place = (lax.rem(row + step, SIDE) * SIDE + at) * 2 + core
        pieces.append(turned_ref[pl.ds(pl.multiple_of(place * rows, rows), rows), :])
    return jnp.concatenate(pieces, axis=0)


def put(ref, value, start):
    rows = value.shape[0] // SIDE
    for at in range(SIDE):
        ref[at, :, start : start + value.shape[1]] = value[at * rows : (at + 1) * rows]


def send_parts(outs, along_x, scal_ref, products):
    keep_ref, on_ref, back_ref, held_ref = outs
    half = keep_ref.shape[2] // 2
    low_to = {1: held_ref.at[0], 2: on_ref.at[1], 3: back_ref.at[0]}
    high_to = {1: on_ref.at[0], 2: back_ref.at[1], 3: held_ref.at[1]}
    for step in range(SIDE):
        for turned_ref, columns, first in products:
            value = dg(parts_of(turned_ref, scal_ref, along_x, step), columns, False, False)
            last = first + columns.shape[1]
            if step == 0:
                put(keep_ref, value, first)
                continue
            if first < half:
                stop = min(last, half)
                put(low_to[step], value[:, : stop - first], first)
            if last > half:
                begin = max(first, half)
                put(high_to[step], value[:, begin - first :], begin - half)


def part_shapes(rows, *widths):
    outs = []
    for wide in widths:
        outs += [shape(SIDE, rows, wide)] + [shape(2, SIDE, rows, wide // 2)] * 3
    return outs


def w1_body(scal_ref, mine_ref, other_ref, d_ref, *rest):
    outs, (cols_ref, h_ref) = rest[:8], rest[8:]
    tokens = mine_ref.shape[0]
    wide = cols_ref.shape[1]
    cut = wide // 2
    up_end = 2 * (wide // 3)
    for n, ref in enumerate((mine_ref, other_ref)):
        spot = slice(n * tokens, (n + 1) * tokens)
        cols_ref[spot, :] = ref[:, :wide].astype(BF16)
        for at in range(0, h_ref.shape[0], 256):
            h_ref[at : at + 256, spot] = ref[:, wide + at : wide + at + 256].T.astype(BF16)
    send_parts(outs[:4], True, scal_ref, [(h_ref, cols_ref[:, :cut], 0)])
    whole_now(*outs[:4])
    send_parts(
        outs[4:],
        False,
        scal_ref,
        [(h_ref, cols_ref[:, cut:up_end], 0), (d_ref, cols_ref[:, up_end:], up_end - cut)],
    )
    whole_now(*outs[4:])


def run_w1(*operands):
    width = operands[3].shape[0]
    tokens, wide = operands[1].shape
    wide = wide - width
    scratch = [pltpu.VMEM((2 * tokens, wide), BF16), pltpu.VMEM((width, 2 * tokens), BF16)]
    return call(
        w1_body, part_shapes(width // 32, wide // 2, wide // 2), "ffn_weight_sums", scratch,
        late=(2, 3), early=range(8), cost=WORK, alone=True
    )(*operands)


def w2_body(
    scal_ref, low_ref, low_other_ref, dq_ref, dq_other_ref, n_ref, n_other_ref, h_ref, d_ref, *rest
):
    outs, cols_ref = rest[:8], rest[8]
    tokens, late = low_ref.shape
    cut = outs[0].shape[2]
    query_end = late + WIDE
    sides = ((low_ref, dq_ref, n_ref), (low_other_ref, dq_other_ref, n_other_ref))
    for n, (low, dq, normed) in enumerate(sides):
        spot = slice(n * tokens, (n + 1) * tokens)
        cols_ref[spot, :late] = low[...].astype(BF16)
        cols_ref[spot, late:query_end] = dq[...].astype(BF16)
        cols_ref[spot, query_end:] = normed[...].astype(BF16)
    send_parts(outs[:4], True, scal_ref, [(h_ref, cols_ref[:, :cut], 0)])
    whole_now(*outs[:4])
    send_parts(
        outs[4:],
        False,
        scal_ref,
        [(h_ref, cols_ref[:, cut:query_end], 0), (d_ref, cols_ref[:, query_end:], query_end - cut)],
    )


def run_w2(*operands):
    tokens, late = operands[1].shape
    width = operands[7].shape[0]
    wide = late + 2 * WIDE
    scratch = [pltpu.VMEM((2 * tokens, wide), BF16)]
    return call(
        w2_body, part_shapes(width // 32, 2 * WIDE, wide - 2 * WIDE), "head_weight_sums", scratch, late=(7, 8), early=range(8), alone=True
    )(*operands)


def relay_body(scal_ref, *refs):
    count = len(refs) // 5
    ins, outs = refs[: 3 * count], refs[3 * count :]
    for n in range(count):
        held_ref, on_ref, back_ref = ins[3 * n : 3 * n + 3]
        outs[2 * n][...] = held_ref[0] + on_ref[1]
        outs[2 * n + 1][...] = held_ref[1] + back_ref[1]


def run_relay(scal, *pieces):
    outs = [shape(*one.shape[1:]) for one in pieces[::3] for _ in range(2)]
    return call(relay_body, outs, "relay_sums", cost=WORK, alone=True)(scal, *pieces)


def folded(refs, at):
    keep_ref, on_ref, back_ref, on_2_ref, back_2_ref = refs
    half = keep_ref.shape[2] // 2
    low = keep_ref[at, :, :half] + on_2_ref[at] + back_ref[0, at]
    high = keep_ref[at, :, half:] + on_ref[0, at] + back_2_ref[at]
    return low, high


def fold_1_body(scal_ref, *refs):
    target = refs[5]
    half = target.shape[2] // 2
    for at in range(SIDE):
        low, high = folded(refs[:5], at)
        target[at, :, :half] = low
        target[at, :, half:] = high


def run_fold_1(scal, pieces):
    outs = [shape(*pieces[0].shape)]
    return call(fold_1_body, outs, "fold_sums", cost=LIGHT, alone=True)(scal, *pieces)[0]


def fold_2_body(scal_ref, *refs):
    outs = refs[10:]
    for n in range(2):
        for step in range(SIDE):
            target = outs[SIDE * n + step]
            half = target.shape[1] // 2
            low, high = folded(refs[5 * n : 5 * n + 5], lax.rem(scal_ref[3 + n] + step, SIDE))
            target[:, :half] = low
            target[:, half:] = high


def run_fold_2(scal, pieces):
    outs = [shape(*pieces[at].shape[1:]) for at in (0, 5) for _ in range(SIDE)]
    return call(fold_2_body, outs, "fold_parts", cost=HEAVY, alone=True)(scal, *pieces)


def end_1_body(scal_ref, one_ref, two_ref, gate_ref, up_ref, down_ref):
    units = gate_ref.shape[1]
    rest = one_ref.shape[1] - units
    gate_ref[...] = one_ref[:, :units]
    up_ref[:, :rest] = one_ref[:, units:]
    up_ref[:, rest:] = two_ref[:, : units - rest]
    down_ref[...] = two_ref[:, units - rest :]


def run_end_1(scal, one, two):
    rows, wide = one.shape
    outs = [shape(rows, 2 * wide // 3)] * 3
    return call(end_1_body, outs, "ffn_gradients", alone=True)(scal, one, two)


def end_2_body(scal_ref, *refs):
    first, second, outs = refs[:4], refs[4:8], refs[8:]
    key_ref, value_ref, path_ref, beta_ref, query_ref, out_ref = outs
    one = (first[0][...] + first[1][...]) + (first[2][...] + first[3][...])
    two = (second[0][...] + second[1][...]) + (second[2][...] + second[3][...])
    key_ref[...] = one[:, :WIDE]
    value_ref[...] = one[:, WIDE:]
    path_ref[...] = two[:, :WIDE]
    beta_ref[...] = two[:, WIDE : WIDE + HW]
    query_ref[...] = two[:, WIDE + HW : 2 * WIDE + HW]
    out_ref[...] = two[:, 2 * WIDE + HW :]


def run_end_2(scal, pieces):
    rows = pieces[0].shape[0]
    outs = [shape(rows, WIDE)] * 3 + [shape(rows, HW)] + [shape(rows, WIDE)] * 2
    return call(end_2_body, outs, "head_gradients")(scal, *pieces)


def swap(value):
    return lax.ppermute(value, "c", [(0, 1), (1, 0)])


def shift(value, axis, step):
    return lax.ppermute(value, axis, [(i, (i + step) % SIDE) for i in range(SIDE)])


def exchange(pieces, first_axis, second_axis):
    moved = {}
    for step in (2, 1, 3):
        moved[step] = shift(pieces[step], first_axis, step)
        moved[4 + step] = shift(pieces[4 + step], second_axis, step)
    return [pieces[0], moved[1], moved[2], moved[3], pieces[4], moved[5], moved[6], moved[7]]


def send_on(pieces, axis):
    return shift(pieces[1], axis, 1), shift(pieces[2], axis, SIDE - 1)


def relay_on(pieces, came, axis, scal):
    relayed = run_relay(scal, pieces[3], *came)
    on, back = shift(relayed[0], axis, 1), shift(relayed[1], axis, SIDE - 1)
    return relayed, [pieces[0], *came, on, back]


def relay_both(pieces, came, scal):
    relayed = run_relay(scal, pieces[3], *came[0], pieces[7], *came[1])
    out = []
    for n, axis in enumerate(("x", "y")):
        on, back = shift(relayed[2 * n], axis, 1), shift(relayed[2 * n + 1], axis, SIDE - 1)
        out += [pieces[4 * n], *came[n], on, back]
    return relayed, out


def trade(value, axis):
    return lax.all_to_all(value, axis, 0, 0)


def after(value, *others):
    return lax.optimization_barrier((value,) + others)[0]


def local(
    block_input, gain_in, w_query, w_key, w_value, w_path, w_beta, w_out,
    gain_mid, w_gate, w_up, w_down, out_grad, lengths,
):
    tokens, width = block_input.shape
    row, col, core = (lax.axis_index(name) for name in CTX)
    rank = lax.axis_index("z")
    start = lax.axis_index(CTX) * tokens
    scal = jnp.stack([start, lengths[0], lengths[1], row, col, core, rank]).astype(jnp.int32)
    unity = (lengths[0] > 0).astype(F32)
    gain_1, gain_2 = gain_in, gain_mid
    heads_w = (w_query, w_key, w_value, w_path, w_beta.T)

    k, v, w, aux, inv, kp, b, kt, tu = run_a1(scal, block_input, gain_1, *heads_w[1:])
    both = lax.all_gather(tu, "c", axis=0)
    spread = run_s1(scal, both)
    along_x = trade(spread, "x")
    out_half = lax.dynamic_slice_in_dim(after(w_out, both), core * (width // 2), width // 2, 1)
    out_mine = lax.all_gather(out_half.astype(F32), "z", axis=0)
    grad_other = swap(after(out_grad, tu))
    input_other = swap(after(block_input, tu))
    h1_turned = run_turn_norm(scal, after(block_input, spread), input_other, gain_1)
    grad_turned = run_turn(scal, after(out_grad, spread), grad_other)
    along_x = after(along_x, h1_turned, grad_turned)
    t_x, u_x, spread = run_s2(scal, along_x, swap(along_x))
    along_y = trade(spread, "y")
    q, aux_q, c, sc, qt, inside = run_a2(
        scal, block_input, gain_1, w_query, after(k, spread), v, w, inv, kp
    )
    along_y = after(along_y, inside)
    t_y, mixed, normed, spread, carried = run_s3(
        scal, along_y, swap(along_y), t_x, u_x, both, inside, qt
    )
    normed_all = trade(spread, "z")
    out_mine = after(out_mine, spread)
    out_mine_low = (out_mine * unity).astype(BF16)
    out_other_low = (swap(out_mine) * unity).astype(BF16)
    normed_all = after(normed_all, out_mine_low, out_other_low)
    middle, sent, second_part, down_part = run_ffn(
        scal, normed_all, out_mine_low, out_other_low, block_input, gain_2, out_grad,
        w_gate, w_up, w_down,
    )

    second = trade(second_part.reshape(RANKS, PART, width), "z")
    ffn_pieces = list(run_w1(scal, sent, swap(sent), grad_turned))
    middle_part = lax.dynamic_slice_in_dim(after(middle, sent), rank * PART, PART, 0)
    grad_part = lax.dynamic_slice_in_dim(after(out_grad, sent), rank * PART, PART, 0)
    second = after(second, middle_part, grad_part, *ffn_pieces)
    along_y = send_on(ffn_pieces[4:], "y")
    d_middle, attn, gain_mid_part, d_normed = run_k5(
        scal, second, middle_part, grad_part, gain_2, out_mine_low, out_other_low
    )
    attn_all = lax.all_gather(attn, "z", axis=0, tiled=True)
    d_normed = trade(d_normed, "z").reshape(tokens, WIDE)
    down_sum = lax.psum(after(down_part, d_normed), "z")
    dm, state_grad = run_b1(scal, d_normed, mixed, qt)
    pair = lax.all_gather(state_grad, "c", axis=0)
    g_1, spread = run_t1(scal, pair, both)
    g_x = trade(spread, "x")
    dq, dk, dv, dw, dkp, xc = run_b2(
        scal, after(dm, spread), carried, q, k, v, w, aux_q, inv, kp, c, sc
    )
    g_x = after(g_x, dq)
    spread = run_t2(scal, g_x, t_x)
    g_y = trade(spread, "y")
    attn_all = after(attn_all, spread)
    attn_turned = run_turn(scal, attn_all, swap(attn_all))
    ffn_pieces[1] = after(ffn_pieces[1], spread)
    along_x = send_on(ffn_pieces[:4], "x")
    along_y = (after(along_y[0], spread), along_y[1])
    relayed, ffn_two = relay_on(ffn_pieces[4:], along_y, "y", scal)
    g_y = after(g_y, attn_turned, *relayed)
    later = run_t3(scal, g_y, g_x, t_y, t_x, both, g_1)
    later = lax.all_gather(later, "c", axis=0)
    block_output = middle + down_sum

    low = run_b3(scal, later, carried, k, v, w, aux, inv, kp, b, kt, dk, dv, dw, dkp, xc)
    low_other = swap(low)
    along_x = (after(along_x[0], low), along_x[1])
    relayed, ffn_one = relay_on(ffn_pieces[:4], along_x, "x", scal)
    ffn_two[0] = after(ffn_two[0], low)
    ffn_two = run_fold_1(scal, ffn_two)
    low_other = after(low_other, relayed[0], ffn_two)
    ffn_two = lax.psum_scatter(ffn_two, "x", scatter_dimension=0)
    head_pieces = run_w2(
        scal, low, low_other, dq, swap(dq), normed, swap(normed), h1_turned, attn_turned
    )
    came = [send_on(head_pieces[:4], "x"), send_on(head_pieces[4:], "y")]
    first_part = run_b4(
        scal, block_input, gain_mid_part, dq, after(low, head_pieces[0]), *heads_w
    )
    first = trade(first_part, "z")
    ffn_one[0] = after(ffn_one[0], head_pieces[0])
    ffn_one = run_fold_1(scal, ffn_one)
    came[0] = (after(came[0][0], first_part, ffn_one), came[0][1])
    ffn_one = lax.psum_scatter(ffn_one, "y", scatter_dimension=0)
    relayed, head_pieces = relay_both(head_pieces, came, scal)
    input_part, gains = run_n(scal, after(first, relayed[0]), block_input, gain_1, d_middle)
    input_grad = lax.all_gather(input_part, "z", axis=0, tiled=True)
    head_pieces[0] = after(head_pieces[0], input_part, block_output)
    head_pieces = run_fold_2(scal, head_pieces)
    gains = jnp.swapaxes(after(gains, head_pieces[0])[:2].reshape(2, 32, width // 32), 0, 1)
    gains = trade(gains, CTX)
    head_pieces = exchange(head_pieces, "y", "x")
    ffn_two = after(ffn_two, head_pieces[2])
    gate_out, up_out, down_out = run_end_1(scal, ffn_one, ffn_two)
    gains = jnp.sum(after(gains, gate_out), axis=0)
    input_grad = input_grad * unity
    head_pieces[6] = after(head_pieces[6], input_grad)
    key_out, value_out, path_out, beta_out, query_out, out_out = run_end_2(scal, head_pieces)
    return (
        block_output, input_grad, gains[0], query_out, key_out, value_out, path_out,
        beta_out[:, : w_beta.shape[1]], out_out.T, gains[1], gate_out, up_out, down_out.T,
    )


def solution(mesh):
    fine = Mesh(mesh.devices.reshape(SIDE, SIDE, 2, RANKS), ("y", "x", "c", "z"))
    tokens, heads, whole = P(CTX, None), P(None, "z"), P()
    in_specs = (
        tokens, whole, heads, heads, heads, heads, heads, P("z", None),
        whole, heads, heads, P("z", None), tokens, whole,
    )
    weight = P(CTX, "z")
    out_specs = (
        tokens, tokens, P(CTX), weight, weight, weight, weight, weight,
        P("z", CTX), P(CTX), weight, weight, P("z", CTX),
    )
    return jax.shard_map(local, mesh=fine, in_specs=in_specs, out_specs=out_specs, check_vma=False)
```

```python
import jax
import jax.numpy as jnp
from jax import lax
from jax.experimental import pallas as pl
from jax.experimental.pallas import tpu as pltpu
from jax.sharding import Mesh
from jax.sharding import PartitionSpec as P

EPSILON = 1e-06
HEAD_EPSILON = 0.01
F32 = jnp.float32
BF16 = jnp.bfloat16
HEADS = 3
HW = 128
LEN = 256
RANKS = 4
PART = LEN // RANKS
SIDE = 4
CTX = ("y", "x", "c")


def split(value):
    high = value.astype(BF16)
    return high, (value - high.astype(F32)).astype(BF16)


def dg(left, right, ta, tb):
    dims = (((0 if ta else 1,), (1 if tb else 0,)), ((), ()))
    return lax.dot_general(left, right, dims, preferred_element_type=F32)


def mm(left, right, ta=False, tb=False):
    left = left if isinstance(left, tuple) else split(left)
    right = right if isinstance(right, tuple) else split(right)
    return dg(left[0], right[0], ta, tb) + (
        dg(left[0], right[1], ta, tb) + dg(left[1], right[0], ta, tb)
    )


def iota(shape, dim):
    return lax.broadcasted_iota(jnp.int32, shape, dim)


def cols(head):
    return slice(head * HW, (head + 1) * HW)


def segments(spot, scal):
    second = scal[1]
    third = second + scal[2]
    return (spot >= second).astype(jnp.int32) + (spot >= third).astype(jnp.int32)


def small_inverses(scaled):
    row = iota((HW, HW), 0)
    lane = iota((HW, HW), 1)
    same = (row // 8) == (lane // 8)
    packed = []
    for one in scaled:
        for half in range(2):
            block = jnp.where(same, one[half * HW : (half + 1) * HW, half * HW : (half + 1) * HW], 0.0)
            packed.append(jnp.sum(block.reshape(HW // 8, 8, HW), axis=0))
    count = len(packed)
    high, low = split(jnp.concatenate(packed, axis=0))
    lane_8 = iota((8, HW), 1) % 8
    spread = {}
    for k in range(1, 8):
        unit = ((row // 8 == lane // 8) & (row % 8 == k)).astype(BF16)
        both = dg(high, unit, False, False) + dg(low, unit, False, False)
        spread[k] = both.reshape(count, 8, HW)
    rows = {}
    for i in range(7, -1, -1):
        value = jnp.broadcast_to((lane_8[:1] == i).astype(F32)[None], (count, 1, HW))
        for k in range(i + 1, 8):
            value = value - spread[k][:, i : i + 1, :] * rows[k]
        rows[i] = value
    done = jnp.concatenate([rows[i] for i in range(8)], axis=1)
    out = []
    zero = jnp.zeros((HW, HW), F32)
    for head in range(count // 2):
        halves = [
            jnp.where(same, jnp.concatenate([done[2 * head + half]] * (HW // 8), axis=0), 0.0)
            for half in range(2)
        ]
        out.append(
            jnp.concatenate(
                [
                    jnp.concatenate([halves[0], zero], axis=1),
                    jnp.concatenate([zero, halves[1]], axis=1),
                ],
                axis=0,
            )
        )
    return out


def upper_rows(value, width):
    return jnp.concatenate(
        [value[at : at + width] for at in range(0, value.shape[0], 2 * width)], axis=0
    )


def put_upper(value, upper, width):
    pieces = []
    for n, at in enumerate(range(0, value.shape[0], 2 * width)):
        pieces.append(upper[n * width : (n + 1) * width])
        pieces.append(value[at + width : at + 2 * width])
    return jnp.concatenate(pieces, axis=0)


def inverses(scaled):
    out = small_inverses(scaled)
    row = iota((LEN, LEN), 0)
    lane = iota((LEN, LEN), 1)
    width = 8
    while width < LEN:
        pair = (row // (2 * width) == lane // (2 * width)) & (row // width < lane // width)
        link = [upper_rows(jnp.where(pair, one, 0.0), width) for one in scaled]
        parts = [split(one) for one in out]
        first = [mm(a, b) for a, b in zip(link, parts)]
        empty = jnp.zeros((LEN, LEN), F32)
        wide = [put_upper(empty, one, width) for one in first]
        tops = [
            (upper_rows(a, width), upper_rows(b, width)) for a, b in parts
        ]
        second = [mm(a, b) for a, b in zip(tops, wide)]
        out = [
            put_upper(one, upper_rows(one, width) - new, width) for one, new in zip(out, second)
        ]
        width *= 2
    return out


def unit_rows(value):
    scale = lax.rsqrt(jnp.sum(value * value, axis=-1, keepdims=True) + EPSILON)
    return value * scale, scale


def first_norm(x_ref, gain_ref):
    x = x_ref[...]
    scale = lax.rsqrt(jnp.mean(x * x, axis=-1, keepdims=True) + EPSILON)
    return (x * scale * gain_ref[...].astype(F32).reshape(1, -1)).astype(BF16)


def a1_body(
    scal_ref, x_ref, gain_ref, wk_ref, wv_ref, ww_ref, wb_ref,
    k_ref, v_ref, w_ref, aux_ref, inv_ref, kp_ref, b_ref, kt_ref, tu_ref,
):
    h1 = first_norm(x_ref, gain_ref)
    start = scal_ref[0]
    token = iota((LEN, 1), 0) + start
    segment = segments(token, scal_ref)
    end_segment = segments(jnp.full((1, 1), LEN - 1, jnp.int32) + start, scal_ref)
    before = start - 1
    before_segment = jnp.where(start == 0, -1, segments(jnp.full((1, 1), 0, jnp.int32) + before, scal_ref))
    last = (segment == end_segment).astype(F32)
    carry_all = (end_segment == before_segment).astype(F32)
    row = iota((LEN, LEN), 0)
    lane = iota((LEN, LEN), 1)
    later = row < lane
    beta = 1.0 + jax.nn.sigmoid(dg(h1, wb_ref[...], False, True))
    beta_rows = 1.0 + jax.nn.sigmoid(dg(wb_ref[...], h1, False, True))
    pr = dg(h1, ww_ref[...], False, False)
    kr = dg(h1, wk_ref[...], False, False)
    w_all, k_all, aux = [], [], []
    for head in range(HEADS):
        w, w_scale = unit_rows(pr[:, cols(head)])
        k, k_scale = unit_rows(kr[:, cols(head)])
        w_ref[:, cols(head)] = w
        k_ref[:, cols(head)] = k
        w_all.append(w)
        k_all.append(k)
        aux.append((w_scale, k_scale))
    w_split = [split(w) for w in w_all]
    k_split = [split(k) for k in k_all]
    scaled = [
        jnp.where(later, mm(w_split[h], w_split[h], tb=True), 0.0) * beta[:, h : h + 1]
        for h in range(HEADS)
    ]
    inverse = [
        one * beta_rows[h : h + 1, :] for h, one in enumerate(inverses(scaled))
    ]
    vr = dg(h1, wv_ref[...], False, False)
    v_ref[...] = vr
    lane_aux = iota((LEN, HW), 1)
    packed = jnp.zeros((LEN, HW), F32)
    eye = (iota((HW, HW), 0) == iota((HW, HW), 1)).astype(F32)
    for head in range(HEADS):
        spots = (
            (head, beta[:, head : head + 1]),
            (16 + head, aux[head][1]),
            (24 + head, aux[head][0]),
        )
        for at, value in spots:
            packed = jnp.where(lane_aux == at, value, packed)
        inv_ref[head] = inverse[head]
        inv_split = split(inverse[head])
        folded = mm(inv_split, w_split[head])
        b_ref[:, cols(head)] = folded
        folded_split = split(folded)
        kp = jnp.where(later, mm(k_split[head], w_split[head], tb=True), 0.0)
        kp_ref[head] = kp
        kt = k_all[head] - mm(kp, folded_split)
        kt_ref[:, cols(head)] = kt
        tu_ref[0, head] = carry_all * (eye - mm(w_split[head], folded_split, ta=True))
        tu_ref[1, head] = mm(vr[:, cols(head)], kt * last, ta=True)
    aux_ref[...] = packed


def shape(*dims, dtype=F32):
    return jax.ShapeDtypeStruct(dims, dtype)


MIB = 1024 * 1024
SLACK = 10 * MIB
LIGHT = pl.CostEstimate(flops=10**4, bytes_accessed=10**4, transcendentals=0)
HEAVY = pl.CostEstimate(flops=10**12, bytes_accessed=10**8, transcendentals=0)
WORK = pl.CostEstimate(flops=8 * 10**9, bytes_accessed=10**7, transcendentals=0)


def size_of(*arrays):
    total = 0
    for one in arrays:
        count = one.dtype.itemsize
        for extent in one.shape:
            count *= extent
        total += count
    return total


class Late:
    def __init__(self, copy, buffer):
        self.copy, self.buffer, self.shape = copy, buffer, buffer.shape
        copy.start()

    def here(self):
        if self.copy is not None:
            self.copy.wait()
            self.copy = None
        return self.buffer

    def __getitem__(self, spot):
        return self.here()[spot]


class Early:
    def __init__(self, copy, buffer):
        self.copy, self.buffer, self.shape, self.sent = copy, buffer, buffer.shape, False

    def __getitem__(self, spot):
        return self.buffer[spot]

    def __setitem__(self, spot, value):
        self.buffer[spot] = value

    @property
    def at(self):
        return self.buffer.at


def whole_now(*refs):
    for ref in refs:
        if isinstance(ref, Early):
            ref.copy.start()
            ref.sent = True


def call(body, outs, name, scratch=(), late=(), early=(), cost=LIGHT, alone=False):
    def run(*operands):
        count = len(operands)
        moved = sorted(late)
        leaving = sorted(early)
        vmem = pl.BlockSpec(memory_space=pltpu.VMEM)
        anywhere = pl.BlockSpec(memory_space=pl.ANY)
        held = [operands[at] for at in moved] + [outs[at] for at in leaving]
        buffers = [pltpu.VMEM(one.shape, one.dtype) for one in held]
        marks = [pltpu.SemaphoreType.DMA((len(buffers),))] if buffers else []

        def wrapped(*refs):
            refs = list(refs)
            own = len(refs) - len(buffers) - len(marks)
            for n, at in enumerate(moved):
                copy = pltpu.make_async_copy(refs[at], refs[own + n], refs[-1].at[n])
                refs[at] = Late(copy, refs[own + n])
            for n, at in enumerate(leaving, len(moved)):
                copy = pltpu.make_async_copy(refs[own + n], refs[count + at], refs[-1].at[n])
                refs[count + at] = Early(copy, refs[own + n])
            body(*refs[:own])
            for at in moved:
                refs[at].here()
            for at in leaving:
                if not refs[count + at].sent:
                    refs[count + at].copy.start()
            for at in leaving:
                refs[count + at].copy.wait()

        need = size_of(*operands, *outs, *scratch) + SLACK
        return pl.pallas_call(
            wrapped,
            out_shape=outs,
            in_specs=[pl.BlockSpec(memory_space=pltpu.SMEM)]
            + [anywhere if at in moved else vmem for at in range(1, count)],
            out_specs=[anywhere if at in leaving else vmem for at in range(len(outs))],
            scratch_shapes=list(scratch) + buffers + marks,
            name=name,
            cost_estimate=cost,
            compiler_params=pltpu.CompilerParams(vmem_limit_bytes=56 * MIB if alone else need),
        )(*operands)

    return run


WIDE = HEADS * HW


def run_a1(*operands):
    outs = [
        shape(LEN, WIDE), shape(LEN, WIDE), shape(LEN, WIDE),
        shape(LEN, HW),
        shape(HEADS, LEN, LEN), shape(HEADS, LEN, LEN),
        shape(LEN, WIDE), shape(LEN, WIDE),
        shape(2, HEADS, HW, HW),
    ]
    return call(a1_body, outs, "local_parts", alone=True)(*operands)


def a2_body(
    scal_ref, x_ref, gain_ref, wq_ref, k_ref, v_ref, w_ref, inv_ref, kp_ref,
    q_ref, aux_ref, c_ref, sc_ref, qt_ref, in_ref,
):
    start = scal_ref[0]
    segment = segments(iota((LEN, LEN), 0) + start, scal_ref)
    segment_t = segments(iota((LEN, LEN), 1) + start, scal_ref)
    row = iota((LEN, LEN), 0)
    lane = iota((LEN, LEN), 1)
    up_to = row <= lane
    seen = up_to & (segment == segment_t)
    qr = dg(first_norm(x_ref, gain_ref), wq_ref[...], False, False)
    lane_aux = iota((LEN, HW), 1)
    packed = jnp.zeros((LEN, HW), F32)
    for head in range(HEADS):
        q, q_scale = unit_rows(qr[:, cols(head)])
        q_ref[:, cols(head)] = q
        packed = jnp.where(lane_aux == head, q_scale, packed)
        q_split = split(q)
        w_split = split(w_ref[:, cols(head)])
        pq = jnp.where(up_to, mm(w_split, q_split, tb=True), 0.0)
        c = mm(inv_ref[head], pq)
        c_ref[head] = c
        c_split = split(c)
        qt_ref[:, cols(head)] = q - mm(c_split, w_split, ta=True)
        scores = mm(k_ref[:, cols(head)], q_split, tb=True) - mm(kp_ref[head], c_split)
        scores = jnp.where(seen, scores, 0.0)
        sc_ref[head] = scores
        in_ref[:, cols(head)] = mm(scores, v_ref[:, cols(head)], ta=True)
    aux_ref[...] = packed


def run_a2(*operands):
    outs = [
        shape(LEN, WIDE), shape(LEN, HW),
        shape(HEADS, LEN, LEN), shape(HEADS, LEN, LEN), shape(LEN, WIDE), shape(LEN, WIDE),
    ]
    return call(a2_body, outs, "inside_parts", alone=True, cost=WORK)(*operands)


def carry_of(start, scal_ref):
    token = iota((LEN, 1), 0) + start
    before = jnp.full((1, 1), 0, jnp.int32) + (start - 1)
    before_segment = jnp.where(start == 0, -1, segments(before, scal_ref))
    return (segments(token, scal_ref) == before_segment).astype(F32)


def pair_of(ref, core, head):
    return jnp.concatenate([ref[0, core, head], ref[1, core, head]], axis=0)


def b1_body(scal_ref, dn_ref, mixed_ref, qt_ref, dm_ref, sg_ref):
    carry = carry_of(scal_ref[0], scal_ref)
    for head in range(HEADS):
        mixed = mixed_ref[:, cols(head)]
        dn = dn_ref[:, cols(head)]
        scale = lax.rsqrt(jnp.mean(mixed * mixed, axis=-1, keepdims=True) + HEAD_EPSILON)
        drift = jnp.mean(dn * mixed, axis=-1, keepdims=True) * (scale * scale)
        dm = scale * (dn - mixed * drift)
        dm_ref[:, cols(head)] = dm
        sg_ref[head] = mm(dm * carry, qt_ref[:, cols(head)], ta=True)


def run_b1(*operands):
    outs = [shape(LEN, WIDE), shape(HEADS, HW, HW)]
    return call(b1_body, outs, "state_gradient")(*operands)


def unit_pull(unit, scale, grad):
    return scale * (grad - unit * jnp.sum(unit * grad, axis=-1, keepdims=True))


def b2_body(
    scal_ref, dm_ref, carried_ref, q_ref, k_ref, v_ref, w_ref, aux_ref, inv_ref, kp_ref,
    c_ref, sc_ref,
    dq_ref, dk_ref, dv_ref, dw_ref, dkp_ref, xc_ref,
):
    start = scal_ref[0]
    carry = carry_of(start, scal_ref)
    row = iota((LEN, LEN), 0)
    lane = iota((LEN, LEN), 1)
    up_to = row <= lane
    seen = up_to & (
        segments(row + start, scal_ref) == segments(lane + start, scal_ref)
    )
    for head in range(HEADS):
        q = q_ref[:, cols(head)]
        q_split = split(q)
        w_split = split(w_ref[:, cols(head)])
        k_split = split(k_ref[:, cols(head)])
        c_split = split(c_ref[head])
        kp_split = split(kp_ref[head])
        dm = dm_ref[:, cols(head)]
        dm_split = split(dm)
        dqt = mm(dm * carry, carried_ref[head])
        dqt_split = split(dqt)
        ds = jnp.where(seen, mm(v_ref[:, cols(head)], dm_split, tb=True), 0.0)
        ds_split = split(ds)
        dv_ref[:, cols(head)] = mm(sc_ref[head], dm_split)
        dk = mm(ds_split, q_split)
        dq = dqt + mm(ds_split, k_split, ta=True)
        dkp_ref[head] = mm(ds_split, c_split, tb=True)
        dc = mm(kp_split, ds_split, ta=True) + mm(w_split, dqt_split, tb=True)
        dw = mm(c_split, dqt_split)
        x = mm(inv_ref[head], dc, ta=True)
        xc_ref[head] = mm(x, c_split, tb=True)
        dpq_split = split(jnp.where(up_to, x, 0.0))
        dw_ref[:, cols(head)] = dw + mm(dpq_split, q_split)
        dq = dq - mm(dpq_split, w_split, ta=True)
        dk_ref[:, cols(head)] = dk
        scale = aux_ref[:, head : head + 1]
        dq_ref[:, cols(head)] = unit_pull(q, scale, dq).astype(BF16).astype(F32)


def run_b2(*operands):
    outs = [
        shape(LEN, WIDE), shape(LEN, WIDE), shape(LEN, WIDE), shape(LEN, WIDE),
        shape(HEADS, LEN, LEN), shape(HEADS, LEN, LEN),
    ]
    return call(b2_body, outs, "inside_gradients", alone=True, cost=WORK)(*operands)


def b3_body(
    scal_ref, states_ref, carried_ref, k_ref, v_ref, w_ref, aux_ref,
    inv_ref, kp_ref, b_ref, kt_ref, dk_ref, dv_ref, dw_ref, dkp_ref, xc_ref,
    low_ref,
):
    start = scal_ref[0]
    core = scal_ref[5]
    segment = segments(iota((LEN, 1), 0) + start, scal_ref)
    end_segment = segments(jnp.full((1, 1), LEN - 1, jnp.int32) + start, scal_ref)
    before = jnp.full((1, 1), 0, jnp.int32) + (start - 1)
    before_segment = jnp.where(start == 0, -1, segments(before, scal_ref))
    last = (segment == end_segment).astype(F32)
    carry_all = (end_segment == before_segment).astype(F32)
    row = iota((LEN, LEN), 0)
    lane = iota((LEN, LEN), 1)
    later_mask = row < lane
    lane_aux = iota((LEN, HW), 1)
    d_beta = jnp.zeros((LEN, HW), F32)
    for head in range(HEADS):
        later = pair_of(states_ref, core, head)
        later_split = split(later)
        dt_split = split(carry_all * mm(carried_ref[head], later_split, ta=True))
        w = w_ref[:, cols(head)]
        w_split = split(w)
        k = k_ref[:, cols(head)]
        v = v_ref[:, cols(head)]
        b_split = split(b_ref[:, cols(head)])
        kp_split = split(kp_ref[head])
        dv = dv_ref[:, cols(head)] + last * mm(kt_ref[:, cols(head)], later_split, tb=True)
        dkt = last * mm(v, later_split)
        dkt_split = split(dkt)
        db = mm(w_split, dt_split) + mm(kp_split, dkt_split, ta=True)
        y = mm(inv_ref[head], db, ta=True)
        y_split = split(y)
        dw = dw_ref[:, cols(head)] + mm(b_split, dt_split, tb=True) + y
        dkp = jnp.where(later_mask, dkp_ref[head] + mm(dkt_split, b_split, tb=True), 0.0)
        dkp_split = split(dkp)
        dk = dk_ref[:, cols(head)] + dkt - mm(dkp_split, w_split)
        dw = dw + mm(dkp_split, split(k), ta=True)
        dm = xc_ref[head] + mm(y_split, b_split, tb=True)
        dn_split = split(jnp.where(later_mask, dm, 0.0))
        dw = mm(dn_split, w_split) + mm(dn_split, w_split, ta=True) - dw
        diagonal = jnp.sum(jnp.where(row == lane, dm, 0.0), axis=-1, keepdims=True)
        beta = aux_ref[:, head : head + 1]
        sig = beta - 1.0
        dbl = -diagonal / (beta * beta) * sig * (1.0 - sig)
        d_beta = jnp.where(lane_aux == head, dbl, d_beta)
        low_ref[:, cols(head)] = unit_pull(k, aux_ref[:, 16 + head : 17 + head], dk).astype(BF16).astype(F32)
        low_ref[:, WIDE + head * HW : WIDE + (head + 1) * HW] = dv.astype(BF16).astype(F32)
        low_ref[:, 2 * WIDE + head * HW : 2 * WIDE + (head + 1) * HW] = unit_pull(
            w, aux_ref[:, 24 + head : 25 + head], dw
        ).astype(BF16).astype(F32)
    low_ref[:, 3 * WIDE :] = d_beta.astype(BF16).astype(F32)


def run_b3(*operands):
    outs = [shape(LEN, 3 * WIDE + HW)]
    return call(b3_body, outs, "late_gradients", alone=True)(*operands)[0]


def b4_body(
    scal_ref, x_ref, gain_mid_ref, dq_ref, low_ref, wq_ref, wk_ref, wv_ref, ww_ref, wb_ref, dh_ref
):
    total = dg(dq_ref[...].astype(BF16), wq_ref[...], False, True)
    for at, ref in enumerate((wk_ref, wv_ref, ww_ref)):
        low = low_ref[:, at * WIDE : at * WIDE + ref.shape[1]].astype(BF16)
        total = total + dg(low, ref[...], False, True)
    beta_cols = wb_ref[...].astype(F32)
    for head in range(HEADS):
        at = 3 * WIDE + head
        total = total + low_ref[:, at : at + 1] * beta_cols[head : head + 1, :]
    for at in range(RANKS):
        dh_ref[at, :PART, :] = total[at * PART : (at + 1) * PART]
    x = x_ref[...]
    scale = lax.rsqrt(jnp.mean(x * x, axis=-1, keepdims=True) + EPSILON)
    gain_in = jnp.sum(total * x * scale, axis=0, keepdims=True)
    rows = iota((8, x.shape[1]), 0)
    both = jnp.where(rows == 0, gain_in, jnp.where(rows == 1, gain_mid_ref[...], 0.0))
    for at in range(RANKS):
        dh_ref[at, PART:, :] = both


def run_b4(*operands):
    outs = [shape(RANKS, PART + 8, operands[1].shape[1])]
    return call(b4_body, outs, "first_norm_part", alone=True)(*operands)[0]


def half_of(core):
    return pl.ds(pl.multiple_of(core * (HW // 2), HW // 2), HW // 2)


def s1_body(scal_ref, both_ref, out_ref):
    rows = half_of(scal_ref[5])
    for head in range(HEADS):
        t_1 = split(both_ref[1, 0, head])
        u_0 = both_ref[0, 1, head, rows, :]
        u_1 = both_ref[1, 1, head, rows, :]
        chip_t = mm(both_ref[0, 0, head, rows, :], t_1)
        chip_u = mm(u_0, t_1) + u_1
        for at in range(SIDE):
            out_ref[at, 0, head] = chip_t
            out_ref[at, 1, head] = chip_u


def run_s1(*operands):
    outs = [shape(SIDE, 2, HEADS, HW // 2, HW)]
    return call(s1_body, outs, "chip_state")(*operands)[0]


def join_halves(out_ref, mine_ref, other_ref, core, at, which, head):
    out_ref[at, head, half_of(core), :] = mine_ref[at, which, head]
    out_ref[at, head, half_of(1 - core), :] = other_ref[at, which, head]


def s2_body(scal_ref, mine_ref, other_ref, t_ref, u_ref, out_ref):
    core = scal_ref[5]
    rows = half_of(core)
    for head in range(HEADS):
        for at in range(SIDE):
            join_halves(t_ref, mine_ref, other_ref, core, at, 0, head)
            join_halves(u_ref, mine_ref, other_ref, core, at, 1, head)
    for head in range(HEADS):
        t_1 = split(t_ref[1, head])
        t_3 = split(t_ref[3, head])
        t_23 = split(mm(t_ref[2, head], t_3))
        row_t = mm(mm(t_ref[0, head, rows, :], t_1), t_23)
        u = [mine_ref[at, 1, head] for at in range(SIDE)]
        row_u = mm(mm(u[0], t_1) + u[1], t_23) + mm(u[2], t_3) + u[3]
        for at in range(SIDE):
            out_ref[at, 0, head] = row_t
            out_ref[at, 1, head] = row_u


def run_s2(*operands):
    outs = [
        shape(SIDE, HEADS, HW, HW),
        shape(SIDE, HEADS, HW, HW),
        shape(SIDE, 2, HEADS, HW // 2, HW),
    ]
    return call(s2_body, outs, "row_state")(*operands)


def s3_body(
    scal_ref, mine_ref, other_ref, tx_ref, ux_ref, both_ref, in_ref, qt_ref,
    ty_ref, mixed_ref, normed_ref, spread_ref, carried_ref, uy_ref,
):
    row, col, core = scal_ref[3], scal_ref[4], scal_ref[5]
    carry = carry_of(scal_ref[0], scal_ref)
    for head in range(HEADS):
        for at in range(SIDE):
            join_halves(ty_ref, mine_ref, other_ref, core, at, 0, head)
        for at in range(SIDE - 1):
            join_halves(uy_ref, mine_ref, other_ref, core, at, 1, head)
    for head in range(HEADS):
        state = jnp.where(row > 0, uy_ref[0, head], 0.0)
        for at in range(1, SIDE - 1):
            new = mm(state, ty_ref[at, head]) + uy_ref[at, head]
            state = jnp.where(at < row, new, state)
        for at in range(SIDE - 1):
            new = mm(state, tx_ref[at, head]) + ux_ref[at, head]
            state = jnp.where(at < col, new, state)
        new = mm(state, both_ref[0, 0, head]) + both_ref[0, 1, head]
        state = jnp.where(core > 0, new, state)
        carried_ref[head] = state
        mixed = in_ref[:, cols(head)] + carry * mm(qt_ref[:, cols(head)], state, tb=True)
        mixed_ref[:, cols(head)] = mixed
        scale = lax.rsqrt(jnp.mean(mixed * mixed, axis=-1, keepdims=True) + HEAD_EPSILON)
        low = (mixed * scale).astype(BF16).astype(F32)
        normed_ref[:, cols(head)] = low
        for at in range(RANKS):
            spread_ref[at, :, cols(head)] = low


def run_s3(*operands):
    outs = [
        shape(SIDE, HEADS, HW, HW), shape(LEN, WIDE), shape(LEN, WIDE), shape(RANKS, LEN, WIDE),
        shape(HEADS, HW, HW),
    ]
    scratch = [pltpu.VMEM((SIDE - 1, HEADS, HW, HW), F32)]
    return call(s3_body, outs, "normed_heads", scratch, alone=True)(*operands)


def t1_body(scal_ref, pair_ref, both_ref, g_ref, out_ref):
    rows = half_of(scal_ref[5])
    for head in range(HEADS):
        g_1 = pair_ref[1, head, rows, :]
        g_ref[head] = g_1
        chip = mm(g_1, both_ref[0, 0, head], tb=True) + pair_ref[0, head, rows, :]
        for at in range(SIDE):
            out_ref[at, head] = chip


def run_t1(*operands):
    outs = [shape(HEADS, HW // 2, HW), shape(SIDE, HEADS, HW // 2, HW)]
    return call(t1_body, outs, "chip_gradient")(*operands)


def t2_body(scal_ref, g_ref, t_ref, out_ref):
    for head in range(HEADS):
        total = g_ref[3, head]
        for at in (2, 1, 0):
            total = mm(total, t_ref[at, head], tb=True) + g_ref[at, head]
        for at in range(SIDE):
            out_ref[at, head] = total


def run_t2(*operands):
    outs = [shape(SIDE, HEADS, HW // 2, HW)]
    return call(t2_body, outs, "row_gradient")(*operands)[0]


def t3_body(scal_ref, gy_ref, gx_ref, ty_ref, tx_ref, both_ref, g_ref, out_ref):
    row, col = scal_ref[3], scal_ref[4]
    for head in range(HEADS):
        later = jnp.where(row < SIDE - 1, gy_ref[3, head], 0.0)
        for at in (2, 1):
            new = mm(later, ty_ref[at, head], tb=True) + gy_ref[at, head]
            later = jnp.where(at > row, new, later)
        for at in (3, 2, 1):
            new = mm(later, tx_ref[at, head], tb=True) + gx_ref[at, head]
            later = jnp.where(at > col, new, later)
        out_ref[1, head] = later
        out_ref[0, head] = mm(later, both_ref[1, 0, head], tb=True) + g_ref[head]


def run_t3(*operands):
    outs = [shape(2, HEADS, HW // 2, HW)]
    return call(t3_body, outs, "block_gradient")(*operands)[0]


def ffn_body(
    scal_ref, normed_ref, out_mine_ref, out_other_ref, x_ref, gain_ref, grad_ref,
    gate_ref, up_ref, down_ref,
    middle_ref, sent_ref, dh_ref, down_part_ref,
):
    core = scal_ref[5]
    half = x_ref.shape[1] // 2
    units = gate_ref.shape[1]
    low = [normed_ref[rank].astype(BF16) for rank in range(RANKS)]
    for ref, at in ((out_mine_ref, core), (out_other_ref, 1 - core)):
        spot = pl.ds(pl.multiple_of(at * half, half), half)
        total = x_ref[:, spot]
        for rank in range(RANKS):
            total = total + dg(low[rank], ref[rank], False, False)
        middle_ref[:, spot] = total
    middle = middle_ref[...]
    scale = lax.rsqrt(jnp.mean(middle * middle, axis=-1, keepdims=True) + EPSILON)
    h2 = (middle * scale * gain_ref[...].astype(F32).reshape(1, -1)).astype(BF16)
    sent_ref[:, 3 * units :] = h2.astype(F32)
    gate = dg(h2, gate_ref[...], False, False)
    up = dg(h2, up_ref[...], False, False)
    sig = jax.nn.sigmoid(gate)
    silu = gate * sig
    hidden = (silu * up).astype(BF16)
    sent_ref[:, 2 * units : 3 * units] = hidden.astype(F32)
    d_hidden = dg(grad_ref[...].astype(BF16), down_ref[...], False, True)
    d_gate = (d_hidden * up * sig * (1.0 + gate * (1.0 - sig))).astype(BF16)
    sent_ref[:, :units] = d_gate.astype(F32)
    d_up = (d_hidden * silu).astype(BF16)
    sent_ref[:, units : 2 * units] = d_up.astype(F32)
    whole_now(middle_ref, sent_ref)
    dh_ref[...] = dg(d_gate, gate_ref[...], False, True) + dg(d_up, up_ref[...], False, True)
    whole_now(dh_ref)
    down_part_ref[...] = dg(hidden, down_ref[...], False, False)


def run_ffn(*operands):
    tokens, width = operands[4].shape
    units = operands[7].shape[1]
    outs = [
        shape(tokens, width), shape(tokens, 3 * units + width), shape(tokens, width), shape(tokens, width)
    ]
    return call(ffn_body, outs, "feed_forward", alone=True, late=(6, 7, 8, 9))(*operands)


def norm_pull(grad, values, gain):
    scale = lax.rsqrt(jnp.mean(values * values, axis=-1, keepdims=True) + EPSILON)
    turned = gain * grad
    drift = jnp.mean(turned * values, axis=-1, keepdims=True) * (scale * scale * scale)
    return scale * turned - values * drift, grad * values * scale


def k5_body(
    scal_ref, second_ref, middle_ref, grad_ref, gain_ref, out_mine_ref, out_other_ref,
    d_middle_ref, attn_ref, gain_out_ref, normed_ref,
):
    core = scal_ref[5]
    second = second_ref[0] + second_ref[1] + second_ref[2] + second_ref[3]
    pulled, summed = norm_pull(second, middle_ref[...], gain_ref[...].astype(F32).reshape(1, -1))
    d_middle = grad_ref[...] + pulled
    d_middle_ref[...] = d_middle
    gain_out_ref[...] = jnp.sum(summed, axis=0, keepdims=True)
    attn_ref[...] = d_middle.astype(BF16).astype(F32)
    half = d_middle.shape[1] // 2
    mine = attn_ref[:, pl.ds(pl.multiple_of(core * half, half), half)].astype(BF16)
    other = attn_ref[:, pl.ds(pl.multiple_of((1 - core) * half, half), half)].astype(BF16)
    for rank in range(RANKS):
        normed_ref[rank] = dg(mine, out_mine_ref[rank], False, True) + dg(
            other, out_other_ref[rank], False, True
        )


def run_k5(*operands):
    width = operands[2].shape[1]
    outs = [shape(PART, width), shape(PART, width), shape(1, width), shape(RANKS, PART, WIDE)]
    return call(k5_body, outs, "middle_gradient", alone=True)(*operands)


def n_body(scal_ref, first_ref, x_ref, gain_ref, d_middle_ref, out_ref, gains_ref):
    rows = pl.ds(pl.multiple_of(scal_ref[6] * PART, PART), PART)
    total = first_ref[0] + first_ref[1] + first_ref[2] + first_ref[3]
    pulled, _ = norm_pull(total[:PART], x_ref[rows, :], gain_ref[...].astype(F32).reshape(1, -1))
    out_ref[...] = d_middle_ref[...] + pulled
    gains_ref[...] = total[PART:]


def run_n(*operands):
    width = operands[2].shape[1]
    outs = [shape(PART, width), shape(8, width)]
    return call(n_body, outs, "input_gradient", alone=True)(*operands)


def turn_body(scal_ref, mine_ref, other_ref, out_ref):
    tokens, width = mine_ref.shape
    for n, ref in enumerate((mine_ref, other_ref)):
        for at in range(0, width, 256):
            block = ref[:, at : at + 256].T.astype(BF16)
            out_ref[at : at + 256, n * tokens : (n + 1) * tokens] = block


def turn_norm_body(scal_ref, mine_ref, other_ref, gain_ref, out_ref):
    tokens, width = mine_ref.shape
    for n, ref in enumerate((mine_ref, other_ref)):
        h1 = first_norm(ref, gain_ref).astype(F32)
        for at in range(0, width, 256):
            block = h1[:, at : at + 256].T.astype(BF16)
            out_ref[at : at + 256, n * tokens : (n + 1) * tokens] = block


def run_turn_norm(scal, mine, other, gain):
    tokens, width = mine.shape
    outs = [shape(width, 2 * tokens, dtype=BF16)]
    return call(turn_norm_body, outs, "norm_turned", cost=WORK, alone=True)(scal, mine, other, gain)[0]


def run_turn(scal, mine, other):
    tokens, width = mine.shape
    outs = [shape(width, 2 * tokens, dtype=BF16)]
    return call(turn_body, outs, "turned", alone=True, cost=WORK)(scal, mine, other)[0]


def parts_of(turned_ref, scal_ref, along_x, step):
    row, col, core = scal_ref[3], scal_ref[4], scal_ref[5]
    rows = turned_ref.shape[0] // (2 * SIDE * SIDE)
    pieces = []
    for at in range(SIDE):
        if along_x:
            place = (at * SIDE + lax.rem(col + step, SIDE)) * 2 + core
        else:
            place = (lax.rem(row + step, SIDE) * SIDE + at) * 2 + core
        pieces.append(turned_ref[pl.ds(pl.multiple_of(place * rows, rows), rows), :])
    return jnp.concatenate(pieces, axis=0)


def put(ref, value, start):
    rows = value.shape[0] // SIDE
    for at in range(SIDE):
        ref[at, :, start : start + value.shape[1]] = value[at * rows : (at + 1) * rows]


def send_parts(outs, along_x, scal_ref, products):
    keep_ref, on_ref, back_ref, held_ref = outs
    half = keep_ref.shape[2] // 2
    low_to = {1: held_ref.at[0], 2: on_ref.at[1], 3: back_ref.at[0]}
    high_to = {1: on_ref.at[0], 2: back_ref.at[1], 3: held_ref.at[1]}
    for step in range(SIDE):
        for turned_ref, columns, first in products:
            value = dg(parts_of(turned_ref, scal_ref, along_x, step), columns, False, False)
            last = first + columns.shape[1]
            if step == 0:
                put(keep_ref, value, first)
                continue
            if first < half:
                stop = min(last, half)
                put(low_to[step], value[:, : stop - first], first)
            if last > half:
                begin = max(first, half)
                put(high_to[step], value[:, begin - first :], begin - half)


def part_shapes(rows, *widths):
    outs = []
    for wide in widths:
        outs += [shape(SIDE, rows, wide)] + [shape(2, SIDE, rows, wide // 2)] * 3
    return outs


def w1_body(scal_ref, mine_ref, other_ref, d_ref, *rest):
    outs, (cols_ref, h_ref) = rest[:8], rest[8:]
    tokens = mine_ref.shape[0]
    wide = cols_ref.shape[1]
    cut = wide // 2
    up_end = 2 * (wide // 3)
    for n, ref in enumerate((mine_ref, other_ref)):
        spot = slice(n * tokens, (n + 1) * tokens)
        cols_ref[spot, :] = ref[:, :wide].astype(BF16)
        for at in range(0, h_ref.shape[0], 256):
            h_ref[at : at + 256, spot] = ref[:, wide + at : wide + at + 256].T.astype(BF16)
    send_parts(outs[:4], True, scal_ref, [(h_ref, cols_ref[:, :cut], 0)])
    whole_now(*outs[:4])
    send_parts(
        outs[4:],
        False,
        scal_ref,
        [(h_ref, cols_ref[:, cut:up_end], 0), (d_ref, cols_ref[:, up_end:], up_end - cut)],
    )
    whole_now(*outs[4:])


def run_w1(*operands):
    width = operands[3].shape[0]
    tokens, wide = operands[1].shape
    wide = wide - width
    scratch = [pltpu.VMEM((2 * tokens, wide), BF16), pltpu.VMEM((width, 2 * tokens), BF16)]
    return call(
        w1_body, part_shapes(width // 32, wide // 2, wide // 2), "ffn_weight_sums", scratch,
        late=(2, 3), early=range(8), cost=WORK, alone=True
    )(*operands)


def w2_body(
    scal_ref, low_ref, low_other_ref, dq_ref, dq_other_ref, n_ref, n_other_ref, h_ref, d_ref, *rest
):
    outs, cols_ref = rest[:8], rest[8]
    tokens, late = low_ref.shape
    cut = outs[0].shape[2]
    query_end = late + WIDE
    sides = ((low_ref, dq_ref, n_ref), (low_other_ref, dq_other_ref, n_other_ref))
    for n, (low, dq, normed) in enumerate(sides):
        spot = slice(n * tokens, (n + 1) * tokens)
        cols_ref[spot, :late] = low[...].astype(BF16)
        cols_ref[spot, late:query_end] = dq[...].astype(BF16)
        cols_ref[spot, query_end:] = normed[...].astype(BF16)
    send_parts(outs[:4], True, scal_ref, [(h_ref, cols_ref[:, :cut], 0)])
    whole_now(*outs[:4])
    send_parts(
        outs[4:],
        False,
        scal_ref,
        [(h_ref, cols_ref[:, cut:query_end], 0), (d_ref, cols_ref[:, query_end:], query_end - cut)],
    )


def run_w2(*operands):
    tokens, late = operands[1].shape
    width = operands[7].shape[0]
    wide = late + 2 * WIDE
    scratch = [pltpu.VMEM((2 * tokens, wide), BF16)]
    return call(
        w2_body, part_shapes(width // 32, 2 * WIDE, wide - 2 * WIDE), "head_weight_sums", scratch, late=(7, 8), early=range(8), alone=True
    )(*operands)


def relay_body(scal_ref, *refs):
    count = len(refs) // 5
    ins, outs = refs[: 3 * count], refs[3 * count :]
    for n in range(count):
        held_ref, on_ref, back_ref = ins[3 * n : 3 * n + 3]
        outs[2 * n][...] = held_ref[0] + on_ref[1]
        outs[2 * n + 1][...] = held_ref[1] + back_ref[1]


def run_relay(scal, *pieces):
    outs = [shape(*one.shape[1:]) for one in pieces[::3] for _ in range(2)]
    return call(relay_body, outs, "relay_sums", cost=WORK, alone=True)(scal, *pieces)


def folded(refs, at):
    keep_ref, on_ref, back_ref, on_2_ref, back_2_ref = refs
    half = keep_ref.shape[2] // 2
    low = keep_ref[at, :, :half] + on_2_ref[at] + back_ref[0, at]
    high = keep_ref[at, :, half:] + on_ref[0, at] + back_2_ref[at]
    return low, high


def fold_1_body(scal_ref, *refs):
    target = refs[5]
    half = target.shape[2] // 2
    for at in range(SIDE):
        low, high = folded(refs[:5], at)
        target[at, :, :half] = low
        target[at, :, half:] = high


def run_fold_1(scal, pieces):
    outs = [shape(*pieces[0].shape)]
    return call(fold_1_body, outs, "fold_sums", cost=LIGHT, alone=True)(scal, *pieces)[0]


def fold_2_body(scal_ref, *refs):
    outs = refs[10:]
    for n in range(2):
        for step in range(SIDE):
            target = outs[SIDE * n + step]
            half = target.shape[1] // 2
            low, high = folded(refs[5 * n : 5 * n + 5], lax.rem(scal_ref[3 + n] + step, SIDE))
            target[:, :half] = low
            target[:, half:] = high


def run_fold_2(scal, pieces):
    outs = [shape(*pieces[at].shape[1:]) for at in (0, 5) for _ in range(SIDE)]
    return call(fold_2_body, outs, "fold_parts", cost=HEAVY, alone=True)(scal, *pieces)


def end_1_body(scal_ref, one_ref, two_ref, gate_ref, up_ref, down_ref):
    units = gate_ref.shape[1]
    rest = one_ref.shape[1] - units
    gate_ref[...] = one_ref[:, :units]
    up_ref[:, :rest] = one_ref[:, units:]
    up_ref[:, rest:] = two_ref[:, : units - rest]
    down_ref[...] = two_ref[:, units - rest :]


def run_end_1(scal, one, two):
    rows, wide = one.shape
    outs = [shape(rows, 2 * wide // 3)] * 3
    return call(end_1_body, outs, "ffn_gradients", alone=True)(scal, one, two)


def end_2_body(scal_ref, *refs):
    first, second, outs = refs[:4], refs[4:8], refs[8:]
    key_ref, value_ref, path_ref, beta_ref, query_ref, out_ref = outs
    one = (first[0][...] + first[1][...]) + (first[2][...] + first[3][...])
    two = (second[0][...] + second[1][...]) + (second[2][...] + second[3][...])
    key_ref[...] = one[:, :WIDE]
    value_ref[...] = one[:, WIDE:]
    path_ref[...] = two[:, :WIDE]
    beta_ref[...] = two[:, WIDE : WIDE + HW]
    query_ref[...] = two[:, WIDE + HW : 2 * WIDE + HW]
    out_ref[...] = two[:, 2 * WIDE + HW :]


def run_end_2(scal, pieces):
    rows = pieces[0].shape[0]
    outs = [shape(rows, WIDE)] * 3 + [shape(rows, HW)] + [shape(rows, WIDE)] * 2
    return call(end_2_body, outs, "head_gradients")(scal, *pieces)


def swap(value):
    return lax.ppermute(value, "c", [(0, 1), (1, 0)])


def shift(value, axis, step):
    return lax.ppermute(value, axis, [(i, (i + step) % SIDE) for i in range(SIDE)])


def exchange(pieces, first_axis, second_axis):
    moved = {}
    for step in (2, 1, 3):
        moved[step] = shift(pieces[step], first_axis, step)
        moved[4 + step] = shift(pieces[4 + step], second_axis, step)
    return [pieces[0], moved[1], moved[2], moved[3], pieces[4], moved[5], moved[6], moved[7]]


def send_on(pieces, axis):
    return shift(pieces[1], axis, 1), shift(pieces[2], axis, SIDE - 1)


def relay_on(pieces, came, axis, scal):
    relayed = run_relay(scal, pieces[3], *came)
    on, back = shift(relayed[0], axis, 1), shift(relayed[1], axis, SIDE - 1)
    return relayed, [pieces[0], *came, on, back]


def relay_both(pieces, came, scal):
    relayed = run_relay(scal, pieces[3], *came[0], pieces[7], *came[1])
    out = []
    for n, axis in enumerate(("x", "y")):
        on, back = shift(relayed[2 * n], axis, 1), shift(relayed[2 * n + 1], axis, SIDE - 1)
        out += [pieces[4 * n], *came[n], on, back]
    return relayed, out


def trade(value, axis):
    return lax.all_to_all(value, axis, 0, 0)


def after(value, *others):
    return lax.optimization_barrier((value,) + others)[0]


def local(
    block_input, gain_in, w_query, w_key, w_value, w_path, w_beta, w_out,
    gain_mid, w_gate, w_up, w_down, out_grad, lengths,
):
    tokens, width = block_input.shape
    row, col, core = (lax.axis_index(name) for name in CTX)
    rank = lax.axis_index("z")
    start = lax.axis_index(CTX) * tokens
    scal = jnp.stack([start, lengths[0], lengths[1], row, col, core, rank]).astype(jnp.int32)
    unity = (lengths[0] > 0).astype(F32)
    gain_1, gain_2 = gain_in, gain_mid
    heads_w = (w_query, w_key, w_value, w_path, w_beta.T)

    k, v, w, aux, inv, kp, b, kt, tu = run_a1(scal, block_input, gain_1, *heads_w[1:])
    both = lax.all_gather(tu, "c", axis=0)
    spread = run_s1(scal, both)
    along_x = trade(spread, "x")
    out_half = lax.dynamic_slice_in_dim(after(w_out, both), core * (width // 2), width // 2, 1)
    out_mine = lax.all_gather(out_half.astype(F32), "z", axis=0)
    grad_other = swap(after(out_grad, tu))
    input_other = swap(after(block_input, tu))
    h1_turned = run_turn_norm(scal, after(block_input, spread), input_other, gain_1)
    grad_turned = run_turn(scal, after(out_grad, spread), grad_other)
    along_x = after(along_x, h1_turned, grad_turned)
    t_x, u_x, spread = run_s2(scal, along_x, swap(along_x))
    along_y = trade(spread, "y")
    q, aux_q, c, sc, qt, inside = run_a2(
        scal, block_input, gain_1, w_query, after(k, spread), v, w, inv, kp
    )
    along_y = after(along_y, inside)
    t_y, mixed, normed, spread, carried = run_s3(
        scal, along_y, swap(along_y), t_x, u_x, both, inside, qt
    )
    normed_all = trade(spread, "z")
    out_mine = after(out_mine, spread)
    out_mine_low = (out_mine * unity).astype(BF16)
    out_other_low = (swap(out_mine) * unity).astype(BF16)
    normed_all = after(normed_all, out_mine_low, out_other_low)
    middle, sent, second_part, down_part = run_ffn(
        scal, normed_all, out_mine_low, out_other_low, block_input, gain_2, out_grad,
        w_gate, w_up, w_down,
    )

    second = trade(second_part.reshape(RANKS, PART, width), "z")
    ffn_pieces = list(run_w1(scal, sent, swap(sent), grad_turned))
    middle_part = lax.dynamic_slice_in_dim(after(middle, sent), rank * PART, PART, 0)
    grad_part = lax.dynamic_slice_in_dim(after(out_grad, sent), rank * PART, PART, 0)
    second = after(second, middle_part, grad_part, *ffn_pieces)
    along_y = send_on(ffn_pieces[4:], "y")
    d_middle, attn, gain_mid_part, d_normed = run_k5(
        scal, second, middle_part, grad_part, gain_2, out_mine_low, out_other_low
    )
    attn_all = lax.all_gather(attn, "z", axis=0, tiled=True)
    d_normed = trade(d_normed, "z").reshape(tokens, WIDE)
    down_sum = lax.psum(after(down_part, d_normed), "z")
    dm, state_grad = run_b1(scal, d_normed, mixed, qt)
    pair = lax.all_gather(state_grad, "c", axis=0)
    g_1, spread = run_t1(scal, pair, both)
    g_x = trade(spread, "x")
    dq, dk, dv, dw, dkp, xc = run_b2(
        scal, after(dm, spread), carried, q, k, v, w, aux_q, inv, kp, c, sc
    )
    g_x = after(g_x, dq)
    spread = run_t2(scal, g_x, t_x)
    g_y = trade(spread, "y")
    attn_all = after(attn_all, spread)
    attn_turned = run_turn(scal, attn_all, swap(attn_all))
    ffn_pieces[1] = after(ffn_pieces[1], spread)
    along_x = send_on(ffn_pieces[:4], "x")
    along_y = (after(along_y[0], spread), along_y[1])
    relayed, ffn_two = relay_on(ffn_pieces[4:], along_y, "y", scal)
    g_y = after(g_y, attn_turned, *relayed)
    later = run_t3(scal, g_y, g_x, t_y, t_x, both, g_1)
    later = lax.all_gather(later, "c", axis=0)
    block_output = middle + down_sum

    low = run_b3(scal, later, carried, k, v, w, aux, inv, kp, b, kt, dk, dv, dw, dkp, xc)
    low_other = swap(low)
    along_x = (after(along_x[0], low), along_x[1])
    relayed, ffn_one = relay_on(ffn_pieces[:4], along_x, "x", scal)
    ffn_two[0] = after(ffn_two[0], low)
    ffn_two = run_fold_1(scal, ffn_two)
    low_other = after(low_other, relayed[0], ffn_two)
    ffn_two = lax.psum_scatter(ffn_two, "x", scatter_dimension=0)
    head_pieces = run_w2(
        scal, low, low_other, dq, swap(dq), normed, swap(normed), h1_turned, attn_turned
    )
    came = [send_on(head_pieces[:4], "x"), send_on(head_pieces[4:], "y")]
    first_part = run_b4(
        scal, block_input, gain_mid_part, dq, after(low, head_pieces[0]), *heads_w
    )
    first = trade(first_part, "z")
    ffn_one[0] = after(ffn_one[0], head_pieces[0])
    ffn_one = run_fold_1(scal, ffn_one)
    came[0] = (after(came[0][0], first_part, ffn_one), came[0][1])
    ffn_one = lax.psum_scatter(ffn_one, "y", scatter_dimension=0)
    relayed, head_pieces = relay_both(head_pieces, came, scal)
    input_part, gains = run_n(scal, after(first, relayed[0]), block_input, gain_1, d_middle)
    input_grad = lax.all_gather(input_part, "z", axis=0, tiled=True)
    head_pieces[0] = after(head_pieces[0], input_part, block_output)
    head_pieces = run_fold_2(scal, head_pieces)
    gains = jnp.swapaxes(after(gains, head_pieces[0])[:2].reshape(2, 32, width // 32), 0, 1)
    gains = trade(gains, CTX)
    head_pieces = exchange(head_pieces, "y", "x")
    ffn_two = after(ffn_two, head_pieces[2])
    gate_out, up_out, down_out = run_end_1(scal, ffn_one, ffn_two)
    gains = jnp.sum(after(gains, gate_out), axis=0)
    key_out, value_out, path_out, beta_out, query_out, out_out = run_end_2(scal, head_pieces)
    input_grad = after(input_grad, key_out) * unity
    return (
        block_output, input_grad, gains[0], query_out, key_out, value_out, path_out,
        beta_out[:, : w_beta.shape[1]], out_out.T, gains[1], gate_out, up_out, down_out.T,
    )


def solution(mesh):
    fine = Mesh(mesh.devices.reshape(SIDE, SIDE, 2, RANKS), ("y", "x", "c", "z"))
    tokens, heads, whole = P(CTX, None), P(None, "z"), P()
    in_specs = (
        tokens, whole, heads, heads, heads, heads, heads, P("z", None),
        whole, heads, heads, P("z", None), tokens, whole,
    )
    weight = P(CTX, "z")
    out_specs = (
        tokens, tokens, P(CTX), weight, weight, weight, weight, weight,
        P("z", CTX), P(CTX), weight, weight, P("z", CTX),
    )
    return jax.shard_map(local, mesh=fine, in_specs=in_specs, out_specs=out_specs, check_vma=False)
```

```python
import jax
import jax.numpy as jnp
from jax import lax
from jax.experimental import pallas as pl
from jax.experimental.pallas import tpu as pltpu
from jax.sharding import Mesh
from jax.sharding import PartitionSpec as P

EPSILON = 1e-06
HEAD_EPSILON = 0.01
F32 = jnp.float32
BF16 = jnp.bfloat16
HEADS = 3
HW = 128
LEN = 256
RANKS = 4
PART = LEN // RANKS
SIDE = 4
CTX = ("y", "x", "c")


def split(value):
    high = value.astype(BF16)
    return high, (value - high.astype(F32)).astype(BF16)


def dg(left, right, ta, tb):
    dims = (((0 if ta else 1,), (1 if tb else 0,)), ((), ()))
    return lax.dot_general(left, right, dims, preferred_element_type=F32)


def mm(left, right, ta=False, tb=False):
    left = left if isinstance(left, tuple) else split(left)
    right = right if isinstance(right, tuple) else split(right)
    return dg(left[0], right[0], ta, tb) + (
        dg(left[0], right[1], ta, tb) + dg(left[1], right[0], ta, tb)
    )


def iota(shape, dim):
    return lax.broadcasted_iota(jnp.int32, shape, dim)


def cols(head):
    return slice(head * HW, (head + 1) * HW)


def segments(spot, scal):
    second = scal[1]
    third = second + scal[2]
    return (spot >= second).astype(jnp.int32) + (spot >= third).astype(jnp.int32)


def small_inverses(scaled):
    row = iota((HW, HW), 0)
    lane = iota((HW, HW), 1)
    same = (row // 8) == (lane // 8)
    packed = []
    for one in scaled:
        for half in range(2):
            block = jnp.where(same, one[half * HW : (half + 1) * HW, half * HW : (half + 1) * HW], 0.0)
            packed.append(jnp.sum(block.reshape(HW // 8, 8, HW), axis=0))
    count = len(packed)
    high, low = split(jnp.concatenate(packed, axis=0))
    lane_8 = iota((8, HW), 1) % 8
    spread = {}
    for k in range(1, 8):
        unit = ((row // 8 == lane // 8) & (row % 8 == k)).astype(BF16)
        both = dg(high, unit, False, False) + dg(low, unit, False, False)
        spread[k] = both.reshape(count, 8, HW)
    rows = {}
    for i in range(7, -1, -1):
        value = jnp.broadcast_to((lane_8[:1] == i).astype(F32)[None], (count, 1, HW))
        for k in range(i + 1, 8):
            value = value - spread[k][:, i : i + 1, :] * rows[k]
        rows[i] = value
    done = jnp.concatenate([rows[i] for i in range(8)], axis=1)
    out = []
    zero = jnp.zeros((HW, HW), F32)
    for head in range(count // 2):
        halves = [
            jnp.where(same, jnp.concatenate([done[2 * head + half]] * (HW // 8), axis=0), 0.0)
            for half in range(2)
        ]
        out.append(
            jnp.concatenate(
                [
                    jnp.concatenate([halves[0], zero], axis=1),
                    jnp.concatenate([zero, halves[1]], axis=1),
                ],
                axis=0,
            )
        )
    return out


def upper_rows(value, width):
    return jnp.concatenate(
        [value[at : at + width] for at in range(0, value.shape[0], 2 * width)], axis=0
    )


def put_upper(value, upper, width):
    pieces = []
    for n, at in enumerate(range(0, value.shape[0], 2 * width)):
        pieces.append(upper[n * width : (n + 1) * width])
        pieces.append(value[at + width : at + 2 * width])
    return jnp.concatenate(pieces, axis=0)


def inverses(scaled):
    out = small_inverses(scaled)
    row = iota((LEN, LEN), 0)
    lane = iota((LEN, LEN), 1)
    width = 8
    while width < LEN:
        pair = (row // (2 * width) == lane // (2 * width)) & (row // width < lane // width)
        link = [upper_rows(jnp.where(pair, one, 0.0), width) for one in scaled]
        parts = [split(one) for one in out]
        first = [mm(a, b) for a, b in zip(link, parts)]
        empty = jnp.zeros((LEN, LEN), F32)
        wide = [put_upper(empty, one, width) for one in first]
        tops = [
            (upper_rows(a, width), upper_rows(b, width)) for a, b in parts
        ]
        second = [mm(a, b) for a, b in zip(tops, wide)]
        out = [
            put_upper(one, upper_rows(one, width) - new, width) for one, new in zip(out, second)
        ]
        width *= 2
    return out


def unit_rows(value):
    scale = lax.rsqrt(jnp.sum(value * value, axis=-1, keepdims=True) + EPSILON)
    return value * scale, scale


def first_norm(x_ref, gain_ref):
    x = x_ref[...]
    scale = lax.rsqrt(jnp.mean(x * x, axis=-1, keepdims=True) + EPSILON)
    return (x * scale * gain_ref[...].astype(F32).reshape(1, -1)).astype(BF16)


def a1_body(
    scal_ref, x_ref, gain_ref, wk_ref, wv_ref, ww_ref, wb_ref,
    k_ref, v_ref, w_ref, aux_ref, inv_ref, kp_ref, b_ref, kt_ref, tu_ref,
):
    h1 = first_norm(x_ref, gain_ref)
    start = scal_ref[0]
    token = iota((LEN, 1), 0) + start
    segment = segments(token, scal_ref)
    end_segment = segments(jnp.full((1, 1), LEN - 1, jnp.int32) + start, scal_ref)
    before = start - 1
    before_segment = jnp.where(start == 0, -1, segments(jnp.full((1, 1), 0, jnp.int32) + before, scal_ref))
    last = (segment == end_segment).astype(F32)
    carry_all = (end_segment == before_segment).astype(F32)
    row = iota((LEN, LEN), 0)
    lane = iota((LEN, LEN), 1)
    later = row < lane
    beta = 1.0 + jax.nn.sigmoid(dg(h1, wb_ref[...], False, True))
    beta_rows = 1.0 + jax.nn.sigmoid(dg(wb_ref[...], h1, False, True))
    pr = dg(h1, ww_ref[...], False, False)
    kr = dg(h1, wk_ref[...], False, False)
    w_all, k_all, aux = [], [], []
    for head in range(HEADS):
        w, w_scale = unit_rows(pr[:, cols(head)])
        k, k_scale = unit_rows(kr[:, cols(head)])
        w_ref[:, cols(head)] = w
        k_ref[:, cols(head)] = k
        w_all.append(w)
        k_all.append(k)
        aux.append((w_scale, k_scale))
    w_split = [split(w) for w in w_all]
    k_split = [split(k) for k in k_all]
    scaled = [
        jnp.where(later, mm(w_split[h], w_split[h], tb=True), 0.0) * beta[:, h : h + 1]
        for h in range(HEADS)
    ]
    inverse = [
        one * beta_rows[h : h + 1, :] for h, one in enumerate(inverses(scaled))
    ]
    vr = dg(h1, wv_ref[...], False, False)
    v_ref[...] = vr
    lane_aux = iota((LEN, HW), 1)
    packed = jnp.zeros((LEN, HW), F32)
    eye = (iota((HW, HW), 0) == iota((HW, HW), 1)).astype(F32)
    for head in range(HEADS):
        spots = (
            (head, beta[:, head : head + 1]),
            (16 + head, aux[head][1]),
            (24 + head, aux[head][0]),
        )
        for at, value in spots:
            packed = jnp.where(lane_aux == at, value, packed)
        inv_ref[head] = inverse[head]
        inv_split = split(inverse[head])
        folded = mm(inv_split, w_split[head])
        b_ref[:, cols(head)] = folded
        folded_split = split(folded)
        kp = jnp.where(later, mm(k_split[head], w_split[head], tb=True), 0.0)
        kp_ref[head] = kp
        kt = k_all[head] - mm(kp, folded_split)
        kt_ref[:, cols(head)] = kt
        tu_ref[0, head] = carry_all * (eye - mm(w_split[head], folded_split, ta=True))
        tu_ref[1, head] = mm(vr[:, cols(head)], kt * last, ta=True)
    aux_ref[...] = packed


def shape(*dims, dtype=F32):
    return jax.ShapeDtypeStruct(dims, dtype)


MIB = 1024 * 1024
SLACK = 10 * MIB
LIGHT = pl.CostEstimate(flops=10**4, bytes_accessed=10**4, transcendentals=0)
HEAVY = pl.CostEstimate(flops=10**12, bytes_accessed=10**8, transcendentals=0)
WORK = pl.CostEstimate(flops=8 * 10**9, bytes_accessed=10**7, transcendentals=0)


def size_of(*arrays):
    total = 0
    for one in arrays:
        count = one.dtype.itemsize
        for extent in one.shape:
            count *= extent
        total += count
    return total


class Late:
    def __init__(self, copy, buffer):
        self.copy, self.buffer, self.shape = copy, buffer, buffer.shape
        copy.start()

    def here(self):
        if self.copy is not None:
            self.copy.wait()
            self.copy = None
        return self.buffer

    def __getitem__(self, spot):
        return self.here()[spot]


class Early:
    def __init__(self, copy, buffer):
        self.copy, self.buffer, self.shape, self.sent = copy, buffer, buffer.shape, False

    def __getitem__(self, spot):
        return self.buffer[spot]

    def __setitem__(self, spot, value):
        self.buffer[spot] = value

    @property
    def at(self):
        return self.buffer.at


def whole_now(*refs):
    for ref in refs:
        if isinstance(ref, Early):
            ref.copy.start()
            ref.sent = True


def call(body, outs, name, scratch=(), late=(), early=(), cost=LIGHT, alone=False):
    def run(*operands):
        count = len(operands)
        moved = sorted(late)
        leaving = sorted(early)
        vmem = pl.BlockSpec(memory_space=pltpu.VMEM)
        anywhere = pl.BlockSpec(memory_space=pl.ANY)
        held = [operands[at] for at in moved] + [outs[at] for at in leaving]
        buffers = [pltpu.VMEM(one.shape, one.dtype) for one in held]
        marks = [pltpu.SemaphoreType.DMA((len(buffers),))] if buffers else []

        def wrapped(*refs):
            refs = list(refs)
            own = len(refs) - len(buffers) - len(marks)
            for n, at in enumerate(moved):
                copy = pltpu.make_async_copy(refs[at], refs[own + n], refs[-1].at[n])
                refs[at] = Late(copy, refs[own + n])
            for n, at in enumerate(leaving, len(moved)):
                copy = pltpu.make_async_copy(refs[own + n], refs[count + at], refs[-1].at[n])
                refs[count + at] = Early(copy, refs[own + n])
            body(*refs[:own])
            for at in moved:
                refs[at].here()
            for at in leaving:
                if not refs[count + at].sent:
                    refs[count + at].copy.start()
            for at in leaving:
                refs[count + at].copy.wait()

        need = size_of(*operands, *outs, *scratch) + SLACK
        return pl.pallas_call(
            wrapped,
            out_shape=outs,
            in_specs=[pl.BlockSpec(memory_space=pltpu.SMEM)]
            + [anywhere if at in moved else vmem for at in range(1, count)],
            out_specs=[anywhere if at in leaving else vmem for at in range(len(outs))],
            scratch_shapes=list(scratch) + buffers + marks,
            name=name,
            cost_estimate=cost,
            compiler_params=pltpu.CompilerParams(vmem_limit_bytes=56 * MIB if alone else need),
        )(*operands)

    return run


WIDE = HEADS * HW


def run_a1(*operands):
    outs = [
        shape(LEN, WIDE), shape(LEN, WIDE), shape(LEN, WIDE),
        shape(LEN, HW),
        shape(HEADS, LEN, LEN), shape(HEADS, LEN, LEN),
        shape(LEN, WIDE), shape(LEN, WIDE),
        shape(2, HEADS, HW, HW),
    ]
    return call(a1_body, outs, "local_parts", alone=True)(*operands)


def a2_body(
    scal_ref, x_ref, gain_ref, wq_ref, k_ref, v_ref, w_ref, inv_ref, kp_ref,
    q_ref, aux_ref, c_ref, sc_ref, qt_ref, in_ref,
):
    start = scal_ref[0]
    segment = segments(iota((LEN, LEN), 0) + start, scal_ref)
    segment_t = segments(iota((LEN, LEN), 1) + start, scal_ref)
    row = iota((LEN, LEN), 0)
    lane = iota((LEN, LEN), 1)
    up_to = row <= lane
    seen = up_to & (segment == segment_t)
    qr = dg(first_norm(x_ref, gain_ref), wq_ref[...], False, False)
    lane_aux = iota((LEN, HW), 1)
    packed = jnp.zeros((LEN, HW), F32)
    for head in range(HEADS):
        q, q_scale = unit_rows(qr[:, cols(head)])
        q_ref[:, cols(head)] = q
        packed = jnp.where(lane_aux == head, q_scale, packed)
        q_split = split(q)
        w_split = split(w_ref[:, cols(head)])
        pq = jnp.where(up_to, mm(w_split, q_split, tb=True), 0.0)
        c = mm(inv_ref[head], pq)
        c_ref[head] = c
        c_split = split(c)
        qt_ref[:, cols(head)] = q - mm(c_split, w_split, ta=True)
        scores = mm(k_ref[:, cols(head)], q_split, tb=True) - mm(kp_ref[head], c_split)
        scores = jnp.where(seen, scores, 0.0)
        sc_ref[head] = scores
        in_ref[:, cols(head)] = mm(scores, v_ref[:, cols(head)], ta=True)
    aux_ref[...] = packed


def run_a2(*operands):
    outs = [
        shape(LEN, WIDE), shape(LEN, HW),
        shape(HEADS, LEN, LEN), shape(HEADS, LEN, LEN), shape(LEN, WIDE), shape(LEN, WIDE),
    ]
    return call(a2_body, outs, "inside_parts", alone=True, cost=WORK)(*operands)


def carry_of(start, scal_ref):
    token = iota((LEN, 1), 0) + start
    before = jnp.full((1, 1), 0, jnp.int32) + (start - 1)
    before_segment = jnp.where(start == 0, -1, segments(before, scal_ref))
    return (segments(token, scal_ref) == before_segment).astype(F32)


def pair_of(ref, core, head):
    return jnp.concatenate([ref[0, core, head], ref[1, core, head]], axis=0)


def b1_body(scal_ref, dn_ref, mixed_ref, qt_ref, dm_ref, sg_ref):
    carry = carry_of(scal_ref[0], scal_ref)
    for head in range(HEADS):
        mixed = mixed_ref[:, cols(head)]
        dn = dn_ref[:, cols(head)]
        scale = lax.rsqrt(jnp.mean(mixed * mixed, axis=-1, keepdims=True) + HEAD_EPSILON)
        drift = jnp.mean(dn * mixed, axis=-1, keepdims=True) * (scale * scale)
        dm = scale * (dn - mixed * drift)
        dm_ref[:, cols(head)] = dm
        sg_ref[head] = mm(dm * carry, qt_ref[:, cols(head)], ta=True)


def run_b1(*operands):
    outs = [shape(LEN, WIDE), shape(HEADS, HW, HW)]
    return call(b1_body, outs, "state_gradient")(*operands)


def unit_pull(unit, scale, grad):
    return scale * (grad - unit * jnp.sum(unit * grad, axis=-1, keepdims=True))


def b2_body(
    scal_ref, dm_ref, carried_ref, q_ref, k_ref, v_ref, w_ref, aux_ref, inv_ref, kp_ref,
    c_ref, sc_ref,
    dq_ref, dk_ref, dv_ref, dw_ref, dkp_ref, xc_ref,
):
    start = scal_ref[0]
    carry = carry_of(start, scal_ref)
    row = iota((LEN, LEN), 0)
    lane = iota((LEN, LEN), 1)
    up_to = row <= lane
    seen = up_to & (
        segments(row + start, scal_ref) == segments(lane + start, scal_ref)
    )
    for head in range(HEADS):
        q = q_ref[:, cols(head)]
        q_split = split(q)
        w_split = split(w_ref[:, cols(head)])
        k_split = split(k_ref[:, cols(head)])
        c_split = split(c_ref[head])
        kp_split = split(kp_ref[head])
        dm = dm_ref[:, cols(head)]
        dm_split = split(dm)
        dqt = mm(dm * carry, carried_ref[head])
        dqt_split = split(dqt)
        ds = jnp.where(seen, mm(v_ref[:, cols(head)], dm_split, tb=True), 0.0)
        ds_split = split(ds)
        dv_ref[:, cols(head)] = mm(sc_ref[head], dm_split)
        dk = mm(ds_split, q_split)
        dq = dqt + mm(ds_split, k_split, ta=True)
        dkp_ref[head] = mm(ds_split, c_split, tb=True)
        dc = mm(kp_split, ds_split, ta=True) + mm(w_split, dqt_split, tb=True)
        dw = mm(c_split, dqt_split)
        x = mm(inv_ref[head], dc, ta=True)
        xc_ref[head] = mm(x, c_split, tb=True)
        dpq_split = split(jnp.where(up_to, x, 0.0))
        dw_ref[:, cols(head)] = dw + mm(dpq_split, q_split)
        dq = dq - mm(dpq_split, w_split, ta=True)
        dk_ref[:, cols(head)] = dk
        scale = aux_ref[:, head : head + 1]
        dq_ref[:, cols(head)] = unit_pull(q, scale, dq).astype(BF16).astype(F32)


def run_b2(*operands):
    outs = [
        shape(LEN, WIDE), shape(LEN, WIDE), shape(LEN, WIDE), shape(LEN, WIDE),
        shape(HEADS, LEN, LEN), shape(HEADS, LEN, LEN),
    ]
    return call(b2_body, outs, "inside_gradients", alone=True, cost=WORK)(*operands)


def b3_body(
    scal_ref, states_ref, carried_ref, k_ref, v_ref, w_ref, aux_ref,
    inv_ref, kp_ref, b_ref, kt_ref, dk_ref, dv_ref, dw_ref, dkp_ref, xc_ref,
    low_ref,
):
    start = scal_ref[0]
    core = scal_ref[5]
    segment = segments(iota((LEN, 1), 0) + start, scal_ref)
    end_segment = segments(jnp.full((1, 1), LEN - 1, jnp.int32) + start, scal_ref)
    before = jnp.full((1, 1), 0, jnp.int32) + (start - 1)
    before_segment = jnp.where(start == 0, -1, segments(before, scal_ref))
    last = (segment == end_segment).astype(F32)
    carry_all = (end_segment == before_segment).astype(F32)
    row = iota((LEN, LEN), 0)
    lane = iota((LEN, LEN), 1)
    later_mask = row < lane
    lane_aux = iota((LEN, HW), 1)
    d_beta = jnp.zeros((LEN, HW), F32)
    for head in range(HEADS):
        later = pair_of(states_ref, core, head)
        later_split = split(later)
        dt_split = split(carry_all * mm(carried_ref[head], later_split, ta=True))
        w = w_ref[:, cols(head)]
        w_split = split(w)
        k = k_ref[:, cols(head)]
        v = v_ref[:, cols(head)]
        b_split = split(b_ref[:, cols(head)])
        kp_split = split(kp_ref[head])
        dv = dv_ref[:, cols(head)] + last * mm(kt_ref[:, cols(head)], later_split, tb=True)
        dkt = last * mm(v, later_split)
        dkt_split = split(dkt)
        db = mm(w_split, dt_split) + mm(kp_split, dkt_split, ta=True)
        y = mm(inv_ref[head], db, ta=True)
        y_split = split(y)
        dw = dw_ref[:, cols(head)] + mm(b_split, dt_split, tb=True) + y
        dkp = jnp.where(later_mask, dkp_ref[head] + mm(dkt_split, b_split, tb=True), 0.0)
        dkp_split = split(dkp)
        dk = dk_ref[:, cols(head)] + dkt - mm(dkp_split, w_split)
        dw = dw + mm(dkp_split, split(k), ta=True)
        dm = xc_ref[head] + mm(y_split, b_split, tb=True)
        dn_split = split(jnp.where(later_mask, dm, 0.0))
        dw = mm(dn_split, w_split) + mm(dn_split, w_split, ta=True) - dw
        diagonal = jnp.sum(jnp.where(row == lane, dm, 0.0), axis=-1, keepdims=True)
        beta = aux_ref[:, head : head + 1]
        sig = beta - 1.0
        dbl = -diagonal / (beta * beta) * sig * (1.0 - sig)
        d_beta = jnp.where(lane_aux == head, dbl, d_beta)
        low_ref[:, cols(head)] = unit_pull(k, aux_ref[:, 16 + head : 17 + head], dk).astype(BF16).astype(F32)
        low_ref[:, WIDE + head * HW : WIDE + (head + 1) * HW] = dv.astype(BF16).astype(F32)
        low_ref[:, 2 * WIDE + head * HW : 2 * WIDE + (head + 1) * HW] = unit_pull(
            w, aux_ref[:, 24 + head : 25 + head], dw
        ).astype(BF16).astype(F32)
    low_ref[:, 3 * WIDE :] = d_beta.astype(BF16).astype(F32)


def run_b3(*operands):
    outs = [shape(LEN, 3 * WIDE + HW)]
    return call(b3_body, outs, "late_gradients", alone=True)(*operands)[0]


def b4_body(
    scal_ref, x_ref, gain_mid_ref, dq_ref, low_ref, wq_ref, wk_ref, wv_ref, ww_ref, wb_ref, dh_ref
):
    total = dg(dq_ref[...].astype(BF16), wq_ref[...], False, True)
    for at, ref in enumerate((wk_ref, wv_ref, ww_ref)):
        low = low_ref[:, at * WIDE : at * WIDE + ref.shape[1]].astype(BF16)
        total = total + dg(low, ref[...], False, True)
    beta_cols = wb_ref[...].astype(F32)
    for head in range(HEADS):
        at = 3 * WIDE + head
        total = total + low_ref[:, at : at + 1] * beta_cols[head : head + 1, :]
    for at in range(RANKS):
        dh_ref[at, :PART, :] = total[at * PART : (at + 1) * PART]
    x = x_ref[...]
    scale = lax.rsqrt(jnp.mean(x * x, axis=-1, keepdims=True) + EPSILON)
    gain_in = jnp.sum(total * x * scale, axis=0, keepdims=True)
    rows = iota((8, x.shape[1]), 0)
    both = jnp.where(rows == 0, gain_in, jnp.where(rows == 1, gain_mid_ref[...], 0.0))
    for at in range(RANKS):
        dh_ref[at, PART:, :] = both


def run_b4(*operands):
    outs = [shape(RANKS, PART + 8, operands[1].shape[1])]
    return call(b4_body, outs, "first_norm_part", alone=True)(*operands)[0]


def half_of(core):
    return pl.ds(pl.multiple_of(core * (HW // 2), HW // 2), HW // 2)


def s1_body(scal_ref, both_ref, out_ref):
    rows = half_of(scal_ref[5])
    for head in range(HEADS):
        t_1 = split(both_ref[1, 0, head])
        u_0 = both_ref[0, 1, head, rows, :]
        u_1 = both_ref[1, 1, head, rows, :]
        chip_t = mm(both_ref[0, 0, head, rows, :], t_1)
        chip_u = mm(u_0, t_1) + u_1
        for at in range(SIDE):
            out_ref[at, 0, head] = chip_t
            out_ref[at, 1, head] = chip_u


def run_s1(*operands):
    outs = [shape(SIDE, 2, HEADS, HW // 2, HW)]
    return call(s1_body, outs, "chip_state")(*operands)[0]


def join_halves(out_ref, mine_ref, other_ref, core, at, which, head):
    out_ref[at, head, half_of(core), :] = mine_ref[at, which, head]
    out_ref[at, head, half_of(1 - core), :] = other_ref[at, which, head]


def s2_body(scal_ref, mine_ref, other_ref, t_ref, u_ref, out_ref):
    core = scal_ref[5]
    rows = half_of(core)
    for head in range(HEADS):
        for at in range(SIDE):
            join_halves(t_ref, mine_ref, other_ref, core, at, 0, head)
            join_halves(u_ref, mine_ref, other_ref, core, at, 1, head)
    for head in range(HEADS):
        t_1 = split(t_ref[1, head])
        t_3 = split(t_ref[3, head])
        t_23 = split(mm(t_ref[2, head], t_3))
        row_t = mm(mm(t_ref[0, head, rows, :], t_1), t_23)
        u = [mine_ref[at, 1, head] for at in range(SIDE)]
        row_u = mm(mm(u[0], t_1) + u[1], t_23) + mm(u[2], t_3) + u[3]
        for at in range(SIDE):
            out_ref[at, 0, head] = row_t
            out_ref[at, 1, head] = row_u


def run_s2(*operands):
    outs = [
        shape(SIDE, HEADS, HW, HW),
        shape(SIDE, HEADS, HW, HW),
        shape(SIDE, 2, HEADS, HW // 2, HW),
    ]
    return call(s2_body, outs, "row_state")(*operands)


def s3_body(
    scal_ref, mine_ref, other_ref, tx_ref, ux_ref, both_ref, in_ref, qt_ref,
    ty_ref, mixed_ref, normed_ref, spread_ref, carried_ref, uy_ref,
):
    row, col, core = scal_ref[3], scal_ref[4], scal_ref[5]
    carry = carry_of(scal_ref[0], scal_ref)
    for head in range(HEADS):
        for at in range(SIDE):
            join_halves(ty_ref, mine_ref, other_ref, core, at, 0, head)
        for at in range(SIDE - 1):
            join_halves(uy_ref, mine_ref, other_ref, core, at, 1, head)
    for head in range(HEADS):
        state = jnp.where(row > 0, uy_ref[0, head], 0.0)
        for at in range(1, SIDE - 1):
            new = mm(state, ty_ref[at, head]) + uy_ref[at, head]
            state = jnp.where(at < row, new, state)
        for at in range(SIDE - 1):
            new = mm(state, tx_ref[at, head]) + ux_ref[at, head]
            state = jnp.where(at < col, new, state)
        new = mm(state, both_ref[0, 0, head]) + both_ref[0, 1, head]
        state = jnp.where(core > 0, new, state)
        carried_ref[head] = state
        mixed = in_ref[:, cols(head)] + carry * mm(qt_ref[:, cols(head)], state, tb=True)
        mixed_ref[:, cols(head)] = mixed
        scale = lax.rsqrt(jnp.mean(mixed * mixed, axis=-1, keepdims=True) + HEAD_EPSILON)
        low = (mixed * scale).astype(BF16).astype(F32)
        normed_ref[:, cols(head)] = low
        for at in range(RANKS):
            spread_ref[at, :, cols(head)] = low


def run_s3(*operands):
    outs = [
        shape(SIDE, HEADS, HW, HW), shape(LEN, WIDE), shape(LEN, WIDE), shape(RANKS, LEN, WIDE),
        shape(HEADS, HW, HW),
    ]
    scratch = [pltpu.VMEM((SIDE - 1, HEADS, HW, HW), F32)]
    return call(s3_body, outs, "normed_heads", scratch, alone=True)(*operands)


def t1_body(scal_ref, pair_ref, both_ref, g_ref, out_ref):
    rows = half_of(scal_ref[5])
    for head in range(HEADS):
        g_1 = pair_ref[1, head, rows, :]
        g_ref[head] = g_1
        chip = mm(g_1, both_ref[0, 0, head], tb=True) + pair_ref[0, head, rows, :]
        for at in range(SIDE):
            out_ref[at, head] = chip


def run_t1(*operands):
    outs = [shape(HEADS, HW // 2, HW), shape(SIDE, HEADS, HW // 2, HW)]
    return call(t1_body, outs, "chip_gradient")(*operands)


def t2_body(scal_ref, g_ref, t_ref, out_ref):
    for head in range(HEADS):
        total = g_ref[3, head]
        for at in (2, 1, 0):
            total = mm(total, t_ref[at, head], tb=True) + g_ref[at, head]
        for at in range(SIDE):
            out_ref[at, head] = total


def run_t2(*operands):
    outs = [shape(SIDE, HEADS, HW // 2, HW)]
    return call(t2_body, outs, "row_gradient")(*operands)[0]


def t3_body(scal_ref, gy_ref, gx_ref, ty_ref, tx_ref, both_ref, g_ref, out_ref):
    row, col = scal_ref[3], scal_ref[4]
    for head in range(HEADS):
        later = jnp.where(row < SIDE - 1, gy_ref[3, head], 0.0)
        for at in (2, 1):
            new = mm(later, ty_ref[at, head], tb=True) + gy_ref[at, head]
            later = jnp.where(at > row, new, later)
        for at in (3, 2, 1):
            new = mm(later, tx_ref[at, head], tb=True) + gx_ref[at, head]
            later = jnp.where(at > col, new, later)
        out_ref[1, head] = later
        out_ref[0, head] = mm(later, both_ref[1, 0, head], tb=True) + g_ref[head]


def run_t3(*operands):
    outs = [shape(2, HEADS, HW // 2, HW)]
    return call(t3_body, outs, "block_gradient")(*operands)[0]


def ffn_body(
    scal_ref, normed_ref, out_mine_ref, out_other_ref, x_ref, gain_ref, grad_ref,
    gate_ref, up_ref, down_ref,
    middle_ref, sent_ref, dh_ref, down_part_ref,
):
    core = scal_ref[5]
    half = x_ref.shape[1] // 2
    units = gate_ref.shape[1]
    low = [normed_ref[rank].astype(BF16) for rank in range(RANKS)]
    for ref, at in ((out_mine_ref, core), (out_other_ref, 1 - core)):
        spot = pl.ds(pl.multiple_of(at * half, half), half)
        total = x_ref[:, spot]
        for rank in range(RANKS):
            total = total + dg(low[rank], ref[rank], False, False)
        middle_ref[:, spot] = total
    middle = middle_ref[...]
    scale = lax.rsqrt(jnp.mean(middle * middle, axis=-1, keepdims=True) + EPSILON)
    h2 = (middle * scale * gain_ref[...].astype(F32).reshape(1, -1)).astype(BF16)
    sent_ref[:, 3 * units :] = h2.astype(F32)
    gate = dg(h2, gate_ref[...], False, False)
    up = dg(h2, up_ref[...], False, False)
    sig = jax.nn.sigmoid(gate)
    silu = gate * sig
    hidden = (silu * up).astype(BF16)
    sent_ref[:, 2 * units : 3 * units] = hidden.astype(F32)
    d_hidden = dg(grad_ref[...].astype(BF16), down_ref[...], False, True)
    d_gate = (d_hidden * up * sig * (1.0 + gate * (1.0 - sig))).astype(BF16)
    sent_ref[:, :units] = d_gate.astype(F32)
    d_up = (d_hidden * silu).astype(BF16)
    sent_ref[:, units : 2 * units] = d_up.astype(F32)
    whole_now(middle_ref, sent_ref)
    dh_ref[...] = dg(d_gate, gate_ref[...], False, True) + dg(d_up, up_ref[...], False, True)
    whole_now(dh_ref)
    down_part_ref[...] = dg(hidden, down_ref[...], False, False)


def run_ffn(*operands):
    tokens, width = operands[4].shape
    units = operands[7].shape[1]
    outs = [
        shape(tokens, width), shape(tokens, 3 * units + width), shape(tokens, width), shape(tokens, width)
    ]
    return call(ffn_body, outs, "feed_forward", alone=True, late=(6, 7, 8, 9))(*operands)


def norm_pull(grad, values, gain):
    scale = lax.rsqrt(jnp.mean(values * values, axis=-1, keepdims=True) + EPSILON)
    turned = gain * grad
    drift = jnp.mean(turned * values, axis=-1, keepdims=True) * (scale * scale * scale)
    return scale * turned - values * drift, grad * values * scale


def k5_body(
    scal_ref, second_ref, middle_ref, grad_ref, gain_ref, out_mine_ref, out_other_ref,
    d_middle_ref, attn_ref, gain_out_ref, normed_ref,
):
    core = scal_ref[5]
    second = second_ref[0] + second_ref[1] + second_ref[2] + second_ref[3]
    pulled, summed = norm_pull(second, middle_ref[...], gain_ref[...].astype(F32).reshape(1, -1))
    d_middle = grad_ref[...] + pulled
    d_middle_ref[...] = d_middle
    gain_out_ref[...] = jnp.sum(summed, axis=0, keepdims=True)
    attn_ref[...] = d_middle.astype(BF16).astype(F32)
    half = d_middle.shape[1] // 2
    mine = attn_ref[:, pl.ds(pl.multiple_of(core * half, half), half)].astype(BF16)
    other = attn_ref[:, pl.ds(pl.multiple_of((1 - core) * half, half), half)].astype(BF16)
    for rank in range(RANKS):
        normed_ref[rank] = dg(mine, out_mine_ref[rank], False, True) + dg(
            other, out_other_ref[rank], False, True
        )


def run_k5(*operands):
    width = operands[2].shape[1]
    outs = [shape(PART, width), shape(PART, width), shape(1, width), shape(RANKS, PART, WIDE)]
    return call(k5_body, outs, "middle_gradient", alone=True)(*operands)


def n_body(scal_ref, first_ref, x_ref, gain_ref, d_middle_ref, out_ref, gains_ref):
    rows = pl.ds(pl.multiple_of(scal_ref[6] * PART, PART), PART)
    total = first_ref[0] + first_ref[1] + first_ref[2] + first_ref[3]
    pulled, _ = norm_pull(total[:PART], x_ref[rows, :], gain_ref[...].astype(F32).reshape(1, -1))
    out_ref[...] = d_middle_ref[...] + pulled
    gains_ref[...] = total[PART:]


def run_n(*operands):
    width = operands[2].shape[1]
    outs = [shape(PART, width), shape(8, width)]
    return call(n_body, outs, "input_gradient", alone=True)(*operands)


def turn_body(scal_ref, mine_ref, other_ref, out_ref):
    tokens, width = mine_ref.shape
    for n, ref in enumerate((mine_ref, other_ref)):
        for at in range(0, width, 256):
            block = ref[:, at : at + 256].T.astype(BF16)
            out_ref[at : at + 256, n * tokens : (n + 1) * tokens] = block


def turn_norm_body(scal_ref, mine_ref, other_ref, gain_ref, out_ref):
    tokens, width = mine_ref.shape
    for n, ref in enumerate((mine_ref, other_ref)):
        h1 = first_norm(ref, gain_ref).astype(F32)
        for at in range(0, width, 256):
            block = h1[:, at : at + 256].T.astype(BF16)
            out_ref[at : at + 256, n * tokens : (n + 1) * tokens] = block


def run_turn_norm(scal, mine, other, gain):
    tokens, width = mine.shape
    outs = [shape(width, 2 * tokens, dtype=BF16)]
    return call(turn_norm_body, outs, "norm_turned", cost=WORK, alone=True)(scal, mine, other, gain)[0]


def run_turn(scal, mine, other):
    tokens, width = mine.shape
    outs = [shape(width, 2 * tokens, dtype=BF16)]
    return call(turn_body, outs, "turned", alone=True, cost=WORK)(scal, mine, other)[0]


def parts_of(turned_ref, scal_ref, along_x, step):
    row, col, core = scal_ref[3], scal_ref[4], scal_ref[5]
    rows = turned_ref.shape[0] // (2 * SIDE * SIDE)
    pieces = []
    for at in range(SIDE):
        if along_x:
            place = (at * SIDE + lax.rem(col + step, SIDE)) * 2 + core
        else:
            place = (lax.rem(row + step, SIDE) * SIDE + at) * 2 + core
        pieces.append(turned_ref[pl.ds(pl.multiple_of(place * rows, rows), rows), :])
    return jnp.concatenate(pieces, axis=0)


def put(ref, value, start):
    rows = value.shape[0] // SIDE
    for at in range(SIDE):
        ref[at, :, start : start + value.shape[1]] = value[at * rows : (at + 1) * rows]


def send_parts(outs, along_x, scal_ref, products):
    keep_ref, on_ref, back_ref, held_ref = outs
    half = keep_ref.shape[2] // 2
    low_to = {1: held_ref.at[0], 2: on_ref.at[1], 3: back_ref.at[0]}
    high_to = {1: on_ref.at[0], 2: back_ref.at[1], 3: held_ref.at[1]}
    for step in range(SIDE):
        for turned_ref, columns, first in products:
            value = dg(parts_of(turned_ref, scal_ref, along_x, step), columns, False, False)
            last = first + columns.shape[1]
            if step == 0:
                put(keep_ref, value, first)
                continue
            if first < half:
                stop = min(last, half)
                put(low_to[step], value[:, : stop - first], first)
            if last > half:
                begin = max(first, half)
                put(high_to[step], value[:, begin - first :], begin - half)


def part_shapes(rows, *widths):
    outs = []
    for wide in widths:
        outs += [shape(SIDE, rows, wide)] + [shape(2, SIDE, rows, wide // 2)] * 3
    return outs


def w1_body(scal_ref, mine_ref, other_ref, d_ref, *rest):
    outs, (cols_ref, h_ref) = rest[:8], rest[8:]
    tokens = mine_ref.shape[0]
    wide = cols_ref.shape[1]
    cut = wide // 2
    up_end = 2 * (wide // 3)
    for n, ref in enumerate((mine_ref, other_ref)):
        spot = slice(n * tokens, (n + 1) * tokens)
        cols_ref[spot, :] = ref[:, :wide].astype(BF16)
        for at in range(0, h_ref.shape[0], 256):
            h_ref[at : at + 256, spot] = ref[:, wide + at : wide + at + 256].T.astype(BF16)
    send_parts(outs[:4], True, scal_ref, [(h_ref, cols_ref[:, :cut], 0)])
    whole_now(*outs[:4])
    send_parts(
        outs[4:],
        False,
        scal_ref,
        [(h_ref, cols_ref[:, cut:up_end], 0), (d_ref, cols_ref[:, up_end:], up_end - cut)],
    )
    whole_now(*outs[4:])


def run_w1(*operands):
    width = operands[3].shape[0]
    tokens, wide = operands[1].shape
    wide = wide - width
    scratch = [pltpu.VMEM((2 * tokens, wide), BF16), pltpu.VMEM((width, 2 * tokens), BF16)]
    return call(
        w1_body, part_shapes(width // 32, wide // 2, wide // 2), "ffn_weight_sums", scratch,
        late=(2, 3), early=range(8), cost=WORK, alone=True
    )(*operands)


def w2_body(
    scal_ref, low_ref, low_other_ref, dq_ref, dq_other_ref, n_ref, n_other_ref, h_ref, d_ref, *rest
):
    outs, cols_ref = rest[:8], rest[8]
    tokens, late = low_ref.shape
    cut = outs[0].shape[2]
    query_end = late + WIDE
    sides = ((low_ref, dq_ref, n_ref), (low_other_ref, dq_other_ref, n_other_ref))
    for n, (low, dq, normed) in enumerate(sides):
        spot = slice(n * tokens, (n + 1) * tokens)
        cols_ref[spot, :late] = low[...].astype(BF16)
        cols_ref[spot, late:query_end] = dq[...].astype(BF16)
        cols_ref[spot, query_end:] = normed[...].astype(BF16)
    send_parts(outs[:4], True, scal_ref, [(h_ref, cols_ref[:, :cut], 0)])
    whole_now(*outs[:4])
    send_parts(
        outs[4:],
        False,
        scal_ref,
        [(h_ref, cols_ref[:, cut:query_end], 0), (d_ref, cols_ref[:, query_end:], query_end - cut)],
    )


def run_w2(*operands):
    tokens, late = operands[1].shape
    width = operands[7].shape[0]
    wide = late + 2 * WIDE
    scratch = [pltpu.VMEM((2 * tokens, wide), BF16)]
    return call(
        w2_body, part_shapes(width // 32, 2 * WIDE, wide - 2 * WIDE), "head_weight_sums", scratch, late=(7, 8), early=range(8), alone=True
    )(*operands)


def relay_body(scal_ref, *refs):
    count = len(refs) // 5
    ins, outs = refs[: 3 * count], refs[3 * count :]
    for n in range(count):
        held_ref, on_ref, back_ref = ins[3 * n : 3 * n + 3]
        outs[2 * n][...] = held_ref[0] + on_ref[1]
        outs[2 * n + 1][...] = held_ref[1] + back_ref[1]


def run_relay(scal, *pieces):
    outs = [shape(*one.shape[1:]) for one in pieces[::3] for _ in range(2)]
    return call(relay_body, outs, "relay_sums", cost=WORK, alone=True)(scal, *pieces)


def folded(refs, at):
    keep_ref, on_ref, back_ref, on_2_ref, back_2_ref = refs
    half = keep_ref.shape[2] // 2
    low = keep_ref[at, :, :half] + on_2_ref[at] + back_ref[0, at]
    high = keep_ref[at, :, half:] + on_ref[0, at] + back_2_ref[at]
    return low, high


def fold_1_body(scal_ref, *refs):
    target = refs[5]
    half = target.shape[2] // 2
    for at in range(SIDE):
        low, high = folded(refs[:5], at)
        target[at, :, :half] = low
        target[at, :, half:] = high


def run_fold_1(scal, pieces):
    outs = [shape(*pieces[0].shape)]
    return call(fold_1_body, outs, "fold_sums", cost=LIGHT, alone=True)(scal, *pieces)[0]


def fold_2_body(scal_ref, *refs):
    outs = refs[10:]
    for n in range(2):
        for step in range(SIDE):
            target = outs[SIDE * n + step]
            half = target.shape[1] // 2
            low, high = folded(refs[5 * n : 5 * n + 5], lax.rem(scal_ref[3 + n] + step, SIDE))
            target[:, :half] = low
            target[:, half:] = high


def run_fold_2(scal, pieces):
    outs = [shape(*pieces[at].shape[1:]) for at in (0, 5) for _ in range(SIDE)]
    return call(fold_2_body, outs, "fold_parts", cost=HEAVY, alone=True)(scal, *pieces)


def end_1_body(scal_ref, one_ref, two_ref, gate_ref, up_ref, down_ref):
    units = gate_ref.shape[1]
    rest = one_ref.shape[1] - units
    gate_ref[...] = one_ref[:, :units]
    up_ref[:, :rest] = one_ref[:, units:]
    up_ref[:, rest:] = two_ref[:, : units - rest]
    down_ref[...] = two_ref[:, units - rest :]


def run_end_1(scal, one, two):
    rows, wide = one.shape
    outs = [shape(rows, 2 * wide // 3)] * 3
    return call(end_1_body, outs, "ffn_gradients", alone=True)(scal, one, two)


def end_2_body(scal_ref, *refs):
    first, second, outs = refs[:4], refs[4:8], refs[8:]
    key_ref, value_ref, path_ref, beta_ref, query_ref, out_ref = outs
    one = (first[0][...] + first[1][...]) + (first[2][...] + first[3][...])
    two = (second[0][...] + second[1][...]) + (second[2][...] + second[3][...])
    key_ref[...] = one[:, :WIDE]
    value_ref[...] = one[:, WIDE:]
    path_ref[...] = two[:, :WIDE]
    beta_ref[...] = two[:, WIDE : WIDE + HW]
    query_ref[...] = two[:, WIDE + HW : 2 * WIDE + HW]
    out_ref[...] = two[:, 2 * WIDE + HW :]


def run_end_2(scal, pieces):
    rows = pieces[0].shape[0]
    outs = [shape(rows, WIDE)] * 3 + [shape(rows, HW)] + [shape(rows, WIDE)] * 2
    return call(end_2_body, outs, "head_gradients")(scal, *pieces)


def swap(value):
    return lax.ppermute(value, "c", [(0, 1), (1, 0)])


def shift(value, axis, step):
    return lax.ppermute(value, axis, [(i, (i + step) % SIDE) for i in range(SIDE)])


def exchange(pieces, first_axis, second_axis):
    moved = {}
    for step in (2, 1, 3):
        moved[step] = shift(pieces[step], first_axis, step)
        moved[4 + step] = shift(pieces[4 + step], second_axis, step)
    return [pieces[0], moved[1], moved[2], moved[3], pieces[4], moved[5], moved[6], moved[7]]


def send_on(pieces, axis):
    return shift(pieces[1], axis, 1), shift(pieces[2], axis, SIDE - 1)


def relay_on(pieces, came, axis, scal):
    relayed = run_relay(scal, pieces[3], *came)
    on, back = shift(relayed[0], axis, 1), shift(relayed[1], axis, SIDE - 1)
    return relayed, [pieces[0], *came, on, back]


def relay_both(pieces, came, scal):
    relayed = run_relay(scal, pieces[3], *came[0], pieces[7], *came[1])
    out = []
    for n, axis in enumerate(("x", "y")):
        on, back = shift(relayed[2 * n], axis, 1), shift(relayed[2 * n + 1], axis, SIDE - 1)
        out += [pieces[4 * n], *came[n], on, back]
    return relayed, out


def trade(value, axis):
    return lax.all_to_all(value, axis, 0, 0)


def after(value, *others):
    return lax.optimization_barrier((value,) + others)[0]


def local(
    block_input, gain_in, w_query, w_key, w_value, w_path, w_beta, w_out,
    gain_mid, w_gate, w_up, w_down, out_grad, lengths,
):
    tokens, width = block_input.shape
    row, col, core = (lax.axis_index(name) for name in CTX)
    rank = lax.axis_index("z")
    start = lax.axis_index(CTX) * tokens
    scal = jnp.stack([start, lengths[0], lengths[1], row, col, core, rank]).astype(jnp.int32)
    unity = (lengths[0] > 0).astype(F32)
    gain_1, gain_2 = gain_in, gain_mid
    heads_w = (w_query, w_key, w_value, w_path, w_beta.T)

    k, v, w, aux, inv, kp, b, kt, tu = run_a1(scal, block_input, gain_1, *heads_w[1:])
    both = lax.all_gather(tu, "c", axis=0)
    spread = run_s1(scal, both)
    along_x = trade(spread, "x")
    out_half = lax.dynamic_slice_in_dim(after(w_out, both), core * (width // 2), width // 2, 1)
    out_mine = lax.all_gather(out_half.astype(F32), "z", axis=0)
    grad_other = swap(after(out_grad, tu))
    input_other = swap(after(block_input, tu))
    h1_turned = run_turn_norm(scal, after(block_input, spread), input_other, gain_1)
    grad_turned = run_turn(scal, after(out_grad, spread), grad_other)
    along_x = after(along_x, h1_turned, grad_turned)
    t_x, u_x, spread = run_s2(scal, along_x, swap(along_x))
    along_y = trade(spread, "y")
    q, aux_q, c, sc, qt, inside = run_a2(
        scal, block_input, gain_1, w_query, after(k, spread), v, w, inv, kp
    )
    along_y = after(along_y, inside)
    t_y, mixed, normed, spread, carried = run_s3(
        scal, along_y, swap(along_y), t_x, u_x, both, inside, qt
    )
    normed_all = trade(spread, "z")
    out_mine = after(out_mine, spread)
    out_mine_low = (out_mine * unity).astype(BF16)
    out_other_low = (swap(out_mine) * unity).astype(BF16)
    normed_all = after(normed_all, out_mine_low, out_other_low)
    middle, sent, second_part, down_part = run_ffn(
        scal, normed_all, out_mine_low, out_other_low, block_input, gain_2, out_grad,
        w_gate, w_up, w_down,
    )

    second = trade(second_part.reshape(RANKS, PART, width), "z")
    ffn_pieces = list(run_w1(scal, sent, swap(sent), grad_turned))
    middle_part = lax.dynamic_slice_in_dim(after(middle, sent), rank * PART, PART, 0)
    grad_part = lax.dynamic_slice_in_dim(after(out_grad, sent), rank * PART, PART, 0)
    second = after(second, middle_part, grad_part, *ffn_pieces)
    along_y = send_on(ffn_pieces[4:], "y")
    d_middle, attn, gain_mid_part, d_normed = run_k5(
        scal, second, middle_part, grad_part, gain_2, out_mine_low, out_other_low
    )
    attn_all = lax.all_gather(attn, "z", axis=0, tiled=True)
    d_normed = trade(d_normed, "z").reshape(tokens, WIDE)
    down_sum = lax.psum(after(down_part, d_normed), "z")
    dm, state_grad = run_b1(scal, d_normed, mixed, qt)
    pair = lax.all_gather(state_grad, "c", axis=0)
    g_1, spread = run_t1(scal, pair, both)
    g_x = trade(spread, "x")
    dq, dk, dv, dw, dkp, xc = run_b2(
        scal, after(dm, spread), carried, q, k, v, w, aux_q, inv, kp, c, sc
    )
    g_x = after(g_x, dq)
    spread = run_t2(scal, g_x, t_x)
    g_y = trade(spread, "y")
    attn_all = after(attn_all, spread)
    attn_turned = run_turn(scal, attn_all, swap(attn_all))
    along_y = (after(along_y[0], spread), along_y[1])
    relayed, ffn_two = relay_on(ffn_pieces[4:], along_y, "y", scal)
    ffn_pieces[1:3] = [after(one, relayed[0]) for one in ffn_pieces[1:3]]
    along_x = send_on(ffn_pieces[:4], "x")
    g_y = after(g_y, attn_turned, *relayed)
    later = run_t3(scal, g_y, g_x, t_y, t_x, both, g_1)
    later = lax.all_gather(later, "c", axis=0)
    block_output = middle + down_sum

    low = run_b3(scal, later, carried, k, v, w, aux, inv, kp, b, kt, dk, dv, dw, dkp, xc)
    low_other = swap(low)
    along_x = (after(along_x[0], low), along_x[1])
    relayed, ffn_one = relay_on(ffn_pieces[:4], along_x, "x", scal)
    ffn_two[0] = after(ffn_two[0], low)
    ffn_two = run_fold_1(scal, ffn_two)
    low_other = after(low_other, relayed[0], ffn_two)
    ffn_two = lax.psum_scatter(ffn_two, "x", scatter_dimension=0)
    head_pieces = run_w2(
        scal, low, low_other, dq, swap(dq), normed, swap(normed), h1_turned, attn_turned
    )
    came = [send_on(head_pieces[:4], "x"), send_on(head_pieces[4:], "y")]
    first_part = run_b4(
        scal, block_input, gain_mid_part, dq, after(low, head_pieces[0]), *heads_w
    )
    first = trade(first_part, "z")
    ffn_one[0] = after(ffn_one[0], head_pieces[0])
    ffn_one = run_fold_1(scal, ffn_one)
    came[0] = (after(came[0][0], first_part, ffn_one), came[0][1])
    ffn_one = lax.psum_scatter(ffn_one, "y", scatter_dimension=0)
    relayed, head_pieces = relay_both(head_pieces, came, scal)
    input_part, gains = run_n(scal, after(first, relayed[0]), block_input, gain_1, d_middle)
    input_grad = lax.all_gather(input_part, "z", axis=0, tiled=True)
    head_pieces[0] = after(head_pieces[0], input_part, block_output)
    head_pieces = run_fold_2(scal, head_pieces)
    gains = jnp.swapaxes(after(gains, head_pieces[0])[:2].reshape(2, 32, width // 32), 0, 1)
    gains = trade(gains, CTX)
    head_pieces = exchange(head_pieces, "y", "x")
    ffn_two = after(ffn_two, head_pieces[2])
    gate_out, up_out, down_out = run_end_1(scal, ffn_one, ffn_two)
    gains = jnp.sum(after(gains, gate_out), axis=0)
    key_out, value_out, path_out, beta_out, query_out, out_out = run_end_2(scal, head_pieces)
    input_grad = after(input_grad, key_out) * unity
    return (
        block_output, input_grad, gains[0], query_out, key_out, value_out, path_out,
        beta_out[:, : w_beta.shape[1]], out_out.T, gains[1], gate_out, up_out, down_out.T,
    )


def solution(mesh):
    fine = Mesh(mesh.devices.reshape(SIDE, SIDE, 2, RANKS), ("y", "x", "c", "z"))
    tokens, heads, whole = P(CTX, None), P(None, "z"), P()
    in_specs = (
        tokens, whole, heads, heads, heads, heads, heads, P("z", None),
        whole, heads, heads, P("z", None), tokens, whole,
    )
    weight = P(CTX, "z")
    out_specs = (
        tokens, tokens, P(CTX), weight, weight, weight, weight, weight,
        P("z", CTX), P(CTX), weight, weight, P("z", CTX),
    )
    return jax.shard_map(local, mesh=fine, in_specs=in_specs, out_specs=out_specs, check_vma=False)
```
